32 devices in a mesh: ens: 2 (over y), gx: 4 (over z), gy: 2 (over x), gz: 2 (over core).
Axes of the slice: x: 2, y: 2, z: 4, core: 2. Of those that a mesh axis runs over, the one named last changes fastest.
Arguments:
- velocity: float32 [3, 128, 64, 256], P(None, ('ens', 'gx'), 'gy', 'gz'), parts along dimension 1, may hold values from -6 to 6
- stress: float32 [6, 128, 64, 256], P(None, ('ens', 'gx'), 'gy', 'gz'), parts along dimension 1, may hold values from -6 to 6
- memory: float32 [6, 128, 64, 256], P(None, ('ens', 'gx'), 'gy', 'gz'), parts along dimension 1, may hold values from -3 to 3
- material: int32 [128, 64, 256], P(('ens', 'gx'), 'gy', 'gz'), parts along dimension 0, may hold values from 0 to 7
- material_table: float32 [5, 16], P(None, 'ens'), parts along dimension 1, may hold values from 0.4 to 1.6
- fault_mask: int32 [128, 256], P(('ens', 'gx', 'gy'), 'gz'), parts along dimension 0, may hold values 0 or 1
- zone_label: int32 [128, 256], P(('ens', 'gx', 'gy'), 'gz'), parts along dimension 0, may hold values from 0 to 3
- patch_anchor: int32 [4], P('ens'), parts along dimension 0, may hold values from 0 to 240, as said below
- friction_table: float32 [3, 8], P(None, 'ens'), parts along dimension 1, may hold values from 0.4 to 1.6
- prestress: float32 [128, 2, 256], P(('ens', 'gx', 'gy'), None, 'gz'), parts along dimension 0, may hold values from -8 to 8
- normal_stress: float32 [128, 256], P(('ens', 'gx', 'gy'), 'gz'), parts along dimension 0, may hold values from 2 to 8
- slip_path: float32 [128, 256], P(('ens', 'gx', 'gy'), 'gz'), parts along dimension 0, may hold values from 0 to 0.4
Outputs:
- new_velocity: float32 [3, 128, 64, 256], P(None, ('ens', 'gx'), 'gy', 'gz'), parts along dimension 1
- new_stress: float32 [6, 128, 64, 256], P(None, ('ens', 'gx'), 'gy', 'gz'), parts along dimension 1
- new_memory: float32 [6, 128, 64, 256], P(None, ('ens', 'gx'), 'gy', 'gz'), parts along dimension 1
- new_slip: float32 [128, 256], P(('ens', 'gx', 'gy'), 'gz'), parts along dimension 0
The draws below stay inside these ranges and needn't reach their ends.
There are 2 independent parts, one for each index of `ens`. The reference program is written for one: setup_inputs(seed, part) draws one part's arguments, and reference() takes and returns one part's arrays. A program takes and returns all parts, laid end to end along the dimension named above; each array names one. Nothing has to cross between parts.
Inputs may be any that keep to these rules, and one draw needn't show every extreme that they name: patch_anchor[0] lies in 0 to 48 and patch_anchor[1] in 0 to 240; the index whose range is longer (the first one if both are equal) is at the far end of its range.
All inputs are finite; a program needn't handle non-finite values. No bound on the sum of `fault_mask` on one device may be relied on, other than what follows from the above.
Results may differ from the reference program's by a relative error of at most 0.0001.
Values sent between devices are 32-bit elements; how exact they have to be, the bound alone decides.
No kernel may reach another device: no remote copies, remote signals or barrier semaphores. Data moves between devices by JAX's collectives and lax.ppermute only.
A program may use at most 64 MiB of HBM per device.

```python
import jax
import jax.numpy as jnp
from jax import lax

STEPS = 2
CLASSES = 8
ZONES = 4
PATCH = 8
NX = 64
NY = 64
NZ = 256


def draw_patch_anchor(key, part):
    key = jax.random.fold_in(key, 7)
    key_strike, key_depth = jax.random.split(key)
    span_along = NX - 2 * PATCH
    span_depth = NZ - 2 * PATCH
    along = jax.random.randint(key_strike, (1,), 0, span_along + 1)
    depth = jax.random.randint(key_depth, (1,), 0, span_depth + 1)
    if span_along >= span_depth:
        along = jnp.full((1,), span_along, jnp.int32)
    else:
        depth = jnp.full((1,), span_depth, jnp.int32)
    return jnp.concatenate([along.astype(jnp.int32), depth.astype(jnp.int32)]).astype(jnp.int32)


def set_ends(result, own_key, low, largest):
    spot = [jax.random.randint(jax.random.fold_in(own_key, axis), (), 0, length) for axis, length in enumerate(result.shape)]
    longest = result.shape.index(max(result.shape))
    beside = spot[:longest] + [(spot[longest] + 1) % result.shape[longest]] + spot[longest + 1:]
    return result.at[tuple(spot)].set(low).at[tuple(beside)].set(largest)


def shard_levels(rng, shape, pieces, low, high):
    gain, own = 1.0, jax.random.fold_in(rng, 6)
    for dim, parts in pieces:
        heights = jnp.exp(jax.random.uniform(jax.random.fold_in(own, dim), (parts,), jnp.float32, low / len(pieces), high / len(pieces)))
        gain = gain * jnp.repeat(heights, shape[dim] // parts).reshape([-1 if axis == dim else 1 for axis in range(len(shape))])
    return gain


def normal_values(rng, dims, width, most, cuts=(), held_as=jnp.bfloat16):
    entries = jax.random.normal(rng, dims, jnp.float32) * width
    if len(cuts) > 0:
        entries = shard_levels(rng, dims, cuts, -0.22, 0.18) * entries
    return jnp.clip(entries, min=-most, max=most).astype(held_as)


def setup_inputs(seed: int = 0, part: int = 0) -> dict:
    splits = jax.random.split(jax.random.key(seed), 13)
    own_keys = jax.random.split(jax.random.fold_in(splits[12], part), 13)
    return {
        "velocity": normal_values(own_keys[0], (3, NX, NY, NZ), 1.0, 6.0, ((1, 4), (2, 2), (3, 2)), jnp.float32),
        "stress": normal_values(own_keys[1], (6, NX, NY, NZ), 1.0, 6.0, ((1, 4), (2, 2), (3, 2)), jnp.float32),
        "memory": normal_values(own_keys[2], (6, NX, NY, NZ), 0.5, 3.0, ((1, 4), (2, 2), (3, 2)), jnp.float32),
        "material": set_ends(jax.random.randint(own_keys[3], (NX, NY, NZ), 0, CLASSES), jax.random.fold_in(own_keys[3], 1), 0, CLASSES - 1).astype(jnp.int32),
        "material_table": jnp.clip(jax.random.uniform(own_keys[4], (5, CLASSES), jnp.float32, 0.4, 1.6), 0.4, 1.6),
        "fault_mask": set_ends((jax.random.randint(own_keys[5], (NX, NZ), 0, 4) < 3).astype(jnp.int32), jax.random.fold_in(own_keys[5], 1), 0, 1),
        "zone_label": set_ends(jax.random.randint(own_keys[6], (NX, NZ), 0, ZONES), jax.random.fold_in(own_keys[6], 1), 0, ZONES - 1).astype(jnp.int32),
        "patch_anchor": draw_patch_anchor(jax.random.fold_in(jax.random.fold_in(splits[12], part), 71), part),
        "friction_table": jnp.clip(jax.random.uniform(own_keys[8], (3, ZONES), jnp.float32, 0.4, 1.6), 0.4, 1.6),
        "prestress": normal_values(own_keys[9], (NX, 2, NZ), 2.0, 8.0, ((0, 8), (2, 2)), jnp.float32),
        "normal_stress": jnp.clip(2.0 + 6.0 * jax.random.uniform(own_keys[10], (NX, NZ), jnp.float32) ** shard_levels(own_keys[10], (NX, NZ), ((0, 8), (1, 2)), -0.2, 0.2), 2.0, 8.0),
        "slip_path": jnp.clip(0.4 * jax.random.uniform(own_keys[11], (NX, NZ), jnp.float32) ** shard_levels(own_keys[11], (NX, NZ), ((0, 8), (1, 2)), -0.2, 0.2), 0.0, 0.4),
    }


coef_near = 9.0 / 8.0
coef_far = -1.0 / 24.0
time_step = 0.15

def shifted(field, axis, start, count):
    return lax.slice_in_dim(field, start, start + count, axis=axis)

def forward_diff(field, axis):
    count = field.shape[axis] - 4
    return coef_near * (shifted(field, axis, 3, count) - shifted(field, axis, 2, count)) + coef_far * (shifted(field, axis, 4, count) - shifted(field, axis, 1, count))

def backward_diff(field, axis):
    count = field.shape[axis] - 4
    return coef_near * (shifted(field, axis, 2, count) - shifted(field, axis, 1, count)) + coef_far * (shifted(field, axis, 3, count) - shifted(field, axis, 0, count))

def accelerate(along_x, along_y, along_z):
    first = forward_diff(along_x[0], 0) + backward_diff(along_y[0], 1) + backward_diff(along_z[0], 2)
    second = backward_diff(along_x[1], 0) + forward_diff(along_y[1], 1) + backward_diff(along_z[1], 2)
    third = backward_diff(along_x[2], 0) + backward_diff(along_y[2], 1) + forward_diff(along_z[2], 2)
    return jnp.stack([first, second, third])

def strain_rates(along_x, along_y, along_z):
    exx = backward_diff(along_x[0], 0)
    eyy = backward_diff(along_y[1], 1)
    ezz = backward_diff(along_z[2], 2)
    exy = forward_diff(along_y[0], 1) + forward_diff(along_x[1], 0)
    exz = forward_diff(along_z[0], 2) + forward_diff(along_x[2], 0)
    eyz = forward_diff(along_z[1], 2) + forward_diff(along_y[2], 1)
    return (exx, eyy, ezz, exy, exz, eyz)

def properties(material, material_table):
    labels = jnp.arange(CLASSES, dtype=jnp.int32)[:, None, None, None]
    onehot = (material[None] == labels).astype(jnp.float32)
    return jnp.einsum('rc,cxyz->rxyz', material_table, onehot, precision=lax.Precision.HIGHEST)

def update_stress(stress, memory, rates, props):
    lame = props[0]
    shear = props[1]
    relax = props[3]
    anelastic = 0.3 * props[4]
    volume = rates[0] + rates[1] + rates[2]
    elastic = jnp.stack([lame * volume + 2.0 * shear * rates[0], lame * volume + 2.0 * shear * rates[1], lame * volume + 2.0 * shear * rates[2], shear * rates[3], shear * rates[4], shear * rates[5]])
    decay = jnp.exp(-time_step / relax)
    new_memory = decay * memory - (1.0 - decay) * anelastic * elastic
    new_stress = stress + time_step * (elastic + new_memory)
    return (new_stress, new_memory)

def friction(faces, prestress, normal_stress, slip, zone_label, fault_mask, inpatch, friction_table):
    labels = jnp.arange(ZONES, dtype=jnp.int32)[:, None, None]
    onehot = (zone_label[None] == labels).astype(jnp.float32)
    params = jnp.einsum('pk,krc->prc', friction_table, onehot, precision=lax.Precision.HIGHEST)
    dynamic = 0.4 * params[0]
    static = jnp.where(inpatch, dynamic, dynamic + 0.5 * params[1])
    distance = 0.2 * params[2]
    minus_x, minus_z, minus_b = (faces[:, 0], faces[:, 1], faces[:, 2])
    plus_x, plus_z, plus_b = (faces[:, 3], faces[:, 4], faces[:, 5])
    bsum = minus_b + plus_b
    trial_x = (plus_x - minus_x) / (time_step * bsum) + prestress[:, 0]
    trial_z = (plus_z - minus_z) / (time_step * bsum) + prestress[:, 1]
    size_trial = jnp.sqrt(trial_x * trial_x + trial_z * trial_z)
    weaken = jnp.minimum(slip / distance, 1.0)
    strength = (static - (static - dynamic) * weaken) * normal_stress
    factor = jnp.where(fault_mask == 1, strength / jnp.maximum(size_trial, strength), 1.0)
    jump_x = trial_x * factor - prestress[:, 0]
    jump_z = trial_z * factor - prestress[:, 1]
    new_slip = slip + time_step * time_step * bsum * (size_trial - size_trial * factor)
    change = jnp.stack([jump_x * time_step * minus_b, jump_z * time_step * minus_b, -jump_x * time_step * plus_b, -jump_z * time_step * plus_b], axis=1)
    return (change, new_slip)

def pad_axis(field, axis):
    widths = [(0, 0)] * field.ndim
    widths[axis] = (2, 2)
    return jnp.pad(field, widths)

def velocity_block(velocity, stress, buoyancy):
    along_x = tuple((pad_axis(stress[comp], 0) for comp in (0, 3, 4)))
    along_y = tuple((pad_axis(stress[comp], 1) for comp in (3, 1, 5)))
    along_z = tuple((pad_axis(stress[comp], 2) for comp in (4, 5, 2)))
    return velocity + time_step * buoyancy * accelerate(along_x, along_y, along_z)

def stress_block(velocity, stress, memory, props):
    along_x = tuple((pad_axis(velocity[comp], 0) for comp in range(3)))
    along_y = tuple((pad_axis(velocity[comp], 1) for comp in range(3)))
    along_z = tuple((pad_axis(velocity[comp], 2) for comp in range(3)))
    return update_stress(stress, memory, strain_rates(along_x, along_y, along_z), props)

def reference(velocity, stress, memory, material, material_table, fault_mask, zone_label, patch_anchor, friction_table, prestress, normal_stress, slip_path):
    props = properties(material, material_table)
    middle = NY // 2
    rows = jnp.arange(NX, dtype=jnp.int32)[:, None]
    depths = jnp.arange(NZ, dtype=jnp.int32)[None, :]
    inpatch = (rows >= patch_anchor[0]) & (rows < patch_anchor[0] + 2 * PATCH) & (depths >= patch_anchor[1]) & (depths < patch_anchor[1] + 2 * PATCH)
    for step in range(STEPS):
        lower = velocity_block(velocity[:, :, :middle], stress[:, :, :middle], props[2][:, :middle])
        upper = velocity_block(velocity[:, :, middle:], stress[:, :, middle:], props[2][:, middle:])
        faces = jnp.stack([lower[0][:, -1, :], lower[2][:, -1, :], props[2][:, middle - 1, :], upper[0][:, 0, :], upper[2][:, 0, :], props[2][:, middle, :]], axis=1)
        change, slip_path = friction(faces, prestress, normal_stress, slip_path, zone_label, fault_mask, inpatch, friction_table)
        lower = lower.at[0, :, -1, :].add(change[:, 0])
        lower = lower.at[2, :, -1, :].add(change[:, 1])
        upper = upper.at[0, :, 0, :].add(change[:, 2])
        upper = upper.at[2, :, 0, :].add(change[:, 3])
        velocity = jnp.concatenate([lower, upper], axis=2)
        stress_low, memory_low = stress_block(lower, stress[:, :, :middle], memory[:, :, :middle], props[:, :, :middle])
        stress_high, memory_high = stress_block(upper, stress[:, :, middle:], memory[:, :, middle:], props[:, :, middle:])
        stress = jnp.concatenate([stress_low, stress_high], axis=2)
        memory = jnp.concatenate([memory_low, memory_high], axis=2)
    return (velocity, stress, memory, slip_path)
```

```python
import functools

import jax
import jax.numpy as jnp
from jax import lax
from jax.experimental import pallas as pl
from jax.experimental.pallas import tpu as pltpu
from jax.sharding import PartitionSpec as P

STEPS = 2
CLASSES = 8
ZONES = 4
PATCH = 8

NEAR = 9.0 / 8.0
FAR = -1.0 / 24.0
DT = 0.15

XX, YY, ZZ, XY, XZ, YZ = range(6)

STRESS_TAIL = ((XX, -1), (XY, -2), (XY, -1), (XZ, -2), (XZ, -1))
STRESS_HEAD = ((XX, 0), (XX, 1), (XY, 0), (XZ, 0))
VEL_TAIL = ((0, -2), (0, -1), (1, -1), (2, -1))
VEL_HEAD = ((0, 0), (1, 0), (1, 1), (2, 0), (2, 1))
STRESS_TAIL_Y = ((YY, -1), (XY, -2), (XY, -1), (YZ, -2), (YZ, -1))
STRESS_HEAD_Y = ((YY, 0), (YY, 1), (XY, 0), (YZ, 0))
VEL_TAIL_Y = ((1, -2), (1, -1), (0, -1), (2, -1))
VEL_HEAD_Y = ((1, 0), (0, 0), (0, 1), (2, 0), (2, 1))
STRESS_SLOTS = (XZ, YZ, ZZ)
VEL_SLOTS = (0, 1, 2)


def forward(before, here, after, after_2):
    return NEAR * (after - here) + FAR * (after_2 - before)


def backward(before_2, before, here, after):
    return NEAR * (here - before) + FAR * (after - before_2)


class Edges:
    def __init__(self, rows, depths):
        self.rows = rows
        self.depths = depths
        lane = lax.broadcasted_iota(jnp.int32, (rows, depths), 1)
        row = lax.broadcasted_iota(jnp.int32, (rows, depths), 0)
        self.row = row
        self.deep = lax.axis_index("gz")
        self.low = {1: lane < 1, 2: lane < 2}
        self.high = {1: lane >= depths - 1, 2: lane >= depths - 2}
        self.top = {1: row < 1, 2: row < 2}
        self.bottom = {1: row >= rows - 1, 2: row >= rows - 2}
        self.slots = [self.slot(lane, k) for k in range(3)]

    def slot(self, lane, k):
        first = jnp.where(self.deep == 0, self.depths - 2 - 8 * k, 8 * k)
        return (lane == first) | (lane == first + 1)

    def turn(self, k):
        return jnp.where(self.deep == 0, self.depths - 8 * k, 8 * k)

    def packed(self, fields):
        out = jnp.where(self.slots[0], fields[0], 0.0)
        for k in (1, 2):
            if fields[k] is not None:
                out = jnp.where(self.slots[k], pltpu.roll(fields[k], self.turn(k), 1), out)
        return out

    def ends(self, strip, k):
        return strip if k == 0 else pltpu.roll(strip, self.turn(k), 1)

    def shallower(self, field, halo, n):
        return pltpu.roll(jnp.where(self.high[n], halo, field), n, 1)

    def deeper(self, field, halo, n):
        return pltpu.roll(jnp.where(self.low[n], halo, field), self.depths - n, 1)

    def forward_z(self, field, strip, k):
        halo = self.ends(strip, k)
        return forward(
            self.shallower(field, halo, 1),
            field,
            self.deeper(field, halo, 1),
            self.deeper(field, halo, 2),
        )

    def backward_z(self, field, strip, k):
        halo = self.ends(strip, k)
        return backward(
            self.shallower(field, halo, 2),
            self.shallower(field, halo, 1),
            field,
            self.deeper(field, halo, 1),
        )

    def before(self, field, n, halo):
        moved = jnp.where(self.top[n], 0.0, pltpu.roll(field, n, 0))
        if halo:
            for i in range(n):
                moved = jnp.where(self.row == i, halo[n - 1 - i], moved)
        return moved

    def after(self, field, n, halo):
        moved = jnp.where(self.bottom[n], 0.0, pltpu.roll(field, self.rows - n, 0))
        if halo:
            for i in range(n):
                moved = jnp.where(self.row == self.rows - n + i, halo[i], moved)
        return moved

    def forward_y(self, field, halos):
        lower, upper = halos
        return forward(
            self.before(field, 1, lower),
            field,
            self.after(field, 1, upper),
            self.after(field, 2, upper),
        )

    def backward_y(self, field, halos):
        lower, upper = halos
        return backward(
            self.before(field, 2, lower),
            self.before(field, 1, lower),
            field,
            self.after(field, 1, upper),
        )


class Planes:
    def __init__(self, ref, left, right, tail, head):
        self.ref = ref
        self.count = ref.shape[1]
        self.left, self.right = left, right
        self.tail, self.head = tail, head

    def __call__(self, comp, x, offset=0):
        if isinstance(x, int):
            place = x + offset
            if place < 0:
                return self.left[self.tail.index((comp, place))]
            if place >= self.count:
                return self.right[self.head.index((comp, place - self.count))]
        return self.ref[comp, x + offset]

    def forward_x(self, comp, x):
        return forward(self(comp, x, -1), self(comp, x), self(comp, x, 1), self(comp, x, 2))

    def backward_x(self, comp, x):
        return backward(self(comp, x, -2), self(comp, x, -1), self(comp, x), self(comp, x, 1))


class Bands:
    def __init__(self, refs, tail, head):
        self.refs = refs
        self.tail, self.head = tail, head

    def __call__(self, comp, x):
        if not self.refs:
            return (None, None)
        lower, upper = self.refs
        before = [
            lower[i, pl.ds(x, 1), :]
            for i in reversed(range(len(self.tail)))
            if self.tail[i][0] == comp
        ]
        after = [
            upper[i, pl.ds(x, 1), :] for i in range(len(self.head)) if self.head[i][0] == comp
        ]
        return (before, after)


def looked_up(labels, table, row, count):
    out = jnp.full(labels.shape, table[row, 0], jnp.float32)
    for k in range(1, count):
        out = jnp.where(labels == k, table[row, k], out)
    return out


def over_planes(count, body):
    for x in (0, 1):
        body(x)

    def step(x, carry):
        body(x)
        return carry

    lax.fori_loop(2, count - 2, step, 0)
    for x in (count - 2, count - 1):
        body(x)


def edge_planes(ref, planes, out):
    count = ref.shape[1]
    for i, (comp, place) in enumerate(planes):
        out[i] = ref[comp, place % count]


def fault_row(rows):
    return jnp.where(lax.axis_index("gy") == lax.axis_size("gy") // 2, 0, rows - 1)


def pack_kernel(stress, tail_out, head_out, strip_out):
    count, rows, depths = stress.shape[1:]
    edges = Edges(rows, depths)
    edge_planes(stress, STRESS_TAIL, tail_out)
    edge_planes(stress, STRESS_HEAD, head_out)

    def body(x, carry):
        strip_out[x] = edges.packed([stress[c, x] for c in STRESS_SLOTS])
        return carry

    lax.fori_loop(0, count, body, 0)


def velocity_kernel(first, banded, *refs):
    velocity, stress, material, table, left, right, strip = refs[:7]
    refs = refs[7:]
    bands = ()
    if banded:
        bands, refs = refs[:2], refs[2:]
    if first and not banded:
        (prestress, normal, slip, zone, mask), refs = refs[:5], refs[5:]
    out, face, tail_out, head_out, strip_out = refs
    count, rows, depths = velocity.shape[1:]
    edges = Edges(rows, depths)
    planes = Planes(stress, left, right, STRESS_TAIL, STRESS_HEAD)
    band = Bands(bands, STRESS_TAIL_Y, STRESS_HEAD_Y)
    fault = fault_row(rows)

    def body(x):
        sxy, sxz, syz = stress[XY, x], stress[XZ, x], stress[YZ, x]
        push = DT * looked_up(material[x], table, 2, CLASSES)
        ends = strip[x]
        along_x = (
            planes.forward_x(XX, x)
            + edges.backward_y(sxy, band(XY, x))
            + edges.backward_z(sxz, ends, 0)
        )
        along_y = (
            planes.backward_x(XY, x)
            + edges.forward_y(stress[YY, x], band(YY, x))
            + edges.backward_z(syz, ends, 1)
        )
        along_z = (
            planes.backward_x(XZ, x)
            + edges.backward_y(syz, band(YZ, x))
            + edges.forward_z(stress[ZZ, x], ends, 2)
        )
        new = [velocity[c, x] + push * rate for c, rate in enumerate((along_x, along_y, along_z))]
        for c in range(3):
            out[c, x] = new[c]
        strip_out[x] = edges.packed(new)
        face[pl.ds(x, 1), :] = out[0, x, pl.ds(fault, 1), :]
        face[pl.ds(count + x, 1), :] = out[2, x, pl.ds(fault, 1), :]
        if first:
            labels = material[x, pl.ds(fault, 1), :]
            face[pl.ds(2 * count + x, 1), :] = looked_up(labels, table, 2, CLASSES)

    over_planes(count, body)
    edge_planes(out, VEL_TAIL, tail_out)
    edge_planes(out, VEL_HEAD, head_out)
    if first and not banded:
        own = normal.shape[0]
        place = 3 * count
        for i in range(own):
            face[pl.ds(place + i, 1), :] = prestress[i, pl.ds(0, 1), :]
            face[pl.ds(place + own + i, 1), :] = prestress[i, pl.ds(1, 1), :]
        for i, field in enumerate((normal, slip, zone, mask)):
            face[pl.ds(place + (2 + i) * own, own), :] = field[...].astype(jnp.float32)


def fault_kernel(first, banded, *refs):
    (own_face, other_face, tail, head, strip, friction_table, anchor), refs = refs[:7], refs[7:]
    if first:
        if banded:
            still, refs = refs[0], refs[1:]
    else:
        (still, own_first, other_first, slip), refs = refs[:4], refs[4:]
    if first:
        own_first, other_first = own_face, other_face
    change, slip_out, tail_out, head_out, strip_out = refs[:5]
    count, rows, depths = strip.shape
    middle = lax.axis_size("gy") // 2
    side = lax.axis_index("gy")
    plus = side == middle
    minus = side == middle - 1

    def pair(own, other, place):
        mine, theirs = own[pl.ds(place, count), :], other[pl.ds(place, count), :]
        return jnp.where(plus, theirs, mine), jnp.where(plus, mine, theirs)

    if first and not banded:
        still = refs[5]
        share = (own_face.shape[0] - 3 * count) // 6
        for i in range(6):
            mine = own_face[pl.ds(3 * count + i * share, share), :]
            theirs = other_face[pl.ds(3 * count + i * share, share), :]
            still[i, pl.ds(0, share), :] = jnp.where(plus, theirs, mine)
            still[i, pl.ds(share, share), :] = jnp.where(plus, mine, theirs)
    pre_x, pre_z, normal = still[0], still[1], still[2]
    slip = still[3] if first else slip[...]
    zone, mask = still[4], still[5]

    row = lax.broadcasted_iota(jnp.int32, (count, depths), 0) + lax.axis_index("gx") * count
    deep = lax.broadcasted_iota(jnp.int32, (count, depths), 1) + lax.axis_index("gz") * depths
    inside = (row >= anchor[0]) & (row < anchor[0] + 2 * PATCH)
    inside = inside & (deep >= anchor[1]) & (deep < anchor[1] + 2 * PATCH)
    dynamic = 0.4 * looked_up(zone, friction_table, 0, ZONES)
    static = jnp.where(
        inside, dynamic, dynamic + 0.5 * looked_up(zone, friction_table, 1, ZONES)
    )
    distance = 0.2 * looked_up(zone, friction_table, 2, ZONES)
    minus_x, plus_x = pair(own_face, other_face, 0)
    minus_z, plus_z = pair(own_face, other_face, count)
    minus_b, plus_b = pair(own_first, other_first, 2 * count)
    bsum = minus_b + plus_b
    trial_x = (plus_x - minus_x) / (DT * bsum) + pre_x
    trial_z = (plus_z - minus_z) / (DT * bsum) + pre_z
    size = jnp.sqrt(trial_x * trial_x + trial_z * trial_z)
    weaken = jnp.minimum(slip / distance, 1.0)
    strength = (static - (static - dynamic) * weaken) * normal
    factor = jnp.where(mask == 1.0, strength / jnp.maximum(size, strength), 1.0)
    slip_out[...] = slip + DT * DT * bsum * (size - size * factor)
    sign = jnp.where(minus, DT, 0.0) * minus_b - jnp.where(plus, DT, 0.0) * plus_b
    change_x = (trial_x * factor - pre_x) * sign
    change_z = (trial_z * factor - pre_z) * sign
    change[0] = change_x
    change[1] = change_z

    fault = fault_row(rows)
    on_fault = lax.broadcasted_iota(jnp.int32, (rows, depths), 0) == fault
    for planes, source, out in ((VEL_TAIL, tail, tail_out), (VEL_HEAD, head, head_out)):
        for i, (comp, place) in enumerate(planes):
            plane = source[i]
            if comp != 1:
                line = change[comp // 2, pl.ds(place % count, 1), :]
                plane = plane + jnp.where(on_fault, line, 0.0)
            out[i] = plane
    flat = Edges(count, depths)
    ends = flat.packed([change_x, None, change_z])
    for x in range(count):
        strip_out[x] = strip[x] + jnp.where(on_fault, ends[x : x + 1, :], 0.0)


def stress_kernel(last, banded, *refs):
    velocity, stress, memory, material, table, change, left, right, strip = refs[:9]
    refs = refs[9:]
    bands = ()
    if banded:
        bands, refs = refs[:2], refs[2:]
    vel_out, stress_out, memory_out = refs[:3]
    if not last:
        tail_out, head_out, strip_out = refs[3:]
    count, rows, depths = velocity.shape[1:]
    edges = Edges(rows, depths)
    on_fault = edges.row == fault_row(rows)
    for x in range(count):
        for c in (0, 2):
            line = change[c // 2, pl.ds(x, 1), :]
            vel_out[c, x] = velocity[c, x] + jnp.where(on_fault, line, 0.0)
        vel_out[1, x] = velocity[1, x]
    planes = Planes(vel_out, left, right, VEL_TAIL, VEL_HEAD)
    band = Bands(bands, VEL_TAIL_Y, VEL_HEAD_Y)

    def body(x):
        vx, vy, vz = vel_out[0, x], vel_out[1, x], vel_out[2, x]
        ends = strip[x]
        exx = planes.backward_x(0, x)
        eyy = edges.backward_y(vy, band(1, x))
        ezz = edges.backward_z(vz, ends, 2)
        exy = edges.forward_y(vx, band(0, x)) + planes.forward_x(1, x)
        exz = edges.forward_z(vx, ends, 0) + planes.forward_x(2, x)
        eyz = edges.forward_z(vy, ends, 1) + edges.forward_y(vz, band(2, x))
        labels = material[x]
        lame = looked_up(labels, table, 0, CLASSES)
        shear = looked_up(labels, table, 1, CLASSES)
        decay = jnp.exp(-DT / looked_up(labels, table, 3, CLASSES))
        gain = (1.0 - decay) * (0.3 * looked_up(labels, table, 4, CLASSES))
        bulk = lame * (exx + eyy + ezz)
        double = 2.0 * shear
        elastic = (
            bulk + double * exx,
            bulk + double * eyy,
            bulk + double * ezz,
            shear * exy,
            shear * exz,
            shear * eyz,
        )
        new = []
        for c in range(6):
            kept = decay * memory[c, x] - gain * elastic[c]
            memory_out[c, x] = kept
            new.append(stress[c, x] + DT * (elastic[c] + kept))
            stress_out[c, x] = new[c]
        if not last:
            strip_out[x] = edges.packed([new[c] for c in STRESS_SLOTS])

    over_planes(count, body)
    if not last:
        edge_planes(stress_out, STRESS_TAIL, tail_out)
        edge_planes(stress_out, STRESS_HEAD, head_out)


def call(kernel, name, operands, outs, scalars=(), cost=0):
    in_specs = [
        pl.BlockSpec(memory_space=pltpu.SMEM if i in scalars else pltpu.VMEM)
        for i in range(len(operands))
    ]
    outs = [jax.ShapeDtypeStruct(shape, jnp.float32) for shape in outs]
    moved = sum(a.size * 4 for a in operands) + sum(4 * o.size for o in outs)
    return pl.pallas_call(
        kernel,
        out_shape=outs,
        in_specs=in_specs,
        out_specs=[pl.BlockSpec(memory_space=pltpu.VMEM) for _ in outs],
        name=name,
        cost_estimate=pl.CostEstimate(flops=cost, bytes_accessed=moved, transcendentals=0),
        compiler_params=pltpu.CompilerParams(vmem_limit_bytes=24 * 2**20),
    )(*operands)


def along(axis, count, skip=()):
    up = [(i, i + 1) for i in range(count - 1) if i not in skip]
    return (axis, up), (axis, [(b, a) for a, b in up])


def sent(block, route):
    return lax.ppermute(block, *route)


def edge_rows(field, rows):
    count = field.shape[2]
    return jnp.stack([field[c, :, place % count, :] for c, place in rows])


def shards(
    velocity,
    stress,
    memory,
    material,
    material_table,
    fault_mask,
    zone_label,
    patch_anchor,
    friction_table,
    prestress,
    normal_stress,
    slip_path,
):
    _, count, rows, depths = velocity.shape
    sides = lax.axis_size("gy")
    middle = sides // 2
    banded = sides > 2
    cells = count * rows * depths
    up, down = along("gx", lax.axis_size("gx"))
    up_y, down_y = along("gy", sides, (middle - 1,))
    across = ("gy", [(middle - 1, middle), (middle, middle - 1)])
    deep = ("gz", [(0, 1), (1, 0)])

    def strike_shape(planes):
        return (len(planes), rows, depths)

    strip_shape = (count, rows, depths)
    block = (count, rows, depths)

    still = None
    if banded:
        still = jnp.stack(
            [
                prestress[:, 0],
                prestress[:, 1],
                normal_stress,
                slip_path,
                zone_label.astype(jnp.float32),
                fault_mask.astype(jnp.float32),
            ]
        )
        still = lax.all_gather(still, "gy", axis=1, tiled=True)

    tail, head, strip = call(
        pack_kernel,
        "pack",
        [stress],
        [strike_shape(STRESS_TAIL), strike_shape(STRESS_HEAD), strip_shape],
    )
    for step in range(STEPS):
        first, last = step == 0, step == STEPS - 1
        strip = sent(strip, deep)
        left = sent(tail, up)
        right = sent(head, down)
        operands = [velocity, stress, material, material_table, left, right, strip]
        if banded:
            operands += [
                sent(edge_rows(stress, STRESS_TAIL_Y), up_y),
                sent(edge_rows(stress, STRESS_HEAD_Y), down_y),
            ]
        face_rows = 2 * count
        if first:
            face_rows += count
            if not banded:
                operands += [prestress, normal_stress, slip_path, zone_label, fault_mask]
                face_rows += 6 * normal_stress.shape[0]
        free, face, tail, head, strip = call(
            functools.partial(velocity_kernel, first, banded),
            "velocity",
            operands,
            [
                (3, *block),
                (face_rows, depths),
                strike_shape(VEL_TAIL),
                strike_shape(VEL_HEAD),
                strip_shape,
            ],
            scalars=(3,),
            cost=60 * cells,
        )
        other = sent(face, across)
        operands = [face, other, tail, head, strip, friction_table, patch_anchor]
        outs = [
            (2, count, depths),
            (count, depths),
            strike_shape(VEL_TAIL),
            strike_shape(VEL_HEAD),
            strip_shape,
        ]
        if first:
            faces = (face, other)
            if banded:
                operands.append(still)
            else:
                outs.append((6, count, depths))
        else:
            operands += [still, *faces, slip]
        result = call(
            functools.partial(fault_kernel, first, banded),
            "fault",
            operands,
            outs,
            scalars=(5, 6),
        )
        change, slip, tail, head, strip = result[:5]
        if first and not banded:
            still = result[5]
        strip = sent(strip, deep)
        left = sent(tail, up)
        right = sent(head, down)
        operands = [free, stress, memory, material, material_table]
        operands += [change, left, right, strip]
        if banded:
            operands += [
                sent(edge_rows(free, VEL_TAIL_Y), up_y),
                sent(edge_rows(free, VEL_HEAD_Y), down_y),
            ]
        outs = [(3, *block), (6, *block), (6, *block)]
        if not last:
            outs += [strike_shape(STRESS_TAIL), strike_shape(STRESS_HEAD), strip_shape]
        result = call(
            functools.partial(stress_kernel, last, banded),
            "stress",
            operands,
            outs,
            scalars=(4,),
            cost=100 * cells,
        )
        velocity, stress, memory = result[:3]
        if not last:
            tail, head, strip = result[3:]
    side = lax.axis_index("gy")
    if banded:
        held = jnp.where(side == middle, slip, 0.0)
        new_slip = lax.psum_scatter(held, "gy", scatter_dimension=0, tiled=True)
    else:
        share = count // sides
        new_slip = lax.dynamic_slice_in_dim(slip, side * share, share, axis=0)
    return (velocity, stress, memory, new_slip)


def solution(mesh):
    in_specs = (
        P(None, ("ens", "gx"), "gy", "gz"),
        P(None, ("ens", "gx"), "gy", "gz"),
        P(None, ("ens", "gx"), "gy", "gz"),
        P(("ens", "gx"), "gy", "gz"),
        P(None, "ens"),
        P(("ens", "gx", "gy"), "gz"),
        P(("ens", "gx", "gy"), "gz"),
        P("ens"),
        P(None, "ens"),
        P(("ens", "gx", "gy"), None, "gz"),
        P(("ens", "gx", "gy"), "gz"),
        P(("ens", "gx", "gy"), "gz"),
    )
    out_specs = (
        P(None, ("ens", "gx"), "gy", "gz"),
        P(None, ("ens", "gx"), "gy", "gz"),
        P(None, ("ens", "gx"), "gy", "gz"),
        P(("ens", "gx", "gy"), "gz"),
    )
    return jax.shard_map(shards, mesh=mesh, in_specs=in_specs, out_specs=out_specs, check_vma=False)
```

```python
import functools

import jax
import jax.numpy as jnp
from jax import lax
from jax.experimental import pallas as pl
from jax.experimental.pallas import tpu as pltpu
from jax.sharding import PartitionSpec as P

STEPS = 2
CLASSES = 8
ZONES = 4
PATCH = 8

NEAR = 9.0 / 8.0
FAR = -1.0 / 24.0
DT = 0.15

XX, YY, ZZ, XY, XZ, YZ = range(6)

STRESS_TAIL = ((XX, -1), (XY, -2), (XY, -1), (XZ, -2), (XZ, -1))
STRESS_HEAD = ((XX, 0), (XX, 1), (XY, 0), (XZ, 0))
VEL_TAIL = ((0, -2), (0, -1), (1, -1), (2, -1))
VEL_HEAD = ((0, 0), (1, 0), (1, 1), (2, 0), (2, 1))
STRESS_TAIL_Y = ((YY, -1), (XY, -2), (XY, -1), (YZ, -2), (YZ, -1))
STRESS_HEAD_Y = ((YY, 0), (YY, 1), (XY, 0), (YZ, 0))
VEL_TAIL_Y = ((1, -2), (1, -1), (0, -1), (2, -1))
VEL_HEAD_Y = ((1, 0), (0, 0), (0, 1), (2, 0), (2, 1))
STRESS_SLOTS = (XZ, YZ, ZZ)
VEL_SLOTS = (0, 1, 2)


def forward(before, here, after, after_2):
    return NEAR * (after - here) + FAR * (after_2 - before)


def backward(before_2, before, here, after):
    return NEAR * (here - before) + FAR * (after - before_2)


class Edges:
    def __init__(self, rows, depths):
        self.rows = rows
        self.depths = depths
        lane = lax.broadcasted_iota(jnp.int32, (rows, depths), 1)
        row = lax.broadcasted_iota(jnp.int32, (rows, depths), 0)
        self.row = row
        self.deep = lax.axis_index("gz")
        self.low = {1: lane < 1, 2: lane < 2}
        self.high = {1: lane >= depths - 1, 2: lane >= depths - 2}
        self.top = {1: row < 1, 2: row < 2}
        self.bottom = {1: row >= rows - 1, 2: row >= rows - 2}
        self.slots = [self.slot(lane, k) for k in range(3)]

    def slot(self, lane, k):
        first = jnp.where(self.deep == 0, self.depths - 2 - 8 * k, 8 * k)
        return (lane == first) | (lane == first + 1)

    def turn(self, k):
        return jnp.where(self.deep == 0, self.depths - 8 * k, 8 * k)

    def packed(self, fields):
        out = jnp.where(self.slots[0], fields[0], 0.0)
        for k in (1, 2):
            if fields[k] is not None:
                out = jnp.where(self.slots[k], pltpu.roll(fields[k], self.turn(k), 1), out)
        return out

    def ends(self, strip, k):
        return strip if k == 0 else pltpu.roll(strip, self.turn(k), 1)

    def shallower(self, field, halo, n):
        return pltpu.roll(jnp.where(self.high[n], halo, field), n, 1)

    def deeper(self, field, halo, n):
        return pltpu.roll(jnp.where(self.low[n], halo, field), self.depths - n, 1)

    def forward_z(self, field, strip, k):
        halo = self.ends(strip, k)
        return forward(
            self.shallower(field, halo, 1),
            field,
            self.deeper(field, halo, 1),
            self.deeper(field, halo, 2),
        )

    def backward_z(self, field, strip, k):
        halo = self.ends(strip, k)
        return backward(
            self.shallower(field, halo, 2),
            self.shallower(field, halo, 1),
            field,
            self.deeper(field, halo, 1),
        )

    def before(self, field, n, halo):
        moved = jnp.where(self.top[n], 0.0, pltpu.roll(field, n, 0))
        if halo:
            for i in range(n):
                moved = jnp.where(self.row == i, halo[n - 1 - i], moved)
        return moved

    def after(self, field, n, halo):
        moved = jnp.where(self.bottom[n], 0.0, pltpu.roll(field, self.rows - n, 0))
        if halo:
            for i in range(n):
                moved = jnp.where(self.row == self.rows - n + i, halo[i], moved)
        return moved

    def forward_y(self, field, halos):
        lower, upper = halos
        return forward(
            self.before(field, 1, lower),
            field,
            self.after(field, 1, upper),
            self.after(field, 2, upper),
        )

    def backward_y(self, field, halos):
        lower, upper = halos
        return backward(
            self.before(field, 2, lower),
            self.before(field, 1, lower),
            field,
            self.after(field, 1, upper),
        )


class Planes:
    def __init__(self, ref, first, second, tail, head):
        self.ref = ref
        self.count = ref.shape[1]
        self.first, self.second = first, second
        self.tail, self.head = tail, head
        self.even = even_strike()
        self.any_left = lax.axis_index("gx") > 0
        self.any_right = lax.axis_index("gx") < lax.axis_size("gx") - 1

    def left(self, i):
        plane = jnp.where(self.even, self.second[i], self.first[i])
        return jnp.where(self.any_left, plane, 0.0)

    def right(self, i):
        plane = jnp.where(self.even, self.first[i], self.second[i])
        return jnp.where(self.any_right, plane, 0.0)

    def __call__(self, comp, x, offset=0):
        if isinstance(x, int):
            place = x + offset
            if place < 0:
                return self.left(self.tail.index((comp, place)))
            if place >= self.count:
                return self.right(self.head.index((comp, place - self.count)))
        return self.ref[comp, x + offset]

    def forward_x(self, comp, x):
        return forward(self(comp, x, -1), self(comp, x), self(comp, x, 1), self(comp, x, 2))

    def backward_x(self, comp, x):
        return backward(self(comp, x, -2), self(comp, x, -1), self(comp, x), self(comp, x, 1))


class Bands:
    def __init__(self, refs, tail, head):
        self.refs = refs
        self.tail, self.head = tail, head

    def __call__(self, comp, x):
        if not self.refs:
            return (None, None)
        lower, upper = self.refs
        before = [
            lower[i, pl.ds(x, 1), :]
            for i in reversed(range(len(self.tail)))
            if self.tail[i][0] == comp
        ]
        after = [
            upper[i, pl.ds(x, 1), :] for i in range(len(self.head)) if self.head[i][0] == comp
        ]
        return (before, after)


def looked_up(labels, table, row, count):
    out = jnp.full(labels.shape, table[row, 0], jnp.float32)
    for k in range(1, count):
        out = jnp.where(labels == k, table[row, k], out)
    return out


def over_planes(count, body):
    for x in (0, 1):
        body(x)

    def step(x, carry):
        body(x)
        return carry

    lax.fori_loop(2, count - 2, step, 0)
    for x in (count - 2, count - 1):
        body(x)


def even_strike():
    return lax.axis_index("gx") % 2 == 0


def edge_planes(ref, tail, head, first_out, second_out):
    count = ref.shape[1]
    even = even_strike()
    for i in range(first_out.shape[0]):
        comp, place = tail[min(i, len(tail) - 1)]
        right = ref[comp, place % count]
        comp, place = head[min(i, len(head) - 1)]
        left = ref[comp, place % count]
        first_out[i] = jnp.where(even, right, left)
        second_out[i] = jnp.where(even, left, right)


def fault_row(rows):
    return jnp.where(lax.axis_index("gy") == lax.axis_size("gy") // 2, 0, rows - 1)


def pack_kernel(stress, first_out, second_out, strip_out):
    count, rows, depths = stress.shape[1:]
    edges = Edges(rows, depths)
    edge_planes(stress, STRESS_TAIL, STRESS_HEAD, first_out, second_out)

    def body(x, carry):
        strip_out[x] = edges.packed([stress[c, x] for c in STRESS_SLOTS])
        return carry

    lax.fori_loop(0, count, body, 0)


def velocity_kernel(first, banded, *refs):
    velocity, stress, material, table, first_edge, second_edge, strip = refs[:7]
    refs = refs[7:]
    bands = ()
    if banded:
        bands, refs = refs[:2], refs[2:]
    if first and not banded:
        (prestress, normal, slip, zone, mask), refs = refs[:5], refs[5:]
    out, face, first_out, second_out, strip_out = refs
    count, rows, depths = velocity.shape[1:]
    edges = Edges(rows, depths)
    planes = Planes(stress, first_edge, second_edge, STRESS_TAIL, STRESS_HEAD)
    band = Bands(bands, STRESS_TAIL_Y, STRESS_HEAD_Y)
    fault = fault_row(rows)

    def body(x):
        sxy, sxz, syz = stress[XY, x], stress[XZ, x], stress[YZ, x]
        push = DT * looked_up(material[x], table, 2, CLASSES)
        ends = strip[x]
        along_x = (
            planes.forward_x(XX, x)
            + edges.backward_y(sxy, band(XY, x))
            + edges.backward_z(sxz, ends, 0)
        )
        along_y = (
            planes.backward_x(XY, x)
            + edges.forward_y(stress[YY, x], band(YY, x))
            + edges.backward_z(syz, ends, 1)
        )
        along_z = (
            planes.backward_x(XZ, x)
            + edges.backward_y(syz, band(YZ, x))
            + edges.forward_z(stress[ZZ, x], ends, 2)
        )
        new = [velocity[c, x] + push * rate for c, rate in enumerate((along_x, along_y, along_z))]
        for c in range(3):
            out[c, x] = new[c]
        strip_out[x] = edges.packed(new)
        face[pl.ds(x, 1), :] = out[0, x, pl.ds(fault, 1), :]
        face[pl.ds(count + x, 1), :] = out[2, x, pl.ds(fault, 1), :]
        if first:
            labels = material[x, pl.ds(fault, 1), :]
            face[pl.ds(2 * count + x, 1), :] = looked_up(labels, table, 2, CLASSES)

    over_planes(count, body)
    edge_planes(out, VEL_TAIL, VEL_HEAD, first_out, second_out)
    if first and not banded:
        own = normal.shape[0]
        place = 3 * count
        for i in range(own):
            face[pl.ds(place + i, 1), :] = prestress[i, pl.ds(0, 1), :]
            face[pl.ds(place + own + i, 1), :] = prestress[i, pl.ds(1, 1), :]
        for i, field in enumerate((normal, slip, zone, mask)):
            face[pl.ds(place + (2 + i) * own, own), :] = field[...].astype(jnp.float32)


def fault_kernel(first, banded, *refs):
    (own_face, other_face, first_edge, second_edge, strip, friction_table, anchor), refs = refs[:7], refs[7:]
    if first:
        if banded:
            still, refs = refs[0], refs[1:]
    else:
        (still, own_first, other_first, slip), refs = refs[:4], refs[4:]
    if first:
        own_first, other_first = own_face, other_face
    change, slip_out, first_out, second_out, strip_out = refs[:5]
    count, rows, depths = strip.shape
    middle = lax.axis_size("gy") // 2
    side = lax.axis_index("gy")
    plus = side == middle
    minus = side == middle - 1

    def pair(own, other, place):
        mine, theirs = own[pl.ds(place, count), :], other[pl.ds(place, count), :]
        return jnp.where(plus, theirs, mine), jnp.where(plus, mine, theirs)

    if first and not banded:
        still = refs[5]
        share = (own_face.shape[0] - 3 * count) // 6
        for i in range(6):
            mine = own_face[pl.ds(3 * count + i * share, share), :]
            theirs = other_face[pl.ds(3 * count + i * share, share), :]
            still[i, pl.ds(0, share), :] = jnp.where(plus, theirs, mine)
            still[i, pl.ds(share, share), :] = jnp.where(plus, mine, theirs)
    pre_x, pre_z, normal = still[0], still[1], still[2]
    slip = still[3] if first else slip[...]
    zone, mask = still[4], still[5]

    row = lax.broadcasted_iota(jnp.int32, (count, depths), 0) + lax.axis_index("gx") * count
    deep = lax.broadcasted_iota(jnp.int32, (count, depths), 1) + lax.axis_index("gz") * depths
    inside = (row >= anchor[0]) & (row < anchor[0] + 2 * PATCH)
    inside = inside & (deep >= anchor[1]) & (deep < anchor[1] + 2 * PATCH)
    dynamic = 0.4 * looked_up(zone, friction_table, 0, ZONES)
    static = jnp.where(
        inside, dynamic, dynamic + 0.5 * looked_up(zone, friction_table, 1, ZONES)
    )
    distance = 0.2 * looked_up(zone, friction_table, 2, ZONES)
    minus_x, plus_x = pair(own_face, other_face, 0)
    minus_z, plus_z = pair(own_face, other_face, count)
    minus_b, plus_b = pair(own_first, other_first, 2 * count)
    bsum = minus_b + plus_b
    trial_x = (plus_x - minus_x) / (DT * bsum) + pre_x
    trial_z = (plus_z - minus_z) / (DT * bsum) + pre_z
    size = jnp.sqrt(trial_x * trial_x + trial_z * trial_z)
    weaken = jnp.minimum(slip / distance, 1.0)
    strength = (static - (static - dynamic) * weaken) * normal
    factor = jnp.where(mask == 1.0, strength / jnp.maximum(size, strength), 1.0)
    slip_out[...] = slip + DT * DT * bsum * (size - size * factor)
    sign = jnp.where(minus, DT, 0.0) * minus_b - jnp.where(plus, DT, 0.0) * plus_b
    change_x = (trial_x * factor - pre_x) * sign
    change_z = (trial_z * factor - pre_z) * sign
    change[0] = change_x
    change[1] = change_z

    fault = fault_row(rows)
    on_fault = lax.broadcasted_iota(jnp.int32, (rows, depths), 0) == fault
    even = even_strike()
    still_line = jnp.zeros((1, depths), jnp.float32)

    def line(planes, i):
        comp, place = planes[min(i, len(planes) - 1)]
        return still_line if comp == 1 else change[comp // 2, pl.ds(place % count, 1), :]

    for i in range(first_out.shape[0]):
        right, left = line(VEL_TAIL, i), line(VEL_HEAD, i)
        one, two = jnp.where(even, right, left), jnp.where(even, left, right)
        first_out[i] = first_edge[i] + jnp.where(on_fault, one, 0.0)
        second_out[i] = second_edge[i] + jnp.where(on_fault, two, 0.0)
    flat = Edges(count, depths)
    ends = flat.packed([change_x, None, change_z])
    for x in range(count):
        strip_out[x] = strip[x] + jnp.where(on_fault, ends[x : x + 1, :], 0.0)


def stress_kernel(last, banded, *refs):
    velocity, stress, memory, material, table, change, first_edge, second_edge, strip = refs[:9]
    refs = refs[9:]
    bands = ()
    if banded:
        bands, refs = refs[:2], refs[2:]
    vel_out, stress_out, memory_out = refs[:3]
    if not last:
        first_out, second_out, strip_out = refs[3:]
    count, rows, depths = velocity.shape[1:]
    edges = Edges(rows, depths)
    on_fault = edges.row == fault_row(rows)
    for x in range(count):
        for c in (0, 2):
            line = change[c // 2, pl.ds(x, 1), :]
            vel_out[c, x] = velocity[c, x] + jnp.where(on_fault, line, 0.0)
        vel_out[1, x] = velocity[1, x]
    planes = Planes(vel_out, first_edge, second_edge, VEL_TAIL, VEL_HEAD)
    band = Bands(bands, VEL_TAIL_Y, VEL_HEAD_Y)

    def body(x):
        vx, vy, vz = vel_out[0, x], vel_out[1, x], vel_out[2, x]
        ends = strip[x]
        exx = planes.backward_x(0, x)
        eyy = edges.backward_y(vy, band(1, x))
        ezz = edges.backward_z(vz, ends, 2)
        exy = edges.forward_y(vx, band(0, x)) + planes.forward_x(1, x)
        exz = edges.forward_z(vx, ends, 0) + planes.forward_x(2, x)
        eyz = edges.forward_z(vy, ends, 1) + edges.forward_y(vz, band(2, x))
        labels = material[x]
        lame = looked_up(labels, table, 0, CLASSES)
        shear = looked_up(labels, table, 1, CLASSES)
        decay = jnp.exp(-DT / looked_up(labels, table, 3, CLASSES))
        gain = (1.0 - decay) * (0.3 * looked_up(labels, table, 4, CLASSES))
        bulk = lame * (exx + eyy + ezz)
        double = 2.0 * shear
        elastic = (
            bulk + double * exx,
            bulk + double * eyy,
            bulk + double * ezz,
            shear * exy,
            shear * exz,
            shear * eyz,
        )
        new = []
        for c in range(6):
            kept = decay * memory[c, x] - gain * elastic[c]
            memory_out[c, x] = kept
            new.append(stress[c, x] + DT * (elastic[c] + kept))
            stress_out[c, x] = new[c]
        if not last:
            strip_out[x] = edges.packed([new[c] for c in STRESS_SLOTS])

    over_planes(count, body)
    if not last:
        edge_planes(stress_out, STRESS_TAIL, STRESS_HEAD, first_out, second_out)


def call(kernel, name, operands, outs, scalars=(), cost=0):
    in_specs = [
        pl.BlockSpec(memory_space=pltpu.SMEM if i in scalars else pltpu.VMEM)
        for i in range(len(operands))
    ]
    outs = [jax.ShapeDtypeStruct(shape, jnp.float32) for shape in outs]
    moved = sum(a.size * 4 for a in operands) + sum(4 * o.size for o in outs)
    return pl.pallas_call(
        kernel,
        out_shape=outs,
        in_specs=in_specs,
        out_specs=[pl.BlockSpec(memory_space=pltpu.VMEM) for _ in outs],
        name=name,
        cost_estimate=pl.CostEstimate(flops=cost, bytes_accessed=moved, transcendentals=0),
        compiler_params=pltpu.CompilerParams(vmem_limit_bytes=24 * 2**20),
    )(*operands)


def along(axis, count, skip=()):
    up = [(i, i + 1) for i in range(count - 1) if i not in skip]
    return (axis, up), (axis, [(b, a) for a, b in up])


def strike_swaps(count):
    routes = []
    for start in (0, 1):
        partner = list(range(count))
        for i in range(start, count - 1, 2):
            partner[i], partner[i + 1] = i + 1, i
        routes.append(("gx", list(enumerate(partner))))
    return routes


def sent(block, route):
    return lax.ppermute(block, *route)


def edge_rows(field, rows):
    count = field.shape[2]
    return jnp.stack([field[c, :, place % count, :] for c, place in rows])


def shards(
    velocity,
    stress,
    memory,
    material,
    material_table,
    fault_mask,
    zone_label,
    patch_anchor,
    friction_table,
    prestress,
    normal_stress,
    slip_path,
):
    _, count, rows, depths = velocity.shape
    sides = lax.axis_size("gy")
    middle = sides // 2
    banded = sides > 2
    cells = count * rows * depths
    swaps = strike_swaps(lax.axis_size("gx"))
    up_y, down_y = along("gy", sides, (middle - 1,))
    across = ("gy", [(middle - 1, middle), (middle, middle - 1)])
    deep = ("gz", [(0, 1), (1, 0)])

    edge_shape = (max(len(STRESS_TAIL), len(STRESS_HEAD)), rows, depths)

    strip_shape = (count, rows, depths)
    block = (count, rows, depths)

    still = None
    if banded:
        still = jnp.stack(
            [
                prestress[:, 0],
                prestress[:, 1],
                normal_stress,
                slip_path,
                zone_label.astype(jnp.float32),
                fault_mask.astype(jnp.float32),
            ]
        )
        still = lax.all_gather(still, "gy", axis=1, tiled=True)

    one, two, strip = call(
        pack_kernel,
        "pack",
        [stress],
        [edge_shape, edge_shape, strip_shape],
    )
    for step in range(STEPS):
        first, last = step == 0, step == STEPS - 1
        strip = sent(strip, deep)
        one = sent(one, swaps[0])
        two = sent(two, swaps[1])
        operands = [velocity, stress, material, material_table, one, two, strip]
        if banded:
            operands += [
                sent(edge_rows(stress, STRESS_TAIL_Y), up_y),
                sent(edge_rows(stress, STRESS_HEAD_Y), down_y),
            ]
        face_rows = 2 * count
        if first:
            face_rows += count
            if not banded:
                operands += [prestress, normal_stress, slip_path, zone_label, fault_mask]
                face_rows += 6 * normal_stress.shape[0]
        free, face, one, two, strip = call(
            functools.partial(velocity_kernel, first, banded),
            "velocity",
            operands,
            [
                (3, *block),
                (face_rows, depths),
                edge_shape,
                edge_shape,
                strip_shape,
            ],
            scalars=(3,),
            cost=60 * cells,
        )
        other = sent(face, across)
        operands = [face, other, one, two, strip, friction_table, patch_anchor]
        outs = [
            (2, count, depths),
            (count, depths),
            edge_shape,
            edge_shape,
            strip_shape,
        ]
        if first:
            faces = (face, other)
            if banded:
                operands.append(still)
            else:
                outs.append((6, count, depths))
        else:
            operands += [still, *faces, slip]
        result = call(
            functools.partial(fault_kernel, first, banded),
            "fault",
            operands,
            outs,
            scalars=(5, 6),
        )
        change, slip, one, two, strip = result[:5]
        if first and not banded:
            still = result[5]
        strip = sent(strip, deep)
        one = sent(one, swaps[0])
        two = sent(two, swaps[1])
        operands = [free, stress, memory, material, material_table]
        operands += [change, one, two, strip]
        if banded:
            operands += [
                sent(edge_rows(free, VEL_TAIL_Y), up_y),
                sent(edge_rows(free, VEL_HEAD_Y), down_y),
            ]
        outs = [(3, *block), (6, *block), (6, *block)]
        if not last:
            outs += [edge_shape, edge_shape, strip_shape]
        result = call(
            functools.partial(stress_kernel, last, banded),
            "stress",
            operands,
            outs,
            scalars=(4,),
            cost=100 * cells,
        )
        velocity, stress, memory = result[:3]
        if not last:
            one, two, strip = result[3:]
    side = lax.axis_index("gy")
    if banded:
        held = jnp.where(side == middle, slip, 0.0)
        new_slip = lax.psum_scatter(held, "gy", scatter_dimension=0, tiled=True)
    else:
        share = count // sides
        new_slip = lax.dynamic_slice_in_dim(slip, side * share, share, axis=0)
    return (velocity, stress, memory, new_slip)


def solution(mesh):
    in_specs = (
        P(None, ("ens", "gx"), "gy", "gz"),
        P(None, ("ens", "gx"), "gy", "gz"),
        P(None, ("ens", "gx"), "gy", "gz"),
        P(("ens", "gx"), "gy", "gz"),
        P(None, "ens"),
        P(("ens", "gx", "gy"), "gz"),
        P(("ens", "gx", "gy"), "gz"),
        P("ens"),
        P(None, "ens"),
        P(("ens", "gx", "gy"), None, "gz"),
        P(("ens", "gx", "gy"), "gz"),
        P(("ens", "gx", "gy"), "gz"),
    )
    out_specs = (
        P(None, ("ens", "gx"), "gy", "gz"),
        P(None, ("ens", "gx"), "gy", "gz"),
        P(None, ("ens", "gx"), "gy", "gz"),
        P(("ens", "gx", "gy"), "gz"),
    )
    return jax.shard_map(shards, mesh=mesh, in_specs=in_specs, out_specs=out_specs, check_vma=False)
```

```python
import functools
import math
import types

import jax
import jax.numpy as jnp
from jax import lax
from jax.experimental import pallas as pl
from jax.experimental.pallas import tpu as pltpu
from jax.sharding import PartitionSpec as P

STEPS = 2
CLASSES = 8
ZONES = 4
PATCH = 8

NEAR = 9.0 / 8.0
FAR = -1.0 / 24.0
DT = 0.15

XX, YY, ZZ, XY, XZ, YZ = range(6)

STRESS_TAIL = ((XX, -1), (XY, -2), (XY, -1), (XZ, -2), (XZ, -1))
STRESS_HEAD = ((XX, 0), (XX, 1), (XY, 0), (XZ, 0))
VEL_TAIL = ((0, -2), (0, -1), (1, -1), (2, -1))
VEL_HEAD = ((0, 0), (1, 0), (1, 1), (2, 0), (2, 1))
STRESS_TAIL_Y = ((YY, -1), (XY, -2), (XY, -1), (YZ, -2), (YZ, -1))
STRESS_HEAD_Y = ((YY, 0), (YY, 1), (XY, 0), (YZ, 0))
VEL_TAIL_Y = ((1, -2), (1, -1), (0, -1), (2, -1))
VEL_HEAD_Y = ((1, 0), (0, 0), (0, 1), (2, 0), (2, 1))
STRESS_SLOTS = (XZ, YZ, ZZ)
VEL_SLOTS = (0, 1, 2)


def forward(before, here, after, after_2):
    return NEAR * (after - here) + FAR * (after_2 - before)


def backward(before_2, before, here, after):
    return NEAR * (here - before) + FAR * (after - before_2)


class Edges:
    def __init__(self, rows, depths):
        self.rows = rows
        self.depths = depths
        lane = lax.broadcasted_iota(jnp.int32, (rows, depths), 1)
        row = lax.broadcasted_iota(jnp.int32, (rows, depths), 0)
        self.row = row
        self.deep = lax.axis_index("gz")
        self.low = {1: lane < 1, 2: lane < 2}
        self.high = {1: lane >= depths - 1, 2: lane >= depths - 2}
        self.top = {1: row < 1, 2: row < 2}
        self.bottom = {1: row >= rows - 1, 2: row >= rows - 2}
        self.slots = [self.slot(lane, k) for k in range(3)]

    def slot(self, lane, k):
        first = jnp.where(self.deep == 0, self.depths - 2 - 8 * k, 8 * k)
        return (lane == first) | (lane == first + 1)

    def turn(self, k):
        return jnp.where(self.deep == 0, self.depths - 8 * k, 8 * k)

    def packed(self, fields):
        out = jnp.where(self.slots[0], fields[0], 0.0)
        for k in (1, 2):
            if fields[k] is not None:
                out = jnp.where(self.slots[k], pltpu.roll(fields[k], self.turn(k), 1), out)
        return out

    def ends(self, strip, k):
        return strip if k == 0 else pltpu.roll(strip, self.turn(k), 1)

    def shallower(self, field, halo, n):
        return pltpu.roll(jnp.where(self.high[n], halo, field), n, 1)

    def deeper(self, field, halo, n):
        return pltpu.roll(jnp.where(self.low[n], halo, field), self.depths - n, 1)

    def forward_z(self, field, strip, k):
        halo = self.ends(strip, k)
        return forward(
            self.shallower(field, halo, 1),
            field,
            self.deeper(field, halo, 1),
            self.deeper(field, halo, 2),
        )

    def backward_z(self, field, strip, k):
        halo = self.ends(strip, k)
        return backward(
            self.shallower(field, halo, 2),
            self.shallower(field, halo, 1),
            field,
            self.deeper(field, halo, 1),
        )

    def before(self, field, n, halo):
        moved = jnp.where(self.top[n], 0.0, pltpu.roll(field, n, 0))
        if halo:
            for i in range(n):
                moved = jnp.where(self.row == i, halo[n - 1 - i], moved)
        return moved

    def after(self, field, n, halo):
        moved = jnp.where(self.bottom[n], 0.0, pltpu.roll(field, self.rows - n, 0))
        if halo:
            for i in range(n):
                moved = jnp.where(self.row == self.rows - n + i, halo[i], moved)
        return moved

    def forward_y(self, field, halos):
        lower, upper = halos
        return forward(
            self.before(field, 1, lower),
            field,
            self.after(field, 1, upper),
            self.after(field, 2, upper),
        )

    def backward_y(self, field, halos):
        lower, upper = halos
        return backward(
            self.before(field, 2, lower),
            self.before(field, 1, lower),
            field,
            self.after(field, 1, upper),
        )


class Field:
    def __init__(self, count, *parts):
        self.count = count
        self.parts = parts

    def __call__(self, comp, x):
        if len(self.parts) == 1:
            return self.parts[0][comp, x]
        inner, edge = self.parts
        if x in inside(self.count):
            return inner[comp, x - 2]
        return edge[comp, ends_of(self.count).index(x)]


def inside(count):
    return range(2, count - 2)


def ends_of(count):
    return (0, 1, count - 2, count - 1)


class Planes:
    def __init__(self, field, tail, head, first=None, second=None):
        self.field = field
        self.count = field.count
        self.first, self.second = first, second
        self.tail, self.head = tail, head
        self.even = even_strike()
        self.any_left = lax.axis_index("gx") > 0
        self.any_right = lax.axis_index("gx") < lax.axis_size("gx") - 1

    def left(self, i):
        plane = jnp.where(self.even, self.second[i], self.first[i])
        return jnp.where(self.any_left, plane, 0.0)

    def right(self, i):
        plane = jnp.where(self.even, self.first[i], self.second[i])
        return jnp.where(self.any_right, plane, 0.0)

    def __call__(self, comp, place):
        if place < 0:
            return self.left(self.tail.index((comp, place)))
        if place >= self.count:
            return self.right(self.head.index((comp, place - self.count)))
        return self.field(comp, place)

    def forward_x(self, comp, x):
        return forward(self(comp, x - 1), self(comp, x), self(comp, x + 1), self(comp, x + 2))

    def backward_x(self, comp, x):
        return backward(self(comp, x - 2), self(comp, x - 1), self(comp, x), self(comp, x + 1))


class Bands:
    def __init__(self, lower, upper, tail, head):
        self.lower, self.upper = lower, upper
        self.tail, self.head = tail, head

    def __call__(self, comp, x):
        if self.lower is None:
            return (None, None)
        places = [i for i, (c, _) in enumerate(self.tail) if c == comp]
        before = [self.lower[i, pl.ds(x, 1), :] for i in reversed(places)]
        places = [i for i, (c, _) in enumerate(self.head) if c == comp]
        after = [self.upper[i, pl.ds(x, 1), :] for i in places]
        return (before, after)


def looked_up(labels, table, row, count):
    out = jnp.full(labels.shape, table[row, 0], jnp.float32)
    for k in range(1, count):
        out = jnp.where(labels == k, table[row, k], out)
    return out


def even_strike():
    return lax.axis_index("gx") % 2 == 0


def edge_planes(field, tail, head, first_out, second_out):
    even = even_strike()
    for i in range(first_out.shape[0]):
        comp, place = tail[min(i, len(tail) - 1)]
        right = field(comp, place % field.count)
        comp, place = head[min(i, len(head) - 1)]
        left = field(comp, place % field.count)
        first_out[i] = jnp.where(even, right, left)
        second_out[i] = jnp.where(even, left, right)


def fault_row(rows):
    return jnp.where(lax.axis_index("gy") == lax.axis_size("gy") // 2, 0, rows - 1)


def pack_kernel(r):
    count, rows, depths = r.stress.shape[1:]
    whole = [(comp, 0, count) for comp in STRESS_SLOTS]
    some = {}
    for comp, place in STRESS_TAIL + STRESS_HEAD:
        if comp not in STRESS_SLOTS:
            some.setdefault((comp, place < 0), []).append(place % count)
    some = [(comp, min(at), max(at) + 1) for (comp, _), at in some.items()]
    copies = []
    for i, (comp, start, stop) in enumerate(some + whole):
        span = pl.ds(start, stop - start)
        copy = pltpu.make_async_copy(r.stress.at[comp, span], r.held.at[comp, span], r.sems.at[i])
        copy.start()
        copies.append(copy)
    edges = Edges(rows, depths)
    for copy in copies:
        copy.wait()
    edge_planes(Field(count, r.held), STRESS_TAIL, STRESS_HEAD, r.one_out, r.two_out)
    for x in range(count):
        r.strip_out[x] = edges.packed([r.held[c, x] for c in STRESS_SLOTS])


def velocity_planes(r, xs, edges, planes, write):
    band = Bands(getattr(r, "lower", None), getattr(r, "upper", None), STRESS_TAIL_Y, STRESS_HEAD_Y)
    for x in xs:
        sxy, sxz, syz = planes(XY, x), planes(XZ, x), planes(YZ, x)
        push = DT * looked_up(r.material[x], r.table, 2, CLASSES)
        ends = r.strip[x]
        along_x = (
            planes.forward_x(XX, x)
            + edges.backward_y(sxy, band(XY, x))
            + edges.backward_z(sxz, ends, 0)
        )
        along_y = (
            planes.backward_x(XY, x)
            + edges.forward_y(planes(YY, x), band(YY, x))
            + edges.backward_z(syz, ends, 1)
        )
        along_z = (
            planes.backward_x(XZ, x)
            + edges.backward_y(syz, band(YZ, x))
            + edges.forward_z(planes(ZZ, x), ends, 2)
        )
        rates = (along_x, along_y, along_z)
        write(x, [r.velocity[c, x] + push * rate for c, rate in enumerate(rates)])


def velocity_inner(r):
    count, rows, depths = r.material.shape
    edges = Edges(rows, depths)
    planes = Planes(stress_of(r), STRESS_TAIL, STRESS_HEAD)

    def write(x, new):
        for c in range(3):
            r.inner_out[c, x - 2] = new[c]
        r.strip_inner_out[x - 2] = edges.packed(new)

    velocity_planes(r, inside(count), edges, planes, write)


def velocity_edge(first, r):
    count, rows, depths = r.material.shape
    edges = Edges(rows, depths)
    planes = Planes(stress_of(r), STRESS_TAIL, STRESS_HEAD, r.one, r.two)
    fault = fault_row(rows)
    places = ends_of(count)
    row = pl.ds(fault, 1)
    for x in inside(count):
        r.face_out[pl.ds(x, 1), :] = r.inner[0, x - 2, row, :]
        r.face_out[pl.ds(count + x, 1), :] = r.inner[2, x - 2, row, :]
        r.strip_out[x] = r.strip_inner[x - 2]
    if first:
        for x in range(count):
            labels = r.material[x, row, :]
            r.face_out[pl.ds(2 * count + x, 1), :] = looked_up(labels, r.table, 2, CLASSES)
    if hasattr(r, "prestress"):
        own = r.normal.shape[0]
        place = 3 * count
        for i in range(own):
            r.face_out[pl.ds(place + i, 1), :] = r.prestress[i, pl.ds(0, 1), :]
            r.face_out[pl.ds(place + own + i, 1), :] = r.prestress[i, pl.ds(1, 1), :]
        for i, field in enumerate((r.normal, r.slip, r.zone, r.mask)):
            r.face_out[pl.ds(place + (2 + i) * own, own), :] = field[...].astype(jnp.float32)

    def write(x, new):
        for c in range(3):
            r.edge_out[c, places.index(x)] = new[c]
        r.strip_out[x] = edges.packed(new)

    velocity_planes(r, places, edges, planes, write)
    for x in places:
        r.face_out[pl.ds(x, 1), :] = r.edge_out[0, places.index(x), row, :]
        r.face_out[pl.ds(count + x, 1), :] = r.edge_out[2, places.index(x), row, :]
    new = Field(count, r.inner, r.edge_out)
    edge_planes(new, VEL_TAIL, VEL_HEAD, r.one_out, r.two_out)


def stress_of(r):
    count = r.material.shape[0]
    if hasattr(r, "stress"):
        return Field(count, r.stress)
    return Field(count, r.stress_inner, r.stress_edge)


def memory_of(r):
    count = r.material.shape[0]
    if hasattr(r, "memory"):
        return Field(count, r.memory)
    return Field(count, r.memory_inner, r.memory_edge)


def fault_kernel(first, r):
    own_face, other_face = r.face, r.other
    own_first, other_first = (own_face, other_face) if first else (r.face_first, r.other_first)
    count, rows, depths = r.strip.shape
    middle = lax.axis_size("gy") // 2
    side = lax.axis_index("gy")
    plus = side == middle
    minus = side == middle - 1

    def pair(own, other, place):
        mine, theirs = own[pl.ds(place, count), :], other[pl.ds(place, count), :]
        return jnp.where(plus, theirs, mine), jnp.where(plus, mine, theirs)

    if hasattr(r, "still"):
        still = r.still
    else:
        still = r.still_out
        share = (own_face.shape[0] - 3 * count) // 6
        for i in range(6):
            mine = own_face[pl.ds(3 * count + i * share, share), :]
            theirs = other_face[pl.ds(3 * count + i * share, share), :]
            still[i, pl.ds(0, share), :] = jnp.where(plus, theirs, mine)
            still[i, pl.ds(share, share), :] = jnp.where(plus, mine, theirs)
    pre_x, pre_z, normal = still[0], still[1], still[2]
    slip = still[3] if first else r.slip[...]
    zone, mask = still[4], still[5]

    row = lax.broadcasted_iota(jnp.int32, (count, depths), 0) + lax.axis_index("gx") * count
    deep = lax.broadcasted_iota(jnp.int32, (count, depths), 1) + lax.axis_index("gz") * depths
    inside = (row >= r.anchor[0]) & (row < r.anchor[0] + 2 * PATCH)
    inside = inside & (deep >= r.anchor[1]) & (deep < r.anchor[1] + 2 * PATCH)
    dynamic = 0.4 * looked_up(zone, r.friction, 0, ZONES)
    static = jnp.where(
        inside, dynamic, dynamic + 0.5 * looked_up(zone, r.friction, 1, ZONES)
    )
    distance = 0.2 * looked_up(zone, r.friction, 2, ZONES)
    minus_x, plus_x = pair(own_face, other_face, 0)
    minus_z, plus_z = pair(own_face, other_face, count)
    minus_b, plus_b = pair(own_first, other_first, 2 * count)
    bsum = minus_b + plus_b
    trial_x = (plus_x - minus_x) / (DT * bsum) + pre_x
    trial_z = (plus_z - minus_z) / (DT * bsum) + pre_z
    size = jnp.sqrt(trial_x * trial_x + trial_z * trial_z)
    weaken = jnp.minimum(slip / distance, 1.0)
    strength = (static - (static - dynamic) * weaken) * normal
    factor = jnp.where(mask == 1.0, strength / jnp.maximum(size, strength), 1.0)
    r.slip_out[...] = slip + DT * DT * bsum * (size - size * factor)
    sign = jnp.where(minus, DT, 0.0) * minus_b - jnp.where(plus, DT, 0.0) * plus_b
    change_x = (trial_x * factor - pre_x) * sign
    change_z = (trial_z * factor - pre_z) * sign
    r.change_out[0] = change_x
    r.change_out[1] = change_z

    fault = fault_row(rows)
    on_fault = lax.broadcasted_iota(jnp.int32, (rows, depths), 0) == fault
    even = even_strike()
    still_line = jnp.zeros((1, depths), jnp.float32)

    def line(planes, i):
        comp, place = planes[min(i, len(planes) - 1)]
        return still_line if comp == 1 else r.change_out[comp // 2, pl.ds(place % count, 1), :]

    for i in range(r.one_out.shape[0]):
        right, left = line(VEL_TAIL, i), line(VEL_HEAD, i)
        one, two = jnp.where(even, right, left), jnp.where(even, left, right)
        r.one_out[i] = r.one[i] + jnp.where(on_fault, one, 0.0)
        r.two_out[i] = r.two[i] + jnp.where(on_fault, two, 0.0)
    flat = Edges(count, depths)
    ends = flat.packed([change_x, None, change_z])
    for x in range(count):
        r.strip_out[x] = r.strip[x] + jnp.where(on_fault, ends[x : x + 1, :], 0.0)


def stress_planes(r, xs, edges, planes, write):
    band = Bands(getattr(r, "lower", None), getattr(r, "upper", None), VEL_TAIL_Y, VEL_HEAD_Y)
    stress, memory = stress_of(r), memory_of(r)
    for x in xs:
        vx, vy, vz = planes(0, x), planes(1, x), planes(2, x)
        ends = r.strip[x]
        exx = planes.backward_x(0, x)
        eyy = edges.backward_y(vy, band(1, x))
        ezz = edges.backward_z(vz, ends, 2)
        exy = edges.forward_y(vx, band(0, x)) + planes.forward_x(1, x)
        exz = edges.forward_z(vx, ends, 0) + planes.forward_x(2, x)
        eyz = edges.forward_z(vy, ends, 1) + edges.forward_y(vz, band(2, x))
        labels = r.material[x]
        lame = looked_up(labels, r.table, 0, CLASSES)
        shear = looked_up(labels, r.table, 1, CLASSES)
        decay = jnp.exp(-DT / looked_up(labels, r.table, 3, CLASSES))
        gain = (1.0 - decay) * (0.3 * looked_up(labels, r.table, 4, CLASSES))
        bulk = lame * (exx + eyy + ezz)
        double = 2.0 * shear
        elastic = (
            bulk + double * exx,
            bulk + double * eyy,
            bulk + double * ezz,
            shear * exy,
            shear * exz,
            shear * eyz,
        )
        kept = [decay * memory(c, x) - gain * elastic[c] for c in range(6)]
        new = [stress(c, x) + DT * (elastic[c] + kept[c]) for c in range(6)]
        write(x, new, kept)


def stress_inner(last, r):
    count, rows, depths = r.material.shape
    edges = Edges(rows, depths)
    on_fault = edges.row == fault_row(rows)
    free = Field(count, r.inner, r.edge)
    for x in range(count):
        for c in (0, 2):
            line = r.change[c // 2, pl.ds(x, 1), :]
            r.velocity_out[c, x] = free(c, x) + jnp.where(on_fault, line, 0.0)
        r.velocity_out[1, x] = free(1, x)
    planes = Planes(Field(count, r.velocity_out), VEL_TAIL, VEL_HEAD)

    def write(x, new, kept):
        for c in range(6):
            r.stress_inner_out[c, x - 2] = new[c]
            r.memory_inner_out[c, x - 2] = kept[c]
        if not last:
            r.strip_inner_out[x - 2] = edges.packed([new[c] for c in STRESS_SLOTS])

    stress_planes(r, inside(count), edges, planes, write)


def stress_edge(last, r):
    count, rows, depths = r.material.shape
    edges = Edges(rows, depths)
    planes = Planes(Field(count, r.velocity), VEL_TAIL, VEL_HEAD, r.one, r.two)
    places = ends_of(count)
    copies = []

    def copy_out(source, out, span):
        copy = pltpu.make_async_copy(source, out.at[:, span], r.sems.at[len(copies)])
        copy.start()
        copies.append(copy)

    if last:
        copy_out(r.velocity, r.velocity_out, pl.ds(0, count))
        copy_out(r.new_stress_inner, r.stress_out, pl.ds(2, count - 4))
        copy_out(r.new_memory_inner, r.memory_out, pl.ds(2, count - 4))
        stress_out, memory_out = r.stress_held, r.memory_held
    else:
        stress_out, memory_out = r.stress_edge_out, r.memory_edge_out
        for x in inside(count):
            r.strip_out[x] = r.strip_inner[x - 2]

    def write(x, new, kept):
        for c in range(6):
            stress_out[c, places.index(x)] = new[c]
            memory_out[c, places.index(x)] = kept[c]
        if not last:
            r.strip_out[x] = edges.packed([new[c] for c in STRESS_SLOTS])

    stress_planes(r, places, edges, planes, write)
    if last:
        for held, out in ((stress_out, r.stress_out), (memory_out, r.memory_out)):
            copy_out(held.at[:, pl.ds(0, 2)], out, pl.ds(0, 2))
            copy_out(held.at[:, pl.ds(2, 2)], out, pl.ds(count - 2, 2))
        for copy in copies:
            copy.wait()
    else:
        new = Field(count, r.new_stress_inner, stress_out)
        edge_planes(new, STRESS_TAIL, STRESS_HEAD, r.one_out, r.two_out)


SCALARS = ("table", "friction", "anchor")


def call(kernel, name, ins, outs, scratch=None, apart=(), cost=0, vmem=14):
    scratch = scratch or {}
    names = [*ins, *(f"{key}_out" for key in outs), *scratch]

    def body(*refs):
        kernel(types.SimpleNamespace(**dict(zip(names, refs))))

    def place(key):
        if key in apart:
            return pl.BlockSpec(memory_space=pltpu.HBM)
        return pl.BlockSpec(memory_space=pltpu.SMEM if key in SCALARS else pltpu.VMEM)

    shapes = [jax.ShapeDtypeStruct(shape, jnp.float32) for shape in outs.values()]
    moved = 4 * (sum(a.size for a in ins.values()) + sum(math.prod(o.shape) for o in shapes))
    result = pl.pallas_call(
        body,
        out_shape=shapes,
        in_specs=[place(key) for key in ins],
        out_specs=[place(f"{key}_out") for key in outs],
        scratch_shapes=list(scratch.values()),
        name=name,
        cost_estimate=pl.CostEstimate(flops=cost, bytes_accessed=moved, transcendentals=0),
        compiler_params=pltpu.CompilerParams(vmem_limit_bytes=vmem * 2**20),
    )(*ins.values())
    return dict(zip(outs, result))


def along(axis, count, skip=()):
    up = [(i, i + 1) for i in range(count - 1) if i not in skip]
    return (axis, up), (axis, [(b, a) for a, b in up])


def strike_swaps(count):
    routes = []
    for start in (0, 1):
        partner = list(range(count))
        for i in range(start, count - 1, 2):
            partner[i], partner[i + 1] = i + 1, i
        routes.append(("gx", list(enumerate(partner))))
    return routes


def sent(block, route):
    return lax.ppermute(block, *route)


def whole(parts, name):
    if name in parts:
        return parts[name]
    inner, edge = parts[f"{name}_inner"], parts[f"{name}_edge"]
    return jnp.concatenate([edge[:, :2], inner, edge[:, 2:]], axis=1)


def edge_rows(field, rows):
    count = field.shape[2]
    return jnp.stack([field[c, :, place % count, :] for c, place in rows])


def shards(
    velocity,
    stress,
    memory,
    material,
    material_table,
    fault_mask,
    zone_label,
    patch_anchor,
    friction_table,
    prestress,
    normal_stress,
    slip_path,
):
    _, count, rows, depths = velocity.shape
    sides = lax.axis_size("gy")
    middle = sides // 2
    banded = sides > 2
    cells = count * rows * depths
    swaps = strike_swaps(lax.axis_size("gx"))
    up_y, down_y = along("gy", sides, (middle - 1,))
    across = ("gy", [(middle - 1, middle), (middle, middle - 1)])
    deep = ("gz", [(0, 1), (1, 0)])

    plane = (rows, depths)
    edge_shape = (max(len(STRESS_TAIL), len(STRESS_HEAD)), *plane)
    travelling = {"one": edge_shape, "two": edge_shape, "strip": (count, *plane)}
    inner, edge = (count - 4, *plane), (4, *plane)

    def travelled(packed):
        two = sent(packed["two"], swaps[1])
        one = sent(packed["one"], swaps[0])
        strip = sent(packed["strip"], deep)
        return {"strip": strip}, {"one": one, "two": two}

    def bands(field, tail, head):
        if not banded:
            return {}
        lower, upper = edge_rows(field, tail), edge_rows(field, head)
        return {"lower": sent(lower, up_y), "upper": sent(upper, down_y)}

    if banded:
        still = jnp.stack(
            [
                prestress[:, 0],
                prestress[:, 1],
                normal_stress,
                slip_path,
                zone_label.astype(jnp.float32),
                fault_mask.astype(jnp.float32),
            ]
        )
        still = {"still": lax.all_gather(still, "gy", axis=1, tiled=True)}
    else:
        still = {}

    parts = {"stress": stress, "memory": memory}
    props = {"material": material, "table": material_table}
    packed = call(
        pack_kernel,
        "pack",
        {"stress": stress},
        travelling,
        scratch={"held": pltpu.VMEM(stress.shape, jnp.float32), "sems": pltpu.SemaphoreType.DMA((8,))},
        apart=("stress",),
        vmem=14,
    )
    for step in range(STEPS):
        first, last = step == 0, step == STEPS - 1
        held_stress = {key: parts[key] for key in parts if key.startswith("stress")}
        strip, halos = travelled(packed)
        ins = {"velocity": velocity, **held_stress, **props, **strip}
        if banded:
            ins.update(bands(whole(parts, "stress"), STRESS_TAIL_Y, STRESS_HEAD_Y))
        free = call(
            velocity_inner,
            "velocity_inner",
            ins,
            {"inner": (3, *inner), "strip_inner": inner},
            cost=60 * cells,
        )
        face_rows = 2 * count
        ins = {**ins, **halos, **free}
        if first:
            face_rows += count
            if not banded:
                ins.update(prestress=prestress, normal=normal_stress, slip=slip_path)
                ins.update(zone=zone_label, mask=fault_mask)
                face_rows += 6 * normal_stress.shape[0]
        packed = call(
            functools.partial(velocity_edge, first),
            "velocity_edge",
            ins,
            {"edge": (3, *edge), "face": (face_rows, depths), **travelling},
            cost=20 * cells,
        )
        free = {"inner": free["inner"], "edge": packed["edge"]}
        face = packed["face"]
        other = sent(face, across)
        ins = {key: packed[key] for key in travelling}
        ins.update(face=face, other=other, friction=friction_table, anchor=patch_anchor, **still)
        if first:
            faces = {"face_first": face, "other_first": other}
        else:
            ins.update(slip=slip, **faces)
        outs = {"change": (2, count, depths), "slip": (count, depths), **travelling}
        if not still:
            outs["still"] = (6, count, depths)
        packed = call(functools.partial(fault_kernel, first), "fault", ins, outs)
        slip = packed["slip"]
        if not still:
            still = {"still": packed["still"]}
        strip, halos = travelled(packed)
        ins = {**free, "change": packed["change"], **parts, **props, **strip}
        if banded:
            joined = jnp.concatenate(
                [free["edge"][:, :2], free["inner"], free["edge"][:, 2:]], axis=1
            )
            band = bands(joined, VEL_TAIL_Y, VEL_HEAD_Y)
        else:
            band = {}
        outs = {"velocity": velocity.shape, "stress_inner": (6, *inner), "memory_inner": (6, *inner)}
        if not last:
            outs["strip_inner"] = inner
        done = call(
            functools.partial(stress_inner, last), "stress_inner", {**ins, **band}, outs, cost=100 * cells
        )
        velocity = done["velocity"]
        ins = {"velocity": velocity, **parts, **props, **strip, **halos, **band}
        ins["new_stress_inner"] = done["stress_inner"]
        if last:
            ins["new_memory_inner"] = done["memory_inner"]
            held = pltpu.VMEM((6, *edge), jnp.float32)
            packed = call(
                functools.partial(stress_edge, last),
                "stress_edge",
                ins,
                {"velocity": velocity.shape, "stress": stress.shape, "memory": memory.shape},
                scratch={
                    "stress_held": held,
                    "memory_held": held,
                    "sems": pltpu.SemaphoreType.DMA((7,)),
                },
                apart=("velocity_out", "stress_out", "memory_out"),
            )
            velocity, stress, memory = packed["velocity"], packed["stress"], packed["memory"]
        else:
            ins["strip_inner"] = done["strip_inner"]
            packed = call(
                functools.partial(stress_edge, last),
                "stress_edge",
                ins,
                {"stress_edge": (6, *edge), "memory_edge": (6, *edge), **travelling},
                cost=30 * cells,
            )
            parts = {
                "stress_inner": done["stress_inner"],
                "stress_edge": packed["stress_edge"],
                "memory_inner": done["memory_inner"],
                "memory_edge": packed["memory_edge"],
            }
    side = lax.axis_index("gy")
    if banded:
        held = jnp.where(side == middle, slip, 0.0)
        new_slip = lax.psum_scatter(held, "gy", scatter_dimension=0, tiled=True)
    else:
        share = count // sides
        new_slip = lax.dynamic_slice_in_dim(slip, side * share, share, axis=0)
    return (velocity, stress, memory, new_slip)


def solution(mesh):
    in_specs = (
        P(None, ("ens", "gx"), "gy", "gz"),
        P(None, ("ens", "gx"), "gy", "gz"),
        P(None, ("ens", "gx"), "gy", "gz"),
        P(("ens", "gx"), "gy", "gz"),
        P(None, "ens"),
        P(("ens", "gx", "gy"), "gz"),
        P(("ens", "gx", "gy"), "gz"),
        P("ens"),
        P(None, "ens"),
        P(("ens", "gx", "gy"), None, "gz"),
        P(("ens", "gx", "gy"), "gz"),
        P(("ens", "gx", "gy"), "gz"),
    )
    out_specs = (
        P(None, ("ens", "gx"), "gy", "gz"),
        P(None, ("ens", "gx"), "gy", "gz"),
        P(None, ("ens", "gx"), "gy", "gz"),
        P(("ens", "gx", "gy"), "gz"),
    )
    return jax.shard_map(shards, mesh=mesh, in_specs=in_specs, out_specs=out_specs, check_vma=False)
```

```python
import functools
import math
import types

import jax
import jax.numpy as jnp
from jax import lax
from jax.experimental import pallas as pl
from jax.experimental.pallas import tpu as pltpu
from jax.sharding import PartitionSpec as P

STEPS = 2
CLASSES = 8
ZONES = 4
PATCH = 8

NEAR = 9.0 / 8.0
FAR = -1.0 / 24.0
DT = 0.15
TILE = 8

XX, YY, ZZ, XY, XZ, YZ = range(6)

STRESS_TAIL = ((XX, -1), (XY, -2), (XY, -1), (XZ, -2), (XZ, -1))
STRESS_HEAD = ((XX, 0), (XX, 1), (XY, 0), (XZ, 0))
VEL_TAIL = ((0, -2), (0, -1), (1, -1), (2, -1))
VEL_HEAD = ((0, 0), (1, 0), (1, 1), (2, 0), (2, 1))
STRESS_TAIL_Y = ((YY, -1), (XY, -2), (XY, -1), (YZ, -2), (YZ, -1))
STRESS_HEAD_Y = ((YY, 0), (YY, 1), (XY, 0), (YZ, 0))
VEL_TAIL_Y = ((1, -2), (1, -1), (0, -1), (2, -1))
VEL_HEAD_Y = ((1, 0), (0, 0), (0, 1), (2, 0), (2, 1))
STRESS_SLOTS = (XZ, YZ, ZZ)
VEL_SLOTS = (0, 1, 2)


def forward(before, here, after, after_2):
    return NEAR * (after - here) + FAR * (after_2 - before)


def backward(before_2, before, here, after):
    return NEAR * (here - before) + FAR * (after - before_2)


class Edges:
    def __init__(self, rows, depths):
        self.rows = rows
        self.depths = depths
        lane = lax.broadcasted_iota(jnp.int32, (rows, depths), 1)
        row = lax.broadcasted_iota(jnp.int32, (TILE, depths), 0)
        self.row = lax.broadcasted_iota(jnp.int32, (rows, depths), 0)
        self.tile_row = row
        self.deep = lax.axis_index("gz")
        self.upper = jnp.where(self.deep == 0, 1.0, 0.0)
        self.zero = jnp.minimum(self.deep, 0)
        self.pair = lane // 2
        self.low = {n: lane < n for n in (1, 2)}
        self.high = {n: lane >= depths - n for n in (1, 2)}
        self.top = {n: row < n for n in (1, 2)}
        self.bottom = {n: row >= TILE - n for n in (1, 2)}

    def packed(self, strip, x, fields):
        first = jnp.where(self.deep == 0, 2, 0)
        for k, field in enumerate(fields):
            turn = lax.rem(first + 8 * x + 2 * k, self.depths)
            strip = jnp.where(self.pair == 4 * x + k, pltpu.roll(field, turn, 1), strip)
        return strip

    def ends(self, strip, x, k):
        back = self.depths - 8 * x - 2 * k
        turn = jnp.where(self.deep == 0, back % self.depths, back - 2)
        halo = pltpu.roll(strip, turn, 1)
        return halo * self.upper, halo * (1.0 - self.upper)

    def shallower(self, field, halo, n):
        return pltpu.roll(jnp.where(self.high[n], halo, field), n, 1)

    def deeper(self, field, halo, n):
        return pltpu.roll(jnp.where(self.low[n], halo, field), self.depths - n, 1)

    def forward_z(self, field, halos):
        after, before = halos
        return forward(
            self.shallower(field, before, 1),
            field,
            self.deeper(field, after, 1),
            self.deeper(field, after, 2),
        )

    def backward_z(self, field, halos):
        after, before = halos
        return backward(
            self.shallower(field, before, 2),
            self.shallower(field, before, 1),
            field,
            self.deeper(field, after, 1),
        )

    def before(self, field, load, n, halo):
        top = jnp.where(self.top[n], 0.0, pltpu.roll(field[:TILE], n, 0))
        if halo:
            for i in range(n):
                top = jnp.where(self.tile_row == i, halo[n - 1 - i], top)
        return jnp.concatenate([top, load(self.zero + (TILE - n), self.rows - TILE)], axis=0)

    def after(self, field, load, n, halo):
        bottom = pltpu.roll(field[self.rows - TILE :], TILE - n, 0)
        bottom = jnp.where(self.bottom[n], 0.0, bottom)
        if halo:
            for i in range(n):
                bottom = jnp.where(self.tile_row == TILE - n + i, halo[i], bottom)
        return jnp.concatenate([load(self.zero + n, self.rows - TILE), bottom], axis=0)

    def forward_y(self, planes, comp, x, halos):
        field, load = planes(comp, x), planes.rows(comp, x)
        lower, upper = halos
        return forward(
            self.before(field, load, 1, lower),
            field,
            self.after(field, load, 1, upper),
            self.after(field, load, 2, upper),
        )

    def backward_y(self, planes, comp, x, halos):
        field, load = planes(comp, x), planes.rows(comp, x)
        lower, upper = halos
        return backward(
            self.before(field, load, 2, lower),
            self.before(field, load, 1, lower),
            field,
            self.after(field, load, 1, upper),
        )


class Field:
    def __init__(self, count, *parts):
        self.count = count
        self.parts = parts

    def place(self, x):
        if len(self.parts) == 1:
            return self.parts[0], x
        inner, edge = self.parts
        if x in inside(self.count):
            return inner, x - 2
        return edge, ends_of(self.count).index(x)

    def __call__(self, comp, x):
        ref, at = self.place(x)
        return ref[comp, at]

    def rows(self, comp, x):
        ref, at = self.place(x)
        return lambda start, size: ref[comp, at, pl.ds(start, size), :]


def inside(count):
    return range(2, count - 2)


def ends_of(count):
    return (0, 1, count - 2, count - 1)


class Planes:
    def __init__(self, field, tail, head, first=None, second=None):
        self.field = field
        self.count = field.count
        self.first, self.second = first, second
        self.tail, self.head = tail, head
        self.even = even_strike()
        self.any_left = lax.axis_index("gx") > 0
        self.any_right = lax.axis_index("gx") < lax.axis_size("gx") - 1

    def left(self, i):
        plane = jnp.where(self.even, self.second[i], self.first[i])
        return jnp.where(self.any_left, plane, 0.0)

    def right(self, i):
        plane = jnp.where(self.even, self.first[i], self.second[i])
        return jnp.where(self.any_right, plane, 0.0)

    def __call__(self, comp, place):
        if place < 0:
            return self.left(self.tail.index((comp, place)))
        if place >= self.count:
            return self.right(self.head.index((comp, place - self.count)))
        return self.field(comp, place)

    def rows(self, comp, x):
        return self.field.rows(comp, x)

    def forward_x(self, comp, x):
        return forward(self(comp, x - 1), self(comp, x), self(comp, x + 1), self(comp, x + 2))

    def backward_x(self, comp, x):
        return backward(self(comp, x - 2), self(comp, x - 1), self(comp, x), self(comp, x + 1))


class Bands:
    def __init__(self, lower, upper, tail, head):
        self.lower, self.upper = lower, upper
        self.tail, self.head = tail, head

    def __call__(self, comp, x):
        if self.lower is None:
            return (None, None)
        places = [i for i, (c, _) in enumerate(self.tail) if c == comp]
        before = [self.lower[i, pl.ds(x, 1), :] for i in reversed(places)]
        places = [i for i, (c, _) in enumerate(self.head) if c == comp]
        after = [self.upper[i, pl.ds(x, 1), :] for i in places]
        return (before, after)


def looked_up(labels, table, row, count):
    out = jnp.full(labels.shape, table[row, 0], jnp.float32)
    for k in range(1, count):
        out = jnp.where(labels == k, table[row, k], out)
    return out


def even_strike():
    return lax.axis_index("gx") % 2 == 0


def edge_planes(field, tail, head, first_out, second_out):
    even = even_strike()
    for i in range(first_out.shape[0]):
        comp, place = tail[min(i, len(tail) - 1)]
        right = field(comp, place % field.count)
        comp, place = head[min(i, len(head) - 1)]
        left = field(comp, place % field.count)
        first_out[i] = jnp.where(even, right, left)
        second_out[i] = jnp.where(even, left, right)


def fault_row(rows):
    return jnp.where(lax.axis_index("gy") == lax.axis_size("gy") // 2, 0, rows - 1)


def pack_kernel(r):
    count, rows, depths = r.stress.shape[1:]
    whole = [(comp, 0, count) for comp in STRESS_SLOTS]
    some = {}
    for comp, place in STRESS_TAIL + STRESS_HEAD:
        if comp not in STRESS_SLOTS:
            some.setdefault((comp, place < 0), []).append(place % count)
    some = [(comp, min(at), max(at) + 1) for (comp, _), at in some.items()]
    copies = []
    for i, (comp, start, stop) in enumerate(some + whole):
        span = pl.ds(start, stop - start)
        copy = pltpu.make_async_copy(r.stress.at[comp, span], r.held.at[comp, span], r.sems.at[i])
        copy.start()
        copies.append(copy)
    edges = Edges(rows, depths)
    for copy in copies:
        copy.wait()
    edge_planes(Field(count, r.held), STRESS_TAIL, STRESS_HEAD, r.one_out, r.two_out)
    strip = jnp.zeros((rows, depths), jnp.float32)
    for x in range(count):
        strip = edges.packed(strip, x, [r.held[c, x] for c in STRESS_SLOTS])
    r.strip_out[...] = strip


def velocity_planes(r, xs, edges, planes, write):
    band = Bands(getattr(r, "lower", None), getattr(r, "upper", None), STRESS_TAIL_Y, STRESS_HEAD_Y)
    strip = r.strip[...]
    for x in xs:
        push = DT * looked_up(r.material[x], r.table, 2, CLASSES)
        along_x = (
            planes.forward_x(XX, x)
            + edges.backward_y(planes, XY, x, band(XY, x))
            + edges.backward_z(planes(XZ, x), edges.ends(strip, x, 0))
        )
        along_y = (
            planes.backward_x(XY, x)
            + edges.forward_y(planes, YY, x, band(YY, x))
            + edges.backward_z(planes(YZ, x), edges.ends(strip, x, 1))
        )
        along_z = (
            planes.backward_x(XZ, x)
            + edges.backward_y(planes, YZ, x, band(YZ, x))
            + edges.forward_z(planes(ZZ, x), edges.ends(strip, x, 2))
        )
        rates = (along_x, along_y, along_z)
        write(x, [r.velocity[c, x] + push * rate for c, rate in enumerate(rates)])


def velocity_inner(r):
    count, rows, depths = r.material.shape
    edges = Edges(rows, depths)
    planes = Planes(stress_of(r), STRESS_TAIL, STRESS_HEAD)
    packed = [jnp.zeros((rows, depths), jnp.float32)]

    def write(x, new):
        for c in range(3):
            r.inner_out[c, x - 2] = new[c]
        packed[0] = edges.packed(packed[0], x, new)

    velocity_planes(r, inside(count), edges, planes, write)
    r.strip_inner_out[...] = packed[0]


def velocity_edge(first, r):
    count, rows, depths = r.material.shape
    edges = Edges(rows, depths)
    planes = Planes(stress_of(r), STRESS_TAIL, STRESS_HEAD, r.one, r.two)
    fault = fault_row(rows)
    places = ends_of(count)
    row = pl.ds(fault, 1)
    for x in inside(count):
        r.face_out[pl.ds(x, 1), :] = r.inner[0, x - 2, row, :]
        r.face_out[pl.ds(count + x, 1), :] = r.inner[2, x - 2, row, :]
    if first:
        for x in range(count):
            labels = r.material[x, row, :]
            r.face_out[pl.ds(2 * count + x, 1), :] = looked_up(labels, r.table, 2, CLASSES)
    if hasattr(r, "prestress"):
        own = r.normal.shape[0]
        place = 3 * count
        for i in range(own):
            r.face_out[pl.ds(place + i, 1), :] = r.prestress[i, pl.ds(0, 1), :]
            r.face_out[pl.ds(place + own + i, 1), :] = r.prestress[i, pl.ds(1, 1), :]
        for i, field in enumerate((r.normal, r.slip, r.zone, r.mask)):
            r.face_out[pl.ds(place + (2 + i) * own, own), :] = field[...].astype(jnp.float32)

    packed = [r.strip_inner[...]]

    def write(x, new):
        for c in range(3):
            r.edge_out[c, places.index(x)] = new[c]
        packed[0] = edges.packed(packed[0], x, new)

    velocity_planes(r, places, edges, planes, write)
    r.strip_out[...] = packed[0]
    for x in places:
        r.face_out[pl.ds(x, 1), :] = r.edge_out[0, places.index(x), row, :]
        r.face_out[pl.ds(count + x, 1), :] = r.edge_out[2, places.index(x), row, :]
    new = Field(count, r.inner, r.edge_out)
    edge_planes(new, VEL_TAIL, VEL_HEAD, r.one_out, r.two_out)


def stress_of(r):
    count = r.material.shape[0]
    if hasattr(r, "stress"):
        return Field(count, r.stress)
    return Field(count, r.stress_inner, r.stress_edge)


def memory_of(r):
    count = r.material.shape[0]
    if hasattr(r, "memory"):
        return Field(count, r.memory)
    return Field(count, r.memory_inner, r.memory_edge)


def fault_kernel(first, r):
    own_face, other_face = r.face, r.other
    own_first, other_first = (own_face, other_face) if first else (r.face_first, r.other_first)
    rows, depths = r.strip.shape
    count = r.change_out.shape[1]
    middle = lax.axis_size("gy") // 2
    side = lax.axis_index("gy")
    plus = side == middle
    minus = side == middle - 1

    def pair(own, other, place):
        mine, theirs = own[pl.ds(place, count), :], other[pl.ds(place, count), :]
        return jnp.where(plus, theirs, mine), jnp.where(plus, mine, theirs)

    if hasattr(r, "still"):
        still = r.still
    else:
        still = r.still_out
        share = (own_face.shape[0] - 3 * count) // 6
        for i in range(6):
            mine = own_face[pl.ds(3 * count + i * share, share), :]
            theirs = other_face[pl.ds(3 * count + i * share, share), :]
            still[i, pl.ds(0, share), :] = jnp.where(plus, theirs, mine)
            still[i, pl.ds(share, share), :] = jnp.where(plus, mine, theirs)
    pre_x, pre_z, normal = still[0], still[1], still[2]
    slip = still[3] if first else r.slip[...]
    zone, mask = still[4], still[5]

    row = lax.broadcasted_iota(jnp.int32, (count, depths), 0) + lax.axis_index("gx") * count
    deep = lax.broadcasted_iota(jnp.int32, (count, depths), 1) + lax.axis_index("gz") * depths
    inside = (row >= r.anchor[0]) & (row < r.anchor[0] + 2 * PATCH)
    inside = inside & (deep >= r.anchor[1]) & (deep < r.anchor[1] + 2 * PATCH)
    dynamic = 0.4 * looked_up(zone, r.friction, 0, ZONES)
    static = jnp.where(
        inside, dynamic, dynamic + 0.5 * looked_up(zone, r.friction, 1, ZONES)
    )
    distance = 0.2 * looked_up(zone, r.friction, 2, ZONES)
    minus_x, plus_x = pair(own_face, other_face, 0)
    minus_z, plus_z = pair(own_face, other_face, count)
    minus_b, plus_b = pair(own_first, other_first, 2 * count)
    bsum = minus_b + plus_b
    trial_x = (plus_x - minus_x) / (DT * bsum) + pre_x
    trial_z = (plus_z - minus_z) / (DT * bsum) + pre_z
    size = jnp.sqrt(trial_x * trial_x + trial_z * trial_z)
    weaken = jnp.minimum(slip / distance, 1.0)
    strength = (static - (static - dynamic) * weaken) * normal
    factor = jnp.where(mask == 1.0, strength / jnp.maximum(size, strength), 1.0)
    new_slip = slip + DT * DT * bsum * (size - size * factor)
    if r.slip_out.shape[0] == count:
        r.slip_out[...] = new_slip
    else:
        half = r.slip_out.shape[0]
        r.slip_out[...] = jnp.where(plus, new_slip[half:], new_slip[:half])
    sign = jnp.where(minus, DT, 0.0) * minus_b - jnp.where(plus, DT, 0.0) * plus_b
    change_x = (trial_x * factor - pre_x) * sign
    change_z = (trial_z * factor - pre_z) * sign
    r.change_out[0] = change_x
    r.change_out[1] = change_z

    fault = fault_row(rows)
    on_fault = lax.broadcasted_iota(jnp.int32, (rows, depths), 0) == fault
    even = even_strike()
    still_line = jnp.zeros((1, depths), jnp.float32)

    def line(planes, i):
        comp, place = planes[min(i, len(planes) - 1)]
        return still_line if comp == 1 else r.change_out[comp // 2, pl.ds(place % count, 1), :]

    for i in range(r.one_out.shape[0]):
        right, left = line(VEL_TAIL, i), line(VEL_HEAD, i)
        one, two = jnp.where(even, right, left), jnp.where(even, left, right)
        r.one_out[i] = r.one[i] + jnp.where(on_fault, one, 0.0)
        r.two_out[i] = r.two[i] + jnp.where(on_fault, two, 0.0)
    ends = jnp.zeros((count, depths), jnp.float32)
    pair = lax.broadcasted_iota(jnp.int32, (count, depths), 1) // 2
    place = 4 * lax.broadcasted_iota(jnp.int32, (count, depths), 0)
    upper = lax.axis_index("gz") == 0
    for k, field in ((0, change_x), (2, change_z)):
        turned = jnp.where(upper, pltpu.roll(field, 2, 1), field)
        turned = pltpu.roll(turned, 2 * k, 1, stride=8, stride_axis=0)
        ends = jnp.where(pair == place + k, turned, ends)
    line = jnp.sum(ends, axis=0, keepdims=True)
    r.strip_out[...] = r.strip[...] + jnp.where(on_fault, line, 0.0)


def stress_planes(r, xs, edges, planes, write):
    band = Bands(getattr(r, "lower", None), getattr(r, "upper", None), VEL_TAIL_Y, VEL_HEAD_Y)
    stress, memory = stress_of(r), memory_of(r)
    strip = r.strip[...]
    for x in xs:
        in_x, in_y, in_z = [edges.ends(strip, x, k) for k in range(3)]
        exx = planes.backward_x(0, x)
        eyy = edges.backward_y(planes, 1, x, band(1, x))
        ezz = edges.backward_z(planes(2, x), in_z)
        exy = edges.forward_y(planes, 0, x, band(0, x)) + planes.forward_x(1, x)
        exz = edges.forward_z(planes(0, x), in_x) + planes.forward_x(2, x)
        eyz = edges.forward_z(planes(1, x), in_y) + edges.forward_y(planes, 2, x, band(2, x))
        labels = r.material[x]
        lame = looked_up(labels, r.table, 0, CLASSES)
        shear = looked_up(labels, r.table, 1, CLASSES)
        decay = jnp.exp(-DT / looked_up(labels, r.table, 3, CLASSES))
        gain = (1.0 - decay) * (0.3 * looked_up(labels, r.table, 4, CLASSES))
        bulk = lame * (exx + eyy + ezz)
        double = 2.0 * shear
        elastic = (
            bulk + double * exx,
            bulk + double * eyy,
            bulk + double * ezz,
            shear * exy,
            shear * exz,
            shear * eyz,
        )
        kept = [decay * memory(c, x) - gain * elastic[c] for c in range(6)]
        new = [stress(c, x) + DT * (elastic[c] + kept[c]) for c in range(6)]
        write(x, new, kept)


def stress_inner(last, r):
    count, rows, depths = r.material.shape
    edges = Edges(rows, depths)
    on_fault = edges.row == fault_row(rows)
    free = Field(count, r.inner, r.edge)
    for x in range(count):
        for c in (0, 2):
            line = r.change[c // 2, pl.ds(x, 1), :]
            r.velocity_out[c, x] = free(c, x) + jnp.where(on_fault, line, 0.0)
        r.velocity_out[1, x] = free(1, x)
    planes = Planes(Field(count, r.velocity_out), VEL_TAIL, VEL_HEAD)
    packed = [jnp.zeros((rows, depths), jnp.float32)]
    if last:
        velocity_copy = pltpu.make_async_copy(
            r.velocity_out, r.new_velocity_out, r.sems.at[0]
        )
        velocity_copy.start()

    def write(x, new, kept):
        for c in range(6):
            r.stress_inner_out[c, x - 2] = new[c]
            r.memory_inner_out[c, x - 2] = kept[c]
        if not last:
            packed[0] = edges.packed(packed[0], x, [new[c] for c in STRESS_SLOTS])

    stress_planes(r, inside(count), edges, planes, write)
    if last:
        velocity_copy.wait()
    else:
        r.strip_inner_out[...] = packed[0]


def stress_edge(last, r):
    count, rows, depths = r.material.shape
    edges = Edges(rows, depths)
    planes = Planes(Field(count, r.velocity), VEL_TAIL, VEL_HEAD, r.one, r.two)
    places = ends_of(count)
    copies = []

    def copy_out(source, out, span):
        copy = pltpu.make_async_copy(source, out.at[:, span], r.sems.at[len(copies)])
        copy.start()
        copies.append(copy)

    if last:
        copy_out(r.new_stress_inner, r.stress_out, pl.ds(2, count - 4))
        copy_out(r.new_memory_inner, r.memory_out, pl.ds(2, count - 4))
        stress_out, memory_out = r.stress_held, r.memory_held
    else:
        stress_out, memory_out = r.stress_edge_out, r.memory_edge_out
        packed = [r.strip_inner[...]]

    def write(x, new, kept):
        for c in range(6):
            stress_out[c, places.index(x)] = new[c]
            memory_out[c, places.index(x)] = kept[c]
        if not last:
            packed[0] = edges.packed(packed[0], x, [new[c] for c in STRESS_SLOTS])

    stress_planes(r, places, edges, planes, write)
    if last:
        for held, out in ((stress_out, r.stress_out), (memory_out, r.memory_out)):
            copy_out(held.at[:, pl.ds(0, 2)], out, pl.ds(0, 2))
            copy_out(held.at[:, pl.ds(2, 2)], out, pl.ds(count - 2, 2))
        for copy in copies:
            copy.wait()
    else:
        r.strip_out[...] = packed[0]
        new = Field(count, r.new_stress_inner, stress_out)
        edge_planes(new, STRESS_TAIL, STRESS_HEAD, r.one_out, r.two_out)


SCALARS = ("table", "friction", "anchor")


def call(kernel, name, ins, outs, scratch=None, apart=(), cost=0, vmem=6):
    scratch = scratch or {}
    names = [*ins, *(f"{key}_out" for key in outs), *scratch]

    def body(*refs):
        kernel(types.SimpleNamespace(**dict(zip(names, refs))))

    def place(key):
        if key in apart:
            return pl.BlockSpec(memory_space=pltpu.HBM)
        return pl.BlockSpec(memory_space=pltpu.SMEM if key in SCALARS else pltpu.VMEM)

    shapes = [jax.ShapeDtypeStruct(shape, jnp.float32) for shape in outs.values()]
    moved = 4 * (sum(a.size for a in ins.values()) + sum(math.prod(o.shape) for o in shapes))
    result = pl.pallas_call(
        body,
        out_shape=shapes,
        in_specs=[place(key) for key in ins],
        out_specs=[place(f"{key}_out") for key in outs],
        scratch_shapes=list(scratch.values()),
        name=name,
        cost_estimate=pl.CostEstimate(flops=cost, bytes_accessed=moved, transcendentals=0),
        compiler_params=pltpu.CompilerParams(vmem_limit_bytes=vmem * 2**20),
    )(*ins.values())
    return dict(zip(outs, result))


def along(axis, count, skip=()):
    up = [(i, i + 1) for i in range(count - 1) if i not in skip]
    return (axis, up), (axis, [(b, a) for a, b in up])


def strike_swaps(count):
    routes = []
    for start in (0, 1):
        partner = list(range(count))
        for i in range(start, count - 1, 2):
            partner[i], partner[i + 1] = i + 1, i
        routes.append(("gx", list(enumerate(partner))))
    return routes


def sent(block, route):
    return lax.ppermute(block, *route)


def whole(parts, name):
    if name in parts:
        return parts[name]
    inner, edge = parts[f"{name}_inner"], parts[f"{name}_edge"]
    return jnp.concatenate([edge[:, :2], inner, edge[:, 2:]], axis=1)


def edge_rows(field, rows):
    count = field.shape[2]
    return jnp.stack([field[c, :, place % count, :] for c, place in rows])


def shards(
    velocity,
    stress,
    memory,
    material,
    material_table,
    fault_mask,
    zone_label,
    patch_anchor,
    friction_table,
    prestress,
    normal_stress,
    slip_path,
):
    _, count, rows, depths = velocity.shape
    sides = lax.axis_size("gy")
    middle = sides // 2
    banded = sides > 2
    cells = count * rows * depths
    swaps = strike_swaps(lax.axis_size("gx"))
    up_y, down_y = along("gy", sides, (middle - 1,))
    across = ("gy", [(middle - 1, middle), (middle, middle - 1)])
    deep = ("gz", [(0, 1), (1, 0)])

    plane = (rows, depths)
    edge_shape = (max(len(STRESS_TAIL), len(STRESS_HEAD)), *plane)
    travelling = {"one": edge_shape, "two": edge_shape, "strip": plane}
    inner, edge = (count - 4, *plane), (4, *plane)

    def travelled(packed):
        two = sent(packed["two"], swaps[1])
        one = sent(packed["one"], swaps[0])
        strip = sent(packed["strip"], deep)
        return {"strip": strip}, {"one": one, "two": two}

    def bands(field, tail, head):
        if not banded:
            return {}
        lower, upper = edge_rows(field, tail), edge_rows(field, head)
        return {"lower": sent(lower, up_y), "upper": sent(upper, down_y)}

    if banded:
        still = jnp.stack(
            [
                prestress[:, 0],
                prestress[:, 1],
                normal_stress,
                slip_path,
                zone_label.astype(jnp.float32),
                fault_mask.astype(jnp.float32),
            ]
        )
        still = {"still": lax.all_gather(still, "gy", axis=1, tiled=True)}
    else:
        still = {}

    parts = {"stress": stress, "memory": memory}
    props = {"material": material, "table": material_table}
    packed = call(
        pack_kernel,
        "pack",
        {"stress": stress},
        travelling,
        scratch={"held": pltpu.VMEM(stress.shape, jnp.float32), "sems": pltpu.SemaphoreType.DMA((8,))},
        apart=("stress",),
        vmem=6,
    )
    for step in range(STEPS):
        first, last = step == 0, step == STEPS - 1
        held_stress = {key: parts[key] for key in parts if key.startswith("stress")}
        strip, halos = travelled(packed)
        ins = {"velocity": velocity, **held_stress, **props, **strip}
        if banded:
            ins.update(bands(whole(parts, "stress"), STRESS_TAIL_Y, STRESS_HEAD_Y))
        free = call(
            velocity_inner,
            "velocity_inner",
            ins,
            {"inner": (3, *inner), "strip_inner": plane},
            cost=60 * cells,
        )
        face_rows = 2 * count
        ins = {**ins, **halos, **free}
        if first:
            face_rows += count
            if not banded:
                ins.update(prestress=prestress, normal=normal_stress, slip=slip_path)
                ins.update(zone=zone_label, mask=fault_mask)
                face_rows += 6 * normal_stress.shape[0]
        packed = call(
            functools.partial(velocity_edge, first),
            "velocity_edge",
            ins,
            {"edge": (3, *edge), "face": (face_rows, depths), **travelling},
            cost=20 * cells,
        )
        free = {"inner": free["inner"], "edge": packed["edge"]}
        face = packed["face"]
        other = sent(face, across)
        ins = {key: packed[key] for key in travelling}
        ins.update(face=face, other=other, friction=friction_table, anchor=patch_anchor, **still)
        if first:
            faces = {"face_first": face, "other_first": other}
        else:
            ins.update(slip=slip, **faces)
        outs = {"change": (2, count, depths), "slip": (count, depths), **travelling}
        if last and not banded:
            outs["slip"] = (count // sides, depths)
        if not still:
            outs["still"] = (6, count, depths)
        packed = call(functools.partial(fault_kernel, first), "fault", ins, outs, vmem=2)
        slip = packed["slip"]
        if not still:
            still = {"still": packed["still"]}
        strip, halos = travelled(packed)
        ins = {**free, "change": packed["change"], **parts, **props, **strip}
        if banded:
            joined = jnp.concatenate(
                [free["edge"][:, :2], free["inner"], free["edge"][:, 2:]], axis=1
            )
            band = bands(joined, VEL_TAIL_Y, VEL_HEAD_Y)
        else:
            band = {}
        outs = {"velocity": velocity.shape, "stress_inner": (6, *inner), "memory_inner": (6, *inner)}
        extra = {}
        if last:
            outs["new_velocity"] = velocity.shape
            extra = {"scratch": {"sems": pltpu.SemaphoreType.DMA((1,))}, "apart": ("new_velocity_out",)}
        else:
            outs["strip_inner"] = plane
        done = call(
            functools.partial(stress_inner, last),
            "stress_inner",
            {**ins, **band},
            outs,
            cost=100 * cells,
            vmem=10,
            **extra,
        )
        velocity = done["velocity"]
        ins = {"velocity": velocity, **parts, **props, **strip, **halos, **band}
        ins["new_stress_inner"] = done["stress_inner"]
        if last:
            ins["new_memory_inner"] = done["memory_inner"]
            held = pltpu.VMEM((6, *edge), jnp.float32)
            packed = call(
                functools.partial(stress_edge, last),
                "stress_edge",
                ins,
                {"stress": stress.shape, "memory": memory.shape},
                scratch={
                    "stress_held": held,
                    "memory_held": held,
                    "sems": pltpu.SemaphoreType.DMA((6,)),
                },
                apart=("stress_out", "memory_out"),
                vmem=10,
            )
            velocity = done["new_velocity"]
            stress, memory = packed["stress"], packed["memory"]
        else:
            ins["strip_inner"] = done["strip_inner"]
            packed = call(
                functools.partial(stress_edge, last),
                "stress_edge",
                ins,
                {"stress_edge": (6, *edge), "memory_edge": (6, *edge), **travelling},
                cost=30 * cells,
                vmem=10,
            )
            parts = {
                "stress_inner": done["stress_inner"],
                "stress_edge": packed["stress_edge"],
                "memory_inner": done["memory_inner"],
                "memory_edge": packed["memory_edge"],
            }
    if banded:
        held = jnp.where(lax.axis_index("gy") == middle, slip, 0.0)
        slip = lax.psum_scatter(held, "gy", scatter_dimension=0, tiled=True)
    return (velocity, stress, memory, slip)


def solution(mesh):
    in_specs = (
        P(None, ("ens", "gx"), "gy", "gz"),
        P(None, ("ens", "gx"), "gy", "gz"),
        P(None, ("ens", "gx"), "gy", "gz"),
        P(("ens", "gx"), "gy", "gz"),
        P(None, "ens"),
        P(("ens", "gx", "gy"), "gz"),
        P(("ens", "gx", "gy"), "gz"),
        P("ens"),
        P(None, "ens"),
        P(("ens", "gx", "gy"), None, "gz"),
        P(("ens", "gx", "gy"), "gz"),
        P(("ens", "gx", "gy"), "gz"),
    )
    out_specs = (
        P(None, ("ens", "gx"), "gy", "gz"),
        P(None, ("ens", "gx"), "gy", "gz"),
        P(None, ("ens", "gx"), "gy", "gz"),
        P(("ens", "gx", "gy"), "gz"),
    )
    return jax.shard_map(shards, mesh=mesh, in_specs=in_specs, out_specs=out_specs, check_vma=False)
```

```python
import functools
import types

import jax
import jax.numpy as jnp
from jax import lax
from jax.experimental import pallas as pl
from jax.experimental.pallas import tpu as pltpu
from jax.sharding import PartitionSpec as P

STEPS = 2
CLASSES = 8
ZONES = 4
PATCH = 8

NEAR = 9.0 / 8.0
FAR = -1.0 / 24.0
DT = 0.15
TILE = 8
STRIP_PLANES = 6

XX, YY, ZZ, XY, XZ, YZ = range(6)

STRESS_TAIL = ((XX, -1), (XY, -2), (XY, -1), (XZ, -2), (XZ, -1))
STRESS_HEAD = ((XX, 0), (XX, 1), (XY, 0), (XZ, 0))
VEL_TAIL = ((0, -2), (0, -1), (1, -1), (2, -1))
VEL_HEAD = ((0, 0), (1, 0), (1, 1), (2, 0), (2, 1))
STRESS_TAIL_Y = ((YY, -1), (XY, -2), (XY, -1), (YZ, -2), (YZ, -1))
STRESS_HEAD_Y = ((YY, 0), (YY, 1), (XY, 0), (YZ, 0))
VEL_TAIL_Y = ((1, -2), (1, -1), (0, -1), (2, -1))
VEL_HEAD_Y = ((1, 0), (0, 0), (0, 1), (2, 0), (2, 1))
STRESS_SLOTS = (XZ, YZ, ZZ)
VEL_SLOTS = (0, 1, 2)


def forward(before, here, after, after_2):
    return NEAR * (after - here) + FAR * (after_2 - before)


def backward(before_2, before, here, after):
    return NEAR * (here - before) + FAR * (after - before_2)


class Edges:
    def __init__(self, rows, depths, by_loads=False):
        self.rows = rows
        self.depths = depths
        lane = lax.broadcasted_iota(jnp.int32, (rows, depths), 1)
        row = lax.broadcasted_iota(jnp.int32, (TILE, depths), 0)
        self.row = lax.broadcasted_iota(jnp.int32, (rows, depths), 0)
        self.tile_row = row
        self.deep = lax.axis_index("gz")
        near = (self.deep == 0) & (lane < 2) | (self.deep == 1) & (lane >= depths - 2)
        self.near = jnp.where(near, 1.0, 0.0)
        self.zero = jnp.minimum(self.deep, 0)
        self.by_loads = by_loads
        self.pair = lane // 2
        self.low = {n: lane < n for n in (1, 2)}
        self.high = {n: lane >= depths - n for n in (1, 2)}
        self.top = {n: row < n for n in (1, 2)}
        self.bottom = {n: row >= TILE - n for n in (1, 2)}

    def packed(self, strip, x, fields):
        first = jnp.where(self.deep == 0, 2, 0)
        for k, field in enumerate(fields):
            turn = lax.rem(first + 8 * x + 2 * k, self.depths)
            strip = jnp.where(self.pair == 4 * x + k, pltpu.roll(field, turn, 1), strip)
        return strip

    def ends(self, strip, x, k):
        back = self.depths - 8 * x - 2 * k
        turn = jnp.where(self.deep == 0, back % self.depths, back - 2)
        return pltpu.roll(strip, turn, 1) * self.near

    def shallower(self, field, halo, n):
        return pltpu.roll(jnp.where(self.high[n], halo, field), n, 1)

    def deeper(self, field, halo, n):
        return pltpu.roll(jnp.where(self.low[n], halo, field), self.depths - n, 1)

    def forward_z(self, field, halo):
        return forward(
            self.shallower(field, halo, 1),
            field,
            self.deeper(field, halo, 1),
            self.deeper(field, halo, 2),
        )

    def backward_z(self, field, halo):
        return backward(
            self.shallower(field, halo, 2),
            self.shallower(field, halo, 1),
            field,
            self.deeper(field, halo, 1),
        )

    def before(self, field, load, n, halo):
        top = jnp.where(self.top[n], 0.0, pltpu.roll(field[:TILE], n, 0))
        if halo:
            for i in range(n):
                top = jnp.where(self.tile_row == i, halo[n - 1 - i], top)
        if load:
            rest = load(self.zero + (TILE - n), self.rows - TILE)
        else:
            rest = pltpu.roll(field, n, 0)[TILE:]
        return jnp.concatenate([top, rest], axis=0)

    def after(self, field, load, n, halo):
        bottom = pltpu.roll(field[self.rows - TILE :], TILE - n, 0)
        bottom = jnp.where(self.bottom[n], 0.0, bottom)
        if halo:
            for i in range(n):
                bottom = jnp.where(self.tile_row == TILE - n + i, halo[i], bottom)
        if load:
            rest = load(self.zero + n, self.rows - TILE)
        else:
            rest = pltpu.roll(field, self.rows - n, 0)[: self.rows - TILE]
        return jnp.concatenate([rest, bottom], axis=0)

    def forward_y(self, planes, comp, x, halos):
        field = planes(comp, x)
        load = planes.rows(comp, x) if self.by_loads else None
        lower, upper = halos
        return forward(
            self.before(field, load, 1, lower),
            field,
            self.after(field, load, 1, upper),
            self.after(field, load, 2, upper),
        )

    def backward_y(self, planes, comp, x, halos):
        field = planes(comp, x)
        load = planes.rows(comp, x) if self.by_loads else None
        lower, upper = halos
        return backward(
            self.before(field, load, 2, lower),
            self.before(field, load, 1, lower),
            field,
            self.after(field, load, 1, upper),
        )


class Field:
    def __init__(self, count, *parts):
        self.count = count
        self.parts = parts

    def place(self, x):
        if len(self.parts) == 1:
            return self.parts[0], x
        inner, edge = self.parts
        if x in inside(self.count):
            return inner, x - 2
        return edge, ends_of(self.count).index(x)

    def __call__(self, comp, x):
        ref, at = self.place(x)
        return ref[comp, at]

    def rows(self, comp, x):
        ref, at = self.place(x)
        return lambda start, size: ref[comp, at, pl.ds(start, size), :]


def inside(count):
    return range(2, count - 2)


def ends_of(count):
    return (0, 1, count - 2, count - 1)


class Planes:
    def __init__(self, field, tail, head, first=None, second=None):
        self.field = field
        self.count = field.count
        self.first, self.second = first, second
        self.tail, self.head = tail, head
        self.even = even_strike()
        self.any_left = lax.axis_index("gx") > 0
        self.any_right = lax.axis_index("gx") < lax.axis_size("gx") - 1

    def left(self, i):
        plane = jnp.where(self.even, self.second[i], self.first[i])
        return jnp.where(self.any_left, plane, 0.0)

    def right(self, i):
        plane = jnp.where(self.even, self.first[i], self.second[i])
        return jnp.where(self.any_right, plane, 0.0)

    def __call__(self, comp, place):
        if place < 0:
            return self.left(self.tail.index((comp, place)))
        if place >= self.count:
            return self.right(self.head.index((comp, place - self.count)))
        return self.field(comp, place)

    def rows(self, comp, x):
        return self.field.rows(comp, x)

    def forward_x(self, comp, x):
        return forward(self(comp, x - 1), self(comp, x), self(comp, x + 1), self(comp, x + 2))

    def backward_x(self, comp, x):
        return backward(self(comp, x - 2), self(comp, x - 1), self(comp, x), self(comp, x + 1))


class Bands:
    def __init__(self, lower, upper, tail, head):
        self.lower, self.upper = lower, upper
        self.tail, self.head = tail, head

    def __call__(self, comp, x):
        if self.lower is None:
            return (None, None)
        places = [i for i, (c, _) in enumerate(self.tail) if c == comp]
        before = [self.lower[i, pl.ds(x, 1), :] for i in reversed(places)]
        places = [i for i, (c, _) in enumerate(self.head) if c == comp]
        after = [self.upper[i, pl.ds(x, 1), :] for i in places]
        return (before, after)


def looked_up(labels, table, row, count):
    out = jnp.full(labels.shape, table[row, 0], jnp.float32)
    for k in range(1, count):
        out = jnp.where(labels == k, table[row, k], out)
    return out


def even_strike():
    return lax.axis_index("gx") % 2 == 0


def edge_planes(field, tail, head, first_out, second_out):
    even = even_strike()
    for i in range(first_out.shape[0]):
        comp, place = tail[min(i, len(tail) - 1)]
        right = field(comp, place % field.count)
        comp, place = head[min(i, len(head) - 1)]
        left = field(comp, place % field.count)
        first_out[i] = jnp.where(even, right, left)
        second_out[i] = jnp.where(even, left, right)


def fault_row(rows):
    return jnp.where(lax.axis_index("gy") == lax.axis_size("gy") // 2, 0, rows - 1)


def pack_kernel(r):
    count, rows, depths = r.stress.shape[1:]
    whole = [(comp, 0, count) for comp in STRESS_SLOTS]
    some = {}
    for comp, place in STRESS_TAIL + STRESS_HEAD:
        if comp not in STRESS_SLOTS:
            some.setdefault((comp, place < 0), []).append(place % count)
    some = [(comp, min(at), max(at) + 1) for (comp, _), at in some.items()]
    copies = []
    for i, (comp, start, stop) in enumerate(some + whole):
        span = pl.ds(start, stop - start)
        copy = pltpu.make_async_copy(r.stress.at[comp, span], r.held.at[comp, span], r.sems.at[i])
        copy.start()
        copies.append(copy)
    edges = Edges(rows, depths)
    for copy in copies:
        copy.wait()
    edge_planes(Field(count, r.held), STRESS_TAIL, STRESS_HEAD, r.one_out, r.two_out)
    strip = jnp.zeros((rows, depths), jnp.float32)
    for x in range(count):
        strip = edges.packed(strip, x, [r.held[c, x] for c in STRESS_SLOTS])
    set_strip(r, strip)


def grouped(xs, size):
    return [xs[i : i + size] for i in range(0, len(xs), size)]


def set_strip(r, strip):
    r.strip_out[0] = strip
    for i in range(1, STRIP_PLANES):
        r.strip_out[i] = jnp.zeros_like(strip)


def unpack(r, xs, edges):
    strip = r.strip[0]
    for i, x in enumerate(xs):
        for k in range(3):
            r.ends[i, k] = edges.ends(strip, x, k)


def velocity_planes(r, xs, edges, planes, write):
    band = Bands(getattr(r, "lower", None), getattr(r, "upper", None), STRESS_TAIL_Y, STRESS_HEAD_Y)
    unpack(r, xs, edges)

    def new(x):
        push = DT * looked_up(r.material[x], r.table, 2, CLASSES)
        ends = [r.ends[xs.index(x), k] for k in range(3)]
        along_x = (
            planes.forward_x(XX, x)
            + edges.backward_y(planes, XY, x, band(XY, x))
            + edges.backward_z(planes(XZ, x), ends[0])
        )
        along_y = (
            planes.backward_x(XY, x)
            + edges.forward_y(planes, YY, x, band(YY, x))
            + edges.backward_z(planes(YZ, x), ends[1])
        )
        along_z = (
            planes.backward_x(XZ, x)
            + edges.backward_y(planes, YZ, x, band(YZ, x))
            + edges.forward_z(planes(ZZ, x), ends[2])
        )
        rates = (along_x, along_y, along_z)
        return [r.velocity[c, x] + push * rate for c, rate in enumerate(rates)]

    for group in grouped(xs, 3 if len(xs) % 3 == 0 else 2):
        for x, values in [(x, new(x)) for x in group]:
            write(x, values)


def velocity_inner(r):
    count, rows, depths = r.material.shape
    edges = Edges(rows, depths)
    planes = Planes(stress_of(r), STRESS_TAIL, STRESS_HEAD)

    def write(x, new):
        for c in range(3):
            r.inner_out[c, x - 2] = new[c]

    velocity_planes(r, inside(count), edges, planes, write)
    strip = jnp.zeros((rows, depths), jnp.float32)
    for x in inside(count):
        strip = edges.packed(strip, x, [r.inner_out[c, x - 2] for c in VEL_SLOTS])
    r.strip_inner_out[...] = strip


def velocity_edge(first, r):
    count, rows, depths = r.material.shape
    edges = Edges(rows, depths)
    planes = Planes(stress_of(r), STRESS_TAIL, STRESS_HEAD, r.one, r.two)
    fault = fault_row(rows)
    places = ends_of(count)
    row = pl.ds(fault, 1)
    for x in inside(count):
        r.face_out[pl.ds(x, 1), :] = r.inner[0, x - 2, row, :]
        r.face_out[pl.ds(count + x, 1), :] = r.inner[2, x - 2, row, :]
    if first:
        for x in range(count):
            labels = r.material[x, row, :]
            r.face_out[pl.ds(2 * count + x, 1), :] = looked_up(labels, r.table, 2, CLASSES)
    if hasattr(r, "prestress"):
        own = r.normal.shape[0]
        place = 3 * count
        for i in range(own):
            r.face_out[pl.ds(place + i, 1), :] = r.prestress[i, pl.ds(0, 1), :]
            r.face_out[pl.ds(place + own + i, 1), :] = r.prestress[i, pl.ds(1, 1), :]
        for i, field in enumerate((r.normal, r.slip, r.zone, r.mask)):
            r.face_out[pl.ds(place + (2 + i) * own, own), :] = field[...].astype(jnp.float32)


    def write(x, new):
        for c in range(3):
            r.edge_out[c, places.index(x)] = new[c]

    velocity_planes(r, places, edges, planes, write)
    strip = r.strip_inner[...]
    for i, x in enumerate(places):
        strip = edges.packed(strip, x, [r.edge_out[c, i] for c in VEL_SLOTS])
    set_strip(r, strip)
    for x in places:
        r.face_out[pl.ds(x, 1), :] = r.edge_out[0, places.index(x), row, :]
        r.face_out[pl.ds(count + x, 1), :] = r.edge_out[2, places.index(x), row, :]
    new = Field(count, r.inner, r.edge_out)
    edge_planes(new, VEL_TAIL, VEL_HEAD, r.one_out, r.two_out)


def stress_of(r):
    count = r.material.shape[0]
    if hasattr(r, "stress"):
        return Field(count, r.stress)
    return Field(count, r.stress_inner, r.stress_edge)


def memory_of(r):
    count = r.material.shape[0]
    if hasattr(r, "memory"):
        return Field(count, r.memory)
    return Field(count, r.memory_inner, r.memory_edge)


def fault_kernel(first, r):
    own_face, other_face = r.face, r.other
    own_first, other_first = (own_face, other_face) if first else (r.face_first, r.other_first)
    rows, depths = r.strip.shape[1:]
    count = r.change_out.shape[1]
    middle = lax.axis_size("gy") // 2
    side = lax.axis_index("gy")
    plus = side == middle
    minus = side == middle - 1

    def pair(own, other, place):
        mine, theirs = own[pl.ds(place, count), :], other[pl.ds(place, count), :]
        return jnp.where(plus, theirs, mine), jnp.where(plus, mine, theirs)

    if hasattr(r, "still"):
        still = r.still
    else:
        still = r.still_out
        share = (own_face.shape[0] - 3 * count) // 6
        for i in range(6):
            mine = own_face[pl.ds(3 * count + i * share, share), :]
            theirs = other_face[pl.ds(3 * count + i * share, share), :]
            still[i, pl.ds(0, share), :] = jnp.where(plus, theirs, mine)
            still[i, pl.ds(share, share), :] = jnp.where(plus, mine, theirs)
    pre_x, pre_z, normal = still[0], still[1], still[2]
    slip = still[3] if first else r.slip[...]
    zone, mask = still[4], still[5]

    row = lax.broadcasted_iota(jnp.int32, (count, depths), 0) + lax.axis_index("gx") * count
    deep = lax.broadcasted_iota(jnp.int32, (count, depths), 1) + lax.axis_index("gz") * depths
    inside = (row >= r.anchor[0]) & (row < r.anchor[0] + 2 * PATCH)
    inside = inside & (deep >= r.anchor[1]) & (deep < r.anchor[1] + 2 * PATCH)
    dynamic = 0.4 * looked_up(zone, r.friction, 0, ZONES)
    static = jnp.where(
        inside, dynamic, dynamic + 0.5 * looked_up(zone, r.friction, 1, ZONES)
    )
    distance = 0.2 * looked_up(zone, r.friction, 2, ZONES)
    minus_x, plus_x = pair(own_face, other_face, 0)
    minus_z, plus_z = pair(own_face, other_face, count)
    minus_b, plus_b = pair(own_first, other_first, 2 * count)
    bsum = minus_b + plus_b
    trial_x = (plus_x - minus_x) / (DT * bsum) + pre_x
    trial_z = (plus_z - minus_z) / (DT * bsum) + pre_z
    size = jnp.sqrt(trial_x * trial_x + trial_z * trial_z)
    weaken = jnp.minimum(slip / distance, 1.0)
    strength = (static - (static - dynamic) * weaken) * normal
    factor = jnp.where(mask == 1.0, strength / jnp.maximum(size, strength), 1.0)
    new_slip = slip + DT * DT * bsum * (size - size * factor)
    if r.slip_out.shape[0] == count:
        r.slip_out[...] = new_slip
    else:
        half = r.slip_out.shape[0]
        r.slip_out[...] = jnp.where(plus, new_slip[half:], new_slip[:half])
    sign = jnp.where(minus, DT, 0.0) * minus_b - jnp.where(plus, DT, 0.0) * plus_b
    change_x = (trial_x * factor - pre_x) * sign
    change_z = (trial_z * factor - pre_z) * sign
    r.change_out[0] = change_x
    r.change_out[1] = change_z

    fault = fault_row(rows)
    on_fault = lax.broadcasted_iota(jnp.int32, (rows, depths), 0) == fault
    even = even_strike()
    still_line = jnp.zeros((1, depths), jnp.float32)

    def line(planes, i):
        comp, place = planes[min(i, len(planes) - 1)]
        return still_line if comp == 1 else r.change_out[comp // 2, pl.ds(place % count, 1), :]

    for i in range(r.one_out.shape[0]):
        right, left = line(VEL_TAIL, i), line(VEL_HEAD, i)
        one, two = jnp.where(even, right, left), jnp.where(even, left, right)
        r.one_out[i] = r.one[i] + jnp.where(on_fault, one, 0.0)
        r.two_out[i] = r.two[i] + jnp.where(on_fault, two, 0.0)
    ends = jnp.zeros((count, depths), jnp.float32)
    pair = lax.broadcasted_iota(jnp.int32, (count, depths), 1) // 2
    place = 4 * lax.broadcasted_iota(jnp.int32, (count, depths), 0)
    upper = lax.axis_index("gz") == 0
    for k, field in ((0, change_x), (2, change_z)):
        turned = jnp.where(upper, pltpu.roll(field, 2, 1), field)
        turned = pltpu.roll(turned, 2 * k, 1, stride=8, stride_axis=0)
        ends = jnp.where(pair == place + k, turned, ends)
    line = jnp.sum(ends, axis=0, keepdims=True)
    set_strip(r, r.strip[0] + jnp.where(on_fault, line, 0.0))


def stress_planes(r, xs, edges, planes, write):
    band = Bands(getattr(r, "lower", None), getattr(r, "upper", None), VEL_TAIL_Y, VEL_HEAD_Y)
    stress, memory = stress_of(r), memory_of(r)
    unpack(r, xs, edges)

    def rates(x):
        in_x, in_y, in_z = [r.ends[xs.index(x), k] for k in range(3)]
        exx = planes.backward_x(0, x)
        eyy = edges.backward_y(planes, 1, x, band(1, x))
        ezz = edges.backward_z(planes(2, x), in_z)
        exy = edges.forward_y(planes, 0, x, band(0, x)) + planes.forward_x(1, x)
        exz = edges.forward_z(planes(0, x), in_x) + planes.forward_x(2, x)
        eyz = edges.forward_z(planes(1, x), in_y) + edges.forward_y(planes, 2, x, band(2, x))
        labels = r.material[x]
        bulk = looked_up(labels, r.table, 0, CLASSES) * (exx + eyy + ezz)
        shear = looked_up(labels, r.table, 1, CLASSES)
        double = 2.0 * shear
        return (
            bulk + double * exx,
            bulk + double * eyy,
            bulk + double * ezz,
            shear * exy,
            shear * exz,
            shear * eyz,
        )

    def new(x, elastic):
        labels = r.material[x]
        decay = jnp.exp(-DT / looked_up(labels, r.table, 3, CLASSES))
        gain = (1.0 - decay) * (0.3 * looked_up(labels, r.table, 4, CLASSES))
        kept = [decay * memory(c, x) - gain * elastic[c] for c in range(6)]
        return [stress(c, x) + DT * (elastic[c] + kept[c]) for c in range(6)], kept

    for group in grouped(xs, 2):
        for x, elastic in [(x, rates(x)) for x in group]:
            write(x, *new(x, elastic))


def stress_inner(last, r):
    count, rows, depths = r.material.shape
    edges = Edges(rows, depths, by_loads=True)
    on_fault = edges.row == fault_row(rows)
    free = Field(count, r.inner, r.edge)
    for x in range(count):
        for c in (0, 2):
            line = r.change[c // 2, pl.ds(x, 1), :]
            r.velocity_out[c, x] = free(c, x) + jnp.where(on_fault, line, 0.0)
        r.velocity_out[1, x] = free(1, x)
    planes = Planes(Field(count, r.velocity_out), VEL_TAIL, VEL_HEAD)
    if last:
        velocity_copy = pltpu.make_async_copy(
            r.velocity_out, r.new_velocity_out, r.sems.at[0]
        )
        velocity_copy.start()

    def write(x, new, kept):
        for c in range(6):
            r.stress_inner_out[c, x - 2] = new[c]
            r.memory_inner_out[c, x - 2] = kept[c]

    stress_planes(r, inside(count), edges, planes, write)
    if last:
        velocity_copy.wait()
    else:
        strip = jnp.zeros((rows, depths), jnp.float32)
        for x in inside(count):
            strip = edges.packed(strip, x, [r.stress_inner_out[c, x - 2] for c in STRESS_SLOTS])
        r.strip_inner_out[...] = strip


def stress_edge(last, r):
    count, rows, depths = r.material.shape
    edges = Edges(rows, depths, by_loads=True)
    planes = Planes(Field(count, r.velocity), VEL_TAIL, VEL_HEAD, r.one, r.two)
    places = ends_of(count)
    copies = []

    def copy_out(source, out, span):
        copy = pltpu.make_async_copy(source, out.at[:, span], r.sems.at[len(copies)])
        copy.start()
        copies.append(copy)

    if last:
        copy_out(r.new_stress_inner, r.stress_out, pl.ds(2, count - 4))
        copy_out(r.new_memory_inner, r.memory_out, pl.ds(2, count - 4))
        stress_out, memory_out = r.stress_held, r.memory_held
    else:
        stress_out, memory_out = r.stress_edge_out, r.memory_edge_out

    def write(x, new, kept):
        for c in range(6):
            stress_out[c, places.index(x)] = new[c]
            memory_out[c, places.index(x)] = kept[c]

    stress_planes(r, places, edges, planes, write)
    if last:
        for held, out in ((stress_out, r.stress_out), (memory_out, r.memory_out)):
            copy_out(held.at[:, pl.ds(0, 2)], out, pl.ds(0, 2))
            copy_out(held.at[:, pl.ds(2, 2)], out, pl.ds(count - 2, 2))
        for copy in copies:
            copy.wait()
    else:
        strip = r.strip_inner[...]
        for i, x in enumerate(places):
            strip = edges.packed(strip, x, [stress_out[c, i] for c in STRESS_SLOTS])
        set_strip(r, strip)
        new = Field(count, r.new_stress_inner, stress_out)
        edge_planes(new, STRESS_TAIL, STRESS_HEAD, r.one_out, r.two_out)


SCALARS = ("table", "friction", "anchor")


def call(kernel, name, ins, outs, scratch=None, apart=(), micros=1, vmem=6):
    scratch = scratch or {}
    names = [*ins, *(f"{key}_out" for key in outs), *scratch]

    def body(*refs):
        kernel(types.SimpleNamespace(**dict(zip(names, refs))))

    def place(key):
        if key in apart:
            return pl.BlockSpec(memory_space=pltpu.HBM)
        return pl.BlockSpec(memory_space=pltpu.SMEM if key in SCALARS else pltpu.VMEM)

    shapes = [jax.ShapeDtypeStruct(shape, jnp.float32) for shape in outs.values()]
    result = pl.pallas_call(
        body,
        out_shape=shapes,
        in_specs=[place(key) for key in ins],
        out_specs=[place(f"{key}_out") for key in outs],
        scratch_shapes=list(scratch.values()),
        name=name,
        cost_estimate=pl.CostEstimate(
            flops=0, bytes_accessed=micros * 3_690_000, transcendentals=0
        ),
        compiler_params=pltpu.CompilerParams(vmem_limit_bytes=vmem * 2**20),
    )(*ins.values())
    return dict(zip(outs, result))


def along(axis, count, skip=()):
    up = [(i, i + 1) for i in range(count - 1) if i not in skip]
    return (axis, up), (axis, [(b, a) for a, b in up])


def strike_swaps(count):
    routes = []
    for start in (0, 1):
        partner = list(range(count))
        for i in range(start, count - 1, 2):
            partner[i], partner[i + 1] = i + 1, i
        routes.append(("gx", list(enumerate(partner))))
    return routes


def sent(block, route):
    return lax.ppermute(block, *route)


def whole(parts, name):
    if name in parts:
        return parts[name]
    inner, edge = parts[f"{name}_inner"], parts[f"{name}_edge"]
    return jnp.concatenate([edge[:, :2], inner, edge[:, 2:]], axis=1)


def edge_rows(field, rows):
    count = field.shape[2]
    return jnp.stack([field[c, :, place % count, :] for c, place in rows])


def shards(
    velocity,
    stress,
    memory,
    material,
    material_table,
    fault_mask,
    zone_label,
    patch_anchor,
    friction_table,
    prestress,
    normal_stress,
    slip_path,
):
    _, count, rows, depths = velocity.shape
    sides = lax.axis_size("gy")
    middle = sides // 2
    banded = sides > 2
    swaps = strike_swaps(lax.axis_size("gx"))
    up_y, down_y = along("gy", sides, (middle - 1,))
    across = ("gy", [(middle - 1, middle), (middle, middle - 1)])
    deep = ("gz", [(0, 1), (1, 0)])

    plane = (rows, depths)
    edge_shape = (max(len(STRESS_TAIL), len(STRESS_HEAD)), *plane)
    travelling = {"one": edge_shape, "two": edge_shape, "strip": (STRIP_PLANES, *plane)}
    inner, edge = (count - 4, *plane), (4, *plane)
    inner_ends = {"ends": pltpu.VMEM((count - 4, 3, *plane), jnp.float32)}
    edge_ends = {"ends": pltpu.VMEM((4, 3, *plane), jnp.float32)}

    def travelled(packed):
        two = sent(packed["two"], swaps[1])
        one = sent(packed["one"], swaps[0])
        strip = sent(packed["strip"], deep)
        return {"strip": strip}, {"two": two, "one": one}

    def bands(field, tail, head):
        if not banded:
            return {}
        lower, upper = edge_rows(field, tail), edge_rows(field, head)
        return {"lower": sent(lower, up_y), "upper": sent(upper, down_y)}

    if banded:
        still = jnp.stack(
            [
                prestress[:, 0],
                prestress[:, 1],
                normal_stress,
                slip_path,
                zone_label.astype(jnp.float32),
                fault_mask.astype(jnp.float32),
            ]
        )
        still = {"still": lax.all_gather(still, "gy", axis=1, tiled=True)}
    else:
        still = {}

    parts = {"stress": stress, "memory": memory}
    props = {"material": material, "table": material_table}
    packed = call(
        pack_kernel,
        "pack",
        {"stress": stress},
        travelling,
        scratch={"held": pltpu.VMEM(stress.shape, jnp.float32), "sems": pltpu.SemaphoreType.DMA((8,))},
        apart=("stress",),
        vmem=6,
    )
    for step in range(STEPS):
        first, last = step == 0, step == STEPS - 1
        held_stress = {key: parts[key] for key in parts if key.startswith("stress")}
        strip, halos = travelled(packed)
        ins = {"velocity": velocity, **held_stress, **props, **strip}
        if banded:
            ins.update(bands(whole(parts, "stress"), STRESS_TAIL_Y, STRESS_HEAD_Y))
        free = call(
            velocity_inner,
            "velocity_inner",
            ins,
            {"inner": (3, *inner), "strip_inner": plane},
            scratch=inner_ends,
            micros=3,
        )
        face_rows = 2 * count
        ins = {**ins, **halos, **free}
        if first:
            face_rows += count
            if not banded:
                ins.update(prestress=prestress, normal=normal_stress, slip=slip_path)
                ins.update(zone=zone_label, mask=fault_mask)
                face_rows += 6 * normal_stress.shape[0]
        packed = call(
            functools.partial(velocity_edge, first),
            "velocity_edge",
            ins,
            {"edge": (3, *edge), "face": (face_rows, depths), **travelling},
            scratch=edge_ends,
        )
        free = {"inner": free["inner"], "edge": packed["edge"]}
        face = packed["face"]
        other = sent(face, across)
        ins = {key: packed[key] for key in travelling}
        ins.update(face=face, other=other, friction=friction_table, anchor=patch_anchor, **still)
        if first:
            faces = {"face_first": face, "other_first": other}
        else:
            ins.update(slip=slip, **faces)
        outs = {"change": (2, count, depths), "slip": (count, depths), **travelling}
        if last and not banded:
            outs["slip"] = (count // sides, depths)
        if not still:
            outs["still"] = (6, count, depths)
        packed = call(functools.partial(fault_kernel, first), "fault", ins, outs, vmem=2)
        slip = packed["slip"]
        if not still:
            still = {"still": packed["still"]}
        strip, halos = travelled(packed)
        ins = {**free, "change": packed["change"], **parts, **props, **strip}
        if banded:
            joined = jnp.concatenate(
                [free["edge"][:, :2], free["inner"], free["edge"][:, 2:]], axis=1
            )
            band = bands(joined, VEL_TAIL_Y, VEL_HEAD_Y)
        else:
            band = {}
        outs = {"velocity": velocity.shape, "stress_inner": (6, *inner), "memory_inner": (6, *inner)}
        extra = {"scratch": inner_ends}
        if last:
            outs["new_velocity"] = velocity.shape
            extra["scratch"] = {"sems": pltpu.SemaphoreType.DMA((1,)), **inner_ends}
            extra["apart"] = ("new_velocity_out",)
        else:
            outs["strip_inner"] = plane
        done = call(
            functools.partial(stress_inner, last),
            "stress_inner",
            {**ins, **band},
            outs,
            micros=3,
            vmem=11,
            **extra,
        )
        velocity = done["velocity"]
        ins = {"velocity": velocity, **parts, **props, **strip, **halos, **band}
        ins["new_stress_inner"] = done["stress_inner"]
        if last:
            ins["new_memory_inner"] = done["memory_inner"]
            held = pltpu.VMEM((6, *edge), jnp.float32)
            packed = call(
                functools.partial(stress_edge, last),
                "stress_edge",
                ins,
                {"stress": stress.shape, "memory": memory.shape},
                scratch={
                    "stress_held": held,
                    "memory_held": held,
                    "sems": pltpu.SemaphoreType.DMA((6,)),
                    **edge_ends,
                },
                apart=("stress_out", "memory_out"),
                vmem=10,
            )
            velocity = done["new_velocity"]
            stress, memory = packed["stress"], packed["memory"]
        else:
            ins["strip_inner"] = done["strip_inner"]
            packed = call(
                functools.partial(stress_edge, last),
                "stress_edge",
                ins,
                {"stress_edge": (6, *edge), "memory_edge": (6, *edge), **travelling},
                scratch=edge_ends,
                vmem=10,
            )
            parts = {
                "stress_inner": done["stress_inner"],
                "stress_edge": packed["stress_edge"],
                "memory_inner": done["memory_inner"],
                "memory_edge": packed["memory_edge"],
            }
    if banded:
        held = jnp.where(lax.axis_index("gy") == middle, slip, 0.0)
        slip = lax.psum_scatter(held, "gy", scatter_dimension=0, tiled=True)
    return (velocity, stress, memory, slip)


def solution(mesh):
    in_specs = (
        P(None, ("ens", "gx"), "gy", "gz"),
        P(None, ("ens", "gx"), "gy", "gz"),
        P(None, ("ens", "gx"), "gy", "gz"),
        P(("ens", "gx"), "gy", "gz"),
        P(None, "ens"),
        P(("ens", "gx", "gy"), "gz"),
        P(("ens", "gx", "gy"), "gz"),
        P("ens"),
        P(None, "ens"),
        P(("ens", "gx", "gy"), None, "gz"),
        P(("ens", "gx", "gy"), "gz"),
        P(("ens", "gx", "gy"), "gz"),
    )
    out_specs = (
        P(None, ("ens", "gx"), "gy", "gz"),
        P(None, ("ens", "gx"), "gy", "gz"),
        P(None, ("ens", "gx"), "gy", "gz"),
        P(("ens", "gx", "gy"), "gz"),
    )
    return jax.shard_map(shards, mesh=mesh, in_specs=in_specs, out_specs=out_specs, check_vma=False)
```

```python
import functools
import types

import jax
import jax.numpy as jnp
from jax import lax
from jax.experimental import pallas as pl
from jax.experimental.pallas import tpu as pltpu
from jax.sharding import PartitionSpec as P

STEPS = 2
CLASSES = 8
ZONES = 4
PATCH = 8

NEAR = 9.0 / 8.0
FAR = -1.0 / 24.0
DT = 0.15
TILE = 8
STRIP_PLANES = 6

XX, YY, ZZ, XY, XZ, YZ = range(6)

STRESS_TAIL = ((XX, -1), (XY, -2), (XY, -1), (XZ, -2), (XZ, -1))
STRESS_HEAD = ((XX, 0), (XX, 1), (XY, 0), (XZ, 0))
VEL_TAIL = ((0, -2), (0, -1), (1, -1), (2, -1))
VEL_HEAD = ((0, 0), (1, 0), (1, 1), (2, 0), (2, 1))
STRESS_TAIL_Y = ((YY, -1), (XY, -2), (XY, -1), (YZ, -2), (YZ, -1))
STRESS_HEAD_Y = ((YY, 0), (YY, 1), (XY, 0), (YZ, 0))
VEL_TAIL_Y = ((1, -2), (1, -1), (0, -1), (2, -1))
VEL_HEAD_Y = ((1, 0), (0, 0), (0, 1), (2, 0), (2, 1))
STRESS_SLOTS = (XZ, YZ, ZZ)
VEL_SLOTS = (0, 1, 2)


def forward(before, here, after, after_2):
    return NEAR * (after - here) + FAR * (after_2 - before)


def backward(before_2, before, here, after):
    return NEAR * (here - before) + FAR * (after - before_2)


class Edges:
    def __init__(self, rows, depths, by_loads=False):
        self.rows = rows
        self.depths = depths
        lane = lax.broadcasted_iota(jnp.int32, (rows, depths), 1)
        row = lax.broadcasted_iota(jnp.int32, (TILE, depths), 0)
        self.row = lax.broadcasted_iota(jnp.int32, (rows, depths), 0)
        self.tile_row = row
        self.deep = lax.axis_index("gz")
        near = (self.deep == 0) & (lane < 2) | (self.deep == 1) & (lane >= depths - 2)
        self.near = jnp.where(near, 1.0, 0.0)
        self.zero = jnp.minimum(self.deep, 0)
        self.by_loads = by_loads
        self.pair = lane // 2
        self.low = {n: lane < n for n in (1, 2)}
        self.high = {n: lane >= depths - n for n in (1, 2)}
        self.top = {n: row < n for n in (1, 2)}
        self.bottom = {n: row >= TILE - n for n in (1, 2)}

    def packed(self, strip, x, fields):
        first = jnp.where(self.deep == 0, 2, 0)
        for k, field in enumerate(fields):
            turn = lax.rem(first + 8 * x + 2 * k, self.depths)
            strip = jnp.where(self.pair == 4 * x + k, pltpu.roll(field, turn, 1), strip)
        return strip

    def ends(self, strip, x, k):
        back = self.depths - 8 * x - 2 * k
        turn = jnp.where(self.deep == 0, back % self.depths, back - 2)
        return pltpu.roll(strip, turn, 1) * self.near

    def shallower(self, field, halo, n):
        return pltpu.roll(jnp.where(self.high[n], halo, field), n, 1)

    def deeper(self, field, halo, n):
        return pltpu.roll(jnp.where(self.low[n], halo, field), self.depths - n, 1)

    def forward_z(self, field, halo):
        return forward(
            self.shallower(field, halo, 1),
            field,
            self.deeper(field, halo, 1),
            self.deeper(field, halo, 2),
        )

    def backward_z(self, field, halo):
        return backward(
            self.shallower(field, halo, 2),
            self.shallower(field, halo, 1),
            field,
            self.deeper(field, halo, 1),
        )

    def before(self, field, load, n, halo):
        top = jnp.where(self.top[n], 0.0, pltpu.roll(field[:TILE], n, 0))
        if halo:
            for i in range(n):
                top = jnp.where(self.tile_row == i, halo[n - 1 - i], top)
        if load:
            rest = load(self.zero + (TILE - n), self.rows - TILE)
        else:
            rest = pltpu.roll(field, n, 0)[TILE:]
        return jnp.concatenate([top, rest], axis=0)

    def after(self, field, load, n, halo):
        bottom = pltpu.roll(field[self.rows - TILE :], TILE - n, 0)
        bottom = jnp.where(self.bottom[n], 0.0, bottom)
        if halo:
            for i in range(n):
                bottom = jnp.where(self.tile_row == TILE - n + i, halo[i], bottom)
        if load:
            rest = load(self.zero + n, self.rows - TILE)
        else:
            rest = pltpu.roll(field, self.rows - n, 0)[: self.rows - TILE]
        return jnp.concatenate([rest, bottom], axis=0)

    def forward_y(self, planes, comp, x, halos):
        field = planes(comp, x)
        load = planes.rows(comp, x) if self.by_loads else None
        lower, upper = halos
        return forward(
            self.before(field, load, 1, lower),
            field,
            self.after(field, load, 1, upper),
            self.after(field, load, 2, upper),
        )

    def backward_y(self, planes, comp, x, halos):
        field = planes(comp, x)
        load = planes.rows(comp, x) if self.by_loads else None
        lower, upper = halos
        return backward(
            self.before(field, load, 2, lower),
            self.before(field, load, 1, lower),
            field,
            self.after(field, load, 1, upper),
        )


class Field:
    def __init__(self, count, *parts):
        self.count = count
        self.parts = parts

    def place(self, x):
        if len(self.parts) == 1:
            return self.parts[0], x
        inner, edge = self.parts
        if x in inside(self.count):
            return inner, x - 2
        return edge, ends_of(self.count).index(x)

    def __call__(self, comp, x):
        ref, at = self.place(x)
        return ref[comp, at]

    def rows(self, comp, x):
        ref, at = self.place(x)
        return lambda start, size: ref[comp, at, pl.ds(start, size), :]


def inside(count):
    return range(2, count - 2)


def ends_of(count):
    return (0, 1, count - 2, count - 1)


class Planes:
    def __init__(self, field, tail, head, first=None, second=None):
        self.field = field
        self.count = field.count
        self.first, self.second = first, second
        self.tail, self.head = tail, head
        self.even = even_strike()
        self.any_left = lax.axis_index("gx") > 0
        self.any_right = lax.axis_index("gx") < lax.axis_size("gx") - 1

    def left(self, i):
        plane = jnp.where(self.even, self.second[i], self.first[i])
        return jnp.where(self.any_left, plane, 0.0)

    def right(self, i):
        plane = jnp.where(self.even, self.first[i], self.second[i])
        return jnp.where(self.any_right, plane, 0.0)

    def __call__(self, comp, place):
        if place < 0:
            return self.left(self.tail.index((comp, place)))
        if place >= self.count:
            return self.right(self.head.index((comp, place - self.count)))
        return self.field(comp, place)

    def rows(self, comp, x):
        return self.field.rows(comp, x)

    def forward_x(self, comp, x):
        return forward(self(comp, x - 1), self(comp, x), self(comp, x + 1), self(comp, x + 2))

    def backward_x(self, comp, x):
        return backward(self(comp, x - 2), self(comp, x - 1), self(comp, x), self(comp, x + 1))


class Bands:
    def __init__(self, lower, upper, tail, head):
        self.lower, self.upper = lower, upper
        self.tail, self.head = tail, head

    def __call__(self, comp, x):
        if self.lower is None:
            return (None, None)
        places = [i for i, (c, _) in enumerate(self.tail) if c == comp]
        before = [self.lower[i, pl.ds(x, 1), :] for i in reversed(places)]
        places = [i for i, (c, _) in enumerate(self.head) if c == comp]
        after = [self.upper[i, pl.ds(x, 1), :] for i in places]
        return (before, after)


def looked_up(labels, table, row, count):
    out = jnp.full(labels.shape, table[row, 0], jnp.float32)
    for k in range(1, count):
        out = jnp.where(labels == k, table[row, k], out)
    return out


def even_strike():
    return lax.axis_index("gx") % 2 == 0


def edge_planes(field, tail, head, first_out, second_out):
    even = even_strike()
    pairs = []
    for i in range(first_out.shape[0]):
        comp, place = tail[min(i, len(tail) - 1)]
        right = field(comp, place % field.count)
        comp, place = head[min(i, len(head) - 1)]
        left = field(comp, place % field.count)
        pairs.append((jnp.where(even, right, left), jnp.where(even, left, right)))
    for i, (one, two) in enumerate(pairs):
        first_out[i] = one
        second_out[i] = two


def fault_row(rows):
    return jnp.where(lax.axis_index("gy") == lax.axis_size("gy") // 2, 0, rows - 1)


def pack_kernel(r):
    count, rows, depths = r.stress.shape[1:]
    whole = [(comp, 0, count) for comp in STRESS_SLOTS]
    some = {}
    for comp, place in STRESS_TAIL + STRESS_HEAD:
        if comp not in STRESS_SLOTS:
            some.setdefault((comp, place < 0), []).append(place % count)
    some = [(comp, min(at), max(at) + 1) for (comp, _), at in some.items()]
    copies = []
    for i, (comp, start, stop) in enumerate(some + whole):
        span = pl.ds(start, stop - start)
        copy = pltpu.make_async_copy(r.stress.at[comp, span], r.held.at[comp, span], r.sems.at[i])
        copy.start()
        copies.append(copy)
    edges = Edges(rows, depths)
    for copy in copies:
        copy.wait()
    edge_planes(Field(count, r.held), STRESS_TAIL, STRESS_HEAD, r.one_out, r.two_out)
    strip = jnp.zeros((rows, depths), jnp.float32)
    for x in range(count):
        strip = edges.packed(strip, x, [r.held[c, x] for c in STRESS_SLOTS])
    set_strip(r, strip)


def grouped(xs, size):
    return [xs[i : i + size] for i in range(0, len(xs), size)]


def set_strip(r, strip):
    r.strip_out[0] = strip
    for i in range(1, STRIP_PLANES):
        r.strip_out[i] = jnp.zeros_like(strip)


def unpack(r, xs, edges):
    strip = r.strip[0]
    for i, x in enumerate(xs):
        for k in range(3):
            r.ends[i, k] = edges.ends(strip, x, k)


def velocity_planes(r, xs, edges, planes, write):
    band = Bands(getattr(r, "lower", None), getattr(r, "upper", None), STRESS_TAIL_Y, STRESS_HEAD_Y)
    unpack(r, xs, edges)

    def new(x):
        push = DT * looked_up(r.material[x], r.table, 2, CLASSES)
        ends = [r.ends[xs.index(x), k] for k in range(3)]
        along_x = (
            planes.forward_x(XX, x)
            + edges.backward_y(planes, XY, x, band(XY, x))
            + edges.backward_z(planes(XZ, x), ends[0])
        )
        along_y = (
            planes.backward_x(XY, x)
            + edges.forward_y(planes, YY, x, band(YY, x))
            + edges.backward_z(planes(YZ, x), ends[1])
        )
        along_z = (
            planes.backward_x(XZ, x)
            + edges.backward_y(planes, YZ, x, band(YZ, x))
            + edges.forward_z(planes(ZZ, x), ends[2])
        )
        rates = (along_x, along_y, along_z)
        return [r.velocity[c, x] + push * rate for c, rate in enumerate(rates)]

    for group in grouped(xs, 3 if len(xs) % 3 == 0 else 2):
        for x, values in [(x, new(x)) for x in group]:
            write(x, values)


def velocity_inner(r):
    count, rows, depths = r.material.shape
    edges = Edges(rows, depths)
    planes = Planes(stress_of(r), STRESS_TAIL, STRESS_HEAD)

    def write(x, new):
        for c in range(3):
            r.inner_out[c, x - 2] = new[c]

    velocity_planes(r, inside(count), edges, planes, write)
    strip = jnp.zeros((rows, depths), jnp.float32)
    for x in inside(count):
        strip = edges.packed(strip, x, [r.inner_out[c, x - 2] for c in VEL_SLOTS])
    r.strip_inner_out[...] = strip


def velocity_edge(first, r):
    count, rows, depths = r.material.shape
    edges = Edges(rows, depths)
    planes = Planes(stress_of(r), STRESS_TAIL, STRESS_HEAD, r.one, r.two)
    fault = fault_row(rows)
    places = ends_of(count)
    row = pl.ds(fault, 1)
    if first:
        labels = [r.material[x, row, :] for x in range(count)]
        lines = [looked_up(label, r.table, 2, CLASSES) for label in labels]
        for x, line in enumerate(lines):
            r.face_out[pl.ds(2 * count + x, 1), :] = line
    if hasattr(r, "prestress"):
        own = r.normal.shape[0]
        place = 3 * count
        lines = [r.prestress[i, pl.ds(c, 1), :] for c in (0, 1) for i in range(own)]
        fields = [field[...] for field in (r.normal, r.slip, r.zone, r.mask)]
        for i, line in enumerate(lines):
            r.face_out[pl.ds(place + i, 1), :] = line
        for i, field in enumerate(fields):
            r.face_out[pl.ds(place + (2 + i) * own, own), :] = field.astype(jnp.float32)


    def write(x, new):
        for c in range(3):
            r.edge_out[c, places.index(x)] = new[c]

    velocity_planes(r, places, edges, planes, write)
    strip = r.strip_inner[...]
    for i, x in enumerate(places):
        strip = edges.packed(strip, x, [r.edge_out[c, i] for c in VEL_SLOTS])
    set_strip(r, strip)
    new = Field(count, r.inner, r.edge_out)
    lines = [new.rows(c, x)(fault, 1) for c in (0, 2) for x in range(count)]
    for i, line in enumerate(lines):
        r.face_out[pl.ds(i, 1), :] = line
    edge_planes(new, VEL_TAIL, VEL_HEAD, r.one_out, r.two_out)


def stress_of(r):
    count = r.material.shape[0]
    if hasattr(r, "stress"):
        return Field(count, r.stress)
    return Field(count, r.stress_inner, r.stress_edge)


def memory_of(r):
    count = r.material.shape[0]
    if hasattr(r, "memory"):
        return Field(count, r.memory)
    return Field(count, r.memory_inner, r.memory_edge)


def fault_kernel(first, r):
    own_face, other_face = r.face, r.other
    own_first, other_first = (own_face, other_face) if first else (r.face_first, r.other_first)
    rows, depths = r.strip.shape[1:]
    count = r.change_out.shape[1]
    middle = lax.axis_size("gy") // 2
    side = lax.axis_index("gy")
    plus = side == middle
    minus = side == middle - 1

    def pair(own, other, place):
        mine, theirs = own[pl.ds(place, count), :], other[pl.ds(place, count), :]
        return jnp.where(plus, theirs, mine), jnp.where(plus, mine, theirs)

    if hasattr(r, "still"):
        still = r.still
    else:
        still = r.still_out
        share = (own_face.shape[0] - 3 * count) // 6
        for i in range(6):
            mine = own_face[pl.ds(3 * count + i * share, share), :]
            theirs = other_face[pl.ds(3 * count + i * share, share), :]
            still[i, pl.ds(0, share), :] = jnp.where(plus, theirs, mine)
            still[i, pl.ds(share, share), :] = jnp.where(plus, mine, theirs)
    pre_x, pre_z, normal = still[0], still[1], still[2]
    slip = still[3] if first else r.slip[...]
    zone, mask = still[4], still[5]

    row = lax.broadcasted_iota(jnp.int32, (count, depths), 0) + lax.axis_index("gx") * count
    deep = lax.broadcasted_iota(jnp.int32, (count, depths), 1) + lax.axis_index("gz") * depths
    inside = (row >= r.anchor[0]) & (row < r.anchor[0] + 2 * PATCH)
    inside = inside & (deep >= r.anchor[1]) & (deep < r.anchor[1] + 2 * PATCH)
    dynamic = 0.4 * looked_up(zone, r.friction, 0, ZONES)
    static = jnp.where(
        inside, dynamic, dynamic + 0.5 * looked_up(zone, r.friction, 1, ZONES)
    )
    distance = 0.2 * looked_up(zone, r.friction, 2, ZONES)
    minus_x, plus_x = pair(own_face, other_face, 0)
    minus_z, plus_z = pair(own_face, other_face, count)
    minus_b, plus_b = pair(own_first, other_first, 2 * count)
    bsum = minus_b + plus_b
    trial_x = (plus_x - minus_x) / (DT * bsum) + pre_x
    trial_z = (plus_z - minus_z) / (DT * bsum) + pre_z
    size = jnp.sqrt(trial_x * trial_x + trial_z * trial_z)
    weaken = jnp.minimum(slip / distance, 1.0)
    strength = (static - (static - dynamic) * weaken) * normal
    factor = jnp.where(mask == 1.0, strength / jnp.maximum(size, strength), 1.0)
    new_slip = slip + DT * DT * bsum * (size - size * factor)
    half = r.slip_out.shape[0]
    if half < count:
        new_slip = jnp.where(plus, new_slip[half:], new_slip[:half])
    r.slip_out[...] = new_slip
    sign = jnp.where(minus, DT, 0.0) * minus_b - jnp.where(plus, DT, 0.0) * plus_b
    change_x = (trial_x * factor - pre_x) * sign
    change_z = (trial_z * factor - pre_z) * sign
    r.change_out[0] = change_x
    r.change_out[1] = change_z

    fault = fault_row(rows)
    on_fault = lax.broadcasted_iota(jnp.int32, (rows, depths), 0) == fault
    even = even_strike()
    still_line = jnp.zeros((1, depths), jnp.float32)

    def line(planes, i):
        comp, place = planes[min(i, len(planes) - 1)]
        return still_line if comp == 1 else r.change_out[comp // 2, pl.ds(place % count, 1), :]

    pairs = []
    for i in range(r.one_out.shape[0]):
        right, left = line(VEL_TAIL, i), line(VEL_HEAD, i)
        one, two = jnp.where(even, right, left), jnp.where(even, left, right)
        one = r.one[i] + jnp.where(on_fault, one, 0.0)
        pairs.append((one, r.two[i] + jnp.where(on_fault, two, 0.0)))
    for i, (one, two) in enumerate(pairs):
        r.one_out[i] = one
        r.two_out[i] = two
    ends = jnp.zeros((count, depths), jnp.float32)
    pair = lax.broadcasted_iota(jnp.int32, (count, depths), 1) // 2
    place = 4 * lax.broadcasted_iota(jnp.int32, (count, depths), 0)
    upper = lax.axis_index("gz") == 0
    for k, field in ((0, change_x), (2, change_z)):
        turned = jnp.where(upper, pltpu.roll(field, 2, 1), field)
        turned = pltpu.roll(turned, 2 * k, 1, stride=8, stride_axis=0)
        ends = jnp.where(pair == place + k, turned, ends)
    line = jnp.sum(ends, axis=0, keepdims=True)
    set_strip(r, r.strip[0] + jnp.where(on_fault, line, 0.0))


def stress_planes(r, xs, edges, planes, write):
    band = Bands(getattr(r, "lower", None), getattr(r, "upper", None), VEL_TAIL_Y, VEL_HEAD_Y)
    stress, memory = stress_of(r), memory_of(r)
    unpack(r, xs, edges)

    def rates(x):
        in_x, in_y, in_z = [r.ends[xs.index(x), k] for k in range(3)]
        exx = planes.backward_x(0, x)
        eyy = edges.backward_y(planes, 1, x, band(1, x))
        ezz = edges.backward_z(planes(2, x), in_z)
        exy = edges.forward_y(planes, 0, x, band(0, x)) + planes.forward_x(1, x)
        exz = edges.forward_z(planes(0, x), in_x) + planes.forward_x(2, x)
        eyz = edges.forward_z(planes(1, x), in_y) + edges.forward_y(planes, 2, x, band(2, x))
        labels = r.material[x]
        bulk = looked_up(labels, r.table, 0, CLASSES) * (exx + eyy + ezz)
        shear = looked_up(labels, r.table, 1, CLASSES)
        double = 2.0 * shear
        return (
            bulk + double * exx,
            bulk + double * eyy,
            bulk + double * ezz,
            shear * exy,
            shear * exz,
            shear * eyz,
        )

    def new(x, elastic):
        labels = r.material[x]
        decay = jnp.exp(-DT / looked_up(labels, r.table, 3, CLASSES))
        gain = (1.0 - decay) * (0.3 * looked_up(labels, r.table, 4, CLASSES))
        kept = [decay * memory(c, x) - gain * elastic[c] for c in range(6)]
        return [stress(c, x) + DT * (elastic[c] + kept[c]) for c in range(6)], kept

    for group in grouped(xs, 2):
        for x, elastic in [(x, rates(x)) for x in group]:
            write(x, *new(x, elastic))


def stress_inner(last, r):
    count, rows, depths = r.material.shape
    edges = Edges(rows, depths, by_loads=True)
    on_fault = edges.row == fault_row(rows)
    free = Field(count, r.inner, r.edge)
    for x in range(count):
        for c in (0, 2):
            line = r.change[c // 2, pl.ds(x, 1), :]
            r.velocity_out[c, x] = free(c, x) + jnp.where(on_fault, line, 0.0)
        r.velocity_out[1, x] = free(1, x)
    planes = Planes(Field(count, r.velocity_out), VEL_TAIL, VEL_HEAD)
    copies = []

    def copy_out(source, out):
        copy = pltpu.make_async_copy(source, out, r.sems.at[len(copies)])
        copy.start()
        copies.append(copy)

    if last:
        copy_out(r.velocity_out, r.new_velocity_out)
        if hasattr(r, "slip"):
            copy_out(r.slip, r.new_slip_out)
        stress_out, memory_out = r.stress_held, r.memory_held
    else:
        stress_out, memory_out = r.stress_inner_out, r.memory_inner_out

    def write(x, new, kept):
        for c in range(6):
            stress_out[c, x - 2] = new[c]
            memory_out[c, x - 2] = kept[c]
        if last and x % 2 == 1:
            held, out = pl.ds(x - 3, 2), pl.ds(x - 1, 2)
            copy_out(stress_out.at[:, held], r.stress_out.at[:, out])
            copy_out(memory_out.at[:, held], r.memory_out.at[:, out])

    stress_planes(r, inside(count), edges, planes, write)
    if last:
        for copy in copies:
            copy.wait()
    else:
        strip = jnp.zeros((rows, depths), jnp.float32)
        for x in inside(count):
            strip = edges.packed(strip, x, [r.stress_inner_out[c, x - 2] for c in STRESS_SLOTS])
        r.strip_inner_out[...] = strip


def stress_edge(last, r):
    count, rows, depths = r.material.shape
    edges = Edges(rows, depths, by_loads=True)
    planes = Planes(Field(count, r.velocity), VEL_TAIL, VEL_HEAD, r.one, r.two)
    places = ends_of(count)
    copies = []

    def copy_out(source, out, span):
        copy = pltpu.make_async_copy(source, out.at[:, span], r.sems.at[len(copies)])
        copy.start()
        copies.append(copy)

    if last:
        stress_out, memory_out = r.stress_held, r.memory_held
    else:
        stress_out, memory_out = r.stress_edge_out, r.memory_edge_out

    def write(x, new, kept):
        for c in range(6):
            stress_out[c, places.index(x)] = new[c]
            memory_out[c, places.index(x)] = kept[c]

    stress_planes(r, places, edges, planes, write)
    if last:
        for held, out in ((stress_out, r.stress_out), (memory_out, r.memory_out)):
            copy_out(held.at[:, pl.ds(0, 2)], out, pl.ds(0, 2))
            copy_out(held.at[:, pl.ds(2, 2)], out, pl.ds(count - 2, 2))
        for copy in copies:
            copy.wait()
    else:
        strip = r.strip_inner[...]
        for i, x in enumerate(places):
            strip = edges.packed(strip, x, [stress_out[c, i] for c in STRESS_SLOTS])
        set_strip(r, strip)
        new = Field(count, r.new_stress_inner, stress_out)
        edge_planes(new, STRESS_TAIL, STRESS_HEAD, r.one_out, r.two_out)


SCALARS = ("table", "friction", "anchor")


def call(kernel, name, ins, outs, scratch=None, apart=(), onto=(), micros=1, vmem=6):
    scratch = scratch or {}
    names = [*ins, *(f"{key}_out" for key in outs), *scratch]

    def body(*refs):
        kernel(types.SimpleNamespace(**dict(zip(names, refs))))

    def place(key):
        if key in apart:
            return pl.BlockSpec(memory_space=pltpu.HBM)
        return pl.BlockSpec(memory_space=pltpu.SMEM if key in SCALARS else pltpu.VMEM)

    shapes = [jax.ShapeDtypeStruct(shape, jnp.float32) for shape in outs.values()]
    result = pl.pallas_call(
        body,
        out_shape=shapes,
        in_specs=[place(key) for key in ins],
        out_specs=[place(f"{key}_out") for key in outs],
        scratch_shapes=list(scratch.values()),
        name=name,
        input_output_aliases={
            list(ins).index(key): list(outs).index(onto[key]) for key in onto
        },
        cost_estimate=pl.CostEstimate(
            flops=0, bytes_accessed=micros * 3_690_000, transcendentals=0
        ),
        compiler_params=pltpu.CompilerParams(vmem_limit_bytes=vmem * 2**20),
    )(*ins.values())
    return dict(zip(outs, result))


def along(axis, count, skip=()):
    up = [(i, i + 1) for i in range(count - 1) if i not in skip]
    return (axis, up), (axis, [(b, a) for a, b in up])


def strike_swaps(count):
    routes = []
    for start in (0, 1):
        partner = list(range(count))
        for i in range(start, count - 1, 2):
            partner[i], partner[i + 1] = i + 1, i
        routes.append(("gx", list(enumerate(partner))))
    return routes


def sent(block, route):
    return lax.ppermute(block, *route)


def whole(parts, name):
    if name in parts:
        return parts[name]
    inner, edge = parts[f"{name}_inner"], parts[f"{name}_edge"]
    return jnp.concatenate([edge[:, :2], inner, edge[:, 2:]], axis=1)


def edge_rows(field, rows):
    count = field.shape[2]
    return jnp.stack([field[c, :, place % count, :] for c, place in rows])


def shards(
    velocity,
    stress,
    memory,
    material,
    material_table,
    fault_mask,
    zone_label,
    patch_anchor,
    friction_table,
    prestress,
    normal_stress,
    slip_path,
):
    _, count, rows, depths = velocity.shape
    sides = lax.axis_size("gy")
    middle = sides // 2
    banded = sides > 2
    swaps = strike_swaps(lax.axis_size("gx"))
    up_y, down_y = along("gy", sides, (middle - 1,))
    across = ("gy", [(middle - 1, middle), (middle, middle - 1)])
    deep = ("gz", [(0, 1), (1, 0)])

    plane = (rows, depths)
    edge_shape = (max(len(STRESS_TAIL), len(STRESS_HEAD)), *plane)
    travelling = {"one": edge_shape, "two": edge_shape, "strip": (STRIP_PLANES, *plane)}
    inner, edge = (count - 4, *plane), (4, *plane)
    inner_ends = {"ends": pltpu.VMEM((count - 4, 3, *plane), jnp.float32)}
    edge_ends = {"ends": pltpu.VMEM((4, 3, *plane), jnp.float32)}

    def travelled(packed):
        two = sent(packed["two"], swaps[1])
        one = sent(packed["one"], swaps[0])
        strip = sent(packed["strip"], deep)
        return {"strip": strip}, {"one": one, "two": two}

    def bands(field, tail, head):
        if not banded:
            return {}
        lower, upper = edge_rows(field, tail), edge_rows(field, head)
        return {"lower": sent(lower, up_y), "upper": sent(upper, down_y)}

    if banded:
        still = jnp.stack(
            [
                prestress[:, 0],
                prestress[:, 1],
                normal_stress,
                slip_path,
                zone_label.astype(jnp.float32),
                fault_mask.astype(jnp.float32),
            ]
        )
        still = {"still": lax.all_gather(still, "gy", axis=1, tiled=True)}
    else:
        still = {}

    parts = {"stress": stress, "memory": memory}
    props = {"material": material, "table": material_table}
    packed = call(
        pack_kernel,
        "pack",
        {"stress": stress},
        travelling,
        scratch={"held": pltpu.VMEM(stress.shape, jnp.float32), "sems": pltpu.SemaphoreType.DMA((8,))},
        apart=("stress",),
        vmem=6,
    )
    for step in range(STEPS):
        first, last = step == 0, step == STEPS - 1
        held_stress = {key: parts[key] for key in parts if key.startswith("stress")}
        strip, halos = travelled(packed)
        ins = {"velocity": velocity, **held_stress, **props, **strip}
        if banded:
            ins.update(bands(whole(parts, "stress"), STRESS_TAIL_Y, STRESS_HEAD_Y))
        free = call(
            velocity_inner,
            "velocity_inner",
            ins,
            {"inner": (3, *inner), "strip_inner": plane},
            scratch=inner_ends,
            micros=3,
        )
        face_rows = 2 * count
        ins = {**ins, **halos, **free}
        if first:
            face_rows += count
            if not banded:
                ins.update(prestress=prestress, normal=normal_stress, slip=slip_path)
                ins.update(zone=zone_label, mask=fault_mask)
                face_rows += 6 * normal_stress.shape[0]
        packed = call(
            functools.partial(velocity_edge, first),
            "velocity_edge",
            ins,
            {"edge": (3, *edge), "face": (face_rows, depths), **travelling},
            scratch=edge_ends,
        )
        free = {"inner": free["inner"], "edge": packed["edge"]}
        face = packed["face"]
        other = sent(face, across)
        ins = {key: packed[key] for key in travelling}
        ins.update(face=face, other=other, friction=friction_table, anchor=patch_anchor, **still)
        if first:
            faces = {"face_first": face, "other_first": other}
        else:
            ins.update(slip=slip, **faces)
        outs = {"change": (2, count, depths), "slip": (count, depths), **travelling}
        if last and not banded:
            outs["slip"] = (count // sides, depths)
        if not still:
            outs["still"] = (6, count, depths)
        packed = call(functools.partial(fault_kernel, first), "fault", ins, outs, vmem=2)
        slip = packed["slip"]
        if not still:
            still = {"still": packed["still"]}
        strip, halos = travelled(packed)
        ins = {**free, "change": packed["change"], **parts, **props, **strip}
        if banded:
            joined = jnp.concatenate(
                [free["edge"][:, :2], free["inner"], free["edge"][:, 2:]], axis=1
            )
            band = bands(joined, VEL_TAIL_Y, VEL_HEAD_Y)
        else:
            band = {}
        outs = {"velocity": velocity.shape}
        extra = {"scratch": inner_ends}
        if last:
            outs.update(new_velocity=velocity.shape, stress=stress.shape, memory=memory.shape)
            extra["apart"] = ["new_velocity_out", "stress_out", "memory_out"]
            if not banded:
                ins["slip"] = slip
                outs["new_slip"] = slip.shape
                extra["apart"].append("new_slip_out")
            held = pltpu.VMEM((6, *inner), jnp.float32)
            sems = pltpu.SemaphoreType.DMA((count,))
            extra["scratch"] = {"stress_held": held, "memory_held": held, "sems": sems, **inner_ends}
        else:
            outs.update(stress_inner=(6, *inner), memory_inner=(6, *inner), strip_inner=plane)
        done = call(
            functools.partial(stress_inner, last),
            "stress_inner",
            {**ins, **band},
            outs,
            micros=3,
            vmem=11,
            **extra,
        )
        velocity = done["velocity"]
        ins = {"velocity": velocity, **parts, **props, **strip, **halos, **band}
        if last:
            ins.update(stress_done=done["stress"], memory_done=done["memory"])
            held = pltpu.VMEM((6, *edge), jnp.float32)
            packed = call(
                functools.partial(stress_edge, last),
                "stress_edge",
                ins,
                {"stress": stress.shape, "memory": memory.shape},
                scratch={
                    "stress_held": held,
                    "memory_held": held,
                    "sems": pltpu.SemaphoreType.DMA((4,)),
                    **edge_ends,
                },
                apart=("stress_done", "memory_done", "stress_out", "memory_out"),
                onto={"stress_done": "stress", "memory_done": "memory"},
                vmem=10,
            )
            velocity = done["new_velocity"]
            stress, memory = packed["stress"], packed["memory"]
            slip = done.get("new_slip", slip)
        else:
            ins.update(new_stress_inner=done["stress_inner"], strip_inner=done["strip_inner"])
            packed = call(
                functools.partial(stress_edge, last),
                "stress_edge",
                ins,
                {"stress_edge": (6, *edge), "memory_edge": (6, *edge), **travelling},
                scratch=edge_ends,
                vmem=10,
            )
            parts = {
                "stress_inner": done["stress_inner"],
                "stress_edge": packed["stress_edge"],
                "memory_inner": done["memory_inner"],
                "memory_edge": packed["memory_edge"],
            }
    if banded:
        held = jnp.where(lax.axis_index("gy") == middle, slip, 0.0)
        slip = lax.psum_scatter(held, "gy", scatter_dimension=0, tiled=True)
    return (velocity, stress, memory, slip)


def solution(mesh):
    in_specs = (
        P(None, ("ens", "gx"), "gy", "gz"),
        P(None, ("ens", "gx"), "gy", "gz"),
        P(None, ("ens", "gx"), "gy", "gz"),
        P(("ens", "gx"), "gy", "gz"),
        P(None, "ens"),
        P(("ens", "gx", "gy"), "gz"),
        P(("ens", "gx", "gy"), "gz"),
        P("ens"),
        P(None, "ens"),
        P(("ens", "gx", "gy"), None, "gz"),
        P(("ens", "gx", "gy"), "gz"),
        P(("ens", "gx", "gy"), "gz"),
    )
    out_specs = (
        P(None, ("ens", "gx"), "gy", "gz"),
        P(None, ("ens", "gx"), "gy", "gz"),
        P(None, ("ens", "gx"), "gy", "gz"),
        P(("ens", "gx", "gy"), "gz"),
    )
    return jax.shard_map(shards, mesh=mesh, in_specs=in_specs, out_specs=out_specs, check_vma=False)
```

```python
import functools
import types

import jax
import jax.numpy as jnp
from jax import lax
from jax.experimental import pallas as pl
from jax.experimental.pallas import tpu as pltpu
from jax.sharding import PartitionSpec as P

STEPS = 2
CLASSES = 8
ZONES = 4
PATCH = 8

NEAR = 9.0 / 8.0
FAR = -1.0 / 24.0
DT = 0.15
TILE = 8
STRIP_PLANES = 6

XX, YY, ZZ, XY, XZ, YZ = range(6)

STRESS_TAIL = ((XX, -1), (XY, -2), (XY, -1), (XZ, -2), (XZ, -1))
STRESS_HEAD = ((XX, 0), (XX, 1), (XY, 0), (XZ, 0))
VEL_TAIL = ((0, -2), (0, -1), (1, -1), (2, -1))
VEL_HEAD = ((0, 0), (1, 0), (1, 1), (2, 0), (2, 1))
STRESS_TAIL_Y = ((YY, -1), (XY, -2), (XY, -1), (YZ, -2), (YZ, -1))
STRESS_HEAD_Y = ((YY, 0), (YY, 1), (XY, 0), (YZ, 0))
VEL_TAIL_Y = ((1, -2), (1, -1), (0, -1), (2, -1))
VEL_HEAD_Y = ((1, 0), (0, 0), (0, 1), (2, 0), (2, 1))
STRESS_SLOTS = (XZ, YZ, ZZ)
VEL_SLOTS = (0, 1, 2)


def forward(before, here, after, after_2):
    return NEAR * (after - here) + FAR * (after_2 - before)


def backward(before_2, before, here, after):
    return NEAR * (here - before) + FAR * (after - before_2)


class Edges:
    def __init__(self, rows, depths, by_loads=False):
        self.rows = rows
        self.depths = depths
        lane = lax.broadcasted_iota(jnp.int32, (rows, depths), 1)
        row = lax.broadcasted_iota(jnp.int32, (TILE, depths), 0)
        self.row = lax.broadcasted_iota(jnp.int32, (rows, depths), 0)
        self.tile_row = row
        self.deep = lax.axis_index("gz")
        near = (self.deep == 0) & (lane < 2) | (self.deep == 1) & (lane >= depths - 2)
        self.near = jnp.where(near, 1.0, 0.0)
        self.zero = jnp.minimum(self.deep, 0)
        self.by_loads = by_loads
        self.pair = lane // 2
        self.low = {n: lane < n for n in (1, 2)}
        self.high = {n: lane >= depths - n for n in (1, 2)}
        self.top = {n: row < n for n in (1, 2)}
        self.bottom = {n: row >= TILE - n for n in (1, 2)}

    def packed(self, strip, x, fields):
        first = jnp.where(self.deep == 0, 2, 0)
        for k, field in enumerate(fields):
            turn = lax.rem(first + 8 * x + 2 * k, self.depths)
            strip = jnp.where(self.pair == 4 * x + k, pltpu.roll(field, turn, 1), strip)
        return strip

    def ends(self, strip, x, k):
        back = self.depths - 8 * x - 2 * k
        turn = jnp.where(self.deep == 0, back % self.depths, back - 2)
        return pltpu.roll(strip, turn, 1) * self.near

    def shallower(self, field, halo, n):
        return pltpu.roll(jnp.where(self.high[n], halo, field), n, 1)

    def deeper(self, field, halo, n):
        return pltpu.roll(jnp.where(self.low[n], halo, field), self.depths - n, 1)

    def forward_z(self, field, halo):
        return forward(
            self.shallower(field, halo, 1),
            field,
            self.deeper(field, halo, 1),
            self.deeper(field, halo, 2),
        )

    def backward_z(self, field, halo):
        return backward(
            self.shallower(field, halo, 2),
            self.shallower(field, halo, 1),
            field,
            self.deeper(field, halo, 1),
        )

    def before(self, field, load, n, halo):
        top = jnp.where(self.top[n], 0.0, pltpu.roll(field[:TILE], n, 0))
        if halo:
            for i in range(n):
                top = jnp.where(self.tile_row == i, halo[n - 1 - i], top)
        if load:
            rest = load(self.zero + (TILE - n), self.rows - TILE)
        else:
            rest = pltpu.roll(field, n, 0)[TILE:]
        return jnp.concatenate([top, rest], axis=0)

    def after(self, field, load, n, halo):
        bottom = pltpu.roll(field[self.rows - TILE :], TILE - n, 0)
        bottom = jnp.where(self.bottom[n], 0.0, bottom)
        if halo:
            for i in range(n):
                bottom = jnp.where(self.tile_row == TILE - n + i, halo[i], bottom)
        if load:
            rest = load(self.zero + n, self.rows - TILE)
        else:
            rest = pltpu.roll(field, self.rows - n, 0)[: self.rows - TILE]
        return jnp.concatenate([rest, bottom], axis=0)

    def forward_y(self, planes, comp, x, halos):
        field = planes(comp, x)
        load = planes.rows(comp, x) if self.by_loads else None
        lower, upper = halos
        return forward(
            self.before(field, load, 1, lower),
            field,
            self.after(field, load, 1, upper),
            self.after(field, load, 2, upper),
        )

    def backward_y(self, planes, comp, x, halos):
        field = planes(comp, x)
        load = planes.rows(comp, x) if self.by_loads else None
        lower, upper = halos
        return backward(
            self.before(field, load, 2, lower),
            self.before(field, load, 1, lower),
            field,
            self.after(field, load, 1, upper),
        )


class Field:
    def __init__(self, count, *parts):
        self.count = count
        self.parts = parts

    def place(self, x):
        if len(self.parts) == 1:
            return self.parts[0], x
        inner, edge = self.parts
        if x in inside(self.count):
            return inner, x - 2
        return edge, ends_of(self.count).index(x)

    def __call__(self, comp, x):
        ref, at = self.place(x)
        return ref[comp, at]

    def rows(self, comp, x):
        ref, at = self.place(x)
        return lambda start, size: ref[comp, at, pl.ds(start, size), :]


def inside(count):
    return range(2, count - 2)


def ends_of(count):
    return (0, 1, count - 2, count - 1)


class Planes:
    def __init__(self, field, tail, head, first=None, second=None):
        self.field = field
        self.count = field.count
        self.first, self.second = first, second
        self.tail, self.head = tail, head
        self.even = even_strike()
        self.any_left = lax.axis_index("gx") > 0
        self.any_right = lax.axis_index("gx") < lax.axis_size("gx") - 1

    def left(self, i):
        plane = jnp.where(self.even, self.second[i], self.first[i])
        return jnp.where(self.any_left, plane, 0.0)

    def right(self, i):
        plane = jnp.where(self.even, self.first[i], self.second[i])
        return jnp.where(self.any_right, plane, 0.0)

    def __call__(self, comp, place):
        if place < 0:
            return self.left(self.tail.index((comp, place)))
        if place >= self.count:
            return self.right(self.head.index((comp, place - self.count)))
        return self.field(comp, place)

    def rows(self, comp, x):
        return self.field.rows(comp, x)

    def forward_x(self, comp, x):
        return forward(self(comp, x - 1), self(comp, x), self(comp, x + 1), self(comp, x + 2))

    def backward_x(self, comp, x):
        return backward(self(comp, x - 2), self(comp, x - 1), self(comp, x), self(comp, x + 1))


class Bands:
    def __init__(self, lower, upper, tail, head):
        self.lower, self.upper = lower, upper
        self.tail, self.head = tail, head

    def __call__(self, comp, x):
        if self.lower is None:
            return (None, None)
        places = [i for i, (c, _) in enumerate(self.tail) if c == comp]
        before = [self.lower[i, pl.ds(x, 1), :] for i in reversed(places)]
        places = [i for i, (c, _) in enumerate(self.head) if c == comp]
        after = [self.upper[i, pl.ds(x, 1), :] for i in places]
        return (before, after)


def looked_up(labels, table, row, count):
    out = jnp.full(labels.shape, table[row, 0], jnp.float32)
    for k in range(1, count):
        out = jnp.where(labels == k, table[row, k], out)
    return out


def even_strike():
    return lax.axis_index("gx") % 2 == 0


def edge_planes(field, tail, head, first_out, second_out):
    even = even_strike()
    pairs = []
    for i in range(first_out.shape[0]):
        comp, place = tail[min(i, len(tail) - 1)]
        right = field(comp, place % field.count)
        comp, place = head[min(i, len(head) - 1)]
        left = field(comp, place % field.count)
        pairs.append((jnp.where(even, right, left), jnp.where(even, left, right)))
    for i, (one, two) in enumerate(pairs):
        first_out[i] = one
        second_out[i] = two


def fault_row(rows):
    return jnp.where(lax.axis_index("gy") == lax.axis_size("gy") // 2, 0, rows - 1)


def pack_kernel(r):
    count, rows, depths = r.stress.shape[1:]
    whole = [(comp, 0, count) for comp in STRESS_SLOTS]
    some = {}
    for comp, place in STRESS_TAIL + STRESS_HEAD:
        if comp not in STRESS_SLOTS:
            some.setdefault((comp, place < 0), []).append(place % count)
    some = [(comp, min(at), max(at) + 1) for (comp, _), at in some.items()]
    copies = []
    for i, (comp, start, stop) in enumerate(some + whole):
        span = pl.ds(start, stop - start)
        copy = pltpu.make_async_copy(r.stress.at[comp, span], r.held.at[comp, span], r.sems.at[i])
        copy.start()
        copies.append(copy)
    edges = Edges(rows, depths)
    for copy in copies:
        copy.wait()
    edge_planes(Field(count, r.held), STRESS_TAIL, STRESS_HEAD, r.one_out, r.two_out)
    strip = jnp.zeros((rows, depths), jnp.float32)
    for x in range(count):
        strip = edges.packed(strip, x, [r.held[c, x] for c in STRESS_SLOTS])
    set_strip(r, strip)


def grouped(xs, size):
    return [xs[i : i + size] for i in range(0, len(xs), size)]


def set_strip(r, strip):
    r.strip_out[0] = strip
    for i in range(1, STRIP_PLANES):
        r.strip_out[i] = jnp.zeros_like(strip)


def unpack(r, xs, edges):
    strip = r.strip[0]
    for i, x in enumerate(xs):
        for k in range(3):
            r.ends[i, k] = edges.ends(strip, x, k)


def velocity_planes(r, xs, edges, planes, write):
    band = Bands(getattr(r, "lower", None), getattr(r, "upper", None), STRESS_TAIL_Y, STRESS_HEAD_Y)
    unpack(r, xs, edges)

    def new(x):
        push = DT * looked_up(r.material[x], r.table, 2, CLASSES)
        ends = [r.ends[xs.index(x), k] for k in range(3)]
        along_x = (
            planes.forward_x(XX, x)
            + edges.backward_y(planes, XY, x, band(XY, x))
            + edges.backward_z(planes(XZ, x), ends[0])
        )
        along_y = (
            planes.backward_x(XY, x)
            + edges.forward_y(planes, YY, x, band(YY, x))
            + edges.backward_z(planes(YZ, x), ends[1])
        )
        along_z = (
            planes.backward_x(XZ, x)
            + edges.backward_y(planes, YZ, x, band(YZ, x))
            + edges.forward_z(planes(ZZ, x), ends[2])
        )
        rates = (along_x, along_y, along_z)
        return [r.velocity[c, x] + push * rate for c, rate in enumerate(rates)]

    for group in grouped(xs, 3 if len(xs) % 3 == 0 else 2):
        for x, values in [(x, new(x)) for x in group]:
            write(x, values)


def velocity_inner(r):
    count, rows, depths = r.material.shape
    edges = Edges(rows, depths)
    planes = Planes(stress_of(r), STRESS_TAIL, STRESS_HEAD)

    def write(x, new):
        for c in range(3):
            r.inner_out[c, x - 2] = new[c]

    velocity_planes(r, inside(count), edges, planes, write)
    strip = jnp.zeros((rows, depths), jnp.float32)
    for x in inside(count):
        strip = edges.packed(strip, x, [r.inner_out[c, x - 2] for c in VEL_SLOTS])
    r.strip_inner_out[...] = strip


def velocity_edge(first, r):
    count, rows, depths = r.material.shape
    edges = Edges(rows, depths)
    planes = Planes(stress_of(r), STRESS_TAIL, STRESS_HEAD, r.one, r.two)
    fault = fault_row(rows)
    places = ends_of(count)
    row = pl.ds(fault, 1)
    if first:
        labels = [r.material[x, row, :] for x in range(count)]
        lines = [looked_up(label, r.table, 2, CLASSES) for label in labels]
        for x, line in enumerate(lines):
            r.face_out[pl.ds(2 * count + x, 1), :] = line
    if hasattr(r, "prestress"):
        own = r.normal.shape[0]
        place = 3 * count
        lines = [r.prestress[i, pl.ds(c, 1), :] for c in (0, 1) for i in range(own)]
        fields = [field[...] for field in (r.normal, r.slip, r.zone, r.mask)]
        for i, line in enumerate(lines):
            r.face_out[pl.ds(place + i, 1), :] = line
        for i, field in enumerate(fields):
            r.face_out[pl.ds(place + (2 + i) * own, own), :] = field.astype(jnp.float32)


    def write(x, new):
        for c in range(3):
            r.edge_out[c, places.index(x)] = new[c]

    velocity_planes(r, places, edges, planes, write)
    strip = r.strip_inner[...]
    for i, x in enumerate(places):
        strip = edges.packed(strip, x, [r.edge_out[c, i] for c in VEL_SLOTS])
    set_strip(r, strip)
    new = Field(count, r.inner, r.edge_out)
    lines = [new.rows(c, x)(fault, 1) for c in (0, 2) for x in range(count)]
    for i, line in enumerate(lines):
        r.face_out[pl.ds(i, 1), :] = line
    edge_planes(new, VEL_TAIL, VEL_HEAD, r.one_out, r.two_out)


def stress_of(r):
    count = r.material.shape[0]
    if hasattr(r, "stress"):
        return Field(count, r.stress)
    return Field(count, r.stress_inner, r.stress_edge)


def memory_of(r):
    count = r.material.shape[0]
    if hasattr(r, "memory"):
        return Field(count, r.memory)
    return Field(count, r.memory_inner, r.memory_edge)


def fault_kernel(first, r):
    own_face, other_face = r.face, r.other
    own_first, other_first = (own_face, other_face) if first else (r.face_first, r.other_first)
    rows, depths = r.strip.shape[1:]
    count = r.change_out.shape[1]
    middle = lax.axis_size("gy") // 2
    side = lax.axis_index("gy")
    plus = side == middle
    minus = side == middle - 1

    def pair(own, other, place):
        mine, theirs = own[pl.ds(place, count), :], other[pl.ds(place, count), :]
        return jnp.where(plus, theirs, mine), jnp.where(plus, mine, theirs)

    if hasattr(r, "still"):
        still = r.still
    else:
        still = r.still_out
        share = (own_face.shape[0] - 3 * count) // 6
        for i in range(6):
            mine = own_face[pl.ds(3 * count + i * share, share), :]
            theirs = other_face[pl.ds(3 * count + i * share, share), :]
            still[i, pl.ds(0, share), :] = jnp.where(plus, theirs, mine)
            still[i, pl.ds(share, share), :] = jnp.where(plus, mine, theirs)
    pre_x, pre_z, normal = still[0], still[1], still[2]
    slip = still[3] if first else r.slip[...]
    zone, mask = still[4], still[5]

    row = lax.broadcasted_iota(jnp.int32, (count, depths), 0) + lax.axis_index("gx") * count
    deep = lax.broadcasted_iota(jnp.int32, (count, depths), 1) + lax.axis_index("gz") * depths
    inside = (row >= r.anchor[0]) & (row < r.anchor[0] + 2 * PATCH)
    inside = inside & (deep >= r.anchor[1]) & (deep < r.anchor[1] + 2 * PATCH)
    dynamic = 0.4 * looked_up(zone, r.friction, 0, ZONES)
    static = jnp.where(
        inside, dynamic, dynamic + 0.5 * looked_up(zone, r.friction, 1, ZONES)
    )
    distance = 0.2 * looked_up(zone, r.friction, 2, ZONES)
    minus_x, plus_x = pair(own_face, other_face, 0)
    minus_z, plus_z = pair(own_face, other_face, count)
    minus_b, plus_b = pair(own_first, other_first, 2 * count)
    bsum = minus_b + plus_b
    trial_x = (plus_x - minus_x) / (DT * bsum) + pre_x
    trial_z = (plus_z - minus_z) / (DT * bsum) + pre_z
    size = jnp.sqrt(trial_x * trial_x + trial_z * trial_z)
    weaken = jnp.minimum(slip / distance, 1.0)
    strength = (static - (static - dynamic) * weaken) * normal
    factor = jnp.where(mask == 1.0, strength / jnp.maximum(size, strength), 1.0)
    new_slip = slip + DT * DT * bsum * (size - size * factor)
    half = r.slip_out.shape[0]
    if half < count:
        new_slip = jnp.where(plus, new_slip[half:], new_slip[:half])
    r.slip_out[...] = new_slip
    sign = jnp.where(minus, DT, 0.0) * minus_b - jnp.where(plus, DT, 0.0) * plus_b
    change_x = (trial_x * factor - pre_x) * sign
    change_z = (trial_z * factor - pre_z) * sign
    r.change_out[0] = change_x
    r.change_out[1] = change_z

    fault = fault_row(rows)
    on_fault = lax.broadcasted_iota(jnp.int32, (rows, depths), 0) == fault
    even = even_strike()
    still_line = jnp.zeros((1, depths), jnp.float32)

    def line(planes, i):
        comp, place = planes[min(i, len(planes) - 1)]
        return still_line if comp == 1 else r.change_out[comp // 2, pl.ds(place % count, 1), :]

    pairs = []
    for i in range(r.one_out.shape[0]):
        right, left = line(VEL_TAIL, i), line(VEL_HEAD, i)
        one, two = jnp.where(even, right, left), jnp.where(even, left, right)
        one = r.one[i] + jnp.where(on_fault, one, 0.0)
        pairs.append((one, r.two[i] + jnp.where(on_fault, two, 0.0)))
    for i, (one, two) in enumerate(pairs):
        r.one_out[i] = one
        r.two_out[i] = two
    ends = jnp.zeros((count, depths), jnp.float32)
    pair = lax.broadcasted_iota(jnp.int32, (count, depths), 1) // 2
    place = 4 * lax.broadcasted_iota(jnp.int32, (count, depths), 0)
    upper = lax.axis_index("gz") == 0
    for k, field in ((0, change_x), (2, change_z)):
        turned = jnp.where(upper, pltpu.roll(field, 2, 1), field)
        turned = pltpu.roll(turned, 2 * k, 1, stride=8, stride_axis=0)
        ends = jnp.where(pair == place + k, turned, ends)
    line = jnp.sum(ends, axis=0, keepdims=True)
    set_strip(r, r.strip[0] + jnp.where(on_fault, line, 0.0))


def stress_planes(r, xs, edges, planes, write):
    band = Bands(getattr(r, "lower", None), getattr(r, "upper", None), VEL_TAIL_Y, VEL_HEAD_Y)
    stress, memory = stress_of(r), memory_of(r)
    unpack(r, xs, edges)

    def rates(x):
        in_x, in_y, in_z = [r.ends[xs.index(x), k] for k in range(3)]
        exx = planes.backward_x(0, x)
        eyy = edges.backward_y(planes, 1, x, band(1, x))
        ezz = edges.backward_z(planes(2, x), in_z)
        exy = edges.forward_y(planes, 0, x, band(0, x)) + planes.forward_x(1, x)
        exz = edges.forward_z(planes(0, x), in_x) + planes.forward_x(2, x)
        eyz = edges.forward_z(planes(1, x), in_y) + edges.forward_y(planes, 2, x, band(2, x))
        labels = r.material[x]
        bulk = looked_up(labels, r.table, 0, CLASSES) * (exx + eyy + ezz)
        shear = looked_up(labels, r.table, 1, CLASSES)
        double = 2.0 * shear
        return (
            bulk + double * exx,
            bulk + double * eyy,
            bulk + double * ezz,
            shear * exy,
            shear * exz,
            shear * eyz,
        )

    def new(x, elastic):
        labels = r.material[x]
        decay = jnp.exp(-DT / looked_up(labels, r.table, 3, CLASSES))
        gain = (1.0 - decay) * (0.3 * looked_up(labels, r.table, 4, CLASSES))
        kept = [decay * memory(c, x) - gain * elastic[c] for c in range(6)]
        return [stress(c, x) + DT * (elastic[c] + kept[c]) for c in range(6)], kept

    for group in grouped(xs, 2):
        for x, elastic in [(x, rates(x)) for x in group]:
            write(x, *new(x, elastic))


def stress_inner(last, r):
    count, rows, depths = r.material.shape
    edges = Edges(rows, depths, by_loads=True)
    on_fault = edges.row == fault_row(rows)
    free = Field(count, r.inner, r.edge)
    for x in range(count):
        for c in (0, 2):
            line = r.change[c // 2, pl.ds(x, 1), :]
            r.velocity_out[c, x] = free(c, x) + jnp.where(on_fault, line, 0.0)
        r.velocity_out[1, x] = free(1, x)
    planes = Planes(Field(count, r.velocity_out), VEL_TAIL, VEL_HEAD)
    copies = []

    def copy_out(source, out):
        copy = pltpu.make_async_copy(source, out, r.sems.at[len(copies)])
        copy.start()
        copies.append(copy)

    if last:
        copy_out(r.velocity_out, r.new_velocity_out)
        if hasattr(r, "slip"):
            copy_out(r.slip, r.new_slip_out)
        stress_out, memory_out = r.stress_held, r.memory_held
    else:
        stress_out, memory_out = r.stress_inner_out, r.memory_inner_out

    def write(x, new, kept):
        for c in range(6):
            stress_out[c, x - 2] = new[c]
            memory_out[c, x - 2] = kept[c]
        if last and x % 2 == 1:
            held, out = pl.ds(x - 3, 2), pl.ds(x - 1, 2)
            copy_out(stress_out.at[:, held], r.stress_out.at[:, out])
            copy_out(memory_out.at[:, held], r.memory_out.at[:, out])

    stress_planes(r, inside(count), edges, planes, write)
    if last:
        for copy in copies:
            copy.wait()
    else:
        strip = jnp.zeros((rows, depths), jnp.float32)
        for x in inside(count):
            strip = edges.packed(strip, x, [r.stress_inner_out[c, x - 2] for c in STRESS_SLOTS])
        r.strip_inner_out[...] = strip


def stress_edge(last, r):
    count, rows, depths = r.material.shape
    edges = Edges(rows, depths, by_loads=True)
    planes = Planes(Field(count, r.velocity), VEL_TAIL, VEL_HEAD, r.one, r.two)
    places = ends_of(count)
    copies = []

    def copy_out(source, out, span):
        copy = pltpu.make_async_copy(source, out.at[:, span], r.sems.at[len(copies)])
        copy.start()
        copies.append(copy)

    if last:
        stress_out, memory_out = r.stress_held, r.memory_held
    else:
        stress_out, memory_out = r.stress_edge_out, r.memory_edge_out

    def write(x, new, kept):
        for c in range(6):
            stress_out[c, places.index(x)] = new[c]
            memory_out[c, places.index(x)] = kept[c]

    stress_planes(r, places, edges, planes, write)
    if last:
        for held, out in ((stress_out, r.stress_out), (memory_out, r.memory_out)):
            copy_out(held.at[:, pl.ds(0, 2)], out, pl.ds(0, 2))
            copy_out(held.at[:, pl.ds(2, 2)], out, pl.ds(count - 2, 2))
        for copy in copies:
            copy.wait()
    else:
        strip = r.strip_inner[...]
        for i, x in enumerate(places):
            strip = edges.packed(strip, x, [stress_out[c, i] for c in STRESS_SLOTS])
        set_strip(r, strip)
        new = Field(count, r.new_stress_inner, stress_out)
        edge_planes(new, STRESS_TAIL, STRESS_HEAD, r.one_out, r.two_out)


SCALARS = ("table", "friction", "anchor")


def call(kernel, name, ins, outs, scratch=None, apart=(), onto=(), micros=1, vmem=6):
    scratch = scratch or {}
    names = [*ins, *(f"{key}_out" for key in outs), *scratch]

    def body(*refs):
        kernel(types.SimpleNamespace(**dict(zip(names, refs))))

    def place(key):
        if key in apart:
            return pl.BlockSpec(memory_space=pltpu.HBM)
        return pl.BlockSpec(memory_space=pltpu.SMEM if key in SCALARS else pltpu.VMEM)

    shapes = [jax.ShapeDtypeStruct(shape, jnp.float32) for shape in outs.values()]
    result = pl.pallas_call(
        body,
        out_shape=shapes,
        in_specs=[place(key) for key in ins],
        out_specs=[place(f"{key}_out") for key in outs],
        scratch_shapes=list(scratch.values()),
        name=name,
        input_output_aliases={
            list(ins).index(key): list(outs).index(onto[key]) for key in onto
        },
        cost_estimate=pl.CostEstimate(
            flops=0, bytes_accessed=micros * 3_690_000, transcendentals=0
        ),
        compiler_params=pltpu.CompilerParams(vmem_limit_bytes=vmem * 2**20),
    )(*ins.values())
    return dict(zip(outs, result))


def along(axis, count, skip=()):
    up = [(i, i + 1) for i in range(count - 1) if i not in skip]
    return (axis, up), (axis, [(b, a) for a, b in up])


def strike_swaps(count):
    halves = lax.axis_size("gz")
    routes = []
    for start in (0, 1):
        partner = {}
        for i in range(start, count - 1, 2):
            for half in range(halves):
                one, other = i * halves + half, (i + 1) * halves + half
                partner[one], partner[other] = other, one
        for i in range(count * halves):
            partner.setdefault(i, i ^ 1)
        routes.append((("gx", "gz"), sorted(partner.items())))
    return routes


def sent(block, route):
    return lax.ppermute(block, *route)


def whole(parts, name):
    if name in parts:
        return parts[name]
    inner, edge = parts[f"{name}_inner"], parts[f"{name}_edge"]
    return jnp.concatenate([edge[:, :2], inner, edge[:, 2:]], axis=1)


def edge_rows(field, rows):
    count = field.shape[2]
    return jnp.stack([field[c, :, place % count, :] for c, place in rows])


def shards(
    velocity,
    stress,
    memory,
    material,
    material_table,
    fault_mask,
    zone_label,
    patch_anchor,
    friction_table,
    prestress,
    normal_stress,
    slip_path,
):
    _, count, rows, depths = velocity.shape
    sides = lax.axis_size("gy")
    middle = sides // 2
    banded = sides > 2
    swaps = strike_swaps(lax.axis_size("gx"))
    up_y, down_y = along("gy", sides, (middle - 1,))
    across = ("gy", [(middle - 1, middle), (middle, middle - 1)])
    deep = ("gz", [(0, 1), (1, 0)])

    plane = (rows, depths)
    edge_shape = (max(len(STRESS_TAIL), len(STRESS_HEAD)), *plane)
    travelling = {"one": edge_shape, "two": edge_shape, "strip": (STRIP_PLANES, *plane)}
    inner, edge = (count - 4, *plane), (4, *plane)
    inner_ends = {"ends": pltpu.VMEM((count - 4, 3, *plane), jnp.float32)}
    edge_ends = {"ends": pltpu.VMEM((4, 3, *plane), jnp.float32)}

    def travelled(packed):
        two = sent(packed["two"], swaps[1])
        one = sent(packed["one"], swaps[0])
        strip = sent(packed["strip"], deep)
        return {"strip": strip}, {"one": one, "two": two}

    def bands(field, tail, head):
        if not banded:
            return {}
        lower, upper = edge_rows(field, tail), edge_rows(field, head)
        return {"lower": sent(lower, up_y), "upper": sent(upper, down_y)}

    if banded:
        still = jnp.stack(
            [
                prestress[:, 0],
                prestress[:, 1],
                normal_stress,
                slip_path,
                zone_label.astype(jnp.float32),
                fault_mask.astype(jnp.float32),
            ]
        )
        still = {"still": lax.all_gather(still, "gy", axis=1, tiled=True)}
    else:
        still = {}

    parts = {"stress": stress, "memory": memory}
    props = {"material": material, "table": material_table}
    packed = call(
        pack_kernel,
        "pack",
        {"stress": stress},
        travelling,
        scratch={"held": pltpu.VMEM(stress.shape, jnp.float32), "sems": pltpu.SemaphoreType.DMA((8,))},
        apart=("stress",),
        vmem=6,
    )
    for step in range(STEPS):
        first, last = step == 0, step == STEPS - 1
        held_stress = {key: parts[key] for key in parts if key.startswith("stress")}
        strip, halos = travelled(packed)
        ins = {"velocity": velocity, **held_stress, **props, **strip}
        if banded:
            ins.update(bands(whole(parts, "stress"), STRESS_TAIL_Y, STRESS_HEAD_Y))
        free = call(
            velocity_inner,
            "velocity_inner",
            ins,
            {"inner": (3, *inner), "strip_inner": plane},
            scratch=inner_ends,
            micros=3,
        )
        face_rows = 2 * count
        ins = {**ins, **halos, **free}
        if first:
            face_rows += count
            if not banded:
                ins.update(prestress=prestress, normal=normal_stress, slip=slip_path)
                ins.update(zone=zone_label, mask=fault_mask)
                face_rows += 6 * normal_stress.shape[0]
        packed = call(
            functools.partial(velocity_edge, first),
            "velocity_edge",
            ins,
            {"edge": (3, *edge), "face": (face_rows, depths), **travelling},
            scratch=edge_ends,
        )
        free = {"inner": free["inner"], "edge": packed["edge"]}
        face = packed["face"]
        other = sent(face, across)
        ins = {key: packed[key] for key in travelling}
        ins.update(face=face, other=other, friction=friction_table, anchor=patch_anchor, **still)
        if first:
            faces = {"face_first": face, "other_first": other}
        else:
            ins.update(slip=slip, **faces)
        outs = {"change": (2, count, depths), "slip": (count, depths), **travelling}
        if last and not banded:
            outs["slip"] = (count // sides, depths)
        if not still:
            outs["still"] = (6, count, depths)
        packed = call(functools.partial(fault_kernel, first), "fault", ins, outs, vmem=2)
        slip = packed["slip"]
        if not still:
            still = {"still": packed["still"]}
        strip, halos = travelled(packed)
        ins = {**free, "change": packed["change"], **parts, **props, **strip}
        if banded:
            joined = jnp.concatenate(
                [free["edge"][:, :2], free["inner"], free["edge"][:, 2:]], axis=1
            )
            band = bands(joined, VEL_TAIL_Y, VEL_HEAD_Y)
        else:
            band = {}
        outs = {"velocity": velocity.shape}
        extra = {"scratch": inner_ends}
        if last:
            outs.update(new_velocity=velocity.shape, stress=stress.shape, memory=memory.shape)
            extra["apart"] = ["new_velocity_out", "stress_out", "memory_out"]
            if not banded:
                ins["slip"] = slip
                outs["new_slip"] = slip.shape
                extra["apart"].append("new_slip_out")
            held = pltpu.VMEM((6, *inner), jnp.float32)
            sems = pltpu.SemaphoreType.DMA((count,))
            extra["scratch"] = {"stress_held": held, "memory_held": held, "sems": sems, **inner_ends}
        else:
            outs.update(stress_inner=(6, *inner), memory_inner=(6, *inner), strip_inner=plane)
        done = call(
            functools.partial(stress_inner, last),
            "stress_inner",
            {**ins, **band},
            outs,
            micros=3,
            vmem=11,
            **extra,
        )
        velocity = done["velocity"]
        ins = {"velocity": velocity, **parts, **props, **strip, **halos, **band}
        if last:
            ins.update(stress_done=done["stress"], memory_done=done["memory"])
            held = pltpu.VMEM((6, *edge), jnp.float32)
            packed = call(
                functools.partial(stress_edge, last),
                "stress_edge",
                ins,
                {"stress": stress.shape, "memory": memory.shape},
                scratch={
                    "stress_held": held,
                    "memory_held": held,
                    "sems": pltpu.SemaphoreType.DMA((4,)),
                    **edge_ends,
                },
                apart=("stress_done", "memory_done", "stress_out", "memory_out"),
                onto={"stress_done": "stress", "memory_done": "memory"},
                vmem=10,
            )
            velocity = done["new_velocity"]
            stress, memory = packed["stress"], packed["memory"]
            slip = done.get("new_slip", slip)
        else:
            ins.update(new_stress_inner=done["stress_inner"], strip_inner=done["strip_inner"])
            packed = call(
                functools.partial(stress_edge, last),
                "stress_edge",
                ins,
                {"stress_edge": (6, *edge), "memory_edge": (6, *edge), **travelling},
                scratch=edge_ends,
                vmem=10,
            )
            parts = {
                "stress_inner": done["stress_inner"],
                "stress_edge": packed["stress_edge"],
                "memory_inner": done["memory_inner"],
                "memory_edge": packed["memory_edge"],
            }
    if banded:
        held = jnp.where(lax.axis_index("gy") == middle, slip, 0.0)
        slip = lax.psum_scatter(held, "gy", scatter_dimension=0, tiled=True)
    return (velocity, stress, memory, slip)


def solution(mesh):
    in_specs = (
        P(None, ("ens", "gx"), "gy", "gz"),
        P(None, ("ens", "gx"), "gy", "gz"),
        P(None, ("ens", "gx"), "gy", "gz"),
        P(("ens", "gx"), "gy", "gz"),
        P(None, "ens"),
        P(("ens", "gx", "gy"), "gz"),
        P(("ens", "gx", "gy"), "gz"),
        P("ens"),
        P(None, "ens"),
        P(("ens", "gx", "gy"), None, "gz"),
        P(("ens", "gx", "gy"), "gz"),
        P(("ens", "gx", "gy"), "gz"),
    )
    out_specs = (
        P(None, ("ens", "gx"), "gy", "gz"),
        P(None, ("ens", "gx"), "gy", "gz"),
        P(None, ("ens", "gx"), "gy", "gz"),
        P(("ens", "gx", "gy"), "gz"),
    )
    return jax.shard_map(shards, mesh=mesh, in_specs=in_specs, out_specs=out_specs, check_vma=False)
```

```python
import functools
import types

import jax
import jax.numpy as jnp
from jax import lax
from jax.experimental import pallas as pl
from jax.experimental.pallas import tpu as pltpu
from jax.sharding import PartitionSpec as P

STEPS = 2
CLASSES = 8
ZONES = 4
PATCH = 8

NEAR = 9.0 / 8.0
FAR = -1.0 / 24.0
DT = 0.15
TILE = 8
ENS, GX, GY, GZ = "ens", "gx", "gy", "gz"

XX, YY, ZZ, XY, XZ, YZ = range(6)

STRESS_TAIL = ((XX, -1), (XY, -2), (XY, -1), (XZ, -2), (XZ, -1))
STRESS_HEAD = ((XX, 0), (XX, 1), (XY, 0), (XZ, 0))
VEL_TAIL = ((0, -2), (0, -1), (1, -1), (2, -1))
VEL_HEAD = ((0, 0), (1, 0), (1, 1), (2, 0), (2, 1))
STRESS_TAIL_Y = ((YY, -1), (XY, -2), (XY, -1), (YZ, -2), (YZ, -1))
STRESS_HEAD_Y = ((YY, 0), (YY, 1), (XY, 0), (YZ, 0))
VEL_TAIL_Y = ((1, -2), (1, -1), (0, -1), (2, -1))
VEL_HEAD_Y = ((1, 0), (0, 0), (0, 1), (2, 0), (2, 1))
STRESS_SLOTS = (XZ, YZ, ZZ)
VEL_SLOTS = (0, 1, 2)


def forward(before, here, after, after_2):
    return NEAR * (after - here) + FAR * (after_2 - before)


def backward(before_2, before, here, after):
    return NEAR * (here - before) + FAR * (after - before_2)


class Edges:
    def __init__(self, rows, depths, by_loads=False):
        self.rows = rows
        self.depths = depths
        lane = lax.broadcasted_iota(jnp.int32, (rows, depths), 1)
        row = lax.broadcasted_iota(jnp.int32, (TILE, depths), 0)
        self.row = lax.broadcasted_iota(jnp.int32, (rows, depths), 0)
        self.tile_row = row
        self.deep = lax.axis_index(GZ)
        near = (self.deep == 0) & (lane < 2) | (self.deep == 1) & (lane >= depths - 2)
        self.near = jnp.where(near, 1.0, 0.0)
        self.zero = jnp.minimum(self.deep, 0)
        self.by_loads = by_loads
        self.pair = lane // 2
        self.low = {n: lane < n for n in (1, 2)}
        self.high = {n: lane >= depths - n for n in (1, 2)}
        self.top = {n: row < n for n in (1, 2)}
        self.bottom = {n: row >= TILE - n for n in (1, 2)}

    def packed(self, strip, x, fields):
        first = jnp.where(self.deep == 0, 2, 0)
        for k, field in enumerate(fields):
            turn = lax.rem(first + 8 * x + 2 * k, self.depths)
            strip = jnp.where(self.pair == 4 * x + k, pltpu.roll(field, turn, 1), strip)
        return strip

    def ends(self, strip, x, k):
        back = self.depths - 8 * x - 2 * k
        turn = jnp.where(self.deep == 0, back % self.depths, back - 2)
        return pltpu.roll(strip, turn, 1) * self.near

    def shallower(self, field, halo, n):
        return pltpu.roll(jnp.where(self.high[n], halo, field), n, 1)

    def deeper(self, field, halo, n):
        return pltpu.roll(jnp.where(self.low[n], halo, field), self.depths - n, 1)

    def forward_z(self, field, halo):
        return forward(
            self.shallower(field, halo, 1),
            field,
            self.deeper(field, halo, 1),
            self.deeper(field, halo, 2),
        )

    def backward_z(self, field, halo):
        return backward(
            self.shallower(field, halo, 2),
            self.shallower(field, halo, 1),
            field,
            self.deeper(field, halo, 1),
        )

    def before(self, field, load, n, halo):
        top = jnp.where(self.top[n], 0.0, pltpu.roll(field[:TILE], n, 0))
        if halo:
            for i in range(n):
                top = jnp.where(self.tile_row == i, halo[n - 1 - i], top)
        if load:
            rest = load(self.zero + (TILE - n), self.rows - TILE)
        else:
            rest = pltpu.roll(field, n, 0)[TILE:]
        return jnp.concatenate([top, rest], axis=0)

    def after(self, field, load, n, halo):
        bottom = pltpu.roll(field[self.rows - TILE :], TILE - n, 0)
        bottom = jnp.where(self.bottom[n], 0.0, bottom)
        if halo:
            for i in range(n):
                bottom = jnp.where(self.tile_row == TILE - n + i, halo[i], bottom)
        if load:
            rest = load(self.zero + n, self.rows - TILE)
        else:
            rest = pltpu.roll(field, self.rows - n, 0)[: self.rows - TILE]
        return jnp.concatenate([rest, bottom], axis=0)

    def forward_y(self, planes, comp, x, halos):
        field = planes(comp, x)
        load = planes.rows(comp, x) if self.by_loads else None
        lower, upper = halos
        return forward(
            self.before(field, load, 1, lower),
            field,
            self.after(field, load, 1, upper),
            self.after(field, load, 2, upper),
        )

    def backward_y(self, planes, comp, x, halos):
        field = planes(comp, x)
        load = planes.rows(comp, x) if self.by_loads else None
        lower, upper = halos
        return backward(
            self.before(field, load, 2, lower),
            self.before(field, load, 1, lower),
            field,
            self.after(field, load, 1, upper),
        )


class Field:
    def __init__(self, count, *parts):
        self.count = count
        self.parts = parts

    def place(self, x):
        if len(self.parts) == 1:
            return self.parts[0], x
        inner, edge = self.parts
        if x in inside(self.count):
            return inner, x - 2
        return edge, ends_of(self.count).index(x)

    def __call__(self, comp, x):
        ref, at = self.place(x)
        return ref[comp, at]

    def rows(self, comp, x):
        ref, at = self.place(x)
        return lambda start, size: ref[comp, at, pl.ds(start, size), :]


def inside(count):
    return range(2, count - 2)


def ends_of(count):
    return (0, 1, count - 2, count - 1)


class Planes:
    def __init__(self, field, tail, head, first=None, second=None, change=None, on_fault=None):
        self.change, self.on_fault = change, on_fault
        self.field = field
        self.count = field.count
        self.first, self.second = first, second
        self.tail, self.head = tail, head
        self.even = even_strike()
        self.any_left = lax.axis_index(GX) > 0
        self.any_right = lax.axis_index(GX) < lax.axis_size(GX) - 1

    def left(self, i):
        return jnp.where(self.even, self.second[i], self.first[i])

    def right(self, i):
        return jnp.where(self.even, self.first[i], self.second[i])

    def changed(self, plane, comp, node):
        if self.change is None or comp == 1:
            return plane
        line = self.change[comp // 2, pl.ds(node, 1), :]
        return plane + jnp.where(self.on_fault, line, 0.0)

    def __call__(self, comp, place):
        if place < 0:
            plane = self.left(self.tail.index((comp, place)))
            return jnp.where(self.any_left, self.changed(plane, comp, place + 2), 0.0)
        if place >= self.count:
            beyond = place - self.count
            plane = self.right(self.head.index((comp, beyond)))
            return jnp.where(self.any_right, self.changed(plane, comp, beyond + 2), 0.0)
        return self.field(comp, place)

    def rows(self, comp, x):
        return self.field.rows(comp, x)

    def forward_x(self, comp, x):
        return forward(self(comp, x - 1), self(comp, x), self(comp, x + 1), self(comp, x + 2))

    def backward_x(self, comp, x):
        return backward(self(comp, x - 2), self(comp, x - 1), self(comp, x), self(comp, x + 1))


class Bands:
    def __init__(self, lower, upper, tail, head):
        self.lower, self.upper = lower, upper
        self.tail, self.head = tail, head

    def __call__(self, comp, x):
        if self.lower is None:
            return (None, None)
        places = [i for i, (c, _) in enumerate(self.tail) if c == comp]
        before = [self.lower[i, pl.ds(x, 1), :] for i in reversed(places)]
        places = [i for i, (c, _) in enumerate(self.head) if c == comp]
        after = [self.upper[i, pl.ds(x, 1), :] for i in places]
        return (before, after)


def looked_up(labels, table, row, count):
    out = jnp.full(labels.shape, table[row, 0], jnp.float32)
    for k in range(1, count):
        out = jnp.where(labels == k, table[row, k], out)
    return out


def even_strike():
    return lax.axis_index(GX) % 2 == 0


def edge_planes(field, tail, head, first_out, second_out):
    even = even_strike()
    pairs = []
    for i in range(max(len(tail), len(head))):
        comp, place = tail[min(i, len(tail) - 1)]
        right = field(comp, place % field.count)
        comp, place = head[min(i, len(head) - 1)]
        left = field(comp, place % field.count)
        pairs.append((jnp.where(even, right, left), jnp.where(even, left, right)))
    for i, (one, two) in enumerate(pairs):
        first_out[i] = one
        second_out[i] = two


def fault_row(rows):
    return jnp.where(lax.axis_index(GY) == lax.axis_size(GY) // 2, 0, rows - 1)


def pack_kernel(r):
    count, rows, depths = r.stress.shape[1:]
    whole = [(comp, 0, count) for comp in STRESS_SLOTS]
    some = {}
    for comp, place in STRESS_TAIL + STRESS_HEAD:
        if comp not in STRESS_SLOTS:
            some.setdefault((comp, place < 0), []).append(place % count)
    some = [(comp, min(at), max(at) + 1) for (comp, _), at in some.items()]
    copies = []
    for i, (comp, start, stop) in enumerate(some + whole):
        span = pl.ds(start, stop - start)
        copy = pltpu.make_async_copy(r.stress.at[comp, span], r.held.at[comp, span], r.sems.at[i])
        copy.start()
        copies.append(copy)
    edges = Edges(rows, depths)
    for copy in copies:
        copy.wait()
    edge_planes(Field(count, r.held), STRESS_TAIL, STRESS_HEAD, r.one_out, r.two_out)
    strip = jnp.zeros((rows, depths), jnp.float32)
    for x in range(count):
        strip = edges.packed(strip, x, [r.held[c, x] for c in STRESS_SLOTS])
    set_strip(r, strip)


def grouped(xs, size):
    return [xs[i : i + size] for i in range(0, len(xs), size)]


def set_strip(r, strip, face=None):
    rows = strip.shape[0]
    filled = 1
    r.strip_out[0] = strip
    if face is not None:
        filled += face.shape[0] // rows
        faces = [face[pl.ds(i * rows, rows), :] for i in range(filled - 1)]
        for i, part in enumerate(faces):
            r.strip_out[1 + i] = part
    for i in range(filled, r.strip_out.shape[0]):
        r.strip_out[i] = jnp.zeros_like(strip)


def unpack(r, xs, edges):
    strip = r.strip[0]
    for i, x in enumerate(xs):
        for k in range(3):
            r.ends[i, k] = edges.ends(strip, x, k)


def velocity_planes(r, xs, edges, planes, write):
    band = Bands(getattr(r, "lower", None), getattr(r, "upper", None), STRESS_TAIL_Y, STRESS_HEAD_Y)
    unpack(r, xs, edges)

    def new(x):
        push = DT * looked_up(r.material[x], r.table, 2, CLASSES)
        ends = [r.ends[xs.index(x), k] for k in range(3)]
        along_x = (
            planes.forward_x(XX, x)
            + edges.backward_y(planes, XY, x, band(XY, x))
            + edges.backward_z(planes(XZ, x), ends[0])
        )
        along_y = (
            planes.backward_x(XY, x)
            + edges.forward_y(planes, YY, x, band(YY, x))
            + edges.backward_z(planes(YZ, x), ends[1])
        )
        along_z = (
            planes.backward_x(XZ, x)
            + edges.backward_y(planes, YZ, x, band(YZ, x))
            + edges.forward_z(planes(ZZ, x), ends[2])
        )
        rates = (along_x, along_y, along_z)
        return [r.velocity[c, x] + push * rate for c, rate in enumerate(rates)]

    for group in grouped(xs, 3 if len(xs) % 3 == 0 else 2):
        for x, values in [(x, new(x)) for x in group]:
            write(x, values)


def velocity_inner(r):
    count, rows, depths = r.material.shape
    edges = Edges(rows, depths)
    planes = Planes(stress_of(r), STRESS_TAIL, STRESS_HEAD)

    def write(x, new):
        for c in range(3):
            r.inner_out[c, x - 2] = new[c]

    velocity_planes(r, inside(count), edges, planes, write)
    strip = jnp.zeros((rows, depths), jnp.float32)
    for x in inside(count):
        strip = edges.packed(strip, x, [r.inner_out[c, x - 2] for c in VEL_SLOTS])
    r.strip_inner_out[...] = strip


def velocity_edge(r):
    count, rows, depths = r.material.shape
    edges = Edges(rows, depths)
    planes = Planes(stress_of(r), STRESS_TAIL, STRESS_HEAD, r.one, r.two)
    fault = fault_row(rows)
    places = ends_of(count)
    row = pl.ds(fault, 1)
    labels = [r.material[x, row, :] for x in range(count)]
    push = [looked_up(label, r.table, 2, CLASSES) for label in labels]
    lines = dict(enumerate(push, 2 * count))
    halves = hasattr(r, "prestress")
    if halves:
        own = r.normal.shape[0]
        still = [[r.prestress[i, pl.ds(c, 1), :] for i in range(own)] for c in (0, 1)]
        for field in (r.normal, r.slip, r.zone, r.mask):
            still.append([field[pl.ds(i, 1), :].astype(jnp.float32) for i in range(own)])
        lines.update(enumerate(sum(still, []), 3 * count))
    else:
        still = [[r.still[i, pl.ds(x, 1), :] for x in range(count)] for i in range(6)]
        still[3] = [r.slip[pl.ds(x, 1), :] for x in range(count)]

    def write(x, new):
        for c in range(3):
            r.edge_out[c, places.index(x)] = new[c]

    velocity_planes(r, places, edges, planes, write)
    strip = r.strip_inner[...]
    for i, x in enumerate(places):
        strip = edges.packed(strip, x, [r.edge_out[c, i] for c in VEL_SLOTS])
    new = Field(count, r.inner, r.edge_out)
    faces = [[new.rows(c, x)(fault, 1) for x in range(count)] for c in (0, 2)]
    lines.update(enumerate(sum(faces, [])))
    for i in range(len(lines), r.face_out.shape[0]):
        lines[i] = jnp.zeros((1, depths), jnp.float32)
    for i, line in lines.items():
        r.face_out[pl.ds(i, 1), :] = line
    set_strip(r, strip, r.face_out)
    edge_planes(new, VEL_TAIL, VEL_HEAD, r.one_out, r.two_out)

    even = even_strike()
    fields = [*faces, push, *still]
    for i, field in enumerate(fields):
        for j in (0, 1):
            tail, head = field[len(field) - 2 + j], field[j]
            at = pl.ds(2 * i + j, 1)
            one, two = jnp.where(even, tail, head), jnp.where(even, head, tail)
            for line, plane, alone in (
                (one, r.one_out, r.line_one_out),
                (two, r.two_out, r.line_two_out),
            ):
                plane[plane.shape[0] - 1, at, :] = line
                alone[at, :] = line


def stress_of(r):
    count = r.material.shape[0]
    if hasattr(r, "stress"):
        return Field(count, r.stress)
    return Field(count, r.stress_inner, r.stress_edge)


def memory_of(r):
    count = r.material.shape[0]
    if hasattr(r, "memory"):
        return Field(count, r.memory)
    return Field(count, r.memory_inner, r.memory_edge)


def slipped(r, own, other, still, slip, row, deep):
    middle = lax.axis_size(GY) // 2
    side = lax.axis_index(GY)
    plus = side == middle
    minus = side == middle - 1
    minus_x, minus_z, minus_b = [jnp.where(plus, b, a) for a, b in zip(own, other)]
    plus_x, plus_z, plus_b = [jnp.where(plus, a, b) for a, b in zip(own, other)]
    pre_x, pre_z, normal, _, zone, mask = still
    inside = (row >= r.anchor[0]) & (row < r.anchor[0] + 2 * PATCH)
    inside = inside & (deep >= r.anchor[1]) & (deep < r.anchor[1] + 2 * PATCH)
    dynamic = 0.4 * looked_up(zone, r.friction, 0, ZONES)
    static = jnp.where(
        inside, dynamic, dynamic + 0.5 * looked_up(zone, r.friction, 1, ZONES)
    )
    distance = 0.2 * looked_up(zone, r.friction, 2, ZONES)
    bsum = minus_b + plus_b
    trial_x = (plus_x - minus_x) / (DT * bsum) + pre_x
    trial_z = (plus_z - minus_z) / (DT * bsum) + pre_z
    size = jnp.sqrt(trial_x * trial_x + trial_z * trial_z)
    weaken = jnp.minimum(slip / distance, 1.0)
    strength = (static - (static - dynamic) * weaken) * normal
    factor = jnp.where(mask == 1.0, strength / jnp.maximum(size, strength), 1.0)
    new_slip = slip + DT * DT * bsum * (size - size * factor)
    sign = jnp.where(minus, DT, 0.0) * minus_b - jnp.where(plus, DT, 0.0) * plus_b
    return (trial_x * factor - pre_x) * sign, (trial_z * factor - pre_z) * sign, new_slip


def fault_kernel(count, r):
    rows, depths = r.strip.shape[1:]
    plus = lax.axis_index(GY) == lax.axis_size(GY) // 2

    def beside(place, size):
        return r.strip[1 + place // rows, pl.ds(place % rows, size), :]

    def nodes(source, source_beside, place, size):
        return source[pl.ds(place, size), :], source_beside(place, size)

    def cross(place, size):
        return r.cross[pl.ds(place, size), :]

    own = [jnp.concatenate(nodes(r.face, beside, i * count, count)) for i in range(3)]
    other = [jnp.concatenate(nodes(r.other, cross, i * count, count)) for i in range(3)]
    if hasattr(r, "still"):
        still = [r.still[i] for i in range(6)]
    else:
        share = count // 2
        still = []
        for i in range(6):
            place = 3 * count + i * share
            mine = nodes(r.face, beside, place, share)
            theirs = nodes(r.other, cross, place, share)
            halves = []
            for a, b in zip(mine, theirs):
                halves += [jnp.where(plus, b, a), jnp.where(plus, a, b)]
            still.append(jnp.concatenate(halves))
        for i in range(6):
            r.still_out[i] = still[i]
    slip = r.slip[...] if hasattr(r, "slip") else still[3]
    deep = lax.axis_index(GZ)
    row = lax.broadcasted_iota(jnp.int32, (2 * count, depths), 0)
    lane = lax.broadcasted_iota(jnp.int32, (2 * count, depths), 1)
    lane = lane + jnp.where(row < count, deep, 1 - deep) * depths
    row = row % count
    place = row + lax.axis_index(GX) * count
    change_x, change_z, new_slip = slipped(r, own, other, still, slip, place, lane)
    r.slip_out[...] = new_slip
    if hasattr(r, "new_slip_out"):
        half = r.new_slip_out.shape[0]
        r.new_slip_out[...] = jnp.where(plus, new_slip[half : 2 * half], new_slip[:half])
    r.change_out[0] = change_x
    r.change_out[1] = change_z

    on_fault = lax.broadcasted_iota(jnp.int32, (rows, depths), 0) == fault_row(rows)
    ends = jnp.zeros((count, depths), jnp.float32)
    pair = lax.broadcasted_iota(jnp.int32, (count, depths), 1) // 2
    first = 4 * lax.broadcasted_iota(jnp.int32, (count, depths), 0)
    for k, field in ((0, change_x[count:]), (2, change_z[count:])):
        turned = jnp.where(deep == 0, field, pltpu.roll(field, 2, 1))
        turned = pltpu.roll(turned, 2 * k, 1, stride=8, stride_axis=0)
        ends = jnp.where(pair == first + k, turned, ends)
    line = jnp.sum(ends, axis=0, keepdims=True)
    r.strip_out[0] = r.strip[0] + jnp.where(on_fault, line, 0.0)


def end_changes(count, r):
    depths = r.line_one.shape[1]
    middle = lax.axis_size(GY) // 2
    side = lax.axis_index(GY)
    even = even_strike()
    last = r.one.shape[0] - 1
    pieces = []
    for i in range(9):
        at = pl.ds(2 * i, 2)
        one, two = r.one[last, at, :], r.two[last, at, :]
        far_one, far_two = r.line_one[at, :], r.line_two[at, :]
        left, right = jnp.where(even, two, one), jnp.where(even, one, two)
        far_left, far_right = jnp.where(even, far_two, far_one), jnp.where(even, far_one, far_two)
        if i < 3:
            pieces += [(i, left, right), (3 + i, far_left, far_right)]
        else:
            left = jnp.where(side == middle, left, far_left)
            right = jnp.where(side == middle, far_right, right)
            pieces.append((3 + i, left, right))
    for i, left, right in pieces:
        r.nodes[i, pl.ds(0, 2), :] = left
        r.nodes[i, pl.ds(2, 2), :] = right
    held = [r.nodes[i, pl.ds(0, 4), :] for i in range(12)]
    row = lax.broadcasted_iota(jnp.int32, (4, depths), 0)
    lane = lax.broadcasted_iota(jnp.int32, (4, depths), 1) + lax.axis_index(GZ) * depths
    place = jnp.where(row < 2, row - 2, count + row - 2) + lax.axis_index(GX) * count
    change = slipped(r, held[:3], held[3:6], held[6:], held[9], place, lane)
    for i in range(2):
        r.nodes[i, pl.ds(0, 4), :] = change[i]


def stress_planes(r, xs, edges, planes, write):
    band = Bands(getattr(r, "lower", None), getattr(r, "upper", None), VEL_TAIL_Y, VEL_HEAD_Y)
    stress, memory = stress_of(r), memory_of(r)
    unpack(r, xs, edges)

    def rates(x):
        in_x, in_y, in_z = [r.ends[xs.index(x), k] for k in range(3)]
        exx = planes.backward_x(0, x)
        eyy = edges.backward_y(planes, 1, x, band(1, x))
        ezz = edges.backward_z(planes(2, x), in_z)
        exy = edges.forward_y(planes, 0, x, band(0, x)) + planes.forward_x(1, x)
        exz = edges.forward_z(planes(0, x), in_x) + planes.forward_x(2, x)
        eyz = edges.forward_z(planes(1, x), in_y) + edges.forward_y(planes, 2, x, band(2, x))
        labels = r.material[x]
        bulk = looked_up(labels, r.table, 0, CLASSES) * (exx + eyy + ezz)
        shear = looked_up(labels, r.table, 1, CLASSES)
        double = 2.0 * shear
        return (
            bulk + double * exx,
            bulk + double * eyy,
            bulk + double * ezz,
            shear * exy,
            shear * exz,
            shear * eyz,
        )

    def new(x, elastic):
        labels = r.material[x]
        decay = jnp.exp(-DT / looked_up(labels, r.table, 3, CLASSES))
        gain = (1.0 - decay) * (0.3 * looked_up(labels, r.table, 4, CLASSES))
        kept = [decay * memory(c, x) - gain * elastic[c] for c in range(6)]
        return [stress(c, x) + DT * (elastic[c] + kept[c]) for c in range(6)], kept

    for group in grouped(xs, 2):
        for x, elastic in [(x, rates(x)) for x in group]:
            write(x, *new(x, elastic))


def stress_inner(last, r):
    count, rows, depths = r.material.shape
    edges = Edges(rows, depths, by_loads=True)
    on_fault = edges.row == fault_row(rows)
    free = Field(count, r.inner, r.edge)
    for x in range(count):
        for c in (0, 2):
            line = r.change[c // 2, pl.ds(x, 1), :]
            r.velocity_out[c, x] = free(c, x) + jnp.where(on_fault, line, 0.0)
        r.velocity_out[1, x] = free(1, x)
    planes = Planes(Field(count, r.velocity_out), VEL_TAIL, VEL_HEAD)
    copies = []

    def copy_out(source, out):
        copy = pltpu.make_async_copy(source, out, r.sems.at[len(copies)])
        copy.start()
        copies.append(copy)

    if last:
        copy_out(r.velocity_out, r.new_velocity_out)
        if hasattr(r, "slip"):
            copy_out(r.slip, r.new_slip_out)
        stress_out, memory_out = r.stress_held, r.memory_held
    else:
        stress_out, memory_out = r.stress_inner_out, r.memory_inner_out

    def write(x, new, kept):
        for c in range(6):
            stress_out[c, x - 2] = new[c]
            memory_out[c, x - 2] = kept[c]
        if last and x % 2 == 1:
            held, out = pl.ds(x - 3, 2), pl.ds(x - 1, 2)
            copy_out(stress_out.at[:, held], r.stress_out.at[:, out])
            copy_out(memory_out.at[:, held], r.memory_out.at[:, out])

    stress_planes(r, inside(count), edges, planes, write)
    if last:
        for copy in copies:
            copy.wait()
    else:
        strip = jnp.zeros((rows, depths), jnp.float32)
        for x in inside(count):
            strip = edges.packed(strip, x, [r.stress_inner_out[c, x - 2] for c in STRESS_SLOTS])
        r.strip_inner_out[...] = strip


def stress_edge(last, r):
    count, rows, depths = r.material.shape
    edges = Edges(rows, depths, by_loads=True)
    end_changes(count, r)
    on_fault = edges.row == fault_row(rows)
    field = Field(count, r.velocity)
    planes = Planes(field, VEL_TAIL, VEL_HEAD, r.one, r.two, r.nodes, on_fault)
    places = ends_of(count)
    copies = []

    def copy_out(source, out, span):
        copy = pltpu.make_async_copy(source, out.at[:, span], r.sems.at[len(copies)])
        copy.start()
        copies.append(copy)

    if last:
        stress_out, memory_out = r.stress_held, r.memory_held
    else:
        stress_out, memory_out = r.stress_edge_out, r.memory_edge_out

    def write(x, new, kept):
        for c in range(6):
            stress_out[c, places.index(x)] = new[c]
            memory_out[c, places.index(x)] = kept[c]

    stress_planes(r, places, edges, planes, write)
    if last:
        for held, out in ((stress_out, r.stress_out), (memory_out, r.memory_out)):
            copy_out(held.at[:, pl.ds(0, 2)], out, pl.ds(0, 2))
            copy_out(held.at[:, pl.ds(2, 2)], out, pl.ds(count - 2, 2))
        for copy in copies:
            copy.wait()
    else:
        strip = r.strip_inner[...]
        for i, x in enumerate(places):
            strip = edges.packed(strip, x, [stress_out[c, i] for c in STRESS_SLOTS])
        set_strip(r, strip)
        new = Field(count, r.new_stress_inner, stress_out)
        edge_planes(new, STRESS_TAIL, STRESS_HEAD, r.one_out, r.two_out)


SCALARS = ("table", "friction", "anchor")


def call(kernel, name, ins, outs, scratch=None, apart=(), onto=(), micros=1, vmem=6):
    scratch = scratch or {}
    names = [*ins, *(f"{key}_out" for key in outs), *scratch]

    def body(*refs):
        kernel(types.SimpleNamespace(**dict(zip(names, refs))))

    def place(key):
        if key in apart:
            return pl.BlockSpec(memory_space=pltpu.HBM)
        return pl.BlockSpec(memory_space=pltpu.SMEM if key in SCALARS else pltpu.VMEM)

    shapes = [jax.ShapeDtypeStruct(shape, jnp.float32) for shape in outs.values()]
    result = pl.pallas_call(
        body,
        out_shape=shapes,
        in_specs=[place(key) for key in ins],
        out_specs=[place(f"{key}_out") for key in outs],
        scratch_shapes=list(scratch.values()),
        name=name,
        input_output_aliases={
            list(ins).index(key): list(outs).index(onto[key]) for key in onto
        },
        cost_estimate=pl.CostEstimate(
            flops=0, bytes_accessed=micros * 3_690_000, transcendentals=0
        ),
        compiler_params=pltpu.CompilerParams(vmem_limit_bytes=vmem * 2**20),
    )(*ins.values())
    return dict(zip(outs, result))


def along(axis, count, skip=()):
    up = [(i, i + 1) for i in range(count - 1) if i not in skip]
    return (axis, up), (axis, [(b, a) for a, b in up])


def strike_swaps(count):
    halves = lax.axis_size(GZ)
    routes = []
    for start in (0, 1):
        partner = {}
        for i in range(start, count - 1, 2):
            for half in range(halves):
                one, other = i * halves + half, (i + 1) * halves + half
                partner[one], partner[other] = other, one
        for i in range(count * halves):
            partner.setdefault(i, i ^ 1)
        routes.append(((GX, GZ), sorted(partner.items())))
    return routes


def fault_swaps(pair, sides):
    across, cross = [], []
    for side in range(sides):
        for half in (0, 1):
            place, over = 2 * side + half, 2 * (sum(pair) - side) + half
            if side not in pair:
                over = place ^ 1
            across.append((place, over))
            cross.append((place, over ^ 1 if side in pair else over))
    return ((GY, GZ), across), ((GY, GZ), cross)


def far_swap(route, pair, sides):
    pairs = []
    for place, partner in route[1]:
        for side in range(sides):
            here = ((place // 2) * sides + side) * 2 + place % 2
            if place // 2 == partner // 2 or side not in pair:
                there = here ^ 1
            else:
                there = ((partner // 2) * sides + sum(pair) - side) * 2 + partner % 2
            pairs.append((here, there))
    return (GX, GY, GZ), sorted(pairs)


def sent(block, route):
    return lax.ppermute(block, *route)


def whole(parts, name):
    if name in parts:
        return parts[name]
    inner, edge = parts[f"{name}_inner"], parts[f"{name}_edge"]
    return jnp.concatenate([edge[:, :2], inner, edge[:, 2:]], axis=1)


def edge_rows(field, rows):
    count = field.shape[2]
    return jnp.stack([field[c, :, place % count, :] for c, place in rows])


def shards(
    velocity,
    stress,
    memory,
    material,
    material_table,
    fault_mask,
    zone_label,
    patch_anchor,
    friction_table,
    prestress,
    normal_stress,
    slip_path,
):
    _, count, rows, depths = velocity.shape
    sides = lax.axis_size(GY)
    middle = sides // 2
    banded = sides > 2
    swaps = strike_swaps(lax.axis_size(GX))
    up_y, down_y = along(GY, sides, (middle - 1,))
    deep = (GZ, [(0, 1), (1, 0)])
    pair = (middle - 1, middle)
    across, cross = fault_swaps(pair, sides)
    far = [far_swap(route, pair, sides) for route in swaps]

    plane = (rows, depths)
    edge_planes = max(len(STRESS_TAIL), len(STRESS_HEAD))

    def travelling(planes):
        return {"one": (planes, *plane), "two": (planes, *plane), "strip": (planes + 1, *plane)}

    inner, edge = (count - 4, *plane), (4, *plane)
    inner_ends = {"ends": pltpu.VMEM((count - 4, 3, *plane), jnp.float32)}
    nodes = pltpu.VMEM((12, TILE, depths), jnp.float32)
    edge_ends = {"ends": pltpu.VMEM((4, 3, *plane), jnp.float32)}

    def travelled(packed):
        two = sent(packed["two"], swaps[1])
        one = sent(packed["one"], swaps[0])
        strip = sent(packed["strip"], deep)
        return {"strip": strip}, {"one": one, "two": two}

    def bands(field, tail, head):
        if not banded:
            return {}
        lower, upper = edge_rows(field, tail), edge_rows(field, head)
        return {"lower": sent(lower, up_y), "upper": sent(upper, down_y)}

    if banded:
        still = jnp.stack(
            [
                prestress[:, 0],
                prestress[:, 1],
                normal_stress,
                slip_path,
                zone_label.astype(jnp.float32),
                fault_mask.astype(jnp.float32),
            ]
        )
        still = lax.all_gather(still, GY, axis=1, tiled=True)
        still = jnp.concatenate([still, sent(still, deep)], axis=1)
        still, slip = {"still": still}, still[3]
    else:
        still = {}

    parts = {"stress": stress, "memory": memory}
    props = {"material": material, "table": material_table}
    packed = call(
        pack_kernel,
        "pack",
        {"stress": stress},
        travelling(edge_planes),
        scratch={"held": pltpu.VMEM(stress.shape, jnp.float32), "sems": pltpu.SemaphoreType.DMA((8,))},
        apart=("stress",),
        vmem=6,
    )
    for step in range(STEPS):
        first, last = step == 0, step == STEPS - 1
        held_stress = {key: parts[key] for key in parts if key.startswith("stress")}
        strip, halos = travelled(packed)
        ins = {"velocity": velocity, **held_stress, **props, **strip}
        if banded:
            ins.update(bands(whole(parts, "stress"), STRESS_TAIL_Y, STRESS_HEAD_Y))
        free = call(
            velocity_inner,
            "velocity_inner",
            ins,
            {"inner": (3, *inner), "strip_inner": plane},
            scratch=inner_ends,
            micros=3,
        )
        face_rows = 3 * count
        ins = {**ins, **halos, **free}
        if still:
            ins.update(slip=slip, **still)
        else:
            ins.update(prestress=prestress, normal=normal_stress, slip=slip_path)
            ins.update(zone=zone_label, mask=fault_mask)
            face_rows += 6 * normal_stress.shape[0]
        face_rows = -(-face_rows // rows) * rows
        outs = {"edge": (3, *edge), "face": (face_rows, depths), "line_one": plane, "line_two": plane}
        packed = call(
            velocity_edge,
            "velocity_edge",
            ins,
            {**outs, **travelling(edge_planes + 1)},
            scratch=edge_ends,
        )
        free = {"inner": free["inner"], "edge": packed["edge"]}
        strip, halos = travelled(packed)
        face = packed["face"]
        rules = {"friction": friction_table, "anchor": patch_anchor}
        ins = {"face": face, "other": sent(face, across), "cross": sent(face, cross), **strip}
        ins.update(rules)
        halos["line_one"] = sent(packed["line_one"], far[0])
        halos["line_two"] = sent(packed["line_two"], far[1])
        halos.update(rules)
        if still:
            ins.update(slip=slip, **still)
        outs = {"change": (2, 2 * count, depths), "slip": (2 * count, depths), "strip": (1, *plane)}
        if last and not banded:
            outs["new_slip"] = (count // sides, depths)
        if not still:
            outs["still"] = (6, 2 * count, depths)
        packed = call(functools.partial(fault_kernel, count), "fault", ins, outs, vmem=3)
        slip = packed["slip"]
        if not still:
            still = {"still": packed["still"]}
        strip = {"strip": packed["strip"]}
        ins = {**free, "change": packed["change"], **parts, **props, **strip}
        if banded:
            joined = jnp.concatenate(
                [free["edge"][:, :2], free["inner"], free["edge"][:, 2:]], axis=1
            )
            band = bands(joined, VEL_TAIL_Y, VEL_HEAD_Y)
        else:
            band = {}
        outs = {"velocity": velocity.shape}
        extra = {"scratch": inner_ends}
        if last:
            outs.update(new_velocity=velocity.shape, stress=stress.shape, memory=memory.shape)
            extra["apart"] = ["new_velocity_out", "stress_out", "memory_out"]
            if not banded:
                ins["slip"] = packed["new_slip"]
                outs["new_slip"] = packed["new_slip"].shape
                extra["apart"].append("new_slip_out")
            held = pltpu.VMEM((6, *inner), jnp.float32)
            sems = pltpu.SemaphoreType.DMA((count,))
            extra["scratch"] = {"stress_held": held, "memory_held": held, "sems": sems, **inner_ends}
        else:
            outs.update(stress_inner=(6, *inner), memory_inner=(6, *inner), strip_inner=plane)
        done = call(
            functools.partial(stress_inner, last),
            "stress_inner",
            {**ins, **band},
            outs,
            micros=3,
            vmem=11,
            **extra,
        )
        velocity = done["velocity"]
        ins = {"velocity": velocity, **parts, **props, **strip, **halos, **band}
        if last:
            ins.update(stress_done=done["stress"], memory_done=done["memory"])
            held = pltpu.VMEM((6, *edge), jnp.float32)
            packed = call(
                functools.partial(stress_edge, last),
                "stress_edge",
                ins,
                {"stress": stress.shape, "memory": memory.shape},
                scratch={
                    "stress_held": held,
                    "memory_held": held,
                    "sems": pltpu.SemaphoreType.DMA((4,)),
                    "nodes": nodes,
                    **edge_ends,
                },
                apart=("stress_done", "memory_done", "stress_out", "memory_out"),
                onto={"stress_done": "stress", "memory_done": "memory"},
                vmem=10,
            )
            velocity = done["new_velocity"]
            stress, memory = packed["stress"], packed["memory"]
            slip = done.get("new_slip", slip)
        else:
            ins.update(new_stress_inner=done["stress_inner"], strip_inner=done["strip_inner"])
            packed = call(
                functools.partial(stress_edge, last),
                "stress_edge",
                ins,
                {
                    "stress_edge": (6, *edge),
                    "memory_edge": (6, *edge),
                    **travelling(edge_planes),
                },
                scratch={"nodes": nodes, **edge_ends},
                vmem=10,
            )
            parts = {
                "stress_inner": done["stress_inner"],
                "stress_edge": packed["stress_edge"],
                "memory_inner": done["memory_inner"],
                "memory_edge": packed["memory_edge"],
            }
    if banded:
        held = jnp.where(lax.axis_index(GY) == middle, slip[:count], 0.0)
        slip = lax.psum_scatter(held, GY, scatter_dimension=0, tiled=True)
    return (velocity, stress, memory, slip)


def solution(mesh):
    in_specs = (
        P(None, (ENS, GX), GY, GZ),
        P(None, (ENS, GX), GY, GZ),
        P(None, (ENS, GX), GY, GZ),
        P((ENS, GX), GY, GZ),
        P(None, ENS),
        P((ENS, GX, GY), GZ),
        P((ENS, GX, GY), GZ),
        P(ENS),
        P(None, ENS),
        P((ENS, GX, GY), None, GZ),
        P((ENS, GX, GY), GZ),
        P((ENS, GX, GY), GZ),
    )
    out_specs = (
        P(None, (ENS, GX), GY, GZ),
        P(None, (ENS, GX), GY, GZ),
        P(None, (ENS, GX), GY, GZ),
        P((ENS, GX, GY), GZ),
    )
    return jax.shard_map(shards, mesh=mesh, in_specs=in_specs, out_specs=out_specs, check_vma=False)
```

```python
import functools
import types

import jax
import jax.numpy as jnp
from jax import lax
from jax.experimental import pallas as pl
from jax.experimental.pallas import tpu as pltpu
from jax.sharding import PartitionSpec as P

STEPS = 2
CLASSES = 8
ZONES = 4
PATCH = 8

NEAR = 9.0 / 8.0
FAR = -1.0 / 24.0
DT = 0.15
TILE = 8
ENS, GX, GY, GZ = "ens", "gx", "gy", "gz"

XX, YY, ZZ, XY, XZ, YZ = range(6)

STRESS_TAIL = ((XX, -1), (XY, -2), (XY, -1), (XZ, -2), (XZ, -1))
STRESS_HEAD = ((XX, 0), (XX, 1), (XY, 0), (XZ, 0))
VEL_TAIL = ((0, -2), (0, -1), (1, -1), (2, -1))
VEL_HEAD = ((0, 0), (1, 0), (1, 1), (2, 0), (2, 1))
STRESS_TAIL_Y = ((YY, -1), (XY, -2), (XY, -1), (YZ, -2), (YZ, -1))
STRESS_HEAD_Y = ((YY, 0), (YY, 1), (XY, 0), (YZ, 0))
VEL_TAIL_Y = ((1, -2), (1, -1), (0, -1), (2, -1))
VEL_HEAD_Y = ((1, 0), (0, 0), (0, 1), (2, 0), (2, 1))
STRESS_SLOTS = (XZ, YZ, ZZ)
VEL_SLOTS = (0, 1, 2)


def forward(before, here, after, after_2):
    return NEAR * (after - here) + FAR * (after_2 - before)


def backward(before_2, before, here, after):
    return NEAR * (here - before) + FAR * (after - before_2)


class Edges:
    def __init__(self, rows, depths, by_loads=False):
        self.rows = rows
        self.depths = depths
        lane = lax.broadcasted_iota(jnp.int32, (rows, depths), 1)
        row = lax.broadcasted_iota(jnp.int32, (TILE, depths), 0)
        self.row = lax.broadcasted_iota(jnp.int32, (rows, depths), 0)
        self.tile_row = row
        self.deep = lax.axis_index(GZ)
        near = (self.deep == 0) & (lane < 2) | (self.deep == 1) & (lane >= depths - 2)
        self.near = jnp.where(near, 1.0, 0.0)
        self.zero = jnp.minimum(self.deep, 0)
        self.by_loads = by_loads
        self.pair = lane // 2
        self.low = {n: lane < n for n in (1, 2)}
        self.high = {n: lane >= depths - n for n in (1, 2)}
        self.top = {n: row < n for n in (1, 2)}
        self.bottom = {n: row >= TILE - n for n in (1, 2)}

    def packed(self, strip, x, fields):
        first = jnp.where(self.deep == 0, 2, 0)
        for k, field in enumerate(fields):
            turn = lax.rem(first + 8 * x + 2 * k, self.depths)
            strip = jnp.where(self.pair == 4 * x + k, pltpu.roll(field, turn, 1), strip)
        return strip

    def ends(self, strip, x, k):
        back = self.depths - 8 * x - 2 * k
        turn = jnp.where(self.deep == 0, back % self.depths, back - 2)
        return pltpu.roll(strip, turn, 1) * self.near

    def shallower(self, field, halo, n):
        return pltpu.roll(jnp.where(self.high[n], halo, field), n, 1)

    def deeper(self, field, halo, n):
        return pltpu.roll(jnp.where(self.low[n], halo, field), self.depths - n, 1)

    def forward_z(self, field, halo):
        return forward(
            self.shallower(field, halo, 1),
            field,
            self.deeper(field, halo, 1),
            self.deeper(field, halo, 2),
        )

    def backward_z(self, field, halo):
        return backward(
            self.shallower(field, halo, 2),
            self.shallower(field, halo, 1),
            field,
            self.deeper(field, halo, 1),
        )

    def before(self, field, load, n, halo):
        top = jnp.where(self.top[n], 0.0, pltpu.roll(field[:TILE], n, 0))
        if halo:
            for i in range(n):
                top = jnp.where(self.tile_row == i, halo[n - 1 - i], top)
        if load:
            rest = load(self.zero + (TILE - n), self.rows - TILE)
        else:
            rest = pltpu.roll(field, n, 0)[TILE:]
        return jnp.concatenate([top, rest], axis=0)

    def after(self, field, load, n, halo):
        bottom = pltpu.roll(field[self.rows - TILE :], TILE - n, 0)
        bottom = jnp.where(self.bottom[n], 0.0, bottom)
        if halo:
            for i in range(n):
                bottom = jnp.where(self.tile_row == TILE - n + i, halo[i], bottom)
        if load:
            rest = load(self.zero + n, self.rows - TILE)
        else:
            rest = pltpu.roll(field, self.rows - n, 0)[: self.rows - TILE]
        return jnp.concatenate([rest, bottom], axis=0)

    def forward_y(self, planes, comp, x, halos):
        field = planes(comp, x)
        load = planes.rows(comp, x) if self.by_loads else None
        lower, upper = halos
        return forward(
            self.before(field, load, 1, lower),
            field,
            self.after(field, load, 1, upper),
            self.after(field, load, 2, upper),
        )

    def backward_y(self, planes, comp, x, halos):
        field = planes(comp, x)
        load = planes.rows(comp, x) if self.by_loads else None
        lower, upper = halos
        return backward(
            self.before(field, load, 2, lower),
            self.before(field, load, 1, lower),
            field,
            self.after(field, load, 1, upper),
        )


class Field:
    def __init__(self, count, *parts):
        self.count = count
        self.parts = parts

    def place(self, x):
        if len(self.parts) == 1:
            return self.parts[0], x
        inner, edge = self.parts
        if x in inside(self.count):
            return inner, x - 2
        return edge, ends_of(self.count).index(x)

    def __call__(self, comp, x):
        ref, at = self.place(x)
        return ref[comp, at]

    def rows(self, comp, x):
        ref, at = self.place(x)
        return lambda start, size: ref[comp, at, pl.ds(start, size), :]


def inside(count):
    return range(2, count - 2)


def ends_of(count):
    return (0, 1, count - 2, count - 1)


class Planes:
    def __init__(self, field, tail, head, first=None, second=None, change=None, on_fault=None):
        self.change, self.on_fault = change, on_fault
        self.field = field
        self.count = field.count
        self.first, self.second = first, second
        self.tail, self.head = tail, head
        self.even = even_strike()
        self.any_left = lax.axis_index(GX) > 0
        self.any_right = lax.axis_index(GX) < lax.axis_size(GX) - 1

    def left(self, i):
        return jnp.where(self.even, self.second[i], self.first[i])

    def right(self, i):
        return jnp.where(self.even, self.first[i], self.second[i])

    def changed(self, plane, comp, end, node):
        if self.change is None or comp == 1:
            return plane
        line = self.change[end, pl.ds(comp + node, 1), :]
        return plane + jnp.where(self.on_fault, line, 0.0)

    def __call__(self, comp, place):
        if place < 0:
            plane = self.left(self.tail.index((comp, place)))
            return jnp.where(self.any_left, self.changed(plane, comp, 0, place + 2), 0.0)
        if place >= self.count:
            beyond = place - self.count
            plane = self.right(self.head.index((comp, beyond)))
            return jnp.where(self.any_right, self.changed(plane, comp, 1, beyond), 0.0)
        return self.field(comp, place)

    def rows(self, comp, x):
        return self.field.rows(comp, x)

    def forward_x(self, comp, x):
        return forward(self(comp, x - 1), self(comp, x), self(comp, x + 1), self(comp, x + 2))

    def backward_x(self, comp, x):
        return backward(self(comp, x - 2), self(comp, x - 1), self(comp, x), self(comp, x + 1))


class Bands:
    def __init__(self, lower, upper, tail, head):
        self.lower, self.upper = lower, upper
        self.tail, self.head = tail, head

    def __call__(self, comp, x):
        if self.lower is None:
            return (None, None)
        places = [i for i, (c, _) in enumerate(self.tail) if c == comp]
        before = [self.lower[i, pl.ds(x, 1), :] for i in reversed(places)]
        places = [i for i, (c, _) in enumerate(self.head) if c == comp]
        after = [self.upper[i, pl.ds(x, 1), :] for i in places]
        return (before, after)


def looked_up(labels, table, row, count):
    out = jnp.full(labels.shape, table[row, 0], jnp.float32)
    for k in range(1, count):
        out = jnp.where(labels == k, table[row, k], out)
    return out


def even_strike():
    return lax.axis_index(GX) % 2 == 0


def edge_planes(field, tail, head, first_out, second_out):
    even = even_strike()
    pairs = []
    for i in range(max(len(tail), len(head))):
        comp, place = tail[min(i, len(tail) - 1)]
        right = field(comp, place % field.count)
        comp, place = head[min(i, len(head) - 1)]
        left = field(comp, place % field.count)
        pairs.append((jnp.where(even, right, left), jnp.where(even, left, right)))
    for i, (one, two) in enumerate(pairs):
        first_out[i] = one
        second_out[i] = two


def fault_row(rows):
    return jnp.where(lax.axis_index(GY) == lax.axis_size(GY) // 2, 0, rows - 1)


def pack_kernel(r):
    count, rows, depths = r.stress.shape[1:]
    whole = [(comp, 0, count) for comp in STRESS_SLOTS]
    some = {}
    for comp, place in STRESS_TAIL + STRESS_HEAD:
        if comp not in STRESS_SLOTS:
            some.setdefault((comp, place < 0), []).append(place % count)
    some = [(comp, min(at), max(at) + 1) for (comp, _), at in some.items()]
    copies = []
    for i, (comp, start, stop) in enumerate(some + whole):
        span = pl.ds(start, stop - start)
        copy = pltpu.make_async_copy(r.stress.at[comp, span], r.held.at[comp, span], r.sems.at[i])
        copy.start()
        copies.append(copy)
    edges = Edges(rows, depths)
    for copy in copies:
        copy.wait()
    edge_planes(Field(count, r.held), STRESS_TAIL, STRESS_HEAD, r.one_out, r.two_out)
    strip = jnp.zeros((rows, depths), jnp.float32)
    for x in range(count):
        strip = edges.packed(strip, x, [r.held[c, x] for c in STRESS_SLOTS])
    set_strip(r, strip)


def grouped(xs, size):
    return [xs[i : i + size] for i in range(0, len(xs), size)]


def set_strip(r, strip, face=None):
    rows = strip.shape[0]
    filled = 1
    r.strip_out[0] = strip
    if face is not None:
        filled += face.shape[0] // rows
        faces = [face[pl.ds(i * rows, rows), :] for i in range(filled - 1)]
        for i, part in enumerate(faces):
            r.strip_out[1 + i] = part
    for i in range(filled, r.strip_out.shape[0]):
        r.strip_out[i] = jnp.zeros_like(strip)


def unpack(r, xs, edges):
    strip = r.strip[0]
    for i, x in enumerate(xs):
        for k in range(3):
            r.ends[i, k] = edges.ends(strip, x, k)


def velocity_planes(r, xs, edges, planes, write):
    band = Bands(getattr(r, "lower", None), getattr(r, "upper", None), STRESS_TAIL_Y, STRESS_HEAD_Y)
    unpack(r, xs, edges)

    def new(x):
        push = DT * looked_up(r.material[x], r.table, 2, CLASSES)
        ends = [r.ends[xs.index(x), k] for k in range(3)]
        along_x = (
            planes.forward_x(XX, x)
            + edges.backward_y(planes, XY, x, band(XY, x))
            + edges.backward_z(planes(XZ, x), ends[0])
        )
        along_y = (
            planes.backward_x(XY, x)
            + edges.forward_y(planes, YY, x, band(YY, x))
            + edges.backward_z(planes(YZ, x), ends[1])
        )
        along_z = (
            planes.backward_x(XZ, x)
            + edges.backward_y(planes, YZ, x, band(YZ, x))
            + edges.forward_z(planes(ZZ, x), ends[2])
        )
        rates = (along_x, along_y, along_z)
        return [r.velocity[c, x] + push * rate for c, rate in enumerate(rates)]

    for group in grouped(xs, 3 if len(xs) % 3 == 0 else 2):
        for x, values in [(x, new(x)) for x in group]:
            write(x, values)


def velocity_inner(r):
    count, rows, depths = r.material.shape
    edges = Edges(rows, depths)
    planes = Planes(stress_of(r), STRESS_TAIL, STRESS_HEAD)

    def write(x, new):
        for c in range(3):
            r.inner_out[c, x - 2] = new[c]

    velocity_planes(r, inside(count), edges, planes, write)
    strip = jnp.zeros((rows, depths), jnp.float32)
    for x in inside(count):
        strip = edges.packed(strip, x, [r.inner_out[c, x - 2] for c in VEL_SLOTS])
    r.strip_inner_out[...] = strip


def velocity_edge(r):
    count, rows, depths = r.material.shape
    edges = Edges(rows, depths)
    planes = Planes(stress_of(r), STRESS_TAIL, STRESS_HEAD, r.one, r.two)
    fault = fault_row(rows)
    places = ends_of(count)
    row = pl.ds(fault, 1)
    labels = [r.material[x, row, :] for x in range(count)]
    push = [looked_up(label, r.table, 2, CLASSES) for label in labels]
    lines = dict(enumerate(push, 2 * count))
    if hasattr(r, "prestress"):
        own = r.normal.shape[0]
        still = [[r.prestress[i, pl.ds(c, 1), :] for i in range(own)] for c in (0, 1)]
        for field in (r.normal, r.slip, r.zone, r.mask):
            still.append([field[pl.ds(i, 1), :].astype(jnp.float32) for i in range(own)])
        lines.update(enumerate(sum(still, []), 3 * count))

    def write(x, new):
        for c in range(3):
            r.edge_out[c, places.index(x)] = new[c]

    velocity_planes(r, places, edges, planes, write)
    strip = r.strip_inner[...]
    for i, x in enumerate(places):
        strip = edges.packed(strip, x, [r.edge_out[c, i] for c in VEL_SLOTS])
    new = Field(count, r.inner, r.edge_out)
    faces = [[new.rows(c, x)(fault, 1) for x in range(count)] for c in (0, 2)]
    lines.update(enumerate(sum(faces, [])))
    for i in range(len(lines), r.face_out.shape[0]):
        lines[i] = jnp.zeros((1, depths), jnp.float32)
    for i, line in lines.items():
        r.face_out[pl.ds(i, 1), :] = line
    set_strip(r, strip, r.face_out)
    edge_planes(new, VEL_TAIL, VEL_HEAD, r.one_out, r.two_out)


def stress_of(r):
    count = r.material.shape[0]
    if hasattr(r, "stress"):
        return Field(count, r.stress)
    return Field(count, r.stress_inner, r.stress_edge)


def memory_of(r):
    count = r.material.shape[0]
    if hasattr(r, "memory"):
        return Field(count, r.memory)
    return Field(count, r.memory_inner, r.memory_edge)


def slipped(r, own, other, still, slip, row, deep):
    middle = lax.axis_size(GY) // 2
    side = lax.axis_index(GY)
    plus = side == middle
    minus = side == middle - 1
    minus_x, minus_z, minus_b = [jnp.where(plus, b, a) for a, b in zip(own, other)]
    plus_x, plus_z, plus_b = [jnp.where(plus, a, b) for a, b in zip(own, other)]
    pre_x, pre_z, normal, _, zone, mask = still
    inside = (row >= r.anchor[0]) & (row < r.anchor[0] + 2 * PATCH)
    inside = inside & (deep >= r.anchor[1]) & (deep < r.anchor[1] + 2 * PATCH)
    dynamic = 0.4 * looked_up(zone, r.friction, 0, ZONES)
    static = jnp.where(
        inside, dynamic, dynamic + 0.5 * looked_up(zone, r.friction, 1, ZONES)
    )
    distance = 0.2 * looked_up(zone, r.friction, 2, ZONES)
    bsum = minus_b + plus_b
    trial_x = (plus_x - minus_x) / (DT * bsum) + pre_x
    trial_z = (plus_z - minus_z) / (DT * bsum) + pre_z
    size = jnp.sqrt(trial_x * trial_x + trial_z * trial_z)
    weaken = jnp.minimum(slip / distance, 1.0)
    strength = (static - (static - dynamic) * weaken) * normal
    factor = jnp.where(mask == 1.0, strength / jnp.maximum(size, strength), 1.0)
    new_slip = slip + DT * DT * bsum * (size - size * factor)
    sign = jnp.where(minus, DT, 0.0) * minus_b - jnp.where(plus, DT, 0.0) * plus_b
    return (trial_x * factor - pre_x) * sign, (trial_z * factor - pre_z) * sign, new_slip


def fault_kernel(count, r):
    rows, depths = r.strip.shape[1:]
    plus = lax.axis_index(GY) == lax.axis_size(GY) // 2

    def beside(place, size):
        return r.strip[1 + place // rows, pl.ds(place % rows, size), :]

    def nodes(source, source_beside, place, size):
        return source[pl.ds(place, size), :], source_beside(place, size)

    def cross(place, size):
        return r.cross[pl.ds(place, size), :]

    own = [jnp.concatenate(nodes(r.face, beside, i * count, count)) for i in range(3)]
    other = [jnp.concatenate(nodes(r.other, cross, i * count, count)) for i in range(3)]
    if hasattr(r, "still"):
        still = [r.still[i] for i in range(6)]
    else:
        share = count // 2
        still = []
        for i in range(6):
            place = 3 * count + i * share
            mine = nodes(r.face, beside, place, share)
            theirs = nodes(r.other, cross, place, share)
            halves = []
            for a, b in zip(mine, theirs):
                halves += [jnp.where(plus, b, a), jnp.where(plus, a, b)]
            still.append(jnp.concatenate(halves))
        for i in range(6):
            r.still_out[i] = still[i]
    slip = r.slip[...] if hasattr(r, "slip") else still[3]
    deep = lax.axis_index(GZ)
    row = lax.broadcasted_iota(jnp.int32, (2 * count, depths), 0)
    lane = lax.broadcasted_iota(jnp.int32, (2 * count, depths), 1)
    lane = lane + jnp.where(row < count, deep, 1 - deep) * depths
    row = row % count
    place = row + lax.axis_index(GX) * count
    change_x, change_z, new_slip = slipped(r, own, other, still, slip, place, lane)
    r.slip_out[...] = new_slip
    if hasattr(r, "new_slip_out"):
        half = r.new_slip_out.shape[0]
        r.new_slip_out[...] = jnp.where(plus, new_slip[half : 2 * half], new_slip[:half])
    r.change_out[0] = change_x
    r.change_out[1] = change_z

    even = even_strike()
    for c, field in enumerate((change_x, change_z)):
        tail, head = field[count - 2 : count], field[:2]
        r.fix_one_out[pl.ds(2 * c, 2), :] = jnp.where(even, tail, head)
        r.fix_two_out[pl.ds(2 * c, 2), :] = jnp.where(even, head, tail)
    for out in (r.fix_one_out, r.fix_two_out):
        out[pl.ds(4, 4), :] = jnp.zeros((4, depths), jnp.float32)

    on_fault = lax.broadcasted_iota(jnp.int32, (rows, depths), 0) == fault_row(rows)
    ends = jnp.zeros((count, depths), jnp.float32)
    pair = lax.broadcasted_iota(jnp.int32, (count, depths), 1) // 2
    first = 4 * lax.broadcasted_iota(jnp.int32, (count, depths), 0)
    for k, field in ((0, change_x[count:]), (2, change_z[count:])):
        turned = jnp.where(deep == 0, field, pltpu.roll(field, 2, 1))
        turned = pltpu.roll(turned, 2 * k, 1, stride=8, stride_axis=0)
        ends = jnp.where(pair == first + k, turned, ends)
    line = jnp.sum(ends, axis=0, keepdims=True)
    r.strip_out[0] = r.strip[0] + jnp.where(on_fault, line, 0.0)


def stress_planes(r, xs, edges, planes, write):
    band = Bands(getattr(r, "lower", None), getattr(r, "upper", None), VEL_TAIL_Y, VEL_HEAD_Y)
    stress, memory = stress_of(r), memory_of(r)
    unpack(r, xs, edges)

    def rates(x):
        in_x, in_y, in_z = [r.ends[xs.index(x), k] for k in range(3)]
        exx = planes.backward_x(0, x)
        eyy = edges.backward_y(planes, 1, x, band(1, x))
        ezz = edges.backward_z(planes(2, x), in_z)
        exy = edges.forward_y(planes, 0, x, band(0, x)) + planes.forward_x(1, x)
        exz = edges.forward_z(planes(0, x), in_x) + planes.forward_x(2, x)
        eyz = edges.forward_z(planes(1, x), in_y) + edges.forward_y(planes, 2, x, band(2, x))
        labels = r.material[x]
        bulk = looked_up(labels, r.table, 0, CLASSES) * (exx + eyy + ezz)
        shear = looked_up(labels, r.table, 1, CLASSES)
        double = 2.0 * shear
        return (
            bulk + double * exx,
            bulk + double * eyy,
            bulk + double * ezz,
            shear * exy,
            shear * exz,
            shear * eyz,
        )

    def new(x, elastic):
        labels = r.material[x]
        decay = jnp.exp(-DT / looked_up(labels, r.table, 3, CLASSES))
        gain = (1.0 - decay) * (0.3 * looked_up(labels, r.table, 4, CLASSES))
        kept = [decay * memory(c, x) - gain * elastic[c] for c in range(6)]
        return [stress(c, x) + DT * (elastic[c] + kept[c]) for c in range(6)], kept

    for group in grouped(xs, 2):
        for x, elastic in [(x, rates(x)) for x in group]:
            write(x, *new(x, elastic))


def stress_inner(last, r):
    count, rows, depths = r.material.shape
    edges = Edges(rows, depths, by_loads=True)
    on_fault = edges.row == fault_row(rows)
    free = Field(count, r.inner, r.edge)
    for x in range(count):
        for c in (0, 2):
            line = r.change[c // 2, pl.ds(x, 1), :]
            r.velocity_out[c, x] = free(c, x) + jnp.where(on_fault, line, 0.0)
        r.velocity_out[1, x] = free(1, x)
    planes = Planes(Field(count, r.velocity_out), VEL_TAIL, VEL_HEAD)
    copies = []

    def copy_out(source, out):
        copy = pltpu.make_async_copy(source, out, r.sems.at[len(copies)])
        copy.start()
        copies.append(copy)

    if last:
        copy_out(r.velocity_out, r.new_velocity_out)
        if hasattr(r, "slip"):
            copy_out(r.slip, r.new_slip_out)
        stress_out, memory_out = r.stress_held, r.memory_held
    else:
        stress_out, memory_out = r.stress_inner_out, r.memory_inner_out

    def write(x, new, kept):
        for c in range(6):
            stress_out[c, x - 2] = new[c]
            memory_out[c, x - 2] = kept[c]
        if last and x % 2 == 1:
            held, out = pl.ds(x - 3, 2), pl.ds(x - 1, 2)
            copy_out(stress_out.at[:, held], r.stress_out.at[:, out])
            copy_out(memory_out.at[:, held], r.memory_out.at[:, out])

    stress_planes(r, inside(count), edges, planes, write)
    if last:
        for copy in copies:
            copy.wait()
    else:
        strip = jnp.zeros((rows, depths), jnp.float32)
        for x in inside(count):
            strip = edges.packed(strip, x, [r.stress_inner_out[c, x - 2] for c in STRESS_SLOTS])
        r.strip_inner_out[...] = strip


def stress_edge(last, r):
    count, rows, depths = r.material.shape
    edges = Edges(rows, depths, by_loads=True)
    even = even_strike()
    r.nodes[0] = jnp.where(even, r.fix_two[...], r.fix_one[...])
    r.nodes[1] = jnp.where(even, r.fix_one[...], r.fix_two[...])
    on_fault = edges.row == fault_row(rows)
    field = Field(count, r.velocity)
    planes = Planes(field, VEL_TAIL, VEL_HEAD, r.one, r.two, r.nodes, on_fault)
    places = ends_of(count)
    copies = []

    def copy_out(source, out, span):
        copy = pltpu.make_async_copy(source, out.at[:, span], r.sems.at[len(copies)])
        copy.start()
        copies.append(copy)

    if last:
        stress_out, memory_out = r.stress_held, r.memory_held
    else:
        stress_out, memory_out = r.stress_edge_out, r.memory_edge_out

    def write(x, new, kept):
        for c in range(6):
            stress_out[c, places.index(x)] = new[c]
            memory_out[c, places.index(x)] = kept[c]

    stress_planes(r, places, edges, planes, write)
    if last:
        for held, out in ((stress_out, r.stress_out), (memory_out, r.memory_out)):
            copy_out(held.at[:, pl.ds(0, 2)], out, pl.ds(0, 2))
            copy_out(held.at[:, pl.ds(2, 2)], out, pl.ds(count - 2, 2))
        for copy in copies:
            copy.wait()
    else:
        strip = r.strip_inner[...]
        for i, x in enumerate(places):
            strip = edges.packed(strip, x, [stress_out[c, i] for c in STRESS_SLOTS])
        set_strip(r, strip)
        new = Field(count, r.new_stress_inner, stress_out)
        edge_planes(new, STRESS_TAIL, STRESS_HEAD, r.one_out, r.two_out)


SCALARS = ("table", "friction", "anchor")


def call(kernel, name, ins, outs, scratch=None, apart=(), onto=(), micros=1, vmem=6):
    scratch = scratch or {}
    names = [*ins, *(f"{key}_out" for key in outs), *scratch]

    def body(*refs):
        kernel(types.SimpleNamespace(**dict(zip(names, refs))))

    def place(key):
        if key in apart:
            return pl.BlockSpec(memory_space=pltpu.HBM)
        return pl.BlockSpec(memory_space=pltpu.SMEM if key in SCALARS else pltpu.VMEM)

    shapes = [jax.ShapeDtypeStruct(shape, jnp.float32) for shape in outs.values()]
    result = pl.pallas_call(
        body,
        out_shape=shapes,
        in_specs=[place(key) for key in ins],
        out_specs=[place(f"{key}_out") for key in outs],
        scratch_shapes=list(scratch.values()),
        name=name,
        input_output_aliases={
            list(ins).index(key): list(outs).index(onto[key]) for key in onto
        },
        cost_estimate=pl.CostEstimate(
            flops=0, bytes_accessed=micros * 3_690_000, transcendentals=0
        ),
        compiler_params=pltpu.CompilerParams(vmem_limit_bytes=vmem * 2**20),
    )(*ins.values())
    return dict(zip(outs, result))


def along(axis, count, skip=()):
    up = [(i, i + 1) for i in range(count - 1) if i not in skip]
    return (axis, up), (axis, [(b, a) for a, b in up])


def strike_swaps(count):
    halves = lax.axis_size(GZ)
    routes = []
    for start in (0, 1):
        partner = {}
        for i in range(start, count - 1, 2):
            for half in range(halves):
                one, other = i * halves + half, (i + 1) * halves + half
                partner[one], partner[other] = other, one
        for i in range(count * halves):
            partner.setdefault(i, i ^ 1)
        routes.append(((GX, GZ), sorted(partner.items())))
    return routes


def fault_swaps(pair, sides):
    across, cross = [], []
    for side in range(sides):
        for half in (0, 1):
            place, over = 2 * side + half, 2 * (sum(pair) - side) + half
            if side not in pair:
                over = place ^ 1
            across.append((place, over))
            cross.append((place, over ^ 1 if side in pair else over))
    return ((GY, GZ), across), ((GY, GZ), cross)


def sent(block, route):
    return lax.ppermute(block, *route)


def whole(parts, name):
    if name in parts:
        return parts[name]
    inner, edge = parts[f"{name}_inner"], parts[f"{name}_edge"]
    return jnp.concatenate([edge[:, :2], inner, edge[:, 2:]], axis=1)


def edge_rows(field, rows):
    count = field.shape[2]
    return jnp.stack([field[c, :, place % count, :] for c, place in rows])


def shards(
    velocity,
    stress,
    memory,
    material,
    material_table,
    fault_mask,
    zone_label,
    patch_anchor,
    friction_table,
    prestress,
    normal_stress,
    slip_path,
):
    _, count, rows, depths = velocity.shape
    sides = lax.axis_size(GY)
    middle = sides // 2
    banded = sides > 2
    swaps = strike_swaps(lax.axis_size(GX))
    up_y, down_y = along(GY, sides, (middle - 1,))
    deep = (GZ, [(0, 1), (1, 0)])
    pair = (middle - 1, middle)
    across, cross = fault_swaps(pair, sides)

    plane = (rows, depths)
    edge_planes = max(len(STRESS_TAIL), len(STRESS_HEAD))

    def travelling(planes):
        return {"one": (planes, *plane), "two": (planes, *plane), "strip": (planes + 1, *plane)}

    inner, edge = (count - 4, *plane), (4, *plane)
    inner_ends = {"ends": pltpu.VMEM((count - 4, 3, *plane), jnp.float32)}
    nodes = pltpu.VMEM((2, TILE, depths), jnp.float32)
    edge_ends = {"ends": pltpu.VMEM((4, 3, *plane), jnp.float32)}

    def travelled(packed):
        two = sent(packed["two"], swaps[1])
        one = sent(packed["one"], swaps[0])
        strip = sent(packed["strip"], deep)
        return {"strip": strip}, {"one": one, "two": two}

    def bands(field, tail, head):
        if not banded:
            return {}
        lower, upper = edge_rows(field, tail), edge_rows(field, head)
        return {"lower": sent(lower, up_y), "upper": sent(upper, down_y)}

    if banded:
        still = jnp.stack(
            [
                prestress[:, 0],
                prestress[:, 1],
                normal_stress,
                slip_path,
                zone_label.astype(jnp.float32),
                fault_mask.astype(jnp.float32),
            ]
        )
        still = lax.all_gather(still, GY, axis=1, tiled=True)
        still = jnp.concatenate([still, sent(still, deep)], axis=1)
        still, slip = {"still": still}, still[3]
    else:
        still = {}

    parts = {"stress": stress, "memory": memory}
    props = {"material": material, "table": material_table}
    packed = call(
        pack_kernel,
        "pack",
        {"stress": stress},
        travelling(edge_planes),
        scratch={"held": pltpu.VMEM(stress.shape, jnp.float32), "sems": pltpu.SemaphoreType.DMA((8,))},
        apart=("stress",),
        vmem=6,
    )
    for step in range(STEPS):
        first, last = step == 0, step == STEPS - 1
        held_stress = {key: parts[key] for key in parts if key.startswith("stress")}
        strip, halos = travelled(packed)
        ins = {"velocity": velocity, **held_stress, **props, **strip}
        if banded:
            ins.update(bands(whole(parts, "stress"), STRESS_TAIL_Y, STRESS_HEAD_Y))
        free = call(
            velocity_inner,
            "velocity_inner",
            ins,
            {"inner": (3, *inner), "strip_inner": plane},
            scratch=inner_ends,
            micros=3,
        )
        face_rows = 3 * count
        ins = {**ins, **halos, **free}
        if not still:
            ins.update(prestress=prestress, normal=normal_stress, slip=slip_path)
            ins.update(zone=zone_label, mask=fault_mask)
            face_rows += 6 * normal_stress.shape[0]
        face_rows = -(-face_rows // rows) * rows
        packed = call(
            velocity_edge,
            "velocity_edge",
            ins,
            {"edge": (3, *edge), "face": (face_rows, depths), **travelling(edge_planes)},
            scratch=edge_ends,
        )
        free = {"inner": free["inner"], "edge": packed["edge"]}
        strip, halos = travelled(packed)
        face = packed["face"]
        ins = {"face": face, "other": sent(face, across), "cross": sent(face, cross), **strip}
        ins.update(friction=friction_table, anchor=patch_anchor)
        if still:
            ins.update(slip=slip, **still)
        outs = {"change": (2, 2 * count, depths), "slip": (2 * count, depths), "strip": (1, *plane)}
        outs.update(fix_one=(TILE, depths), fix_two=(TILE, depths))
        if last and not banded:
            outs["new_slip"] = (count // sides, depths)
        if not still:
            outs["still"] = (6, 2 * count, depths)
        packed = call(functools.partial(fault_kernel, count), "fault", ins, outs, vmem=3)
        slip = packed["slip"]
        if not still:
            still = {"still": packed["still"]}
        strip = {"strip": packed["strip"]}
        halos["fix_one"] = sent(packed["fix_one"], swaps[0])
        halos["fix_two"] = sent(packed["fix_two"], swaps[1])
        ins = {**free, "change": packed["change"], **parts, **props, **strip}
        if banded:
            joined = jnp.concatenate(
                [free["edge"][:, :2], free["inner"], free["edge"][:, 2:]], axis=1
            )
            band = bands(joined, VEL_TAIL_Y, VEL_HEAD_Y)
        else:
            band = {}
        outs = {"velocity": velocity.shape}
        extra = {"scratch": inner_ends}
        if last:
            outs.update(new_velocity=velocity.shape, stress=stress.shape, memory=memory.shape)
            extra["apart"] = ["new_velocity_out", "stress_out", "memory_out"]
            if not banded:
                ins["slip"] = packed["new_slip"]
                outs["new_slip"] = packed["new_slip"].shape
                extra["apart"].append("new_slip_out")
            held = pltpu.VMEM((6, *inner), jnp.float32)
            sems = pltpu.SemaphoreType.DMA((count,))
            extra["scratch"] = {"stress_held": held, "memory_held": held, "sems": sems, **inner_ends}
        else:
            outs.update(stress_inner=(6, *inner), memory_inner=(6, *inner), strip_inner=plane)
        done = call(
            functools.partial(stress_inner, last),
            "stress_inner",
            {**ins, **band},
            outs,
            micros=3,
            vmem=11,
            **extra,
        )
        velocity = done["velocity"]
        ins = {"velocity": velocity, **parts, **props, **strip, **halos, **band}
        if last:
            ins.update(stress_done=done["stress"], memory_done=done["memory"])
            held = pltpu.VMEM((6, *edge), jnp.float32)
            packed = call(
                functools.partial(stress_edge, last),
                "stress_edge",
                ins,
                {"stress": stress.shape, "memory": memory.shape},
                scratch={
                    "stress_held": held,
                    "memory_held": held,
                    "sems": pltpu.SemaphoreType.DMA((4,)),
                    "nodes": nodes,
                    **edge_ends,
                },
                apart=("stress_done", "memory_done", "stress_out", "memory_out"),
                onto={"stress_done": "stress", "memory_done": "memory"},
                vmem=10,
            )
            velocity = done["new_velocity"]
            stress, memory = packed["stress"], packed["memory"]
            slip = done.get("new_slip", slip)
        else:
            ins.update(new_stress_inner=done["stress_inner"], strip_inner=done["strip_inner"])
            packed = call(
                functools.partial(stress_edge, last),
                "stress_edge",
                ins,
                {
                    "stress_edge": (6, *edge),
                    "memory_edge": (6, *edge),
                    **travelling(edge_planes),
                },
                scratch={"nodes": nodes, **edge_ends},
                vmem=10,
            )
            parts = {
                "stress_inner": done["stress_inner"],
                "stress_edge": packed["stress_edge"],
                "memory_inner": done["memory_inner"],
                "memory_edge": packed["memory_edge"],
            }
    if banded:
        held = jnp.where(lax.axis_index(GY) == middle, slip[:count], 0.0)
        slip = lax.psum_scatter(held, GY, scatter_dimension=0, tiled=True)
    return (velocity, stress, memory, slip)


def solution(mesh):
    in_specs = (
        P(None, (ENS, GX), GY, GZ),
        P(None, (ENS, GX), GY, GZ),
        P(None, (ENS, GX), GY, GZ),
        P((ENS, GX), GY, GZ),
        P(None, ENS),
        P((ENS, GX, GY), GZ),
        P((ENS, GX, GY), GZ),
        P(ENS),
        P(None, ENS),
        P((ENS, GX, GY), None, GZ),
        P((ENS, GX, GY), GZ),
        P((ENS, GX, GY), GZ),
    )
    out_specs = (
        P(None, (ENS, GX), GY, GZ),
        P(None, (ENS, GX), GY, GZ),
        P(None, (ENS, GX), GY, GZ),
        P((ENS, GX, GY), GZ),
    )
    return jax.shard_map(shards, mesh=mesh, in_specs=in_specs, out_specs=out_specs, check_vma=False)
```

```python
import functools
import types

import jax
import jax.numpy as jnp
from jax import lax
from jax.experimental import pallas as pl
from jax.experimental.pallas import tpu as pltpu
from jax.sharding import PartitionSpec as P

STEPS = 2
CLASSES = 8
ZONES = 4
PATCH = 8

NEAR = 9.0 / 8.0
FAR = -1.0 / 24.0
DT = 0.15
TILE = 8
ENS, GX, GY, GZ = "ens", "gx", "gy", "gz"
STRIP_PLANES = 6

XX, YY, ZZ, XY, XZ, YZ = range(6)

STRESS_TAIL = ((XX, -1), (XY, -2), (XY, -1), (XZ, -2), (XZ, -1))
STRESS_HEAD = ((XX, 0), (XX, 1), (XY, 0), (XZ, 0))
VEL_TAIL = ((0, -2), (0, -1), (1, -1), (2, -1))
VEL_HEAD = ((0, 0), (1, 0), (1, 1), (2, 0), (2, 1))
STRESS_TAIL_Y = ((YY, -1), (XY, -2), (XY, -1), (YZ, -2), (YZ, -1))
STRESS_HEAD_Y = ((YY, 0), (YY, 1), (XY, 0), (YZ, 0))
VEL_TAIL_Y = ((1, -2), (1, -1), (0, -1), (2, -1))
VEL_HEAD_Y = ((1, 0), (0, 0), (0, 1), (2, 0), (2, 1))
STRESS_SLOTS = (XZ, YZ, ZZ)
VEL_SLOTS = (0, 1, 2)


def forward(before, here, after, after_2):
    return NEAR * (after - here) + FAR * (after_2 - before)


def backward(before_2, before, here, after):
    return NEAR * (here - before) + FAR * (after - before_2)


class Edges:
    def __init__(self, rows, depths, by_loads=False):
        self.rows = rows
        self.depths = depths
        lane = lax.broadcasted_iota(jnp.int32, (rows, depths), 1)
        row = lax.broadcasted_iota(jnp.int32, (TILE, depths), 0)
        self.row = lax.broadcasted_iota(jnp.int32, (rows, depths), 0)
        self.tile_row = row
        self.deep = lax.axis_index(GZ)
        near = (self.deep == 0) & (lane < 2) | (self.deep == 1) & (lane >= depths - 2)
        self.near = jnp.where(near, 1.0, 0.0)
        self.zero = jnp.minimum(self.deep, 0)
        self.by_loads = by_loads
        self.pair = lane // 2
        self.low = {n: lane < n for n in (1, 2)}
        self.high = {n: lane >= depths - n for n in (1, 2)}
        self.top = {n: row < n for n in (1, 2)}
        self.bottom = {n: row >= TILE - n for n in (1, 2)}

    def packed(self, strip, x, fields):
        first = jnp.where(self.deep == 0, 2, 0)
        for k, field in enumerate(fields):
            turn = lax.rem(first + 8 * x + 2 * k, self.depths)
            strip = jnp.where(self.pair == 4 * x + k, pltpu.roll(field, turn, 1), strip)
        return strip

    def ends(self, strip, x, k):
        back = self.depths - 8 * x - 2 * k
        turn = jnp.where(self.deep == 0, back % self.depths, back - 2)
        return pltpu.roll(strip, turn, 1) * self.near

    def shallower(self, field, halo, n):
        return pltpu.roll(jnp.where(self.high[n], halo, field), n, 1)

    def deeper(self, field, halo, n):
        return pltpu.roll(jnp.where(self.low[n], halo, field), self.depths - n, 1)

    def forward_z(self, field, halo):
        return forward(
            self.shallower(field, halo, 1),
            field,
            self.deeper(field, halo, 1),
            self.deeper(field, halo, 2),
        )

    def backward_z(self, field, halo):
        return backward(
            self.shallower(field, halo, 2),
            self.shallower(field, halo, 1),
            field,
            self.deeper(field, halo, 1),
        )

    def before(self, field, load, n, halo):
        top = jnp.where(self.top[n], 0.0, pltpu.roll(field[:TILE], n, 0))
        if halo:
            for i in range(n):
                top = jnp.where(self.tile_row == i, halo[n - 1 - i], top)
        if load:
            rest = load(self.zero + (TILE - n), self.rows - TILE)
        else:
            rest = pltpu.roll(field, n, 0)[TILE:]
        return jnp.concatenate([top, rest], axis=0)

    def after(self, field, load, n, halo):
        bottom = pltpu.roll(field[self.rows - TILE :], TILE - n, 0)
        bottom = jnp.where(self.bottom[n], 0.0, bottom)
        if halo:
            for i in range(n):
                bottom = jnp.where(self.tile_row == TILE - n + i, halo[i], bottom)
        if load:
            rest = load(self.zero + n, self.rows - TILE)
        else:
            rest = pltpu.roll(field, self.rows - n, 0)[: self.rows - TILE]
        return jnp.concatenate([rest, bottom], axis=0)

    def forward_y(self, planes, comp, x, halos):
        field = planes(comp, x)
        load = planes.rows(comp, x) if self.by_loads else None
        lower, upper = halos
        return forward(
            self.before(field, load, 1, lower),
            field,
            self.after(field, load, 1, upper),
            self.after(field, load, 2, upper),
        )

    def backward_y(self, planes, comp, x, halos):
        field = planes(comp, x)
        load = planes.rows(comp, x) if self.by_loads else None
        lower, upper = halos
        return backward(
            self.before(field, load, 2, lower),
            self.before(field, load, 1, lower),
            field,
            self.after(field, load, 1, upper),
        )


class Field:
    def __init__(self, count, *parts):
        self.count = count
        self.parts = parts

    def place(self, x):
        if len(self.parts) == 1:
            return self.parts[0], x
        inner, edge = self.parts
        if x in inside(self.count):
            return inner, x - 2
        return edge, ends_of(self.count).index(x)

    def __call__(self, comp, x):
        ref, at = self.place(x)
        return ref[comp, at]

    def rows(self, comp, x):
        ref, at = self.place(x)
        return lambda start, size: ref[comp, at, pl.ds(start, size), :]


def inside(count):
    return range(2, count - 2)


def ends_of(count):
    return (0, 1, count - 2, count - 1)


class Planes:
    def __init__(self, field, tail, head, first=None, second=None):
        self.field = field
        self.count = field.count
        self.first, self.second = first, second
        self.tail, self.head = tail, head
        self.even = even_strike()
        self.any_left = lax.axis_index(GX) > 0
        self.any_right = lax.axis_index(GX) < lax.axis_size(GX) - 1

    def left(self, i):
        plane = jnp.where(self.even, self.second[i], self.first[i])
        return jnp.where(self.any_left, plane, 0.0)

    def right(self, i):
        plane = jnp.where(self.even, self.first[i], self.second[i])
        return jnp.where(self.any_right, plane, 0.0)

    def __call__(self, comp, place):
        if place < 0:
            return self.left(self.tail.index((comp, place)))
        if place >= self.count:
            return self.right(self.head.index((comp, place - self.count)))
        return self.field(comp, place)

    def rows(self, comp, x):
        return self.field.rows(comp, x)

    def forward_x(self, comp, x):
        return forward(self(comp, x - 1), self(comp, x), self(comp, x + 1), self(comp, x + 2))

    def backward_x(self, comp, x):
        return backward(self(comp, x - 2), self(comp, x - 1), self(comp, x), self(comp, x + 1))


class Bands:
    def __init__(self, lower, upper, tail, head):
        self.lower, self.upper = lower, upper
        self.tail, self.head = tail, head

    def __call__(self, comp, x):
        if self.lower is None:
            return (None, None)
        places = [i for i, (c, _) in enumerate(self.tail) if c == comp]
        before = [self.lower[i, pl.ds(x, 1), :] for i in reversed(places)]
        places = [i for i, (c, _) in enumerate(self.head) if c == comp]
        after = [self.upper[i, pl.ds(x, 1), :] for i in places]
        return (before, after)


def looked_up(labels, table, row, count):
    out = jnp.full(labels.shape, table[row, 0], jnp.float32)
    for k in range(1, count):
        out = jnp.where(labels == k, table[row, k], out)
    return out


def even_strike():
    return lax.axis_index(GX) % 2 == 0


def edge_planes(field, tail, head, first_out, second_out):
    even = even_strike()
    pairs = []
    for i in range(first_out.shape[0]):
        comp, place = tail[min(i, len(tail) - 1)]
        right = field(comp, place % field.count)
        comp, place = head[min(i, len(head) - 1)]
        left = field(comp, place % field.count)
        pairs.append((jnp.where(even, right, left), jnp.where(even, left, right)))
    for i, (one, two) in enumerate(pairs):
        first_out[i] = one
        second_out[i] = two


def fault_row(rows):
    return jnp.where(lax.axis_index(GY) == lax.axis_size(GY) // 2, 0, rows - 1)


def pack_kernel(r):
    count, rows, depths = r.stress.shape[1:]
    whole = [(comp, 0, count) for comp in STRESS_SLOTS]
    some = {}
    for comp, place in STRESS_TAIL + STRESS_HEAD:
        if comp not in STRESS_SLOTS:
            some.setdefault((comp, place < 0), []).append(place % count)
    some = [(comp, min(at), max(at) + 1) for (comp, _), at in some.items()]
    copies = []
    for i, (comp, start, stop) in enumerate(some + whole):
        span = pl.ds(start, stop - start)
        copy = pltpu.make_async_copy(r.stress.at[comp, span], r.held.at[comp, span], r.sems.at[i])
        copy.start()
        copies.append(copy)
    edges = Edges(rows, depths)
    for copy in copies:
        copy.wait()
    edge_planes(Field(count, r.held), STRESS_TAIL, STRESS_HEAD, r.one_out, r.two_out)
    strip = jnp.zeros((rows, depths), jnp.float32)
    for x in range(count):
        strip = edges.packed(strip, x, [r.held[c, x] for c in STRESS_SLOTS])
    set_strip(r, strip)


def grouped(xs, size):
    return [xs[i : i + size] for i in range(0, len(xs), size)]


def set_strip(r, strip):
    r.strip_out[0] = strip
    for i in range(1, STRIP_PLANES):
        r.strip_out[i] = jnp.zeros_like(strip)


def unpack(count, r, edges):
    strip = r.strip[0]
    for x in range(count):
        for k in range(3):
            r.ends[x, k] = edges.ends(strip, x, k)


def velocity_across(planes, x):
    return planes.forward_x(XX, x), planes.backward_x(XY, x), planes.backward_x(XZ, x)


def velocity_inner(first, r):
    count, rows, depths = r.material.shape
    edges = Edges(rows, depths)
    planes = Planes(stress_of(count, r), STRESS_TAIL, STRESS_HEAD)
    band = Bands(getattr(r, "lower", None), getattr(r, "upper", None), STRESS_TAIL_Y, STRESS_HEAD_Y)
    unpack(count, r, edges)

    def beside(x):
        ends = [r.ends[x, k] for k in range(3)]
        return (
            edges.backward_y(planes, XY, x, band(XY, x)) + edges.backward_z(planes(XZ, x), ends[0]),
            edges.forward_y(planes, YY, x, band(YY, x)) + edges.backward_z(planes(YZ, x), ends[1]),
            edges.backward_y(planes, YZ, x, band(YZ, x)) + edges.forward_z(planes(ZZ, x), ends[2]),
        )

    def push(x):
        return DT * looked_up(r.material[x], r.table, 2, CLASSES)

    def new(x):
        rates = zip(velocity_across(planes, x), beside(x))
        return [r.velocity[c, x] + push(x) * (a + b) for c, (a, b) in enumerate(rates)]

    for group in grouped(inside(count), 3 if (count - 4) % 3 == 0 else 2):
        for x, values in [(x, new(x)) for x in group]:
            for c in range(3):
                r.inner_out[c, x - 2] = values[c]
    for group in grouped(ends_of(count), 2):
        for x, values in [(x, (*beside(x), push(x))) for x in group]:
            for c in range(4):
                r.part_out[c, ends_of(count).index(x)] = values[c]
    strip = jnp.zeros((rows, depths), jnp.float32)
    for x in inside(count):
        strip = edges.packed(strip, x, [r.inner_out[c, x - 2] for c in VEL_SLOTS])
    r.strip_inner_out[...] = strip

    row = pl.ds(fault_row(rows), 1)
    lines = {}
    for x in inside(count):
        for i, c in enumerate((0, 2)):
            lines[i * count + x] = r.inner_out[c, x - 2, row, :]
    if first:
        for x in range(count):
            labels = r.material[x, row, :]
            lines[2 * count + x] = looked_up(labels, r.table, 2, CLASSES)
    if hasattr(r, "prestress"):
        own = r.normal.shape[0]
        place = 3 * count
        for c in (0, 1):
            for i in range(own):
                lines[place + c * own + i] = r.prestress[i, pl.ds(c, 1), :]
        for j, field in enumerate((r.normal, r.slip, r.zone, r.mask), 2):
            for i in range(own):
                lines[place + j * own + i] = field[pl.ds(i, 1), :].astype(jnp.float32)
    for i, line in lines.items():
        r.face_inner_out[pl.ds(i, 1), :] = line


def velocity_edge(count, r):
    rows, depths = r.one.shape[1:]
    edges = Edges(rows, depths)
    planes = Planes(stress_of(count, r), STRESS_TAIL, STRESS_HEAD, r.one, r.two)
    places = ends_of(count)
    new = []
    for i, x in enumerate(places):
        rates = [a + r.part[c, i] for c, a in enumerate(velocity_across(planes, x))]
        new.append([r.velocity[c, x] + r.part[3, i] * rate for c, rate in enumerate(rates)])
    faces = r.face_inner[...]
    strip = r.strip_inner[...]
    for i, x in enumerate(places):
        strip = edges.packed(strip, x, [new[i][c] for c in VEL_SLOTS])
        for c in range(3):
            r.edge_out[c, i] = new[i][c]
    r.face_out[...] = faces
    set_strip(r, strip)
    fault = fault_row(rows)
    edge = Field(count, None, r.edge_out)
    lines = {i * count + x: edge.rows(c, x)(fault, 1) for x in places for i, c in enumerate((0, 2))}
    for i, line in lines.items():
        r.face_out[pl.ds(i, 1), :] = line
    edge_planes(edge, VEL_TAIL, VEL_HEAD, r.one_out, r.two_out)


def stress_of(count, r):
    if hasattr(r, "stress"):
        return Field(count, r.stress)
    return Field(count, r.stress_inner, r.stress_edge)


def memory_of(count, r):
    if hasattr(r, "memory"):
        return Field(count, r.memory)
    return Field(count, r.memory_inner, r.memory_edge)


def fault_kernel(first, r):
    own_face, other_face = r.face, r.other
    own_first, other_first = (own_face, other_face) if first else (r.face_first, r.other_first)
    rows, depths = r.strip.shape[1:]
    count = r.change_out.shape[1]
    middle = lax.axis_size(GY) // 2
    side = lax.axis_index(GY)
    plus = side == middle
    minus = side == middle - 1

    def pair(own, other, place):
        mine, theirs = own[pl.ds(place, count), :], other[pl.ds(place, count), :]
        return jnp.where(plus, theirs, mine), jnp.where(plus, mine, theirs)

    if hasattr(r, "still"):
        still = r.still
    else:
        still = r.still_out
        share = (own_face.shape[0] - 3 * count) // 6
        for i in range(6):
            mine = own_face[pl.ds(3 * count + i * share, share), :]
            theirs = other_face[pl.ds(3 * count + i * share, share), :]
            still[i, pl.ds(0, share), :] = jnp.where(plus, theirs, mine)
            still[i, pl.ds(share, share), :] = jnp.where(plus, mine, theirs)
    pre_x, pre_z, normal = still[0], still[1], still[2]
    slip = still[3] if first else r.slip[...]
    zone, mask = still[4], still[5]

    row = lax.broadcasted_iota(jnp.int32, (count, depths), 0) + lax.axis_index(GX) * count
    deep = lax.broadcasted_iota(jnp.int32, (count, depths), 1) + lax.axis_index(GZ) * depths
    inside = (row >= r.anchor[0]) & (row < r.anchor[0] + 2 * PATCH)
    inside = inside & (deep >= r.anchor[1]) & (deep < r.anchor[1] + 2 * PATCH)
    dynamic = 0.4 * looked_up(zone, r.friction, 0, ZONES)
    static = jnp.where(
        inside, dynamic, dynamic + 0.5 * looked_up(zone, r.friction, 1, ZONES)
    )
    distance = 0.2 * looked_up(zone, r.friction, 2, ZONES)
    minus_x, plus_x = pair(own_face, other_face, 0)
    minus_z, plus_z = pair(own_face, other_face, count)
    minus_b, plus_b = pair(own_first, other_first, 2 * count)
    bsum = minus_b + plus_b
    trial_x = (plus_x - minus_x) / (DT * bsum) + pre_x
    trial_z = (plus_z - minus_z) / (DT * bsum) + pre_z
    size = jnp.sqrt(trial_x * trial_x + trial_z * trial_z)
    weaken = jnp.minimum(slip / distance, 1.0)
    strength = (static - (static - dynamic) * weaken) * normal
    factor = jnp.where(mask == 1.0, strength / jnp.maximum(size, strength), 1.0)
    new_slip = slip + DT * DT * bsum * (size - size * factor)
    half = r.slip_out.shape[0]
    if half < count:
        new_slip = jnp.where(plus, new_slip[half:], new_slip[:half])
    r.slip_out[...] = new_slip
    sign = jnp.where(minus, DT, 0.0) * minus_b - jnp.where(plus, DT, 0.0) * plus_b
    change_x = (trial_x * factor - pre_x) * sign
    change_z = (trial_z * factor - pre_z) * sign
    r.change_out[0] = change_x
    r.change_out[1] = change_z

    fault = fault_row(rows)
    on_fault = lax.broadcasted_iota(jnp.int32, (rows, depths), 0) == fault
    even = even_strike()
    still_line = jnp.zeros((1, depths), jnp.float32)

    def line(planes, i):
        comp, place = planes[min(i, len(planes) - 1)]
        return still_line if comp == 1 else r.change_out[comp // 2, pl.ds(place % count, 1), :]

    pairs = []
    for i in range(r.one_out.shape[0]):
        right, left = line(VEL_TAIL, i), line(VEL_HEAD, i)
        one, two = jnp.where(even, right, left), jnp.where(even, left, right)
        one = r.one[i] + jnp.where(on_fault, one, 0.0)
        pairs.append((one, r.two[i] + jnp.where(on_fault, two, 0.0)))
    for i, (one, two) in enumerate(pairs):
        r.one_out[i] = one
        r.two_out[i] = two
    ends = jnp.zeros((count, depths), jnp.float32)
    pair = lax.broadcasted_iota(jnp.int32, (count, depths), 1) // 2
    place = 4 * lax.broadcasted_iota(jnp.int32, (count, depths), 0)
    upper = lax.axis_index(GZ) == 0
    for k, field in ((0, change_x), (2, change_z)):
        turned = jnp.where(upper, pltpu.roll(field, 2, 1), field)
        turned = pltpu.roll(turned, 2 * k, 1, stride=8, stride_axis=0)
        ends = jnp.where(pair == place + k, turned, ends)
    line = jnp.sum(ends, axis=0, keepdims=True)
    set_strip(r, r.strip[0] + jnp.where(on_fault, line, 0.0))


def elastic_rates(planes, x, beside, lame, shear):
    eyy, ezz, eyz, along_y, along_z = beside
    exx = planes.backward_x(0, x)
    exy = along_y + planes.forward_x(1, x)
    exz = along_z + planes.forward_x(2, x)
    bulk = lame * (exx + eyy + ezz)
    double = 2.0 * shear
    return (
        bulk + double * exx,
        bulk + double * eyy,
        bulk + double * ezz,
        shear * exy,
        shear * exz,
        shear * eyz,
    )


def stress_new(x, elastic, decay, gain, stress, memory):
    kept = [decay * memory(c, x) - gain * elastic[c] for c in range(6)]
    return [stress(c, x) + DT * (elastic[c] + kept[c]) for c in range(6)], kept


def stress_inner(last, r):
    count, rows, depths = r.material.shape
    edges = Edges(rows, depths, by_loads=True)
    on_fault = edges.row == fault_row(rows)
    free = Field(count, r.inner, r.edge)
    for x in range(count):
        for c in (0, 2):
            line = r.change[c // 2, pl.ds(x, 1), :]
            r.velocity_out[c, x] = free(c, x) + jnp.where(on_fault, line, 0.0)
        r.velocity_out[1, x] = free(1, x)
    planes = Planes(Field(count, r.velocity_out), VEL_TAIL, VEL_HEAD)
    copies = []

    def copy_out(source, out):
        copy = pltpu.make_async_copy(source, out, r.sems.at[len(copies)])
        copy.start()
        copies.append(copy)

    if last:
        copy_out(r.velocity_out, r.new_velocity_out)
        if hasattr(r, "slip"):
            copy_out(r.slip, r.new_slip_out)
        stress_out, memory_out = r.stress_held, r.memory_held
    else:
        stress_out, memory_out = r.stress_inner_out, r.memory_inner_out

    def write(x, new, kept):
        for c in range(6):
            stress_out[c, x - 2] = new[c]
            memory_out[c, x - 2] = kept[c]
        if last and x % 2 == 1:
            held, out = pl.ds(x - 3, 2), pl.ds(x - 1, 2)
            copy_out(stress_out.at[:, held], r.stress_out.at[:, out])
            copy_out(memory_out.at[:, held], r.memory_out.at[:, out])

    band = Bands(getattr(r, "lower", None), getattr(r, "upper", None), VEL_TAIL_Y, VEL_HEAD_Y)
    stress, memory = stress_of(count, r), memory_of(count, r)
    unpack(count, r, edges)

    def beside(x):
        in_x, in_y, in_z = [r.ends[x, k] for k in range(3)]
        return (
            edges.backward_y(planes, 1, x, band(1, x)),
            edges.backward_z(planes(2, x), in_z),
            edges.forward_z(planes(1, x), in_y) + edges.forward_y(planes, 2, x, band(2, x)),
            edges.forward_y(planes, 0, x, band(0, x)),
            edges.forward_z(planes(0, x), in_x),
        )

    def moduli(x):
        return [looked_up(r.material[x], r.table, i, CLASSES) for i in (0, 1)]

    def fading(x):
        labels = r.material[x]
        decay = jnp.exp(-DT / looked_up(labels, r.table, 3, CLASSES))
        return decay, (1.0 - decay) * (0.3 * looked_up(labels, r.table, 4, CLASSES))

    for group in grouped(inside(count), 2):
        for x, elastic in [(x, elastic_rates(planes, x, beside(x), *moduli(x))) for x in group]:
            write(x, *stress_new(x, elastic, *fading(x), stress, memory))
    for group in grouped(ends_of(count), 2):
        for x, values in [(x, (*beside(x), *moduli(x), *fading(x))) for x in group]:
            for c in range(9):
                r.part_out[c, ends_of(count).index(x)] = values[c]
    if last:
        for copy in copies:
            copy.wait()
    else:
        strip = jnp.zeros((rows, depths), jnp.float32)
        for x in inside(count):
            strip = edges.packed(strip, x, [r.stress_inner_out[c, x - 2] for c in STRESS_SLOTS])
        r.strip_inner_out[...] = strip


def stress_edge(count, last, r):
    rows, depths = r.one.shape[1:]
    edges = Edges(rows, depths)
    planes = Planes(Field(count, r.velocity), VEL_TAIL, VEL_HEAD, r.one, r.two)
    places = ends_of(count)
    stress, memory = stress_of(count, r), memory_of(count, r)
    copies = []

    def copy_out(source, out, span):
        copy = pltpu.make_async_copy(source, out.at[:, span], r.sems.at[len(copies)])
        copy.start()
        copies.append(copy)

    if last:
        stress_out, memory_out = r.stress_held, r.memory_held
    else:
        stress_out, memory_out = r.stress_edge_out, r.memory_edge_out

    def elastic(i, x):
        part = [r.part[c, i] for c in range(7)]
        return elastic_rates(planes, x, part[:5], *part[5:])

    for group in grouped(list(enumerate(places)), 2):
        for (i, x), rates in [(at, elastic(*at)) for at in group]:
            new, kept = stress_new(x, rates, r.part[7, i], r.part[8, i], stress, memory)
            for c in range(6):
                stress_out[c, i] = new[c]
                memory_out[c, i] = kept[c]
        if last:
            held, span = pl.ds(group[0][0], 2), pl.ds(group[0][1], 2)
            copy_out(stress_out.at[:, held], r.stress_out, span)
            copy_out(memory_out.at[:, held], r.memory_out, span)
    if last:
        for copy in copies:
            copy.wait()
    else:
        strip = r.strip_inner[...]
        for i, x in enumerate(places):
            strip = edges.packed(strip, x, [stress_out[c, i] for c in STRESS_SLOTS])
        set_strip(r, strip)
        edge = Field(count, None, stress_out)
        edge_planes(edge, STRESS_TAIL, STRESS_HEAD, r.one_out, r.two_out)


SCALARS = ("table", "friction", "anchor")


def call(kernel, name, ins, outs, scratch=None, apart=(), onto=(), micros=1, vmem=6):
    scratch = scratch or {}
    names = [*ins, *(f"{key}_out" for key in outs), *scratch]

    def body(*refs):
        kernel(types.SimpleNamespace(**dict(zip(names, refs))))

    def place(key):
        if key in apart:
            return pl.BlockSpec(memory_space=pltpu.HBM)
        return pl.BlockSpec(memory_space=pltpu.SMEM if key in SCALARS else pltpu.VMEM)

    shapes = [jax.ShapeDtypeStruct(shape, jnp.float32) for shape in outs.values()]
    result = pl.pallas_call(
        body,
        out_shape=shapes,
        in_specs=[place(key) for key in ins],
        out_specs=[place(f"{key}_out") for key in outs],
        scratch_shapes=list(scratch.values()),
        name=name,
        input_output_aliases={
            list(ins).index(key): list(outs).index(onto[key]) for key in onto
        },
        cost_estimate=pl.CostEstimate(
            flops=0, bytes_accessed=micros * 3_690_000, transcendentals=0
        ),
        compiler_params=pltpu.CompilerParams(vmem_limit_bytes=vmem * 2**20),
    )(*ins.values())
    return dict(zip(outs, result))


def along(axis, count, skip=()):
    up = [(i, i + 1) for i in range(count - 1) if i not in skip]
    return (axis, up), (axis, [(b, a) for a, b in up])


def strike_swaps(count):
    halves = lax.axis_size(GZ)
    routes = []
    for start in (0, 1):
        partner = {}
        for i in range(start, count - 1, 2):
            for half in range(halves):
                one, other = i * halves + half, (i + 1) * halves + half
                partner[one], partner[other] = other, one
        for i in range(count * halves):
            partner.setdefault(i, i ^ 1)
        routes.append(((GX, GZ), sorted(partner.items())))
    return routes


def sent(block, route):
    return lax.ppermute(block, *route)


def whole(parts, name):
    if name in parts:
        return parts[name]
    inner, edge = parts[f"{name}_inner"], parts[f"{name}_edge"]
    return jnp.concatenate([edge[:, :2], inner, edge[:, 2:]], axis=1)


def edge_rows(field, rows):
    count = field.shape[2]
    return jnp.stack([field[c, :, place % count, :] for c, place in rows])


def shards(
    velocity,
    stress,
    memory,
    material,
    material_table,
    fault_mask,
    zone_label,
    patch_anchor,
    friction_table,
    prestress,
    normal_stress,
    slip_path,
):
    _, count, rows, depths = velocity.shape
    sides = lax.axis_size(GY)
    middle = sides // 2
    banded = sides > 2
    swaps = strike_swaps(lax.axis_size(GX))
    up_y, down_y = along(GY, sides, (middle - 1,))
    across = (GY, [(middle - 1, middle), (middle, middle - 1)])
    deep = (GZ, [(0, 1), (1, 0)])

    plane = (rows, depths)
    edge_shape = (max(len(STRESS_TAIL), len(STRESS_HEAD)), *plane)
    travelling = {"one": edge_shape, "two": edge_shape, "strip": (STRIP_PLANES, *plane)}
    inner, edge = (count - 4, *plane), (4, *plane)
    ends = {"ends": pltpu.VMEM((count, 3, *plane), jnp.float32)}

    def travelled(packed):
        two = sent(packed["two"], swaps[1])
        one = sent(packed["one"], swaps[0])
        strip = sent(packed["strip"], deep)
        return {"strip": strip}, {"one": one, "two": two}

    def bands(field, tail, head):
        if not banded:
            return {}
        lower, upper = edge_rows(field, tail), edge_rows(field, head)
        return {"lower": sent(lower, up_y), "upper": sent(upper, down_y)}

    if banded:
        still = jnp.stack(
            [
                prestress[:, 0],
                prestress[:, 1],
                normal_stress,
                slip_path,
                zone_label.astype(jnp.float32),
                fault_mask.astype(jnp.float32),
            ]
        )
        still = {"still": lax.all_gather(still, GY, axis=1, tiled=True)}
    else:
        still = {}

    parts = {"stress": stress, "memory": memory}
    props = {"material": material, "table": material_table}
    packed = call(
        pack_kernel,
        "pack",
        {"stress": stress},
        travelling,
        scratch={"held": pltpu.VMEM(stress.shape, jnp.float32), "sems": pltpu.SemaphoreType.DMA((8,))},
        apart=("stress",),
        vmem=6,
    )
    for step in range(STEPS):
        first, last = step == 0, step == STEPS - 1
        held_stress = {key: parts[key] for key in parts if key.startswith("stress")}
        strip, halos = travelled(packed)
        ins = {"velocity": velocity, **held_stress, **props, **strip}
        if banded:
            ins.update(bands(whole(parts, "stress"), STRESS_TAIL_Y, STRESS_HEAD_Y))
        face_rows = 2 * count
        if first:
            face_rows += count
            if not banded:
                ins.update(prestress=prestress, normal=normal_stress, slip=slip_path)
                ins.update(zone=zone_label, mask=fault_mask)
                face_rows += 6 * normal_stress.shape[0]
        outs = {"inner": (3, *inner), "part": (4, *edge), "strip_inner": plane}
        outs["face_inner"] = (face_rows, depths)
        free = call(
            functools.partial(velocity_inner, first),
            "velocity_inner",
            ins,
            outs,
            scratch=ends,
            micros=3,
        )
        ins = {"velocity": velocity, **held_stress, **halos}
        ins.update({key: free[key] for key in outs if key != "inner"})
        packed = call(
            functools.partial(velocity_edge, count),
            "velocity_edge",
            ins,
            {"edge": (3, *edge), "face": (face_rows, depths), **travelling},
        )
        free = {"inner": free["inner"], "edge": packed["edge"]}
        face = packed["face"]
        other = sent(face, across)
        ins = {key: packed[key] for key in travelling}
        ins.update(face=face, other=other, friction=friction_table, anchor=patch_anchor, **still)
        if first:
            faces = {"face_first": face, "other_first": other}
        else:
            ins.update(slip=slip, **faces)
        outs = {"change": (2, count, depths), "slip": (count, depths), **travelling}
        if last and not banded:
            outs["slip"] = (count // sides, depths)
        if not still:
            outs["still"] = (6, count, depths)
        packed = call(functools.partial(fault_kernel, first), "fault", ins, outs, vmem=2)
        slip = packed["slip"]
        if not still:
            still = {"still": packed["still"]}
        strip, halos = travelled(packed)
        ins = {**free, "change": packed["change"], **parts, **props, **strip}
        if banded:
            joined = jnp.concatenate(
                [free["edge"][:, :2], free["inner"], free["edge"][:, 2:]], axis=1
            )
            band = bands(joined, VEL_TAIL_Y, VEL_HEAD_Y)
        else:
            band = {}
        outs = {"velocity": velocity.shape, "part": (9, *edge)}
        extra = {"scratch": ends}
        if last:
            outs.update(new_velocity=velocity.shape, stress=stress.shape, memory=memory.shape)
            extra["apart"] = ["new_velocity_out", "stress_out", "memory_out"]
            if not banded:
                ins["slip"] = slip
                outs["new_slip"] = slip.shape
                extra["apart"].append("new_slip_out")
            held = pltpu.VMEM((6, *inner), jnp.float32)
            sems = pltpu.SemaphoreType.DMA((count,))
            extra["scratch"] = {"stress_held": held, "memory_held": held, "sems": sems, **ends}
        else:
            outs.update(stress_inner=(6, *inner), memory_inner=(6, *inner), strip_inner=plane)
        done = call(
            functools.partial(stress_inner, last),
            "stress_inner",
            {**ins, **band},
            outs,
            micros=3,
            vmem=11,
            **extra,
        )
        velocity = done["velocity"]
        ins = {"velocity": velocity, "part": done["part"], **parts, **halos}
        if last:
            ins.update(stress_done=done["stress"], memory_done=done["memory"])
            held = pltpu.VMEM((6, *edge), jnp.float32)
            packed = call(
                functools.partial(stress_edge, count, last),
                "stress_edge",
                ins,
                {"stress": stress.shape, "memory": memory.shape},
                scratch={
                    "stress_held": held,
                    "memory_held": held,
                    "sems": pltpu.SemaphoreType.DMA((4,)),
                },
                apart=("stress_done", "memory_done", "stress_out", "memory_out"),
                onto={"stress_done": "stress", "memory_done": "memory"},
                vmem=10,
            )
            velocity = done["new_velocity"]
            stress, memory = packed["stress"], packed["memory"]
            slip = done.get("new_slip", slip)
        else:
            ins["strip_inner"] = done["strip_inner"]
            packed = call(
                functools.partial(stress_edge, count, last),
                "stress_edge",
                ins,
                {"stress_edge": (6, *edge), "memory_edge": (6, *edge), **travelling},
                vmem=10,
            )
            parts = {
                "stress_inner": done["stress_inner"],
                "stress_edge": packed["stress_edge"],
                "memory_inner": done["memory_inner"],
                "memory_edge": packed["memory_edge"],
            }
    if banded:
        held = jnp.where(lax.axis_index(GY) == middle, slip, 0.0)
        slip = lax.psum_scatter(held, GY, scatter_dimension=0, tiled=True)
    return (velocity, stress, memory, slip)


def solution(mesh):
    in_specs = (
        P(None, (ENS, GX), GY, GZ),
        P(None, (ENS, GX), GY, GZ),
        P(None, (ENS, GX), GY, GZ),
        P((ENS, GX), GY, GZ),
        P(None, ENS),
        P((ENS, GX, GY), GZ),
        P((ENS, GX, GY), GZ),
        P(ENS),
        P(None, ENS),
        P((ENS, GX, GY), None, GZ),
        P((ENS, GX, GY), GZ),
        P((ENS, GX, GY), GZ),
    )
    out_specs = (
        P(None, (ENS, GX), GY, GZ),
        P(None, (ENS, GX), GY, GZ),
        P(None, (ENS, GX), GY, GZ),
        P((ENS, GX, GY), GZ),
    )
    return jax.shard_map(shards, mesh=mesh, in_specs=in_specs, out_specs=out_specs, check_vma=False)
```

```python
import functools
import types

import jax
import jax.numpy as jnp
from jax import lax
from jax.experimental import pallas as pl
from jax.experimental.pallas import tpu as pltpu
from jax.sharding import PartitionSpec as P

STEPS = 2
CLASSES = 8
ZONES = 4
PATCH = 8

NEAR = 9.0 / 8.0
FAR = -1.0 / 24.0
DT = 0.15
TILE = 8
ENS, GX, GY, GZ = "ens", "gx", "gy", "gz"
STRIP_PLANES = 6

XX, YY, ZZ, XY, XZ, YZ = range(6)

STRESS_TAIL = ((XX, -1), (XY, -2), (XY, -1), (XZ, -2), (XZ, -1))
STRESS_HEAD = ((XX, 0), (XX, 1), (XY, 0), (XZ, 0))
VEL_TAIL = ((0, -2), (0, -1), (1, -1), (2, -1))
VEL_HEAD = ((0, 0), (1, 0), (1, 1), (2, 0), (2, 1))
STRESS_TAIL_Y = ((YY, -1), (XY, -2), (XY, -1), (YZ, -2), (YZ, -1))
STRESS_HEAD_Y = ((YY, 0), (YY, 1), (XY, 0), (YZ, 0))
VEL_TAIL_Y = ((1, -2), (1, -1), (0, -1), (2, -1))
VEL_HEAD_Y = ((1, 0), (0, 0), (0, 1), (2, 0), (2, 1))
STRESS_SLOTS = (XZ, YZ, ZZ)
VEL_SLOTS = (0, 1, 2)


def forward(before, here, after, after_2):
    return NEAR * (after - here) + FAR * (after_2 - before)


def backward(before_2, before, here, after):
    return NEAR * (here - before) + FAR * (after - before_2)


class Edges:
    def __init__(self, rows, depths, by_loads=False):
        self.rows = rows
        self.depths = depths
        lane = lax.broadcasted_iota(jnp.int32, (rows, depths), 1)
        row = lax.broadcasted_iota(jnp.int32, (TILE, depths), 0)
        self.row = lax.broadcasted_iota(jnp.int32, (rows, depths), 0)
        self.tile_row = row
        self.deep = lax.axis_index(GZ)
        near = (self.deep == 0) & (lane < 2) | (self.deep == 1) & (lane >= depths - 2)
        self.near = jnp.where(near, 1.0, 0.0)
        self.zero = jnp.minimum(self.deep, 0)
        self.by_loads = by_loads
        self.pair = lane // 2
        self.low = {n: lane < n for n in (1, 2)}
        self.high = {n: lane >= depths - n for n in (1, 2)}
        self.top = {n: row < n for n in (1, 2)}
        self.bottom = {n: row >= TILE - n for n in (1, 2)}

    def packed(self, strip, x, fields):
        first = jnp.where(self.deep == 0, 2, 0)
        for k, field in enumerate(fields):
            turn = lax.rem(first + 8 * x + 2 * k, self.depths)
            strip = jnp.where(self.pair == 4 * x + k, pltpu.roll(field, turn, 1), strip)
        return strip

    def ends(self, strip, x, k):
        back = self.depths - 8 * x - 2 * k
        turn = jnp.where(self.deep == 0, back % self.depths, back - 2)
        return pltpu.roll(strip, turn, 1) * self.near

    def shallower(self, field, halo, n):
        return pltpu.roll(jnp.where(self.high[n], halo, field), n, 1)

    def deeper(self, field, halo, n):
        return pltpu.roll(jnp.where(self.low[n], halo, field), self.depths - n, 1)

    def forward_z(self, field, halo):
        return forward(
            self.shallower(field, halo, 1),
            field,
            self.deeper(field, halo, 1),
            self.deeper(field, halo, 2),
        )

    def backward_z(self, field, halo):
        return backward(
            self.shallower(field, halo, 2),
            self.shallower(field, halo, 1),
            field,
            self.deeper(field, halo, 1),
        )

    def before(self, field, load, n, halo):
        top = jnp.where(self.top[n], 0.0, pltpu.roll(field[:TILE], n, 0))
        if halo:
            for i in range(n):
                top = jnp.where(self.tile_row == i, halo[n - 1 - i], top)
        if load:
            rest = load(self.zero + (TILE - n), self.rows - TILE)
        else:
            rest = pltpu.roll(field, n, 0)[TILE:]
        return jnp.concatenate([top, rest], axis=0)

    def after(self, field, load, n, halo):
        bottom = pltpu.roll(field[self.rows - TILE :], TILE - n, 0)
        bottom = jnp.where(self.bottom[n], 0.0, bottom)
        if halo:
            for i in range(n):
                bottom = jnp.where(self.tile_row == TILE - n + i, halo[i], bottom)
        if load:
            rest = load(self.zero + n, self.rows - TILE)
        else:
            rest = pltpu.roll(field, self.rows - n, 0)[: self.rows - TILE]
        return jnp.concatenate([rest, bottom], axis=0)

    def forward_y(self, planes, comp, x, halos):
        field = planes(comp, x)
        load = planes.rows(comp, x) if self.by_loads else None
        lower, upper = halos
        return forward(
            self.before(field, load, 1, lower),
            field,
            self.after(field, load, 1, upper),
            self.after(field, load, 2, upper),
        )

    def backward_y(self, planes, comp, x, halos):
        field = planes(comp, x)
        load = planes.rows(comp, x) if self.by_loads else None
        lower, upper = halos
        return backward(
            self.before(field, load, 2, lower),
            self.before(field, load, 1, lower),
            field,
            self.after(field, load, 1, upper),
        )


class Field:
    def __init__(self, count, *parts):
        self.count = count
        self.parts = parts

    def place(self, x):
        if len(self.parts) == 1:
            return self.parts[0], x
        inner, edge = self.parts
        if x in inside(self.count):
            return inner, x - 2
        return edge, ends_of(self.count).index(x)

    def __call__(self, comp, x):
        ref, at = self.place(x)
        return ref[comp, at]

    def rows(self, comp, x):
        ref, at = self.place(x)
        return lambda start, size: ref[comp, at, pl.ds(start, size), :]


def inside(count):
    return range(2, count - 2)


def ends_of(count):
    return (0, 1, count - 2, count - 1)


class Planes:
    def __init__(self, field, tail, head, first=None, second=None):
        self.field = field
        self.count = field.count
        self.first, self.second = first, second
        self.tail, self.head = tail, head
        self.even = even_strike()
        self.any_left = lax.axis_index(GX) > 0
        self.any_right = lax.axis_index(GX) < lax.axis_size(GX) - 1

    def left(self, i):
        plane = jnp.where(self.even, self.second[i], self.first[i])
        return jnp.where(self.any_left, plane, 0.0)

    def right(self, i):
        plane = jnp.where(self.even, self.first[i], self.second[i])
        return jnp.where(self.any_right, plane, 0.0)

    def __call__(self, comp, place):
        if place < 0:
            return self.left(self.tail.index((comp, place)))
        if place >= self.count:
            return self.right(self.head.index((comp, place - self.count)))
        return self.field(comp, place)

    def rows(self, comp, x):
        return self.field.rows(comp, x)

    def forward_x(self, comp, x):
        return forward(self(comp, x - 1), self(comp, x), self(comp, x + 1), self(comp, x + 2))

    def backward_x(self, comp, x):
        return backward(self(comp, x - 2), self(comp, x - 1), self(comp, x), self(comp, x + 1))


class Bands:
    def __init__(self, lower, upper, tail, head):
        self.lower, self.upper = lower, upper
        self.tail, self.head = tail, head

    def __call__(self, comp, x):
        if self.lower is None:
            return (None, None)
        places = [i for i, (c, _) in enumerate(self.tail) if c == comp]
        before = [self.lower[i, pl.ds(x, 1), :] for i in reversed(places)]
        places = [i for i, (c, _) in enumerate(self.head) if c == comp]
        after = [self.upper[i, pl.ds(x, 1), :] for i in places]
        return (before, after)


def looked_up(labels, table, row, count):
    out = jnp.full(labels.shape, table[row, 0], jnp.float32)
    for k in range(1, count):
        out = jnp.where(labels == k, table[row, k], out)
    return out


def even_strike():
    return lax.axis_index(GX) % 2 == 0


def edge_planes(field, tail, head, first_out, second_out):
    even = even_strike()
    pairs = []
    for i in range(first_out.shape[0]):
        comp, place = tail[min(i, len(tail) - 1)]
        right = field(comp, place % field.count)
        comp, place = head[min(i, len(head) - 1)]
        left = field(comp, place % field.count)
        pairs.append((jnp.where(even, right, left), jnp.where(even, left, right)))
    for i, (one, two) in enumerate(pairs):
        first_out[i] = one
        second_out[i] = two


def fault_row(rows):
    return jnp.where(lax.axis_index(GY) == lax.axis_size(GY) // 2, 0, rows - 1)


def pack_kernel(names, r):
    count, rows, depths = r.stress.shape[1:]
    order = (XZ, YZ, ZZ, XX, XY, YY)
    pairs = [(r.stress.at[c], r.stress_out.at[c]) for c in order]
    pairs += [(getattr(r, key), getattr(r, f"{key}_out")) for key in names]
    copies = []
    for i, (source, out) in enumerate(pairs):
        copy = pltpu.make_async_copy(source, out, r.sems.at[i])
        copy.start()
        copies.append(copy)
    edges = Edges(rows, depths)
    for copy in copies[:5]:
        copy.wait()
    edge_planes(Field(count, r.stress_out), STRESS_TAIL, STRESS_HEAD, r.one_out, r.two_out)
    strip = jnp.zeros((rows, depths), jnp.float32)
    for x in range(count):
        strip = edges.packed(strip, x, [r.stress_out[c, x] for c in STRESS_SLOTS])
    set_strip(r, strip)
    for copy in copies[5:]:
        copy.wait()


def grouped(xs, size):
    return [xs[i : i + size] for i in range(0, len(xs), size)]


def set_strip(r, strip):
    r.strip_out[0] = strip
    for i in range(1, STRIP_PLANES):
        r.strip_out[i] = jnp.zeros_like(strip)


def unpack(count, r, edges):
    strip = r.strip[0]
    for x in range(count):
        for k in range(3):
            r.ends[x, k] = edges.ends(strip, x, k)


def velocity_across(planes, x):
    return planes.forward_x(XX, x), planes.backward_x(XY, x), planes.backward_x(XZ, x)


def velocity_inner(first, r):
    count, rows, depths = r.material.shape
    edges = Edges(rows, depths)
    planes = Planes(stress_of(count, r), STRESS_TAIL, STRESS_HEAD)
    band = Bands(getattr(r, "lower", None), getattr(r, "upper", None), STRESS_TAIL_Y, STRESS_HEAD_Y)
    unpack(count, r, edges)

    def beside(x):
        ends = [r.ends[x, k] for k in range(3)]
        return (
            edges.backward_y(planes, XY, x, band(XY, x)) + edges.backward_z(planes(XZ, x), ends[0]),
            edges.forward_y(planes, YY, x, band(YY, x)) + edges.backward_z(planes(YZ, x), ends[1]),
            edges.backward_y(planes, YZ, x, band(YZ, x)) + edges.forward_z(planes(ZZ, x), ends[2]),
        )

    def push(x):
        return DT * looked_up(r.material[x], r.table, 2, CLASSES)

    def new(x):
        rates = zip(velocity_across(planes, x), beside(x))
        return [r.velocity[c, x] + push(x) * (a + b) for c, (a, b) in enumerate(rates)]

    for group in grouped(inside(count), 3 if (count - 4) % 3 == 0 else 2):
        for x, values in [(x, new(x)) for x in group]:
            for c in range(3):
                r.inner_out[c, x - 2] = values[c]
    for group in grouped(ends_of(count), 2):
        for x, values in [(x, (*beside(x), push(x))) for x in group]:
            for c in range(4):
                r.part_out[c, ends_of(count).index(x)] = values[c]
    strip = jnp.zeros((rows, depths), jnp.float32)
    for x in inside(count):
        strip = edges.packed(strip, x, [r.inner_out[c, x - 2] for c in VEL_SLOTS])
    r.strip_inner_out[...] = strip

    row = pl.ds(fault_row(rows), 1)
    lines = {}
    for x in inside(count):
        for i, c in enumerate((0, 2)):
            lines[i * count + x] = r.inner_out[c, x - 2, row, :]
    if first:
        for x in range(count):
            labels = r.material[x, row, :]
            lines[2 * count + x] = looked_up(labels, r.table, 2, CLASSES)
    if hasattr(r, "prestress"):
        own = r.normal.shape[0]
        place = 3 * count
        for c in (0, 1):
            for i in range(own):
                lines[place + c * own + i] = r.prestress[i, pl.ds(c, 1), :]
        for j, field in enumerate((r.normal, r.slip, r.zone, r.mask), 2):
            for i in range(own):
                lines[place + j * own + i] = field[pl.ds(i, 1), :].astype(jnp.float32)
    for i, line in lines.items():
        r.face_inner_out[pl.ds(i, 1), :] = line


def velocity_edge(count, r):
    rows, depths = r.one.shape[1:]
    edges = Edges(rows, depths)
    planes = Planes(stress_of(count, r), STRESS_TAIL, STRESS_HEAD, r.one, r.two)
    places = ends_of(count)
    new = []
    for i, x in enumerate(places):
        rates = [a + r.part[c, i] for c, a in enumerate(velocity_across(planes, x))]
        new.append([r.velocity[c, x] + r.part[3, i] * rate for c, rate in enumerate(rates)])
    faces = r.face_inner[...]
    strip = r.strip_inner[...]
    for i, x in enumerate(places):
        strip = edges.packed(strip, x, [new[i][c] for c in VEL_SLOTS])
        for c in range(3):
            r.edge_out[c, i] = new[i][c]
    r.face_out[...] = faces
    set_strip(r, strip)
    fault = fault_row(rows)
    edge = Field(count, None, r.edge_out)
    lines = {i * count + x: edge.rows(c, x)(fault, 1) for x in places for i, c in enumerate((0, 2))}
    for i, line in lines.items():
        r.face_out[pl.ds(i, 1), :] = line
    edge_planes(edge, VEL_TAIL, VEL_HEAD, r.one_out, r.two_out)


def stress_of(count, r):
    if hasattr(r, "stress"):
        return Field(count, r.stress)
    return Field(count, r.stress_inner, r.stress_edge)


def memory_of(count, r):
    if hasattr(r, "memory"):
        return Field(count, r.memory)
    return Field(count, r.memory_inner, r.memory_edge)


def fault_kernel(first, r):
    own_face, other_face = r.face, r.other
    own_first, other_first = (own_face, other_face) if first else (r.face_first, r.other_first)
    rows, depths = r.strip.shape[1:]
    count = r.change_out.shape[1]
    middle = lax.axis_size(GY) // 2
    side = lax.axis_index(GY)
    plus = side == middle
    minus = side == middle - 1

    def pair(own, other, place):
        mine, theirs = own[pl.ds(place, count), :], other[pl.ds(place, count), :]
        return jnp.where(plus, theirs, mine), jnp.where(plus, mine, theirs)

    if hasattr(r, "still"):
        still = r.still
    else:
        still = r.still_out
        share = (own_face.shape[0] - 3 * count) // 6
        for i in range(6):
            mine = own_face[pl.ds(3 * count + i * share, share), :]
            theirs = other_face[pl.ds(3 * count + i * share, share), :]
            still[i, pl.ds(0, share), :] = jnp.where(plus, theirs, mine)
            still[i, pl.ds(share, share), :] = jnp.where(plus, mine, theirs)
    pre_x, pre_z, normal = still[0], still[1], still[2]
    slip = still[3] if first else r.slip[...]
    zone, mask = still[4], still[5]

    row = lax.broadcasted_iota(jnp.int32, (count, depths), 0) + lax.axis_index(GX) * count
    deep = lax.broadcasted_iota(jnp.int32, (count, depths), 1) + lax.axis_index(GZ) * depths
    inside = (row >= r.anchor[0]) & (row < r.anchor[0] + 2 * PATCH)
    inside = inside & (deep >= r.anchor[1]) & (deep < r.anchor[1] + 2 * PATCH)
    dynamic = 0.4 * looked_up(zone, r.friction, 0, ZONES)
    static = jnp.where(
        inside, dynamic, dynamic + 0.5 * looked_up(zone, r.friction, 1, ZONES)
    )
    distance = 0.2 * looked_up(zone, r.friction, 2, ZONES)
    minus_x, plus_x = pair(own_face, other_face, 0)
    minus_z, plus_z = pair(own_face, other_face, count)
    minus_b, plus_b = pair(own_first, other_first, 2 * count)
    bsum = minus_b + plus_b
    trial_x = (plus_x - minus_x) / (DT * bsum) + pre_x
    trial_z = (plus_z - minus_z) / (DT * bsum) + pre_z
    size = jnp.sqrt(trial_x * trial_x + trial_z * trial_z)
    weaken = jnp.minimum(slip / distance, 1.0)
    strength = (static - (static - dynamic) * weaken) * normal
    factor = jnp.where(mask == 1.0, strength / jnp.maximum(size, strength), 1.0)
    new_slip = slip + DT * DT * bsum * (size - size * factor)
    half = r.slip_out.shape[0]
    if half < count:
        new_slip = jnp.where(plus, new_slip[half:], new_slip[:half])
    r.slip_out[...] = new_slip
    sign = jnp.where(minus, DT, 0.0) * minus_b - jnp.where(plus, DT, 0.0) * plus_b
    change_x = (trial_x * factor - pre_x) * sign
    change_z = (trial_z * factor - pre_z) * sign
    r.change_out[0] = change_x
    r.change_out[1] = change_z

    fault = fault_row(rows)
    on_fault = lax.broadcasted_iota(jnp.int32, (rows, depths), 0) == fault
    even = even_strike()
    still_line = jnp.zeros((1, depths), jnp.float32)

    def line(planes, i):
        comp, place = planes[min(i, len(planes) - 1)]
        return still_line if comp == 1 else r.change_out[comp // 2, pl.ds(place % count, 1), :]

    pairs = []
    for i in range(r.one_out.shape[0]):
        right, left = line(VEL_TAIL, i), line(VEL_HEAD, i)
        one, two = jnp.where(even, right, left), jnp.where(even, left, right)
        one = r.one[i] + jnp.where(on_fault, one, 0.0)
        pairs.append((one, r.two[i] + jnp.where(on_fault, two, 0.0)))
    for i, (one, two) in enumerate(pairs):
        r.one_out[i] = one
        r.two_out[i] = two
    ends = jnp.zeros((count, depths), jnp.float32)
    pair = lax.broadcasted_iota(jnp.int32, (count, depths), 1) // 2
    place = 4 * lax.broadcasted_iota(jnp.int32, (count, depths), 0)
    upper = lax.axis_index(GZ) == 0
    for k, field in ((0, change_x), (2, change_z)):
        turned = jnp.where(upper, pltpu.roll(field, 2, 1), field)
        turned = pltpu.roll(turned, 2 * k, 1, stride=8, stride_axis=0)
        ends = jnp.where(pair == place + k, turned, ends)
    line = jnp.sum(ends, axis=0, keepdims=True)
    set_strip(r, r.strip[0] + jnp.where(on_fault, line, 0.0))


def elastic_rates(planes, x, beside, lame, shear):
    eyy, ezz, eyz, along_y, along_z = beside
    exx = planes.backward_x(0, x)
    exy = along_y + planes.forward_x(1, x)
    exz = along_z + planes.forward_x(2, x)
    bulk = lame * (exx + eyy + ezz)
    double = 2.0 * shear
    return (
        bulk + double * exx,
        bulk + double * eyy,
        bulk + double * ezz,
        shear * exy,
        shear * exz,
        shear * eyz,
    )


def stress_new(x, elastic, decay, gain, stress, memory):
    kept = [decay * memory(c, x) - gain * elastic[c] for c in range(6)]
    return [stress(c, x) + DT * (elastic[c] + kept[c]) for c in range(6)], kept


def stress_inner(last, r):
    count, rows, depths = r.material.shape
    edges = Edges(rows, depths, by_loads=True)
    on_fault = edges.row == fault_row(rows)
    free = Field(count, r.inner, r.edge)
    for x in range(count):
        for c in (0, 2):
            line = r.change[c // 2, pl.ds(x, 1), :]
            r.velocity_out[c, x] = free(c, x) + jnp.where(on_fault, line, 0.0)
        r.velocity_out[1, x] = free(1, x)
    planes = Planes(Field(count, r.velocity_out), VEL_TAIL, VEL_HEAD)
    copies = []

    def copy_out(source, out):
        copy = pltpu.make_async_copy(source, out, r.sems.at[len(copies)])
        copy.start()
        copies.append(copy)

    if last:
        copy_out(r.velocity_out, r.new_velocity_out)
        if hasattr(r, "slip"):
            copy_out(r.slip, r.new_slip_out)
        stress_out, memory_out = r.stress_held, r.memory_held
    else:
        stress_out, memory_out = r.stress_inner_out, r.memory_inner_out

    def write(x, new, kept):
        for c in range(6):
            stress_out[c, x - 2] = new[c]
            memory_out[c, x - 2] = kept[c]
        if last and x % 2 == 1:
            held, out = pl.ds(x - 3, 2), pl.ds(x - 1, 2)
            copy_out(stress_out.at[:, held], r.stress_out.at[:, out])
            copy_out(memory_out.at[:, held], r.memory_out.at[:, out])

    band = Bands(getattr(r, "lower", None), getattr(r, "upper", None), VEL_TAIL_Y, VEL_HEAD_Y)
    stress, memory = stress_of(count, r), memory_of(count, r)
    unpack(count, r, edges)

    def beside(x):
        in_x, in_y, in_z = [r.ends[x, k] for k in range(3)]
        return (
            edges.backward_y(planes, 1, x, band(1, x)),
            edges.backward_z(planes(2, x), in_z),
            edges.forward_z(planes(1, x), in_y) + edges.forward_y(planes, 2, x, band(2, x)),
            edges.forward_y(planes, 0, x, band(0, x)),
            edges.forward_z(planes(0, x), in_x),
        )

    def moduli(x):
        return [looked_up(r.material[x], r.table, i, CLASSES) for i in (0, 1)]

    def fading(x):
        labels = r.material[x]
        decay = jnp.exp(-DT / looked_up(labels, r.table, 3, CLASSES))
        return decay, (1.0 - decay) * (0.3 * looked_up(labels, r.table, 4, CLASSES))

    for group in grouped(inside(count), 2):
        for x, elastic in [(x, elastic_rates(planes, x, beside(x), *moduli(x))) for x in group]:
            write(x, *stress_new(x, elastic, *fading(x), stress, memory))
    for group in grouped(ends_of(count), 2):
        for x, values in [(x, (*beside(x), *moduli(x), *fading(x))) for x in group]:
            for c in range(9):
                r.part_out[c, ends_of(count).index(x)] = values[c]
    if last:
        for copy in copies:
            copy.wait()
    else:
        strip = jnp.zeros((rows, depths), jnp.float32)
        for x in inside(count):
            strip = edges.packed(strip, x, [r.stress_inner_out[c, x - 2] for c in STRESS_SLOTS])
        r.strip_inner_out[...] = strip


def stress_edge(count, last, r):
    rows, depths = r.one.shape[1:]
    edges = Edges(rows, depths)
    planes = Planes(Field(count, r.velocity), VEL_TAIL, VEL_HEAD, r.one, r.two)
    places = ends_of(count)
    stress, memory = stress_of(count, r), memory_of(count, r)
    copies = []

    def copy_out(source, out, span):
        copy = pltpu.make_async_copy(source, out.at[:, span], r.sems.at[len(copies)])
        copy.start()
        copies.append(copy)

    if last:
        stress_out, memory_out = r.stress_held, r.memory_held
    else:
        stress_out, memory_out = r.stress_edge_out, r.memory_edge_out

    def elastic(i, x):
        part = [r.part[c, i] for c in range(7)]
        return elastic_rates(planes, x, part[:5], *part[5:])

    for group in grouped(list(enumerate(places)), 2):
        for (i, x), rates in [(at, elastic(*at)) for at in group]:
            new, kept = stress_new(x, rates, r.part[7, i], r.part[8, i], stress, memory)
            for c in range(6):
                stress_out[c, i] = new[c]
                memory_out[c, i] = kept[c]
        if last:
            held, span = pl.ds(group[0][0], 2), pl.ds(group[0][1], 2)
            copy_out(stress_out.at[:, held], r.stress_out, span)
            copy_out(memory_out.at[:, held], r.memory_out, span)
    if last:
        for copy in copies:
            copy.wait()
    else:
        strip = r.strip_inner[...]
        for i, x in enumerate(places):
            strip = edges.packed(strip, x, [stress_out[c, i] for c in STRESS_SLOTS])
        set_strip(r, strip)
        edge = Field(count, None, stress_out)
        edge_planes(edge, STRESS_TAIL, STRESS_HEAD, r.one_out, r.two_out)


SCALARS = ("table", "friction", "anchor")


def call(kernel, name, ins, outs, scratch=None, apart=(), onto=(), micros=1, vmem=6):
    scratch = scratch or {}
    names = [*ins, *(f"{key}_out" for key in outs), *scratch]

    def body(*refs):
        kernel(types.SimpleNamespace(**dict(zip(names, refs))))

    def place(key):
        if key in apart:
            return pl.BlockSpec(memory_space=pltpu.HBM)
        return pl.BlockSpec(memory_space=pltpu.SMEM if key in SCALARS else pltpu.VMEM)

    shapes = [
        shape if hasattr(shape, "dtype") else jax.ShapeDtypeStruct(shape, jnp.float32)
        for shape in outs.values()
    ]
    result = pl.pallas_call(
        body,
        out_shape=shapes,
        in_specs=[place(key) for key in ins],
        out_specs=[place(f"{key}_out") for key in outs],
        scratch_shapes=list(scratch.values()),
        name=name,
        input_output_aliases={
            list(ins).index(key): list(outs).index(onto[key]) for key in onto
        },
        cost_estimate=pl.CostEstimate(
            flops=0, bytes_accessed=micros * 3_690_000, transcendentals=0
        ),
        compiler_params=pltpu.CompilerParams(vmem_limit_bytes=vmem * 2**20),
    )(*ins.values())
    return dict(zip(outs, result))


def along(axis, count, skip=()):
    up = [(i, i + 1) for i in range(count - 1) if i not in skip]
    return (axis, up), (axis, [(b, a) for a, b in up])


def strike_swaps(count):
    halves = lax.axis_size(GZ)
    routes = []
    for start in (0, 1):
        partner = {}
        for i in range(start, count - 1, 2):
            for half in range(halves):
                one, other = i * halves + half, (i + 1) * halves + half
                partner[one], partner[other] = other, one
        for i in range(count * halves):
            partner.setdefault(i, i ^ 1)
        routes.append(((GX, GZ), sorted(partner.items())))
    return routes


def sent(block, route):
    return lax.ppermute(block, *route)


def whole(parts, name):
    if name in parts:
        return parts[name]
    inner, edge = parts[f"{name}_inner"], parts[f"{name}_edge"]
    return jnp.concatenate([edge[:, :2], inner, edge[:, 2:]], axis=1)


def edge_rows(field, rows):
    count = field.shape[2]
    return jnp.stack([field[c, :, place % count, :] for c, place in rows])


def shards(
    velocity,
    stress,
    memory,
    material,
    material_table,
    fault_mask,
    zone_label,
    patch_anchor,
    friction_table,
    prestress,
    normal_stress,
    slip_path,
):
    _, count, rows, depths = velocity.shape
    sides = lax.axis_size(GY)
    middle = sides // 2
    banded = sides > 2
    swaps = strike_swaps(lax.axis_size(GX))
    up_y, down_y = along(GY, sides, (middle - 1,))
    across = (GY, [(middle - 1, middle), (middle, middle - 1)])
    deep = (GZ, [(0, 1), (1, 0)])

    plane = (rows, depths)
    edge_shape = (max(len(STRESS_TAIL), len(STRESS_HEAD)), *plane)
    travelling = {"one": edge_shape, "two": edge_shape, "strip": (STRIP_PLANES, *plane)}
    inner, edge = (count - 4, *plane), (4, *plane)
    ends = {"ends": pltpu.VMEM((count, 3, *plane), jnp.float32)}

    def travelled(packed):
        two = sent(packed["two"], swaps[1])
        one = sent(packed["one"], swaps[0])
        strip = sent(packed["strip"], deep)
        return {"strip": strip}, {"one": one, "two": two}

    def bands(field, tail, head):
        if not banded:
            return {}
        lower, upper = edge_rows(field, tail), edge_rows(field, head)
        return {"lower": sent(lower, up_y), "upper": sent(upper, down_y)}

    if banded:
        still = jnp.stack(
            [
                prestress[:, 0],
                prestress[:, 1],
                normal_stress,
                slip_path,
                zone_label.astype(jnp.float32),
                fault_mask.astype(jnp.float32),
            ]
        )
        still = {"still": lax.all_gather(still, GY, axis=1, tiled=True)}
    else:
        still = {}

    held = {"velocity": velocity, "material": material}
    if not banded:
        held.update(prestress=prestress, normal=normal_stress, slip=slip_path)
        held.update(zone=zone_label, mask=fault_mask)
    ins = {"stress": stress, **held}
    packed = call(
        functools.partial(pack_kernel, list(held)),
        "pack",
        {key: pltpu.with_memory_space_constraint(a, pltpu.HBM) for key, a in ins.items()},
        {**travelling, **{key: jax.ShapeDtypeStruct(a.shape, a.dtype) for key, a in ins.items()}},
        scratch={"sems": pltpu.SemaphoreType.DMA((6 + len(held),))},
        apart=list(ins),
    )
    velocity = packed["velocity"]
    parts = {"stress": packed["stress"], "memory": memory}
    props = {"material": packed["material"], "table": material_table}
    friction_ins = {key: packed[key] for key in held if key not in ("velocity", "material")}
    for step in range(STEPS):
        first, last = step == 0, step == STEPS - 1
        held_stress = {key: parts[key] for key in parts if key.startswith("stress")}
        strip, halos = travelled(packed)
        ins = {"velocity": velocity, **held_stress, **props, **strip}
        if banded:
            ins.update(bands(whole(parts, "stress"), STRESS_TAIL_Y, STRESS_HEAD_Y))
        face_rows = 2 * count
        if first:
            face_rows += count
            if not banded:
                ins.update(friction_ins)
                face_rows += 6 * normal_stress.shape[0]
        outs = {"inner": (3, *inner), "part": (4, *edge), "strip_inner": plane}
        outs["face_inner"] = (face_rows, depths)
        free = call(
            functools.partial(velocity_inner, first),
            "velocity_inner",
            ins,
            outs,
            scratch=ends,
            micros=3,
        )
        ins = {"velocity": velocity, **held_stress, **halos}
        ins.update({key: free[key] for key in outs if key != "inner"})
        packed = call(
            functools.partial(velocity_edge, count),
            "velocity_edge",
            ins,
            {"edge": (3, *edge), "face": (face_rows, depths), **travelling},
        )
        free = {"inner": free["inner"], "edge": packed["edge"]}
        face = packed["face"]
        other = sent(face, across)
        ins = {key: packed[key] for key in travelling}
        ins.update(face=face, other=other, friction=friction_table, anchor=patch_anchor, **still)
        if first:
            faces = {"face_first": face, "other_first": other}
        else:
            ins.update(slip=slip, **faces)
        outs = {"change": (2, count, depths), "slip": (count, depths), **travelling}
        if last and not banded:
            outs["slip"] = (count // sides, depths)
        if not still:
            outs["still"] = (6, count, depths)
        packed = call(functools.partial(fault_kernel, first), "fault", ins, outs, vmem=2)
        slip = packed["slip"]
        if not still:
            still = {"still": packed["still"]}
        strip, halos = travelled(packed)
        ins = {**free, "change": packed["change"], **parts, **props, **strip}
        if banded:
            joined = jnp.concatenate(
                [free["edge"][:, :2], free["inner"], free["edge"][:, 2:]], axis=1
            )
            band = bands(joined, VEL_TAIL_Y, VEL_HEAD_Y)
        else:
            band = {}
        outs = {"velocity": velocity.shape, "part": (9, *edge)}
        extra = {"scratch": ends}
        if last:
            outs.update(new_velocity=velocity.shape, stress=stress.shape, memory=memory.shape)
            extra["apart"] = ["new_velocity_out", "stress_out", "memory_out"]
            if not banded:
                ins["slip"] = slip
                outs["new_slip"] = slip.shape
                extra["apart"].append("new_slip_out")
            held = pltpu.VMEM((6, *inner), jnp.float32)
            sems = pltpu.SemaphoreType.DMA((count,))
            extra["scratch"] = {"stress_held": held, "memory_held": held, "sems": sems, **ends}
        else:
            outs.update(stress_inner=(6, *inner), memory_inner=(6, *inner), strip_inner=plane)
        done = call(
            functools.partial(stress_inner, last),
            "stress_inner",
            {**ins, **band},
            outs,
            micros=3,
            vmem=11,
            **extra,
        )
        velocity = done["velocity"]
        ins = {"velocity": velocity, "part": done["part"], **parts, **halos}
        if last:
            ins.update(stress_done=done["stress"], memory_done=done["memory"])
            held = pltpu.VMEM((6, *edge), jnp.float32)
            packed = call(
                functools.partial(stress_edge, count, last),
                "stress_edge",
                ins,
                {"stress": stress.shape, "memory": memory.shape},
                scratch={
                    "stress_held": held,
                    "memory_held": held,
                    "sems": pltpu.SemaphoreType.DMA((4,)),
                },
                apart=("stress_done", "memory_done", "stress_out", "memory_out"),
                onto={"stress_done": "stress", "memory_done": "memory"},
                vmem=10,
            )
            velocity = done["new_velocity"]
            stress, memory = packed["stress"], packed["memory"]
            slip = done.get("new_slip", slip)
        else:
            ins["strip_inner"] = done["strip_inner"]
            packed = call(
                functools.partial(stress_edge, count, last),
                "stress_edge",
                ins,
                {"stress_edge": (6, *edge), "memory_edge": (6, *edge), **travelling},
                vmem=10,
            )
            parts = {
                "stress_inner": done["stress_inner"],
                "stress_edge": packed["stress_edge"],
                "memory_inner": done["memory_inner"],
                "memory_edge": packed["memory_edge"],
            }
    if banded:
        held = jnp.where(lax.axis_index(GY) == middle, slip, 0.0)
        slip = lax.psum_scatter(held, GY, scatter_dimension=0, tiled=True)
    return (velocity, stress, memory, slip)


def solution(mesh):
    in_specs = (
        P(None, (ENS, GX), GY, GZ),
        P(None, (ENS, GX), GY, GZ),
        P(None, (ENS, GX), GY, GZ),
        P((ENS, GX), GY, GZ),
        P(None, ENS),
        P((ENS, GX, GY), GZ),
        P((ENS, GX, GY), GZ),
        P(ENS),
        P(None, ENS),
        P((ENS, GX, GY), None, GZ),
        P((ENS, GX, GY), GZ),
        P((ENS, GX, GY), GZ),
    )
    out_specs = (
        P(None, (ENS, GX), GY, GZ),
        P(None, (ENS, GX), GY, GZ),
        P(None, (ENS, GX), GY, GZ),
        P((ENS, GX, GY), GZ),
    )
    return jax.shard_map(shards, mesh=mesh, in_specs=in_specs, out_specs=out_specs, check_vma=False)
```

```python
import functools
import types

import jax
import jax.numpy as jnp
from jax import lax
from jax.experimental import pallas as pl
from jax.experimental.pallas import tpu as pltpu
from jax.sharding import PartitionSpec as P

STEPS = 2
CLASSES = 8
ZONES = 4
PATCH = 8

NEAR = 9.0 / 8.0
FAR = -1.0 / 24.0
DT = 0.15
TILE = 8
ENS, GX, GY, GZ = "ens", "gx", "gy", "gz"
STRIP_PLANES = 6

XX, YY, ZZ, XY, XZ, YZ = range(6)

STRESS_TAIL = ((XX, -1), (XY, -2), (XY, -1), (XZ, -2), (XZ, -1))
STRESS_HEAD = ((XX, 0), (XX, 1), (XY, 0), (XZ, 0))
VEL_TAIL = ((0, -2), (0, -1), (1, -1), (2, -1))
VEL_HEAD = ((0, 0), (1, 0), (1, 1), (2, 0), (2, 1))
STRESS_TAIL_Y = ((YY, -1), (XY, -2), (XY, -1), (YZ, -2), (YZ, -1))
STRESS_HEAD_Y = ((YY, 0), (YY, 1), (XY, 0), (YZ, 0))
VEL_TAIL_Y = ((1, -2), (1, -1), (0, -1), (2, -1))
VEL_HEAD_Y = ((1, 0), (0, 0), (0, 1), (2, 0), (2, 1))
STRESS_SLOTS = (XZ, YZ, ZZ)
VEL_SLOTS = (0, 1, 2)


def forward(before, here, after, after_2):
    return NEAR * (after - here) + FAR * (after_2 - before)


def backward(before_2, before, here, after):
    return NEAR * (here - before) + FAR * (after - before_2)


class Edges:
    def __init__(self, rows, depths, by_loads=False):
        self.rows = rows
        self.depths = depths
        lane = lax.broadcasted_iota(jnp.int32, (rows, depths), 1)
        row = lax.broadcasted_iota(jnp.int32, (TILE, depths), 0)
        self.row = lax.broadcasted_iota(jnp.int32, (rows, depths), 0)
        self.tile_row = row
        self.deep = lax.axis_index(GZ)
        near = (self.deep == 0) & (lane < 2) | (self.deep == 1) & (lane >= depths - 2)
        self.near = jnp.where(near, 1.0, 0.0)
        self.zero = jnp.minimum(self.deep, 0)
        self.by_loads = by_loads
        self.pair = lane // 2
        self.low = {n: lane < n for n in (1, 2)}
        self.high = {n: lane >= depths - n for n in (1, 2)}
        self.top = {n: row < n for n in (1, 2)}
        self.bottom = {n: row >= TILE - n for n in (1, 2)}

    def packed(self, strip, x, fields):
        first = jnp.where(self.deep == 0, 2, 0)
        for k, field in enumerate(fields):
            turn = lax.rem(first + 8 * x + 2 * k, self.depths)
            strip = jnp.where(self.pair == 4 * x + k, pltpu.roll(field, turn, 1), strip)
        return strip

    def ends(self, strip, x, k):
        back = self.depths - 8 * x - 2 * k
        turn = jnp.where(self.deep == 0, back % self.depths, back - 2)
        return pltpu.roll(strip, turn, 1) * self.near

    def shallower(self, field, halo, n):
        return pltpu.roll(jnp.where(self.high[n], halo, field), n, 1)

    def deeper(self, field, halo, n):
        return pltpu.roll(jnp.where(self.low[n], halo, field), self.depths - n, 1)

    def forward_z(self, field, halo):
        return forward(
            self.shallower(field, halo, 1),
            field,
            self.deeper(field, halo, 1),
            self.deeper(field, halo, 2),
        )

    def backward_z(self, field, halo):
        return backward(
            self.shallower(field, halo, 2),
            self.shallower(field, halo, 1),
            field,
            self.deeper(field, halo, 1),
        )

    def before(self, field, load, n, halo):
        top = jnp.where(self.top[n], 0.0, pltpu.roll(field[:TILE], n, 0))
        if halo:
            for i in range(n):
                top = jnp.where(self.tile_row == i, halo[n - 1 - i], top)
        if load:
            rest = load(self.zero + (TILE - n), self.rows - TILE)
        else:
            rest = pltpu.roll(field, n, 0)[TILE:]
        return jnp.concatenate([top, rest], axis=0)

    def after(self, field, load, n, halo):
        bottom = pltpu.roll(field[self.rows - TILE :], TILE - n, 0)
        bottom = jnp.where(self.bottom[n], 0.0, bottom)
        if halo:
            for i in range(n):
                bottom = jnp.where(self.tile_row == TILE - n + i, halo[i], bottom)
        if load:
            rest = load(self.zero + n, self.rows - TILE)
        else:
            rest = pltpu.roll(field, self.rows - n, 0)[: self.rows - TILE]
        return jnp.concatenate([rest, bottom], axis=0)

    def forward_y(self, planes, comp, x, halos):
        field = planes(comp, x)
        load = planes.rows(comp, x) if self.by_loads else None
        lower, upper = halos
        return forward(
            self.before(field, load, 1, lower),
            field,
            self.after(field, load, 1, upper),
            self.after(field, load, 2, upper),
        )

    def backward_y(self, planes, comp, x, halos):
        field = planes(comp, x)
        load = planes.rows(comp, x) if self.by_loads else None
        lower, upper = halos
        return backward(
            self.before(field, load, 2, lower),
            self.before(field, load, 1, lower),
            field,
            self.after(field, load, 1, upper),
        )


class Field:
    def __init__(self, count, *parts):
        self.count = count
        self.parts = parts

    def place(self, x):
        if len(self.parts) == 1:
            return self.parts[0], x
        inner, edge = self.parts
        if x in inside(self.count):
            return inner, x - 2
        return edge, ends_of(self.count).index(x)

    def __call__(self, comp, x):
        ref, at = self.place(x)
        return ref[comp, at]

    def rows(self, comp, x):
        ref, at = self.place(x)
        return lambda start, size: ref[comp, at, pl.ds(start, size), :]


def inside(count):
    return range(2, count - 2)


def ends_of(count):
    return (0, 1, count - 2, count - 1)


class Planes:
    def __init__(self, field, tail, head, first=None, second=None):
        self.field = field
        self.count = field.count
        self.first, self.second = first, second
        self.tail, self.head = tail, head
        self.even = even_strike()
        self.any_left = lax.axis_index(GX) > 0
        self.any_right = lax.axis_index(GX) < lax.axis_size(GX) - 1

    def left(self, i):
        plane = jnp.where(self.even, self.second[i], self.first[i])
        return jnp.where(self.any_left, plane, 0.0)

    def right(self, i):
        plane = jnp.where(self.even, self.first[i], self.second[i])
        return jnp.where(self.any_right, plane, 0.0)

    def __call__(self, comp, place):
        if place < 0:
            return self.left(self.tail.index((comp, place)))
        if place >= self.count:
            return self.right(self.head.index((comp, place - self.count)))
        return self.field(comp, place)

    def rows(self, comp, x):
        return self.field.rows(comp, x)

    def forward_x(self, comp, x):
        return forward(self(comp, x - 1), self(comp, x), self(comp, x + 1), self(comp, x + 2))

    def backward_x(self, comp, x):
        return backward(self(comp, x - 2), self(comp, x - 1), self(comp, x), self(comp, x + 1))


class Bands:
    def __init__(self, lower, upper, tail, head):
        self.lower, self.upper = lower, upper
        self.tail, self.head = tail, head

    def __call__(self, comp, x):
        if self.lower is None:
            return (None, None)
        places = [i for i, (c, _) in enumerate(self.tail) if c == comp]
        before = [self.lower[i, pl.ds(x, 1), :] for i in reversed(places)]
        places = [i for i, (c, _) in enumerate(self.head) if c == comp]
        after = [self.upper[i, pl.ds(x, 1), :] for i in places]
        return (before, after)


def looked_up(labels, table, row, count):
    out = jnp.full(labels.shape, table[row, 0], jnp.float32)
    for k in range(1, count):
        out = jnp.where(labels == k, table[row, k], out)
    return out


def even_strike():
    return lax.axis_index(GX) % 2 == 0


def edge_planes(field, tail, head, first_out, second_out):
    even = even_strike()
    pairs = []
    for i in range(first_out.shape[0]):
        comp, place = tail[min(i, len(tail) - 1)]
        right = field(comp, place % field.count)
        comp, place = head[min(i, len(head) - 1)]
        left = field(comp, place % field.count)
        pairs.append((jnp.where(even, right, left), jnp.where(even, left, right)))
    for i, (one, two) in enumerate(pairs):
        first_out[i] = one
        second_out[i] = two


def fault_row(rows):
    return jnp.where(lax.axis_index(GY) == lax.axis_size(GY) // 2, 0, rows - 1)


def pack_kernel(r):
    count, rows, depths = r.stress.shape[1:]
    pieces = [(comp, 0, count) for comp in STRESS_SLOTS]
    some = {}
    for comp, place in STRESS_TAIL + STRESS_HEAD:
        if comp not in STRESS_SLOTS:
            some.setdefault((comp, place < 0), []).append(place % count)
    pieces += [(comp, min(at), max(at) + 1) for (comp, _), at in some.items()]
    copies = []
    for i, (comp, start, stop) in enumerate(pieces):
        span = pl.ds(start, stop - start)
        copy = pltpu.make_async_copy(r.stress.at[comp, span], r.held.at[comp, span], r.sems.at[i])
        copy.start()
        copies.append(copy)
    edges = Edges(rows, depths)
    for copy in copies:
        copy.wait()
    edge_planes(Field(count, r.held), STRESS_TAIL, STRESS_HEAD, r.one_out, r.two_out)
    strip = jnp.zeros((rows, depths), jnp.float32)
    for x in range(count):
        strip = edges.packed(strip, x, [r.held[c, x] for c in STRESS_SLOTS])
    set_strip(r, strip)


def bring_kernel(names, r):
    copies = []
    for i, key in enumerate(names):
        source, out = getattr(r, key), getattr(r, f"{key}_out")
        copies.append(pltpu.make_async_copy(source, out, r.sems.at[i]))
    for copy in copies:
        copy.start()
    for copy in copies:
        copy.wait()


def grouped(xs, size):
    return [xs[i : i + size] for i in range(0, len(xs), size)]


def set_strip(r, strip):
    r.strip_out[0] = strip
    for i in range(1, STRIP_PLANES):
        r.strip_out[i] = jnp.zeros_like(strip)


def unpack(count, r, edges):
    strip = r.strip[0]
    for x in range(count):
        for k in range(3):
            r.ends[x, k] = edges.ends(strip, x, k)


def velocity_across(planes, x):
    return planes.forward_x(XX, x), planes.backward_x(XY, x), planes.backward_x(XZ, x)


def velocity_inner(first, r):
    count, rows, depths = r.material.shape
    edges = Edges(rows, depths)
    planes = Planes(stress_of(count, r), STRESS_TAIL, STRESS_HEAD)
    band = Bands(getattr(r, "lower", None), getattr(r, "upper", None), STRESS_TAIL_Y, STRESS_HEAD_Y)
    unpack(count, r, edges)

    def beside(x):
        ends = [r.ends[x, k] for k in range(3)]
        return (
            edges.backward_y(planes, XY, x, band(XY, x)) + edges.backward_z(planes(XZ, x), ends[0]),
            edges.forward_y(planes, YY, x, band(YY, x)) + edges.backward_z(planes(YZ, x), ends[1]),
            edges.backward_y(planes, YZ, x, band(YZ, x)) + edges.forward_z(planes(ZZ, x), ends[2]),
        )

    def push(x):
        return DT * looked_up(r.material[x], r.table, 2, CLASSES)

    def new(x):
        rates = zip(velocity_across(planes, x), beside(x))
        return [r.velocity[c, x] + push(x) * (a + b) for c, (a, b) in enumerate(rates)]

    for group in grouped(inside(count), 3 if (count - 4) % 3 == 0 else 2):
        for x, values in [(x, new(x)) for x in group]:
            for c in range(3):
                r.inner_out[c, x - 2] = values[c]
    for group in grouped(ends_of(count), 2):
        for x, values in [(x, (*beside(x), push(x))) for x in group]:
            for c in range(4):
                r.part_out[c, ends_of(count).index(x)] = values[c]
    strip = jnp.zeros((rows, depths), jnp.float32)
    for x in inside(count):
        strip = edges.packed(strip, x, [r.inner_out[c, x - 2] for c in VEL_SLOTS])
    r.strip_inner_out[...] = strip

    row = pl.ds(fault_row(rows), 1)
    lines = {}
    for x in inside(count):
        for i, c in enumerate((0, 2)):
            lines[i * count + x] = r.inner_out[c, x - 2, row, :]
    if first:
        for x in range(count):
            labels = r.material[x, row, :]
            lines[2 * count + x] = looked_up(labels, r.table, 2, CLASSES)
    if hasattr(r, "prestress"):
        own = r.normal.shape[0]
        place = 3 * count
        for c in (0, 1):
            for i in range(own):
                lines[place + c * own + i] = r.prestress[i, pl.ds(c, 1), :]
        for j, field in enumerate((r.normal, r.slip, r.zone, r.mask), 2):
            for i in range(own):
                lines[place + j * own + i] = field[pl.ds(i, 1), :].astype(jnp.float32)
    for i, line in lines.items():
        r.face_inner_out[pl.ds(i, 1), :] = line


def velocity_edge(count, r):
    rows, depths = r.one.shape[1:]
    edges = Edges(rows, depths)
    planes = Planes(stress_of(count, r), STRESS_TAIL, STRESS_HEAD, r.one, r.two)
    places = ends_of(count)
    new = []
    for i, x in enumerate(places):
        rates = [a + r.part[c, i] for c, a in enumerate(velocity_across(planes, x))]
        new.append([r.velocity[c, x] + r.part[3, i] * rate for c, rate in enumerate(rates)])
    faces = r.face_inner[...]
    strip = r.strip_inner[...]
    for i, x in enumerate(places):
        strip = edges.packed(strip, x, [new[i][c] for c in VEL_SLOTS])
        for c in range(3):
            r.edge_out[c, i] = new[i][c]
    r.face_out[...] = faces
    set_strip(r, strip)
    fault = fault_row(rows)
    edge = Field(count, None, r.edge_out)
    lines = {i * count + x: edge.rows(c, x)(fault, 1) for x in places for i, c in enumerate((0, 2))}
    for i, line in lines.items():
        r.face_out[pl.ds(i, 1), :] = line
    edge_planes(edge, VEL_TAIL, VEL_HEAD, r.one_out, r.two_out)


def stress_of(count, r):
    if hasattr(r, "stress"):
        return Field(count, r.stress)
    return Field(count, r.stress_inner, r.stress_edge)


def memory_of(count, r):
    if hasattr(r, "memory"):
        return Field(count, r.memory)
    return Field(count, r.memory_inner, r.memory_edge)


def fault_kernel(first, r):
    own_face, other_face = r.face, r.other
    own_first, other_first = (own_face, other_face) if first else (r.face_first, r.other_first)
    rows, depths = r.strip.shape[1:]
    count = r.change_out.shape[1]
    middle = lax.axis_size(GY) // 2
    side = lax.axis_index(GY)
    plus = side == middle
    minus = side == middle - 1

    def pair(own, other, place):
        mine, theirs = own[pl.ds(place, count), :], other[pl.ds(place, count), :]
        return jnp.where(plus, theirs, mine), jnp.where(plus, mine, theirs)

    if hasattr(r, "still"):
        still = r.still
    else:
        still = r.still_out
        share = (own_face.shape[0] - 3 * count) // 6
        for i in range(6):
            mine = own_face[pl.ds(3 * count + i * share, share), :]
            theirs = other_face[pl.ds(3 * count + i * share, share), :]
            still[i, pl.ds(0, share), :] = jnp.where(plus, theirs, mine)
            still[i, pl.ds(share, share), :] = jnp.where(plus, mine, theirs)
    pre_x, pre_z, normal = still[0], still[1], still[2]
    slip = still[3] if first else r.slip[...]
    zone, mask = still[4], still[5]

    row = lax.broadcasted_iota(jnp.int32, (count, depths), 0) + lax.axis_index(GX) * count
    deep = lax.broadcasted_iota(jnp.int32, (count, depths), 1) + lax.axis_index(GZ) * depths
    inside = (row >= r.anchor[0]) & (row < r.anchor[0] + 2 * PATCH)
    inside = inside & (deep >= r.anchor[1]) & (deep < r.anchor[1] + 2 * PATCH)
    dynamic = 0.4 * looked_up(zone, r.friction, 0, ZONES)
    static = jnp.where(
        inside, dynamic, dynamic + 0.5 * looked_up(zone, r.friction, 1, ZONES)
    )
    distance = 0.2 * looked_up(zone, r.friction, 2, ZONES)
    minus_x, plus_x = pair(own_face, other_face, 0)
    minus_z, plus_z = pair(own_face, other_face, count)
    minus_b, plus_b = pair(own_first, other_first, 2 * count)
    bsum = minus_b + plus_b
    trial_x = (plus_x - minus_x) / (DT * bsum) + pre_x
    trial_z = (plus_z - minus_z) / (DT * bsum) + pre_z
    size = jnp.sqrt(trial_x * trial_x + trial_z * trial_z)
    weaken = jnp.minimum(slip / distance, 1.0)
    strength = (static - (static - dynamic) * weaken) * normal
    factor = jnp.where(mask == 1.0, strength / jnp.maximum(size, strength), 1.0)
    new_slip = slip + DT * DT * bsum * (size - size * factor)
    half = r.slip_out.shape[0]
    if half < count:
        new_slip = jnp.where(plus, new_slip[half:], new_slip[:half])
    r.slip_out[...] = new_slip
    sign = jnp.where(minus, DT, 0.0) * minus_b - jnp.where(plus, DT, 0.0) * plus_b
    change_x = (trial_x * factor - pre_x) * sign
    change_z = (trial_z * factor - pre_z) * sign
    r.change_out[0] = change_x
    r.change_out[1] = change_z

    fault = fault_row(rows)
    on_fault = lax.broadcasted_iota(jnp.int32, (rows, depths), 0) == fault
    even = even_strike()
    still_line = jnp.zeros((1, depths), jnp.float32)

    def line(planes, i):
        comp, place = planes[min(i, len(planes) - 1)]
        return still_line if comp == 1 else r.change_out[comp // 2, pl.ds(place % count, 1), :]

    pairs = []
    for i in range(r.one_out.shape[0]):
        right, left = line(VEL_TAIL, i), line(VEL_HEAD, i)
        one, two = jnp.where(even, right, left), jnp.where(even, left, right)
        one = r.one[i] + jnp.where(on_fault, one, 0.0)
        pairs.append((one, r.two[i] + jnp.where(on_fault, two, 0.0)))
    for i, (one, two) in enumerate(pairs):
        r.one_out[i] = one
        r.two_out[i] = two
    ends = jnp.zeros((count, depths), jnp.float32)
    pair = lax.broadcasted_iota(jnp.int32, (count, depths), 1) // 2
    place = 4 * lax.broadcasted_iota(jnp.int32, (count, depths), 0)
    upper = lax.axis_index(GZ) == 0
    for k, field in ((0, change_x), (2, change_z)):
        turned = jnp.where(upper, pltpu.roll(field, 2, 1), field)
        turned = pltpu.roll(turned, 2 * k, 1, stride=8, stride_axis=0)
        ends = jnp.where(pair == place + k, turned, ends)
    line = jnp.sum(ends, axis=0, keepdims=True)
    set_strip(r, r.strip[0] + jnp.where(on_fault, line, 0.0))


def elastic_rates(planes, x, beside, lame, shear):
    eyy, ezz, eyz, along_y, along_z = beside
    exx = planes.backward_x(0, x)
    exy = along_y + planes.forward_x(1, x)
    exz = along_z + planes.forward_x(2, x)
    bulk = lame * (exx + eyy + ezz)
    double = 2.0 * shear
    return (
        bulk + double * exx,
        bulk + double * eyy,
        bulk + double * ezz,
        shear * exy,
        shear * exz,
        shear * eyz,
    )


def stress_new(x, elastic, decay, gain, stress, memory):
    kept = [decay * memory(c, x) - gain * elastic[c] for c in range(6)]
    return [stress(c, x) + DT * (elastic[c] + kept[c]) for c in range(6)], kept


def stress_inner(last, r):
    count, rows, depths = r.material.shape
    edges = Edges(rows, depths, by_loads=True)
    on_fault = edges.row == fault_row(rows)
    free = Field(count, r.inner, r.edge)
    for x in range(count):
        for c in (0, 2):
            line = r.change[c // 2, pl.ds(x, 1), :]
            r.velocity_out[c, x] = free(c, x) + jnp.where(on_fault, line, 0.0)
        r.velocity_out[1, x] = free(1, x)
    planes = Planes(Field(count, r.velocity_out), VEL_TAIL, VEL_HEAD)
    copies = []

    def copy_out(source, out):
        copy = pltpu.make_async_copy(source, out, r.sems.at[len(copies)])
        copy.start()
        copies.append(copy)

    if last:
        copy_out(r.velocity_out, r.new_velocity_out)
        if hasattr(r, "slip"):
            copy_out(r.slip, r.new_slip_out)
        stress_out, memory_out = r.stress_held, r.memory_held
    else:
        stress_out, memory_out = r.stress_inner_out, r.memory_inner_out

    def write(x, new, kept):
        for c in range(6):
            stress_out[c, x - 2] = new[c]
            memory_out[c, x - 2] = kept[c]
        if last and x % 2 == 1:
            held, out = pl.ds(x - 3, 2), pl.ds(x - 1, 2)
            copy_out(stress_out.at[:, held], r.stress_out.at[:, out])
            copy_out(memory_out.at[:, held], r.memory_out.at[:, out])

    band = Bands(getattr(r, "lower", None), getattr(r, "upper", None), VEL_TAIL_Y, VEL_HEAD_Y)
    stress, memory = stress_of(count, r), memory_of(count, r)
    unpack(count, r, edges)

    def beside(x):
        in_x, in_y, in_z = [r.ends[x, k] for k in range(3)]
        return (
            edges.backward_y(planes, 1, x, band(1, x)),
            edges.backward_z(planes(2, x), in_z),
            edges.forward_z(planes(1, x), in_y) + edges.forward_y(planes, 2, x, band(2, x)),
            edges.forward_y(planes, 0, x, band(0, x)),
            edges.forward_z(planes(0, x), in_x),
        )

    def moduli(x):
        return [looked_up(r.material[x], r.table, i, CLASSES) for i in (0, 1)]

    def fading(x):
        labels = r.material[x]
        decay = jnp.exp(-DT / looked_up(labels, r.table, 3, CLASSES))
        return decay, (1.0 - decay) * (0.3 * looked_up(labels, r.table, 4, CLASSES))

    for group in grouped(inside(count), 2):
        for x, elastic in [(x, elastic_rates(planes, x, beside(x), *moduli(x))) for x in group]:
            write(x, *stress_new(x, elastic, *fading(x), stress, memory))
    for group in grouped(ends_of(count), 2):
        for x, values in [(x, (*beside(x), *moduli(x), *fading(x))) for x in group]:
            for c in range(9):
                r.part_out[c, ends_of(count).index(x)] = values[c]
    if last:
        for copy in copies:
            copy.wait()
    else:
        strip = jnp.zeros((rows, depths), jnp.float32)
        for x in inside(count):
            strip = edges.packed(strip, x, [r.stress_inner_out[c, x - 2] for c in STRESS_SLOTS])
        r.strip_inner_out[...] = strip


def stress_edge(count, last, r):
    rows, depths = r.one.shape[1:]
    edges = Edges(rows, depths)
    planes = Planes(Field(count, r.velocity), VEL_TAIL, VEL_HEAD, r.one, r.two)
    places = ends_of(count)
    stress, memory = stress_of(count, r), memory_of(count, r)
    copies = []

    def copy_out(source, out, span):
        copy = pltpu.make_async_copy(source, out.at[:, span], r.sems.at[len(copies)])
        copy.start()
        copies.append(copy)

    if last:
        stress_out, memory_out = r.stress_held, r.memory_held
    else:
        stress_out, memory_out = r.stress_edge_out, r.memory_edge_out

    def elastic(i, x):
        part = [r.part[c, i] for c in range(7)]
        return elastic_rates(planes, x, part[:5], *part[5:])

    for group in grouped(list(enumerate(places)), 2):
        for (i, x), rates in [(at, elastic(*at)) for at in group]:
            new, kept = stress_new(x, rates, r.part[7, i], r.part[8, i], stress, memory)
            for c in range(6):
                stress_out[c, i] = new[c]
                memory_out[c, i] = kept[c]
        if last:
            held, span = pl.ds(group[0][0], 2), pl.ds(group[0][1], 2)
            copy_out(stress_out.at[:, held], r.stress_out, span)
            copy_out(memory_out.at[:, held], r.memory_out, span)
    if last:
        for copy in copies:
            copy.wait()
    else:
        strip = r.strip_inner[...]
        for i, x in enumerate(places):
            strip = edges.packed(strip, x, [stress_out[c, i] for c in STRESS_SLOTS])
        set_strip(r, strip)
        edge = Field(count, None, stress_out)
        edge_planes(edge, STRESS_TAIL, STRESS_HEAD, r.one_out, r.two_out)


SCALARS = ("table", "friction", "anchor")


def call(kernel, name, ins, outs, scratch=None, apart=(), onto=(), micros=1, vmem=6):
    scratch = scratch or {}
    names = [*ins, *(f"{key}_out" for key in outs), *scratch]

    def body(*refs):
        kernel(types.SimpleNamespace(**dict(zip(names, refs))))

    def place(key):
        if key in apart:
            return pl.BlockSpec(memory_space=pltpu.HBM)
        return pl.BlockSpec(memory_space=pltpu.SMEM if key in SCALARS else pltpu.VMEM)

    shapes = [
        shape if hasattr(shape, "dtype") else jax.ShapeDtypeStruct(shape, jnp.float32)
        for shape in outs.values()
    ]
    result = pl.pallas_call(
        body,
        out_shape=shapes,
        in_specs=[place(key) for key in ins],
        out_specs=[place(f"{key}_out") for key in outs],
        scratch_shapes=list(scratch.values()),
        name=name,
        input_output_aliases={
            list(ins).index(key): list(outs).index(onto[key]) for key in onto
        },
        cost_estimate=pl.CostEstimate(
            flops=0, bytes_accessed=micros * 3_690_000, transcendentals=0
        ),
        compiler_params=pltpu.CompilerParams(vmem_limit_bytes=vmem * 2**20),
    )(*ins.values())
    return dict(zip(outs, result))


def along(axis, count, skip=()):
    up = [(i, i + 1) for i in range(count - 1) if i not in skip]
    return (axis, up), (axis, [(b, a) for a, b in up])


def strike_swaps(count):
    halves = lax.axis_size(GZ)
    routes = []
    for start in (0, 1):
        partner = {}
        for i in range(start, count - 1, 2):
            for half in range(halves):
                one, other = i * halves + half, (i + 1) * halves + half
                partner[one], partner[other] = other, one
        for i in range(count * halves):
            partner.setdefault(i, i ^ 1)
        routes.append(((GX, GZ), sorted(partner.items())))
    return routes


def sent(block, route):
    return lax.ppermute(block, *route)


def whole(parts, name):
    if name in parts:
        return parts[name]
    inner, edge = parts[f"{name}_inner"], parts[f"{name}_edge"]
    return jnp.concatenate([edge[:, :2], inner, edge[:, 2:]], axis=1)


def edge_rows(field, rows):
    count = field.shape[2]
    return jnp.stack([field[c, :, place % count, :] for c, place in rows])


def shards(
    velocity,
    stress,
    memory,
    material,
    material_table,
    fault_mask,
    zone_label,
    patch_anchor,
    friction_table,
    prestress,
    normal_stress,
    slip_path,
):
    _, count, rows, depths = velocity.shape
    sides = lax.axis_size(GY)
    middle = sides // 2
    banded = sides > 2
    swaps = strike_swaps(lax.axis_size(GX))
    up_y, down_y = along(GY, sides, (middle - 1,))
    across = (GY, [(middle - 1, middle), (middle, middle - 1)])
    deep = (GZ, [(0, 1), (1, 0)])

    plane = (rows, depths)
    edge_shape = (max(len(STRESS_TAIL), len(STRESS_HEAD)), *plane)
    travelling = {"one": edge_shape, "two": edge_shape, "strip": (STRIP_PLANES, *plane)}
    inner, edge = (count - 4, *plane), (4, *plane)
    ends = {"ends": pltpu.VMEM((count, 3, *plane), jnp.float32)}

    def travelled(packed):
        two = sent(packed["two"], swaps[1])
        one = sent(packed["one"], swaps[0])
        strip = sent(packed["strip"], deep)
        return {"strip": strip}, {"one": one, "two": two}

    def bands(field, tail, head):
        if not banded:
            return {}
        lower, upper = edge_rows(field, tail), edge_rows(field, head)
        return {"lower": sent(lower, up_y), "upper": sent(upper, down_y)}

    if banded:
        still = jnp.stack(
            [
                prestress[:, 0],
                prestress[:, 1],
                normal_stress,
                slip_path,
                zone_label.astype(jnp.float32),
                fault_mask.astype(jnp.float32),
            ]
        )
        still = {"still": lax.all_gather(still, GY, axis=1, tiled=True)}
    else:
        still = {}

    held = {"velocity": velocity, "material": material}
    if not banded:
        held.update(prestress=prestress, normal=normal_stress, slip=slip_path)
        held.update(zone=zone_label, mask=fault_mask)
    ins = {"stress": stress, **held}
    ins = {key: pltpu.with_memory_space_constraint(a, pltpu.HBM) for key, a in ins.items()}
    sems = {"sems": pltpu.SemaphoreType.DMA((8,))}
    packed = call(
        pack_kernel,
        "pack",
        {"stress": ins["stress"]},
        travelling,
        scratch={"held": pltpu.VMEM(stress.shape, jnp.float32), **sems},
        apart=("stress",),
    )
    brought = call(
        functools.partial(bring_kernel, list(ins)),
        "bring",
        ins,
        {key: jax.ShapeDtypeStruct(a.shape, a.dtype) for key, a in ins.items()},
        scratch=sems,
        apart=list(ins),
    )
    velocity = brought["velocity"]
    parts = {"stress": brought["stress"], "memory": memory}
    props = {"material": brought["material"], "table": material_table}
    friction_ins = {key: brought[key] for key in held if key not in ("velocity", "material")}
    for step in range(STEPS):
        first, last = step == 0, step == STEPS - 1
        held_stress = {key: parts[key] for key in parts if key.startswith("stress")}
        strip, halos = travelled(packed)
        ins = {"velocity": velocity, **held_stress, **props, **strip}
        if banded:
            ins.update(bands(whole(parts, "stress"), STRESS_TAIL_Y, STRESS_HEAD_Y))
        face_rows = 2 * count
        if first:
            face_rows += count
            if not banded:
                ins.update(friction_ins)
                face_rows += 6 * normal_stress.shape[0]
        outs = {"inner": (3, *inner), "part": (4, *edge), "strip_inner": plane}
        outs["face_inner"] = (face_rows, depths)
        free = call(
            functools.partial(velocity_inner, first),
            "velocity_inner",
            ins,
            outs,
            scratch=ends,
            micros=3,
        )
        ins = {"velocity": velocity, **held_stress, **halos}
        ins.update({key: free[key] for key in outs if key != "inner"})
        packed = call(
            functools.partial(velocity_edge, count),
            "velocity_edge",
            ins,
            {"edge": (3, *edge), "face": (face_rows, depths), **travelling},
        )
        free = {"inner": free["inner"], "edge": packed["edge"]}
        face = packed["face"]
        other = sent(face, across)
        ins = {key: packed[key] for key in travelling}
        ins.update(face=face, other=other, friction=friction_table, anchor=patch_anchor, **still)
        if first:
            faces = {"face_first": face, "other_first": other}
        else:
            ins.update(slip=slip, **faces)
        outs = {"change": (2, count, depths), "slip": (count, depths), **travelling}
        if last and not banded:
            outs["slip"] = (count // sides, depths)
        if not still:
            outs["still"] = (6, count, depths)
        packed = call(functools.partial(fault_kernel, first), "fault", ins, outs, vmem=2)
        slip = packed["slip"]
        if not still:
            still = {"still": packed["still"]}
        strip, halos = travelled(packed)
        ins = {**free, "change": packed["change"], **parts, **props, **strip}
        if banded:
            joined = jnp.concatenate(
                [free["edge"][:, :2], free["inner"], free["edge"][:, 2:]], axis=1
            )
            band = bands(joined, VEL_TAIL_Y, VEL_HEAD_Y)
        else:
            band = {}
        outs = {"velocity": velocity.shape, "part": (9, *edge)}
        extra = {"scratch": ends}
        if last:
            outs.update(new_velocity=velocity.shape, stress=stress.shape, memory=memory.shape)
            extra["apart"] = ["new_velocity_out", "stress_out", "memory_out"]
            if not banded:
                ins["slip"] = slip
                outs["new_slip"] = slip.shape
                extra["apart"].append("new_slip_out")
            held = pltpu.VMEM((6, *inner), jnp.float32)
            sems = pltpu.SemaphoreType.DMA((count,))
            extra["scratch"] = {"stress_held": held, "memory_held": held, "sems": sems, **ends}
        else:
            outs.update(stress_inner=(6, *inner), memory_inner=(6, *inner), strip_inner=plane)
        done = call(
            functools.partial(stress_inner, last),
            "stress_inner",
            {**ins, **band},
            outs,
            micros=3,
            vmem=11,
            **extra,
        )
        velocity = done["velocity"]
        ins = {"velocity": velocity, "part": done["part"], **parts, **halos}
        if last:
            ins.update(stress_done=done["stress"], memory_done=done["memory"])
            held = pltpu.VMEM((6, *edge), jnp.float32)
            packed = call(
                functools.partial(stress_edge, count, last),
                "stress_edge",
                ins,
                {"stress": stress.shape, "memory": memory.shape},
                scratch={
                    "stress_held": held,
                    "memory_held": held,
                    "sems": pltpu.SemaphoreType.DMA((4,)),
                },
                apart=("stress_done", "memory_done", "stress_out", "memory_out"),
                onto={"stress_done": "stress", "memory_done": "memory"},
                vmem=10,
            )
            velocity = done["new_velocity"]
            stress, memory = packed["stress"], packed["memory"]
            slip = done.get("new_slip", slip)
        else:
            ins["strip_inner"] = done["strip_inner"]
            packed = call(
                functools.partial(stress_edge, count, last),
                "stress_edge",
                ins,
                {"stress_edge": (6, *edge), "memory_edge": (6, *edge), **travelling},
                vmem=10,
            )
            parts = {
                "stress_inner": done["stress_inner"],
                "stress_edge": packed["stress_edge"],
                "memory_inner": done["memory_inner"],
                "memory_edge": packed["memory_edge"],
            }
    if banded:
        held = jnp.where(lax.axis_index(GY) == middle, slip, 0.0)
        slip = lax.psum_scatter(held, GY, scatter_dimension=0, tiled=True)
    return (velocity, stress, memory, slip)


def solution(mesh):
    in_specs = (
        P(None, (ENS, GX), GY, GZ),
        P(None, (ENS, GX), GY, GZ),
        P(None, (ENS, GX), GY, GZ),
        P((ENS, GX), GY, GZ),
        P(None, ENS),
        P((ENS, GX, GY), GZ),
        P((ENS, GX, GY), GZ),
        P(ENS),
        P(None, ENS),
        P((ENS, GX, GY), None, GZ),
        P((ENS, GX, GY), GZ),
        P((ENS, GX, GY), GZ),
    )
    out_specs = (
        P(None, (ENS, GX), GY, GZ),
        P(None, (ENS, GX), GY, GZ),
        P(None, (ENS, GX), GY, GZ),
        P((ENS, GX, GY), GZ),
    )
    return jax.shard_map(shards, mesh=mesh, in_specs=in_specs, out_specs=out_specs, check_vma=False)
```

```python
import functools
import types

import jax
import jax.numpy as jnp
from jax import lax
from jax.experimental import pallas as pl
from jax.experimental.pallas import tpu as pltpu
from jax.sharding import PartitionSpec as P

STEPS = 2
CLASSES = 8
ZONES = 4
PATCH = 8

NEAR = 9.0 / 8.0
FAR = -1.0 / 24.0
DT = 0.15
TILE = 8
ENS, GX, GY, GZ = "ens", "gx", "gy", "gz"
STRIP_PLANES = 6

XX, YY, ZZ, XY, XZ, YZ = range(6)

STRESS_TAIL = ((XX, -1), (XY, -2), (XY, -1), (XZ, -2), (XZ, -1))
STRESS_HEAD = ((XX, 0), (XX, 1), (XY, 0), (XZ, 0))
VEL_TAIL = ((0, -2), (0, -1), (1, -1), (2, -1))
VEL_HEAD = ((0, 0), (1, 0), (1, 1), (2, 0), (2, 1))
STRESS_TAIL_Y = ((YY, -1), (XY, -2), (XY, -1), (YZ, -2), (YZ, -1))
STRESS_HEAD_Y = ((YY, 0), (YY, 1), (XY, 0), (YZ, 0))
VEL_TAIL_Y = ((1, -2), (1, -1), (0, -1), (2, -1))
VEL_HEAD_Y = ((1, 0), (0, 0), (0, 1), (2, 0), (2, 1))
STRESS_SLOTS = (XZ, YZ, ZZ)
VEL_SLOTS = (0, 1, 2)


def forward(before, here, after, after_2):
    return NEAR * (after - here) + FAR * (after_2 - before)


def backward(before_2, before, here, after):
    return NEAR * (here - before) + FAR * (after - before_2)


class Edges:
    def __init__(self, rows, depths, by_loads=False):
        self.rows = rows
        self.depths = depths
        lane = lax.broadcasted_iota(jnp.int32, (rows, depths), 1)
        row = lax.broadcasted_iota(jnp.int32, (TILE, depths), 0)
        self.row = lax.broadcasted_iota(jnp.int32, (rows, depths), 0)
        self.tile_row = row
        self.deep = lax.axis_index(GZ)
        near = (self.deep == 0) & (lane < 2) | (self.deep == 1) & (lane >= depths - 2)
        self.near = jnp.where(near, 1.0, 0.0)
        self.zero = jnp.minimum(self.deep, 0)
        self.by_loads = by_loads
        self.pair = lane // 2
        self.low = {n: lane < n for n in (1, 2)}
        self.high = {n: lane >= depths - n for n in (1, 2)}
        self.top = {n: row < n for n in (1, 2)}
        self.bottom = {n: row >= TILE - n for n in (1, 2)}

    def packed(self, strip, x, fields):
        first = jnp.where(self.deep == 0, 2, 0)
        for k, field in enumerate(fields):
            turn = lax.rem(first + 8 * x + 2 * k, self.depths)
            strip = jnp.where(self.pair == 4 * x + k, pltpu.roll(field, turn, 1), strip)
        return strip

    def ends(self, strip, x, k):
        back = self.depths - 8 * x - 2 * k
        turn = jnp.where(self.deep == 0, back % self.depths, back - 2)
        return pltpu.roll(strip, turn, 1) * self.near

    def shallower(self, field, halo, n):
        return pltpu.roll(jnp.where(self.high[n], halo, field), n, 1)

    def deeper(self, field, halo, n):
        return pltpu.roll(jnp.where(self.low[n], halo, field), self.depths - n, 1)

    def forward_z(self, field, halo):
        return forward(
            self.shallower(field, halo, 1),
            field,
            self.deeper(field, halo, 1),
            self.deeper(field, halo, 2),
        )

    def backward_z(self, field, halo):
        return backward(
            self.shallower(field, halo, 2),
            self.shallower(field, halo, 1),
            field,
            self.deeper(field, halo, 1),
        )

    def before(self, field, load, n, halo):
        top = jnp.where(self.top[n], 0.0, pltpu.roll(field[:TILE], n, 0))
        if halo:
            for i in range(n):
                top = jnp.where(self.tile_row == i, halo[n - 1 - i], top)
        if load:
            rest = load(self.zero + (TILE - n), self.rows - TILE)
        else:
            rest = pltpu.roll(field, n, 0)[TILE:]
        return jnp.concatenate([top, rest], axis=0)

    def after(self, field, load, n, halo):
        bottom = pltpu.roll(field[self.rows - TILE :], TILE - n, 0)
        bottom = jnp.where(self.bottom[n], 0.0, bottom)
        if halo:
            for i in range(n):
                bottom = jnp.where(self.tile_row == TILE - n + i, halo[i], bottom)
        if load:
            rest = load(self.zero + n, self.rows - TILE)
        else:
            rest = pltpu.roll(field, self.rows - n, 0)[: self.rows - TILE]
        return jnp.concatenate([rest, bottom], axis=0)

    def forward_y(self, planes, comp, x, halos):
        field = planes(comp, x)
        load = planes.rows(comp, x) if self.by_loads else None
        lower, upper = halos
        return forward(
            self.before(field, load, 1, lower),
            field,
            self.after(field, load, 1, upper),
            self.after(field, load, 2, upper),
        )

    def backward_y(self, planes, comp, x, halos):
        field = planes(comp, x)
        load = planes.rows(comp, x) if self.by_loads else None
        lower, upper = halos
        return backward(
            self.before(field, load, 2, lower),
            self.before(field, load, 1, lower),
            field,
            self.after(field, load, 1, upper),
        )


class Field:
    def __init__(self, count, *parts):
        self.count = count
        self.parts = parts

    def place(self, x):
        if len(self.parts) == 1:
            return self.parts[0], x
        inner, edge = self.parts
        if x in inside(self.count):
            return inner, x - 2
        return edge, ends_of(self.count).index(x)

    def __call__(self, comp, x):
        ref, at = self.place(x)
        return ref[comp, at]

    def rows(self, comp, x):
        ref, at = self.place(x)
        return lambda start, size: ref[comp, at, pl.ds(start, size), :]


def inside(count):
    return range(2, count - 2)


def ends_of(count):
    return (0, 1, count - 2, count - 1)


class Planes:
    def __init__(self, field, tail, head, first=None, second=None):
        self.field = field
        self.count = field.count
        self.first, self.second = first, second
        self.tail, self.head = tail, head
        self.even = even_strike()
        self.any_left = lax.axis_index(GX) > 0
        self.any_right = lax.axis_index(GX) < lax.axis_size(GX) - 1

    def left(self, i):
        plane = jnp.where(self.even, self.second[i], self.first[i])
        return jnp.where(self.any_left, plane, 0.0)

    def right(self, i):
        plane = jnp.where(self.even, self.first[i], self.second[i])
        return jnp.where(self.any_right, plane, 0.0)

    def __call__(self, comp, place):
        if place < 0:
            return self.left(self.tail.index((comp, place)))
        if place >= self.count:
            return self.right(self.head.index((comp, place - self.count)))
        return self.field(comp, place)

    def rows(self, comp, x):
        return self.field.rows(comp, x)

    def forward_x(self, comp, x):
        return forward(self(comp, x - 1), self(comp, x), self(comp, x + 1), self(comp, x + 2))

    def backward_x(self, comp, x):
        return backward(self(comp, x - 2), self(comp, x - 1), self(comp, x), self(comp, x + 1))


class Bands:
    def __init__(self, lower, upper, tail, head):
        self.lower, self.upper = lower, upper
        self.tail, self.head = tail, head

    def __call__(self, comp, x):
        if self.lower is None:
            return (None, None)
        places = [i for i, (c, _) in enumerate(self.tail) if c == comp]
        before = [self.lower[i, pl.ds(x, 1), :] for i in reversed(places)]
        places = [i for i, (c, _) in enumerate(self.head) if c == comp]
        after = [self.upper[i, pl.ds(x, 1), :] for i in places]
        return (before, after)


def looked_up(labels, table, row, count):
    out = jnp.full(labels.shape, table[row, 0], jnp.float32)
    for k in range(1, count):
        out = jnp.where(labels == k, table[row, k], out)
    return out


def even_strike():
    return lax.axis_index(GX) % 2 == 0


def edge_planes(field, tail, head, first_out, second_out):
    even = even_strike()
    pairs = []
    for i in range(first_out.shape[0]):
        comp, place = tail[min(i, len(tail) - 1)]
        right = field(comp, place % field.count)
        comp, place = head[min(i, len(head) - 1)]
        left = field(comp, place % field.count)
        pairs.append((jnp.where(even, right, left), jnp.where(even, left, right)))
    for i, (one, two) in enumerate(pairs):
        first_out[i] = one
        second_out[i] = two


def fault_row(rows):
    return jnp.where(lax.axis_index(GY) == lax.axis_size(GY) // 2, 0, rows - 1)


def pack_kernel(names, r):
    count, rows, depths = r.stress.shape[1:]
    order = (XZ, YZ, ZZ, XX, XY, YY)
    pairs = [(r.stress.at[c], r.stress_out.at[c]) for c in order]
    pairs += [(getattr(r, key), getattr(r, f"{key}_out")) for key in names]
    copies = []
    for i, (source, out) in enumerate(pairs):
        copy = pltpu.make_async_copy(source, out, r.sems.at[i])
        copy.start()
        copies.append(copy)
    edges = Edges(rows, depths)
    for copy in copies[:3]:
        copy.wait()
    strip = jnp.zeros((rows, depths), jnp.float32)
    for x in range(count):
        strip = edges.packed(strip, x, [r.stress_out[c, x] for c in STRESS_SLOTS])
    set_strip(r, strip)
    for copy in copies[3:5]:
        copy.wait()
    edge_planes(Field(count, r.stress_out), STRESS_TAIL, STRESS_HEAD, r.one_out, r.two_out)
    for copy in copies[5:]:
        copy.wait()


def grouped(xs, size):
    return [xs[i : i + size] for i in range(0, len(xs), size)]


def set_strip(r, strip):
    r.strip_out[0] = strip
    for i in range(1, STRIP_PLANES):
        r.strip_out[i] = jnp.zeros_like(strip)


def unpack(count, r, edges):
    strip = r.strip[0]
    for x in range(count):
        for k in range(3):
            r.ends[x, k] = edges.ends(strip, x, k)


def velocity_across(planes, x):
    return planes.forward_x(XX, x), planes.backward_x(XY, x), planes.backward_x(XZ, x)


def velocity_inner(first, r):
    count, rows, depths = r.material.shape
    edges = Edges(rows, depths)
    planes = Planes(stress_of(count, r), STRESS_TAIL, STRESS_HEAD)
    band = Bands(getattr(r, "lower", None), getattr(r, "upper", None), STRESS_TAIL_Y, STRESS_HEAD_Y)
    unpack(count, r, edges)

    def beside(x):
        ends = [r.ends[x, k] for k in range(3)]
        return (
            edges.backward_y(planes, XY, x, band(XY, x)) + edges.backward_z(planes(XZ, x), ends[0]),
            edges.forward_y(planes, YY, x, band(YY, x)) + edges.backward_z(planes(YZ, x), ends[1]),
            edges.backward_y(planes, YZ, x, band(YZ, x)) + edges.forward_z(planes(ZZ, x), ends[2]),
        )

    def push(x):
        return DT * looked_up(r.material[x], r.table, 2, CLASSES)

    def new(x):
        rates = zip(velocity_across(planes, x), beside(x))
        return [r.velocity[c, x] + push(x) * (a + b) for c, (a, b) in enumerate(rates)]

    for group in grouped(inside(count), 3 if (count - 4) % 3 == 0 else 2):
        for x, values in [(x, new(x)) for x in group]:
            for c in range(3):
                r.inner_out[c, x - 2] = values[c]
    for group in grouped(ends_of(count), 2):
        for x, values in [(x, (*beside(x), push(x))) for x in group]:
            for c in range(4):
                r.part_out[c, ends_of(count).index(x)] = values[c]
    strip = jnp.zeros((rows, depths), jnp.float32)
    for x in inside(count):
        strip = edges.packed(strip, x, [r.inner_out[c, x - 2] for c in VEL_SLOTS])
    r.strip_inner_out[...] = strip

    row = pl.ds(fault_row(rows), 1)
    lines = {}
    for x in inside(count):
        for i, c in enumerate((0, 2)):
            lines[i * count + x] = r.inner_out[c, x - 2, row, :]
    if first:
        for x in range(count):
            labels = r.material[x, row, :]
            lines[2 * count + x] = looked_up(labels, r.table, 2, CLASSES)
    if hasattr(r, "prestress"):
        own = r.normal.shape[0]
        place = 3 * count
        for c in (0, 1):
            for i in range(own):
                lines[place + c * own + i] = r.prestress[i, pl.ds(c, 1), :]
        for j, field in enumerate((r.normal, r.slip, r.zone, r.mask), 2):
            for i in range(own):
                lines[place + j * own + i] = field[pl.ds(i, 1), :].astype(jnp.float32)
    for i, line in lines.items():
        r.face_inner_out[pl.ds(i, 1), :] = line


def velocity_edge(count, r):
    rows, depths = r.one.shape[1:]
    edges = Edges(rows, depths)
    planes = Planes(stress_of(count, r), STRESS_TAIL, STRESS_HEAD, r.one, r.two)
    places = ends_of(count)
    new = []
    for i, x in enumerate(places):
        rates = [a + r.part[c, i] for c, a in enumerate(velocity_across(planes, x))]
        new.append([r.velocity[c, x] + r.part[3, i] * rate for c, rate in enumerate(rates)])
    faces = r.face_inner[...]
    strip = r.strip_inner[...]
    for i, x in enumerate(places):
        strip = edges.packed(strip, x, [new[i][c] for c in VEL_SLOTS])
        for c in range(3):
            r.edge_out[c, i] = new[i][c]
    r.face_out[...] = faces
    set_strip(r, strip)
    fault = fault_row(rows)
    edge = Field(count, None, r.edge_out)
    lines = {i * count + x: edge.rows(c, x)(fault, 1) for x in places for i, c in enumerate((0, 2))}
    for i, line in lines.items():
        r.face_out[pl.ds(i, 1), :] = line
    edge_planes(edge, VEL_TAIL, VEL_HEAD, r.one_out, r.two_out)


def stress_of(count, r):
    if hasattr(r, "stress"):
        return Field(count, r.stress)
    return Field(count, r.stress_inner, r.stress_edge)


def memory_of(count, r):
    if hasattr(r, "memory"):
        return Field(count, r.memory)
    return Field(count, r.memory_inner, r.memory_edge)


def fault_kernel(first, r):
    own_face, other_face = r.face, r.other
    own_first, other_first = (own_face, other_face) if first else (r.face_first, r.other_first)
    rows, depths = r.strip.shape[1:]
    count = r.change_out.shape[1]
    middle = lax.axis_size(GY) // 2
    side = lax.axis_index(GY)
    plus = side == middle
    minus = side == middle - 1

    def pair(own, other, place):
        mine, theirs = own[pl.ds(place, count), :], other[pl.ds(place, count), :]
        return jnp.where(plus, theirs, mine), jnp.where(plus, mine, theirs)

    if hasattr(r, "still"):
        still = r.still
    else:
        still = r.still_out
        share = (own_face.shape[0] - 3 * count) // 6
        for i in range(6):
            mine = own_face[pl.ds(3 * count + i * share, share), :]
            theirs = other_face[pl.ds(3 * count + i * share, share), :]
            still[i, pl.ds(0, share), :] = jnp.where(plus, theirs, mine)
            still[i, pl.ds(share, share), :] = jnp.where(plus, mine, theirs)
    pre_x, pre_z, normal = still[0], still[1], still[2]
    slip = still[3] if first else r.slip[...]
    zone, mask = still[4], still[5]

    row = lax.broadcasted_iota(jnp.int32, (count, depths), 0) + lax.axis_index(GX) * count
    deep = lax.broadcasted_iota(jnp.int32, (count, depths), 1) + lax.axis_index(GZ) * depths
    inside = (row >= r.anchor[0]) & (row < r.anchor[0] + 2 * PATCH)
    inside = inside & (deep >= r.anchor[1]) & (deep < r.anchor[1] + 2 * PATCH)
    dynamic = 0.4 * looked_up(zone, r.friction, 0, ZONES)
    static = jnp.where(
        inside, dynamic, dynamic + 0.5 * looked_up(zone, r.friction, 1, ZONES)
    )
    distance = 0.2 * looked_up(zone, r.friction, 2, ZONES)
    minus_x, plus_x = pair(own_face, other_face, 0)
    minus_z, plus_z = pair(own_face, other_face, count)
    minus_b, plus_b = pair(own_first, other_first, 2 * count)
    bsum = minus_b + plus_b
    trial_x = (plus_x - minus_x) / (DT * bsum) + pre_x
    trial_z = (plus_z - minus_z) / (DT * bsum) + pre_z
    size = jnp.sqrt(trial_x * trial_x + trial_z * trial_z)
    weaken = jnp.minimum(slip / distance, 1.0)
    strength = (static - (static - dynamic) * weaken) * normal
    factor = jnp.where(mask == 1.0, strength / jnp.maximum(size, strength), 1.0)
    new_slip = slip + DT * DT * bsum * (size - size * factor)
    half = r.slip_out.shape[0]
    if half < count:
        new_slip = jnp.where(plus, new_slip[half:], new_slip[:half])
    r.slip_out[...] = new_slip
    sign = jnp.where(minus, DT, 0.0) * minus_b - jnp.where(plus, DT, 0.0) * plus_b
    change_x = (trial_x * factor - pre_x) * sign
    change_z = (trial_z * factor - pre_z) * sign
    r.change_out[0] = change_x
    r.change_out[1] = change_z

    fault = fault_row(rows)
    on_fault = lax.broadcasted_iota(jnp.int32, (rows, depths), 0) == fault
    even = even_strike()
    still_line = jnp.zeros((1, depths), jnp.float32)

    def line(planes, i):
        comp, place = planes[min(i, len(planes) - 1)]
        at = place % count
        return still_line if comp == 1 else (change_x, change_z)[comp // 2][at : at + 1]

    pairs = []
    for i in range(r.one_out.shape[0]):
        right, left = line(VEL_TAIL, i), line(VEL_HEAD, i)
        one, two = jnp.where(even, right, left), jnp.where(even, left, right)
        one = r.one[i] + jnp.where(on_fault, one, 0.0)
        pairs.append((one, r.two[i] + jnp.where(on_fault, two, 0.0)))
    for i, (one, two) in enumerate(pairs):
        r.one_out[i] = one
        r.two_out[i] = two
    ends = jnp.zeros((count, depths), jnp.float32)
    pair = lax.broadcasted_iota(jnp.int32, (count, depths), 1) // 2
    place = 4 * lax.broadcasted_iota(jnp.int32, (count, depths), 0)
    upper = lax.axis_index(GZ) == 0
    for k, field in ((0, change_x), (2, change_z)):
        turned = jnp.where(upper, pltpu.roll(field, 2, 1), field)
        turned = pltpu.roll(turned, 2 * k, 1, stride=8, stride_axis=0)
        ends = jnp.where(pair == place + k, turned, ends)
    line = jnp.sum(ends, axis=0, keepdims=True)
    set_strip(r, r.strip[0] + jnp.where(on_fault, line, 0.0))


def elastic_rates(planes, x, beside, lame, shear):
    eyy, ezz, eyz, along_y, along_z = beside
    exx = planes.backward_x(0, x)
    exy = along_y + planes.forward_x(1, x)
    exz = along_z + planes.forward_x(2, x)
    bulk = lame * (exx + eyy + ezz)
    double = 2.0 * shear
    return (
        bulk + double * exx,
        bulk + double * eyy,
        bulk + double * ezz,
        shear * exy,
        shear * exz,
        shear * eyz,
    )


def stress_new(x, elastic, decay, gain, stress, memory):
    kept = [decay * memory(c, x) - gain * elastic[c] for c in range(6)]
    return [stress(c, x) + DT * (elastic[c] + kept[c]) for c in range(6)], kept


def stress_inner(last, r):
    count, rows, depths = r.material.shape
    edges = Edges(rows, depths, by_loads=True)
    on_fault = edges.row == fault_row(rows)
    free = Field(count, r.inner, r.edge)
    for x in range(count):
        for c in (0, 2):
            line = r.change[c // 2, pl.ds(x, 1), :]
            r.velocity_out[c, x] = free(c, x) + jnp.where(on_fault, line, 0.0)
        r.velocity_out[1, x] = free(1, x)
    planes = Planes(Field(count, r.velocity_out), VEL_TAIL, VEL_HEAD)
    copies = []

    def copy_out(source, out):
        copy = pltpu.make_async_copy(source, out, r.sems.at[len(copies)])
        copy.start()
        copies.append(copy)

    if last:
        copy_out(r.velocity_out, r.new_velocity_out)
        if hasattr(r, "slip"):
            copy_out(r.slip, r.new_slip_out)
        stress_out, memory_out = r.stress_held, r.memory_held
    else:
        stress_out, memory_out = r.stress_inner_out, r.memory_inner_out

    def write(x, new, kept):
        for c in range(6):
            stress_out[c, x - 2] = new[c]
            memory_out[c, x - 2] = kept[c]
        if last and x % 2 == 1:
            held, out = pl.ds(x - 3, 2), pl.ds(x - 1, 2)
            copy_out(stress_out.at[:, held], r.stress_out.at[:, out])
            copy_out(memory_out.at[:, held], r.memory_out.at[:, out])

    band = Bands(getattr(r, "lower", None), getattr(r, "upper", None), VEL_TAIL_Y, VEL_HEAD_Y)
    stress, memory = stress_of(count, r), memory_of(count, r)
    unpack(count, r, edges)

    def beside(x):
        in_x, in_y, in_z = [r.ends[x, k] for k in range(3)]
        return (
            edges.backward_y(planes, 1, x, band(1, x)),
            edges.backward_z(planes(2, x), in_z),
            edges.forward_z(planes(1, x), in_y) + edges.forward_y(planes, 2, x, band(2, x)),
            edges.forward_y(planes, 0, x, band(0, x)),
            edges.forward_z(planes(0, x), in_x),
        )

    def moduli(x):
        return [looked_up(r.material[x], r.table, i, CLASSES) for i in (0, 1)]

    def fading(x):
        labels = r.material[x]
        decay = jnp.exp(-DT / looked_up(labels, r.table, 3, CLASSES))
        return decay, (1.0 - decay) * (0.3 * looked_up(labels, r.table, 4, CLASSES))

    for group in grouped(inside(count), 2):
        for x, elastic in [(x, elastic_rates(planes, x, beside(x), *moduli(x))) for x in group]:
            write(x, *stress_new(x, elastic, *fading(x), stress, memory))
    for group in grouped(ends_of(count), 2):
        for x, values in [(x, (*beside(x), *moduli(x), *fading(x))) for x in group]:
            for c in range(9):
                r.part_out[c, ends_of(count).index(x)] = values[c]
    if last:
        for copy in copies:
            copy.wait()
    else:
        strip = jnp.zeros((rows, depths), jnp.float32)
        for x in inside(count):
            strip = edges.packed(strip, x, [r.stress_inner_out[c, x - 2] for c in STRESS_SLOTS])
        r.strip_inner_out[...] = strip


def stress_edge(count, last, r):
    rows, depths = r.one.shape[1:]
    edges = Edges(rows, depths)
    planes = Planes(Field(count, r.velocity), VEL_TAIL, VEL_HEAD, r.one, r.two)
    places = ends_of(count)
    stress, memory = stress_of(count, r), memory_of(count, r)
    copies = []

    def copy_out(source, out, span):
        copy = pltpu.make_async_copy(source, out.at[:, span], r.sems.at[len(copies)])
        copy.start()
        copies.append(copy)

    if last:
        stress_out, memory_out = r.stress_held, r.memory_held
    else:
        stress_out, memory_out = r.stress_edge_out, r.memory_edge_out

    def elastic(i, x):
        part = [r.part[c, i] for c in range(7)]
        return elastic_rates(planes, x, part[:5], *part[5:])

    for group in grouped(list(enumerate(places)), 2):
        for (i, x), rates in [(at, elastic(*at)) for at in group]:
            new, kept = stress_new(x, rates, r.part[7, i], r.part[8, i], stress, memory)
            for c in range(6):
                stress_out[c, i] = new[c]
                memory_out[c, i] = kept[c]
        if last:
            held, span = pl.ds(group[0][0], 2), pl.ds(group[0][1], 2)
            copy_out(stress_out.at[:, held], r.stress_out, span)
            copy_out(memory_out.at[:, held], r.memory_out, span)
    if last:
        for copy in copies:
            copy.wait()
    else:
        strip = r.strip_inner[...]
        for i, x in enumerate(places):
            strip = edges.packed(strip, x, [stress_out[c, i] for c in STRESS_SLOTS])
        set_strip(r, strip)
        edge = Field(count, None, stress_out)
        edge_planes(edge, STRESS_TAIL, STRESS_HEAD, r.one_out, r.two_out)


SCALARS = ("table", "friction", "anchor")


def call(kernel, name, ins, outs, scratch=None, apart=(), onto=(), micros=1, vmem=6):
    scratch = scratch or {}
    names = [*ins, *(f"{key}_out" for key in outs), *scratch]

    def body(*refs):
        kernel(types.SimpleNamespace(**dict(zip(names, refs))))

    def place(key):
        if key in apart:
            return pl.BlockSpec(memory_space=pltpu.HBM)
        return pl.BlockSpec(memory_space=pltpu.SMEM if key in SCALARS else pltpu.VMEM)

    shapes = [
        shape if hasattr(shape, "dtype") else jax.ShapeDtypeStruct(shape, jnp.float32)
        for shape in outs.values()
    ]
    result = pl.pallas_call(
        body,
        out_shape=shapes,
        in_specs=[place(key) for key in ins],
        out_specs=[place(f"{key}_out") for key in outs],
        scratch_shapes=list(scratch.values()),
        name=name,
        input_output_aliases={
            list(ins).index(key): list(outs).index(onto[key]) for key in onto
        },
        cost_estimate=pl.CostEstimate(
            flops=0, bytes_accessed=micros * 3_690_000, transcendentals=0
        ),
        compiler_params=pltpu.CompilerParams(vmem_limit_bytes=vmem * 2**20),
    )(*ins.values())
    return dict(zip(outs, result))


def along(axis, count, skip=()):
    up = [(i, i + 1) for i in range(count - 1) if i not in skip]
    return (axis, up), (axis, [(b, a) for a, b in up])


def strike_swaps(count):
    halves = lax.axis_size(GZ)
    routes = []
    for start in (0, 1):
        partner = {}
        for i in range(start, count - 1, 2):
            for half in range(halves):
                one, other = i * halves + half, (i + 1) * halves + half
                partner[one], partner[other] = other, one
        for i in range(count * halves):
            partner.setdefault(i, i ^ 1)
        routes.append(((GX, GZ), sorted(partner.items())))
    return routes


def sent(block, route):
    return lax.ppermute(block, *route)


def whole(parts, name):
    if name in parts:
        return parts[name]
    inner, edge = parts[f"{name}_inner"], parts[f"{name}_edge"]
    return jnp.concatenate([edge[:, :2], inner, edge[:, 2:]], axis=1)


def edge_rows(field, rows):
    count = field.shape[2]
    return jnp.stack([field[c, :, place % count, :] for c, place in rows])


def shards(
    velocity,
    stress,
    memory,
    material,
    material_table,
    fault_mask,
    zone_label,
    patch_anchor,
    friction_table,
    prestress,
    normal_stress,
    slip_path,
):
    _, count, rows, depths = velocity.shape
    sides = lax.axis_size(GY)
    middle = sides // 2
    banded = sides > 2
    swaps = strike_swaps(lax.axis_size(GX))
    up_y, down_y = along(GY, sides, (middle - 1,))
    across = (GY, [(middle - 1, middle), (middle, middle - 1)])
    deep = (GZ, [(0, 1), (1, 0)])

    plane = (rows, depths)
    edge_shape = (max(len(STRESS_TAIL), len(STRESS_HEAD)), *plane)
    travelling = {"one": edge_shape, "two": edge_shape, "strip": (STRIP_PLANES, *plane)}
    inner, edge = (count - 4, *plane), (4, *plane)
    ends = {"ends": pltpu.VMEM((count, 3, *plane), jnp.float32)}

    def travelled(packed):
        two = sent(packed["two"], swaps[1])
        one = sent(packed["one"], swaps[0])
        strip = sent(packed["strip"], deep)
        return {"strip": strip}, {"one": one, "two": two}

    def bands(field, tail, head):
        if not banded:
            return {}
        lower, upper = edge_rows(field, tail), edge_rows(field, head)
        return {"lower": sent(lower, up_y), "upper": sent(upper, down_y)}

    if banded:
        still = jnp.stack(
            [
                prestress[:, 0],
                prestress[:, 1],
                normal_stress,
                slip_path,
                zone_label.astype(jnp.float32),
                fault_mask.astype(jnp.float32),
            ]
        )
        still = {"still": lax.all_gather(still, GY, axis=1, tiled=True)}
    else:
        still = {}

    held = {"velocity": velocity, "material": material}
    if not banded:
        held.update(prestress=prestress, normal=normal_stress, slip=slip_path)
        held.update(zone=zone_label, mask=fault_mask)
    ins = {"stress": stress, **held}
    packed = call(
        functools.partial(pack_kernel, list(held)),
        "pack",
        {key: pltpu.with_memory_space_constraint(a, pltpu.HBM) for key, a in ins.items()},
        {**travelling, **{key: jax.ShapeDtypeStruct(a.shape, a.dtype) for key, a in ins.items()}},
        scratch={"sems": pltpu.SemaphoreType.DMA((6 + len(held),))},
        apart=list(ins),
    )
    velocity = packed["velocity"]
    parts = {"stress": packed["stress"], "memory": memory}
    props = {"material": packed["material"], "table": material_table}
    friction_ins = {key: packed[key] for key in held if key not in ("velocity", "material")}
    for step in range(STEPS):
        first, last = step == 0, step == STEPS - 1
        held_stress = {key: parts[key] for key in parts if key.startswith("stress")}
        strip, halos = travelled(packed)
        ins = {"velocity": velocity, **held_stress, **props, **strip}
        if banded:
            ins.update(bands(whole(parts, "stress"), STRESS_TAIL_Y, STRESS_HEAD_Y))
        face_rows = 2 * count
        if first:
            face_rows += count
            if not banded:
                ins.update(friction_ins)
                face_rows += 6 * normal_stress.shape[0]
        outs = {"inner": (3, *inner), "part": (4, *edge), "strip_inner": plane}
        outs["face_inner"] = (face_rows, depths)
        free = call(
            functools.partial(velocity_inner, first),
            "velocity_inner",
            ins,
            outs,
            scratch=ends,
            micros=3,
        )
        ins = {"velocity": velocity, **held_stress, **halos}
        ins.update({key: free[key] for key in outs if key != "inner"})
        packed = call(
            functools.partial(velocity_edge, count),
            "velocity_edge",
            ins,
            {"edge": (3, *edge), "face": (face_rows, depths), **travelling},
        )
        free = {"inner": free["inner"], "edge": packed["edge"]}
        face = packed["face"]
        other = sent(face, across)
        ins = {key: packed[key] for key in travelling}
        ins.update(face=face, other=other, friction=friction_table, anchor=patch_anchor, **still)
        if first:
            faces = {"face_first": face, "other_first": other}
        else:
            ins.update(slip=slip, **faces)
        outs = {"change": (2, count, depths), "slip": (count, depths), **travelling}
        if last and not banded:
            outs["slip"] = (count // sides, depths)
        if not still:
            outs["still"] = (6, count, depths)
        packed = call(functools.partial(fault_kernel, first), "fault", ins, outs, vmem=2)
        slip = packed["slip"]
        if not still:
            still = {"still": packed["still"]}
        strip, halos = travelled(packed)
        ins = {**free, "change": packed["change"], **parts, **props, **strip}
        if banded:
            joined = jnp.concatenate(
                [free["edge"][:, :2], free["inner"], free["edge"][:, 2:]], axis=1
            )
            band = bands(joined, VEL_TAIL_Y, VEL_HEAD_Y)
        else:
            band = {}
        outs = {"velocity": velocity.shape, "part": (9, *edge)}
        extra = {"scratch": ends}
        if last:
            outs.update(new_velocity=velocity.shape, stress=stress.shape, memory=memory.shape)
            extra["apart"] = ["new_velocity_out", "stress_out", "memory_out"]
            if not banded:
                ins["slip"] = slip
                outs["new_slip"] = slip.shape
                extra["apart"].append("new_slip_out")
            held = pltpu.VMEM((6, *inner), jnp.float32)
            sems = pltpu.SemaphoreType.DMA((count,))
            extra["scratch"] = {"stress_held": held, "memory_held": held, "sems": sems, **ends}
        else:
            outs.update(stress_inner=(6, *inner), memory_inner=(6, *inner), strip_inner=plane)
        done = call(
            functools.partial(stress_inner, last),
            "stress_inner",
            {**ins, **band},
            outs,
            micros=3,
            vmem=11,
            **extra,
        )
        velocity = done["velocity"]
        ins = {"velocity": velocity, "part": done["part"], **parts, **halos}
        if last:
            ins.update(stress_done=done["stress"], memory_done=done["memory"])
            held = pltpu.VMEM((6, *edge), jnp.float32)
            packed = call(
                functools.partial(stress_edge, count, last),
                "stress_edge",
                ins,
                {"stress": stress.shape, "memory": memory.shape},
                scratch={
                    "stress_held": held,
                    "memory_held": held,
                    "sems": pltpu.SemaphoreType.DMA((4,)),
                },
                apart=("stress_done", "memory_done", "stress_out", "memory_out"),
                onto={"stress_done": "stress", "memory_done": "memory"},
                vmem=10,
            )
            velocity = done["new_velocity"]
            stress, memory = packed["stress"], packed["memory"]
            slip = done.get("new_slip", slip)
        else:
            ins["strip_inner"] = done["strip_inner"]
            packed = call(
                functools.partial(stress_edge, count, last),
                "stress_edge",
                ins,
                {"stress_edge": (6, *edge), "memory_edge": (6, *edge), **travelling},
                vmem=10,
            )
            parts = {
                "stress_inner": done["stress_inner"],
                "stress_edge": packed["stress_edge"],
                "memory_inner": done["memory_inner"],
                "memory_edge": packed["memory_edge"],
            }
    if banded:
        held = jnp.where(lax.axis_index(GY) == middle, slip, 0.0)
        slip = lax.psum_scatter(held, GY, scatter_dimension=0, tiled=True)
    return (velocity, stress, memory, slip)


def solution(mesh):
    in_specs = (
        P(None, (ENS, GX), GY, GZ),
        P(None, (ENS, GX), GY, GZ),
        P(None, (ENS, GX), GY, GZ),
        P((ENS, GX), GY, GZ),
        P(None, ENS),
        P((ENS, GX, GY), GZ),
        P((ENS, GX, GY), GZ),
        P(ENS),
        P(None, ENS),
        P((ENS, GX, GY), None, GZ),
        P((ENS, GX, GY), GZ),
        P((ENS, GX, GY), GZ),
    )
    out_specs = (
        P(None, (ENS, GX), GY, GZ),
        P(None, (ENS, GX), GY, GZ),
        P(None, (ENS, GX), GY, GZ),
        P((ENS, GX, GY), GZ),
    )
    return jax.shard_map(shards, mesh=mesh, in_specs=in_specs, out_specs=out_specs, check_vma=False)
```

```python
import functools
import types

import jax
import jax.numpy as jnp
from jax import lax
from jax.experimental import pallas as pl
from jax.experimental.pallas import tpu as pltpu
from jax.sharding import PartitionSpec as P

STEPS = 2
CLASSES = 8
ZONES = 4
PATCH = 8

NEAR = 9.0 / 8.0
FAR = -1.0 / 24.0
DT = 0.15
TILE = 8
ENS, GX, GY, GZ = "ens", "gx", "gy", "gz"
STRIP_PLANES = 6

XX, YY, ZZ, XY, XZ, YZ = range(6)

STRESS_TAIL = ((XX, -1), (XY, -2), (XY, -1), (XZ, -2), (XZ, -1))
STRESS_HEAD = ((XX, 0), (XX, 1), (XY, 0), (XZ, 0))
VEL_TAIL = ((0, -2), (0, -1), (1, -1), (2, -1))
VEL_HEAD = ((0, 0), (1, 0), (1, 1), (2, 0), (2, 1))
STRESS_TAIL_Y = ((YY, -1), (XY, -2), (XY, -1), (YZ, -2), (YZ, -1))
STRESS_HEAD_Y = ((YY, 0), (YY, 1), (XY, 0), (YZ, 0))
VEL_TAIL_Y = ((1, -2), (1, -1), (0, -1), (2, -1))
VEL_HEAD_Y = ((1, 0), (0, 0), (0, 1), (2, 0), (2, 1))
STRESS_SLOTS = (XZ, YZ, ZZ)
VEL_SLOTS = (0, 1, 2)


def forward(before, here, after, after_2):
    return NEAR * (after - here) + FAR * (after_2 - before)


def backward(before_2, before, here, after):
    return NEAR * (here - before) + FAR * (after - before_2)


class Edges:
    def __init__(self, rows, depths, by_loads=False):
        self.rows = rows
        self.depths = depths
        lane = lax.broadcasted_iota(jnp.int32, (rows, depths), 1)
        row = lax.broadcasted_iota(jnp.int32, (TILE, depths), 0)
        self.row = lax.broadcasted_iota(jnp.int32, (rows, depths), 0)
        self.tile_row = row
        self.deep = lax.axis_index(GZ)
        near = (self.deep == 0) & (lane < 2) | (self.deep == 1) & (lane >= depths - 2)
        self.near = jnp.where(near, 1.0, 0.0)
        self.zero = jnp.minimum(self.deep, 0)
        self.by_loads = by_loads
        self.pair = lane // 2
        self.low = {n: lane < n for n in (1, 2)}
        self.high = {n: lane >= depths - n for n in (1, 2)}
        self.top = {n: row < n for n in (1, 2)}
        self.bottom = {n: row >= TILE - n for n in (1, 2)}

    def packed(self, strip, x, fields):
        first = jnp.where(self.deep == 0, 2, 0)
        for k, field in enumerate(fields):
            turn = lax.rem(first + 8 * x + 2 * k, self.depths)
            strip = jnp.where(self.pair == 4 * x + k, pltpu.roll(field, turn, 1), strip)
        return strip

    def ends(self, strip, x, k):
        back = self.depths - 8 * x - 2 * k
        turn = jnp.where(self.deep == 0, back % self.depths, back - 2)
        return pltpu.roll(strip, turn, 1) * self.near

    def shallower(self, field, halo, n):
        return pltpu.roll(jnp.where(self.high[n], halo, field), n, 1)

    def deeper(self, field, halo, n):
        return pltpu.roll(jnp.where(self.low[n], halo, field), self.depths - n, 1)

    def forward_z(self, field, halo):
        return forward(
            self.shallower(field, halo, 1),
            field,
            self.deeper(field, halo, 1),
            self.deeper(field, halo, 2),
        )

    def backward_z(self, field, halo):
        return backward(
            self.shallower(field, halo, 2),
            self.shallower(field, halo, 1),
            field,
            self.deeper(field, halo, 1),
        )

    def before(self, field, load, n, halo):
        top = jnp.where(self.top[n], 0.0, pltpu.roll(field[:TILE], n, 0))
        if halo:
            for i in range(n):
                top = jnp.where(self.tile_row == i, halo[n - 1 - i], top)
        if load:
            rest = load(self.zero + (TILE - n), self.rows - TILE)
        else:
            rest = pltpu.roll(field, n, 0)[TILE:]
        return jnp.concatenate([top, rest], axis=0)

    def after(self, field, load, n, halo):
        bottom = pltpu.roll(field[self.rows - TILE :], TILE - n, 0)
        bottom = jnp.where(self.bottom[n], 0.0, bottom)
        if halo:
            for i in range(n):
                bottom = jnp.where(self.tile_row == TILE - n + i, halo[i], bottom)
        if load:
            rest = load(self.zero + n, self.rows - TILE)
        else:
            rest = pltpu.roll(field, self.rows - n, 0)[: self.rows - TILE]
        return jnp.concatenate([rest, bottom], axis=0)

    def forward_y(self, planes, comp, x, halos):
        field = planes(comp, x)
        load = planes.rows(comp, x) if self.by_loads else None
        lower, upper = halos
        return forward(
            self.before(field, load, 1, lower),
            field,
            self.after(field, load, 1, upper),
            self.after(field, load, 2, upper),
        )

    def backward_y(self, planes, comp, x, halos):
        field = planes(comp, x)
        load = planes.rows(comp, x) if self.by_loads else None
        lower, upper = halos
        return backward(
            self.before(field, load, 2, lower),
            self.before(field, load, 1, lower),
            field,
            self.after(field, load, 1, upper),
        )


class Field:
    def __init__(self, count, *parts):
        self.count = count
        self.parts = parts

    def place(self, x):
        if len(self.parts) == 1:
            return self.parts[0], x
        inner, edge = self.parts
        if x in inside(self.count):
            return inner, x - 2
        return edge, ends_of(self.count).index(x)

    def __call__(self, comp, x):
        ref, at = self.place(x)
        return ref[comp, at]

    def rows(self, comp, x):
        ref, at = self.place(x)
        return lambda start, size: ref[comp, at, pl.ds(start, size), :]


def inside(count):
    return range(2, count - 2)


def ends_of(count):
    return (0, 1, count - 2, count - 1)


class Planes:
    def __init__(self, field, tail, head, first=None, second=None):
        self.field = field
        self.count = field.count
        self.first, self.second = first, second
        self.tail, self.head = tail, head
        self.even = even_strike()
        self.any_left = lax.axis_index(GX) > 0
        self.any_right = lax.axis_index(GX) < lax.axis_size(GX) - 1

    def left(self, i):
        plane = jnp.where(self.even, self.second[i], self.first[i])
        return jnp.where(self.any_left, plane, 0.0)

    def right(self, i):
        plane = jnp.where(self.even, self.first[i], self.second[i])
        return jnp.where(self.any_right, plane, 0.0)

    def __call__(self, comp, place):
        if place < 0:
            return self.left(self.tail.index((comp, place)))
        if place >= self.count:
            return self.right(self.head.index((comp, place - self.count)))
        return self.field(comp, place)

    def rows(self, comp, x):
        return self.field.rows(comp, x)

    def forward_x(self, comp, x):
        return forward(self(comp, x - 1), self(comp, x), self(comp, x + 1), self(comp, x + 2))

    def backward_x(self, comp, x):
        return backward(self(comp, x - 2), self(comp, x - 1), self(comp, x), self(comp, x + 1))


class Bands:
    def __init__(self, lower, upper, tail, head):
        self.lower, self.upper = lower, upper
        self.tail, self.head = tail, head

    def __call__(self, comp, x):
        if self.lower is None:
            return (None, None)
        places = [i for i, (c, _) in enumerate(self.tail) if c == comp]
        before = [self.lower[i, pl.ds(x, 1), :] for i in reversed(places)]
        places = [i for i, (c, _) in enumerate(self.head) if c == comp]
        after = [self.upper[i, pl.ds(x, 1), :] for i in places]
        return (before, after)


def looked_up(labels, table, row, count):
    out = jnp.full(labels.shape, table[row, 0], jnp.float32)
    for k in range(1, count):
        out = jnp.where(labels == k, table[row, k], out)
    return out


def even_strike():
    return lax.axis_index(GX) % 2 == 0


def edge_planes(field, tail, head, first_out, second_out):
    even = even_strike()
    pairs = []
    for i in range(first_out.shape[0]):
        comp, place = tail[min(i, len(tail) - 1)]
        right = field(comp, place % field.count)
        comp, place = head[min(i, len(head) - 1)]
        left = field(comp, place % field.count)
        pairs.append((jnp.where(even, right, left), jnp.where(even, left, right)))
    for i, (one, two) in enumerate(pairs):
        first_out[i] = one
        second_out[i] = two


def fault_row(rows):
    return jnp.where(lax.axis_index(GY) == lax.axis_size(GY) // 2, 0, rows - 1)


def pack_kernel(names, r):
    count, rows, depths = r.stress.shape[1:]
    order = (XZ, YZ, ZZ, XX, XY, YY)
    pairs = [(r.stress.at[c], r.stress_out.at[c]) for c in order]
    pairs += [(getattr(r, key), getattr(r, f"{key}_out")) for key in names]
    copies = []
    for i, (source, out) in enumerate(pairs):
        copy = pltpu.make_async_copy(source, out, r.sems.at[i])
        copy.start()
        copies.append(copy)
    edges = Edges(rows, depths)
    for copy in copies[:3]:
        copy.wait()
    strip = jnp.zeros((rows, depths), jnp.float32)
    for x in range(count):
        strip = edges.packed(strip, x, [r.stress_out[c, x] for c in STRESS_SLOTS])
    set_strip(r, strip)
    for copy in copies[3:5]:
        copy.wait()
    edge_planes(Field(count, r.stress_out), STRESS_TAIL, STRESS_HEAD, r.one_out, r.two_out)
    for copy in copies[5:]:
        copy.wait()


def grouped(xs, size):
    return [xs[i : i + size] for i in range(0, len(xs), size)]


def set_strip(r, strip):
    r.strip_out[0] = strip
    for i in range(1, STRIP_PLANES):
        r.strip_out[i] = jnp.zeros_like(strip)


def unpack(count, r, edges):
    strip = r.strip[0]
    for x in range(count):
        for k in range(3):
            r.ends[x, k] = edges.ends(strip, x, k)


def velocity_across(planes, x):
    return planes.forward_x(XX, x), planes.backward_x(XY, x), planes.backward_x(XZ, x)


def velocity_inner(first, r):
    count, rows, depths = r.material.shape
    edges = Edges(rows, depths)
    planes = Planes(stress_of(count, r), STRESS_TAIL, STRESS_HEAD)
    band = Bands(getattr(r, "lower", None), getattr(r, "upper", None), STRESS_TAIL_Y, STRESS_HEAD_Y)
    unpack(count, r, edges)

    def beside(x):
        ends = [r.ends[x, k] for k in range(3)]
        return (
            edges.backward_y(planes, XY, x, band(XY, x)) + edges.backward_z(planes(XZ, x), ends[0]),
            edges.forward_y(planes, YY, x, band(YY, x)) + edges.backward_z(planes(YZ, x), ends[1]),
            edges.backward_y(planes, YZ, x, band(YZ, x)) + edges.forward_z(planes(ZZ, x), ends[2]),
        )

    def push(x):
        return DT * looked_up(r.material[x], r.table, 2, CLASSES)

    def new(x):
        rates = zip(velocity_across(planes, x), beside(x))
        return [r.velocity[c, x] + push(x) * (a + b) for c, (a, b) in enumerate(rates)]

    for group in grouped(inside(count), 3 if (count - 4) % 3 == 0 else 2):
        for x, values in [(x, new(x)) for x in group]:
            for c in range(3):
                r.inner_out[c, x - 2] = values[c]
    for group in grouped(ends_of(count), 2):
        for x, values in [(x, (*beside(x), push(x))) for x in group]:
            for c in range(4):
                r.part_out[c, ends_of(count).index(x)] = values[c]
    strip = jnp.zeros((rows, depths), jnp.float32)
    for x in inside(count):
        strip = edges.packed(strip, x, [r.inner_out[c, x - 2] for c in VEL_SLOTS])
    r.strip_inner_out[...] = strip

    row = pl.ds(fault_row(rows), 1)
    lines = {}
    for x in inside(count):
        for i, c in enumerate((0, 2)):
            lines[i * count + x] = r.inner_out[c, x - 2, row, :]
    if first:
        for x in range(count):
            labels = r.material[x, row, :]
            lines[2 * count + x] = looked_up(labels, r.table, 2, CLASSES)
    if hasattr(r, "prestress"):
        own = r.normal.shape[0]
        place = 3 * count
        for c in (0, 1):
            for i in range(own):
                lines[place + c * own + i] = r.prestress[i, pl.ds(c, 1), :]
        for j, field in enumerate((r.normal, r.slip, r.zone, r.mask), 2):
            for i in range(own):
                lines[place + j * own + i] = field[pl.ds(i, 1), :].astype(jnp.float32)
    for i, line in lines.items():
        r.face_inner_out[pl.ds(i, 1), :] = line


def velocity_edge(count, r):
    rows, depths = r.one.shape[1:]
    edges = Edges(rows, depths)
    planes = Planes(stress_of(count, r), STRESS_TAIL, STRESS_HEAD, r.one, r.two)
    places = ends_of(count)
    new = []
    for i, x in enumerate(places):
        rates = [a + r.part[c, i] for c, a in enumerate(velocity_across(planes, x))]
        new.append([r.velocity[c, x] + r.part[3, i] * rate for c, rate in enumerate(rates)])
    faces = r.face_inner[...]
    strip = r.strip_inner[...]
    for i, x in enumerate(places):
        strip = edges.packed(strip, x, [new[i][c] for c in VEL_SLOTS])
        for c in range(3):
            r.edge_out[c, i] = new[i][c]
    r.face_out[...] = faces
    set_strip(r, strip)
    fault = fault_row(rows)
    edge = Field(count, None, r.edge_out)
    lines = {i * count + x: edge.rows(c, x)(fault, 1) for x in places for i, c in enumerate((0, 2))}
    for i, line in lines.items():
        r.face_out[pl.ds(i, 1), :] = line
    edge_planes(edge, VEL_TAIL, VEL_HEAD, r.one_out, r.two_out)


def stress_of(count, r):
    if hasattr(r, "stress"):
        return Field(count, r.stress)
    return Field(count, r.stress_inner, r.stress_edge)


def memory_of(count, r):
    if hasattr(r, "memory"):
        return Field(count, r.memory)
    return Field(count, r.memory_inner, r.memory_edge)


def fault_kernel(first, r):
    own_face, other_face = r.face, r.other
    own_first, other_first = (own_face, other_face) if first else (r.face_first, r.other_first)
    rows, depths = r.strip.shape[1:]
    count = r.change_out.shape[1]
    middle = lax.axis_size(GY) // 2
    side = lax.axis_index(GY)
    plus = side == middle
    minus = side == middle - 1

    def pair(own, other, place):
        mine, theirs = own[pl.ds(place, count), :], other[pl.ds(place, count), :]
        return jnp.where(plus, theirs, mine), jnp.where(plus, mine, theirs)

    if hasattr(r, "still"):
        still = r.still
    else:
        still = r.still_out
        share = (own_face.shape[0] - 3 * count) // 6
        for i in range(6):
            mine = own_face[pl.ds(3 * count + i * share, share), :]
            theirs = other_face[pl.ds(3 * count + i * share, share), :]
            still[i, pl.ds(0, share), :] = jnp.where(plus, theirs, mine)
            still[i, pl.ds(share, share), :] = jnp.where(plus, mine, theirs)
    pre_x, pre_z, normal = still[0], still[1], still[2]
    slip = still[3] if first else r.slip[...]
    zone, mask = still[4], still[5]

    row = lax.broadcasted_iota(jnp.int32, (count, depths), 0) + lax.axis_index(GX) * count
    deep = lax.broadcasted_iota(jnp.int32, (count, depths), 1) + lax.axis_index(GZ) * depths
    inside = (row >= r.anchor[0]) & (row < r.anchor[0] + 2 * PATCH)
    inside = inside & (deep >= r.anchor[1]) & (deep < r.anchor[1] + 2 * PATCH)
    dynamic = 0.4 * looked_up(zone, r.friction, 0, ZONES)
    static = jnp.where(
        inside, dynamic, dynamic + 0.5 * looked_up(zone, r.friction, 1, ZONES)
    )
    distance = 0.2 * looked_up(zone, r.friction, 2, ZONES)
    minus_x, plus_x = pair(own_face, other_face, 0)
    minus_z, plus_z = pair(own_face, other_face, count)
    minus_b, plus_b = pair(own_first, other_first, 2 * count)
    bsum = minus_b + plus_b
    trial_x = (plus_x - minus_x) / (DT * bsum) + pre_x
    trial_z = (plus_z - minus_z) / (DT * bsum) + pre_z
    size = jnp.sqrt(trial_x * trial_x + trial_z * trial_z)
    weaken = jnp.minimum(slip / distance, 1.0)
    strength = (static - (static - dynamic) * weaken) * normal
    factor = jnp.where(mask == 1.0, strength / jnp.maximum(size, strength), 1.0)
    new_slip = slip + DT * DT * bsum * (size - size * factor)
    half = r.slip_out.shape[0]
    if half < count:
        new_slip = jnp.where(plus, new_slip[half:], new_slip[:half])
    sign = jnp.where(minus, DT, 0.0) * minus_b - jnp.where(plus, DT, 0.0) * plus_b
    change_x = (trial_x * factor - pre_x) * sign
    change_z = (trial_z * factor - pre_z) * sign

    fault = fault_row(rows)
    on_fault = lax.broadcasted_iota(jnp.int32, (rows, depths), 0) == fault
    even = even_strike()
    still_line = jnp.zeros((1, depths), jnp.float32)

    def line(planes, i):
        comp, place = planes[min(i, len(planes) - 1)]
        at = place % count
        return still_line if comp == 1 else (change_x, change_z)[comp // 2][at : at + 1]

    pairs = []
    for i in range(r.one_out.shape[0]):
        right, left = line(VEL_TAIL, i), line(VEL_HEAD, i)
        one, two = jnp.where(even, right, left), jnp.where(even, left, right)
        one = r.one[i] + jnp.where(on_fault, one, 0.0)
        pairs.append((one, r.two[i] + jnp.where(on_fault, two, 0.0)))
    ends = jnp.zeros((count, depths), jnp.float32)
    pair = lax.broadcasted_iota(jnp.int32, (count, depths), 1) // 2
    place = 4 * lax.broadcasted_iota(jnp.int32, (count, depths), 0)
    upper = lax.axis_index(GZ) == 0
    for k, field in ((0, change_x), (2, change_z)):
        turned = jnp.where(upper, pltpu.roll(field, 2, 1), field)
        turned = pltpu.roll(turned, 2 * k, 1, stride=8, stride_axis=0)
        ends = jnp.where(pair == place + k, turned, ends)
    line = jnp.sum(ends, axis=0, keepdims=True)
    strip = r.strip[0] + jnp.where(on_fault, line, 0.0)

    for i, (one, two) in enumerate(pairs):
        r.one_out[i] = one
        r.two_out[i] = two
    set_strip(r, strip)
    r.slip_out[...] = new_slip
    r.change_out[0] = change_x
    r.change_out[1] = change_z


def elastic_rates(planes, x, beside, lame, shear):
    eyy, ezz, eyz, along_y, along_z = beside
    exx = planes.backward_x(0, x)
    exy = along_y + planes.forward_x(1, x)
    exz = along_z + planes.forward_x(2, x)
    bulk = lame * (exx + eyy + ezz)
    double = 2.0 * shear
    return (
        bulk + double * exx,
        bulk + double * eyy,
        bulk + double * ezz,
        shear * exy,
        shear * exz,
        shear * eyz,
    )


def stress_new(x, elastic, decay, gain, stress, memory):
    kept = [decay * memory(c, x) - gain * elastic[c] for c in range(6)]
    return [stress(c, x) + DT * (elastic[c] + kept[c]) for c in range(6)], kept


def stress_inner(last, r):
    count, rows, depths = r.material.shape
    edges = Edges(rows, depths, by_loads=True)
    on_fault = edges.row == fault_row(rows)
    free = Field(count, r.inner, r.edge)
    for x in range(count):
        for c in (0, 2):
            line = r.change[c // 2, pl.ds(x, 1), :]
            r.velocity_out[c, x] = free(c, x) + jnp.where(on_fault, line, 0.0)
        r.velocity_out[1, x] = free(1, x)
    planes = Planes(Field(count, r.velocity_out), VEL_TAIL, VEL_HEAD)
    copies = []

    def copy_out(source, out):
        copy = pltpu.make_async_copy(source, out, r.sems.at[len(copies)])
        copy.start()
        copies.append(copy)

    if last:
        copy_out(r.velocity_out, r.new_velocity_out)
        if hasattr(r, "slip"):
            copy_out(r.slip, r.new_slip_out)
        stress_out, memory_out = r.stress_held, r.memory_held
    else:
        stress_out, memory_out = r.stress_inner_out, r.memory_inner_out

    def write(x, new, kept):
        for c in range(6):
            stress_out[c, x - 2] = new[c]
            memory_out[c, x - 2] = kept[c]
        if last and x % 2 == 1:
            held, out = pl.ds(x - 3, 2), pl.ds(x - 1, 2)
            copy_out(stress_out.at[:, held], r.stress_out.at[:, out])
            copy_out(memory_out.at[:, held], r.memory_out.at[:, out])

    band = Bands(getattr(r, "lower", None), getattr(r, "upper", None), VEL_TAIL_Y, VEL_HEAD_Y)
    stress, memory = stress_of(count, r), memory_of(count, r)
    unpack(count, r, edges)

    def beside(x):
        in_x, in_y, in_z = [r.ends[x, k] for k in range(3)]
        return (
            edges.backward_y(planes, 1, x, band(1, x)),
            edges.backward_z(planes(2, x), in_z),
            edges.forward_z(planes(1, x), in_y) + edges.forward_y(planes, 2, x, band(2, x)),
            edges.forward_y(planes, 0, x, band(0, x)),
            edges.forward_z(planes(0, x), in_x),
        )

    def moduli(x):
        return [looked_up(r.material[x], r.table, i, CLASSES) for i in (0, 1)]

    def fading(x):
        labels = r.material[x]
        decay = jnp.exp(-DT / looked_up(labels, r.table, 3, CLASSES))
        return decay, (1.0 - decay) * (0.3 * looked_up(labels, r.table, 4, CLASSES))

    for group in grouped(inside(count), 2):
        for x, elastic in [(x, elastic_rates(planes, x, beside(x), *moduli(x))) for x in group]:
            write(x, *stress_new(x, elastic, *fading(x), stress, memory))
    for group in grouped(ends_of(count), 2):
        for x, values in [(x, (*beside(x), *moduli(x), *fading(x))) for x in group]:
            for c in range(9):
                r.part_out[c, ends_of(count).index(x)] = values[c]
    if last:
        for copy in copies:
            copy.wait()
    else:
        strip = jnp.zeros((rows, depths), jnp.float32)
        for x in inside(count):
            strip = edges.packed(strip, x, [r.stress_inner_out[c, x - 2] for c in STRESS_SLOTS])
        r.strip_inner_out[...] = strip


def stress_edge(count, last, r):
    rows, depths = r.one.shape[1:]
    edges = Edges(rows, depths)
    planes = Planes(Field(count, r.velocity), VEL_TAIL, VEL_HEAD, r.one, r.two)
    places = ends_of(count)
    stress, memory = stress_of(count, r), memory_of(count, r)
    copies = []

    def copy_out(source, out, span):
        copy = pltpu.make_async_copy(source, out.at[:, span], r.sems.at[len(copies)])
        copy.start()
        copies.append(copy)

    if last:
        stress_out, memory_out = r.stress_held, r.memory_held
    else:
        stress_out, memory_out = r.stress_edge_out, r.memory_edge_out

    def elastic(i, x):
        part = [r.part[c, i] for c in range(7)]
        return elastic_rates(planes, x, part[:5], *part[5:])

    for group in grouped(list(enumerate(places)), 2):
        for (i, x), rates in [(at, elastic(*at)) for at in group]:
            new, kept = stress_new(x, rates, r.part[7, i], r.part[8, i], stress, memory)
            for c in range(6):
                stress_out[c, i] = new[c]
                memory_out[c, i] = kept[c]
        if last:
            held, span = pl.ds(group[0][0], 2), pl.ds(group[0][1], 2)
            copy_out(stress_out.at[:, held], r.stress_out, span)
            copy_out(memory_out.at[:, held], r.memory_out, span)
    if last:
        for copy in copies:
            copy.wait()
    else:
        strip = r.strip_inner[...]
        for i, x in enumerate(places):
            strip = edges.packed(strip, x, [stress_out[c, i] for c in STRESS_SLOTS])
        set_strip(r, strip)
        edge = Field(count, None, stress_out)
        edge_planes(edge, STRESS_TAIL, STRESS_HEAD, r.one_out, r.two_out)


SCALARS = ("table", "friction", "anchor")


def call(kernel, name, ins, outs, scratch=None, apart=(), onto=(), micros=1, vmem=6):
    scratch = scratch or {}
    names = [*ins, *(f"{key}_out" for key in outs), *scratch]

    def body(*refs):
        kernel(types.SimpleNamespace(**dict(zip(names, refs))))

    def place(key):
        if key in apart:
            return pl.BlockSpec(memory_space=pltpu.HBM)
        return pl.BlockSpec(memory_space=pltpu.SMEM if key in SCALARS else pltpu.VMEM)

    shapes = [
        shape if hasattr(shape, "dtype") else jax.ShapeDtypeStruct(shape, jnp.float32)
        for shape in outs.values()
    ]
    result = pl.pallas_call(
        body,
        out_shape=shapes,
        in_specs=[place(key) for key in ins],
        out_specs=[place(f"{key}_out") for key in outs],
        scratch_shapes=list(scratch.values()),
        name=name,
        input_output_aliases={
            list(ins).index(key): list(outs).index(onto[key]) for key in onto
        },
        cost_estimate=pl.CostEstimate(
            flops=0, bytes_accessed=micros * 3_690_000, transcendentals=0
        ),
        compiler_params=pltpu.CompilerParams(vmem_limit_bytes=vmem * 2**20),
    )(*ins.values())
    return dict(zip(outs, result))


def along(axis, count, skip=()):
    up = [(i, i + 1) for i in range(count - 1) if i not in skip]
    return (axis, up), (axis, [(b, a) for a, b in up])


def strike_swaps(count):
    halves = lax.axis_size(GZ)
    routes = []
    for start in (0, 1):
        partner = {}
        for i in range(start, count - 1, 2):
            for half in range(halves):
                one, other = i * halves + half, (i + 1) * halves + half
                partner[one], partner[other] = other, one
        for i in range(count * halves):
            partner.setdefault(i, i ^ 1)
        routes.append(((GX, GZ), sorted(partner.items())))
    return routes


def sent(block, route):
    return lax.ppermute(block, *route)


def whole(parts, name):
    if name in parts:
        return parts[name]
    inner, edge = parts[f"{name}_inner"], parts[f"{name}_edge"]
    return jnp.concatenate([edge[:, :2], inner, edge[:, 2:]], axis=1)


def edge_rows(field, rows):
    count = field.shape[2]
    return jnp.stack([field[c, :, place % count, :] for c, place in rows])


def shards(
    velocity,
    stress,
    memory,
    material,
    material_table,
    fault_mask,
    zone_label,
    patch_anchor,
    friction_table,
    prestress,
    normal_stress,
    slip_path,
):
    _, count, rows, depths = velocity.shape
    sides = lax.axis_size(GY)
    middle = sides // 2
    banded = sides > 2
    swaps = strike_swaps(lax.axis_size(GX))
    up_y, down_y = along(GY, sides, (middle - 1,))
    across = (GY, [(middle - 1, middle), (middle, middle - 1)])
    deep = (GZ, [(0, 1), (1, 0)])

    plane = (rows, depths)
    edge_shape = (max(len(STRESS_TAIL), len(STRESS_HEAD)), *plane)
    travelling = {"one": edge_shape, "two": edge_shape, "strip": (STRIP_PLANES, *plane)}
    inner, edge = (count - 4, *plane), (4, *plane)
    ends = {"ends": pltpu.VMEM((count, 3, *plane), jnp.float32)}

    def travelled(packed):
        two = sent(packed["two"], swaps[1])
        one = sent(packed["one"], swaps[0])
        strip = sent(packed["strip"], deep)
        return {"strip": strip}, {"one": one, "two": two}

    def bands(field, tail, head):
        if not banded:
            return {}
        lower, upper = edge_rows(field, tail), edge_rows(field, head)
        return {"lower": sent(lower, up_y), "upper": sent(upper, down_y)}

    if banded:
        still = jnp.stack(
            [
                prestress[:, 0],
                prestress[:, 1],
                normal_stress,
                slip_path,
                zone_label.astype(jnp.float32),
                fault_mask.astype(jnp.float32),
            ]
        )
        still = {"still": lax.all_gather(still, GY, axis=1, tiled=True)}
    else:
        still = {}

    held = {"velocity": velocity, "material": material}
    if not banded:
        held.update(prestress=prestress, normal=normal_stress, slip=slip_path)
        held.update(zone=zone_label, mask=fault_mask)
    ins = {"stress": stress, **held}
    packed = call(
        functools.partial(pack_kernel, list(held)),
        "pack",
        {key: pltpu.with_memory_space_constraint(a, pltpu.HBM) for key, a in ins.items()},
        {**travelling, **{key: jax.ShapeDtypeStruct(a.shape, a.dtype) for key, a in ins.items()}},
        scratch={"sems": pltpu.SemaphoreType.DMA((6 + len(held),))},
        apart=list(ins),
    )
    velocity = packed["velocity"]
    parts = {"stress": packed["stress"], "memory": memory}
    props = {"material": packed["material"], "table": material_table}
    friction_ins = {key: packed[key] for key in held if key not in ("velocity", "material")}
    for step in range(STEPS):
        first, last = step == 0, step == STEPS - 1
        held_stress = {key: parts[key] for key in parts if key.startswith("stress")}
        strip, halos = travelled(packed)
        ins = {"velocity": velocity, **held_stress, **props, **strip}
        if banded:
            ins.update(bands(whole(parts, "stress"), STRESS_TAIL_Y, STRESS_HEAD_Y))
        face_rows = 2 * count
        if first:
            face_rows += count
            if not banded:
                ins.update(friction_ins)
                face_rows += 6 * normal_stress.shape[0]
        outs = {"inner": (3, *inner), "part": (4, *edge), "strip_inner": plane}
        outs["face_inner"] = (face_rows, depths)
        free = call(
            functools.partial(velocity_inner, first),
            "velocity_inner",
            ins,
            outs,
            scratch=ends,
            micros=3,
        )
        ins = {"velocity": velocity, **held_stress, **halos}
        ins.update({key: free[key] for key in outs if key != "inner"})
        packed = call(
            functools.partial(velocity_edge, count),
            "velocity_edge",
            ins,
            {"edge": (3, *edge), "face": (face_rows, depths), **travelling},
        )
        free = {"inner": free["inner"], "edge": packed["edge"]}
        face = packed["face"]
        other = sent(face, across)
        ins = {key: packed[key] for key in travelling}
        ins.update(face=face, other=other, friction=friction_table, anchor=patch_anchor, **still)
        if first:
            faces = {"face_first": face, "other_first": other}
        else:
            ins.update(slip=slip, **faces)
        outs = {"change": (2, count, depths), "slip": (count, depths), **travelling}
        if last and not banded:
            outs["slip"] = (count // sides, depths)
        if not still:
            outs["still"] = (6, count, depths)
        packed = call(functools.partial(fault_kernel, first), "fault", ins, outs, vmem=2)
        slip = packed["slip"]
        if not still:
            still = {"still": packed["still"]}
        strip, halos = travelled(packed)
        ins = {**free, "change": packed["change"], **parts, **props, **strip}
        if banded:
            joined = jnp.concatenate(
                [free["edge"][:, :2], free["inner"], free["edge"][:, 2:]], axis=1
            )
            band = bands(joined, VEL_TAIL_Y, VEL_HEAD_Y)
        else:
            band = {}
        outs = {"velocity": velocity.shape, "part": (9, *edge)}
        extra = {"scratch": ends}
        if last:
            outs.update(new_velocity=velocity.shape, stress=stress.shape, memory=memory.shape)
            extra["apart"] = ["new_velocity_out", "stress_out", "memory_out"]
            if not banded:
                ins["slip"] = slip
                outs["new_slip"] = slip.shape
                extra["apart"].append("new_slip_out")
            held = pltpu.VMEM((6, *inner), jnp.float32)
            sems = pltpu.SemaphoreType.DMA((count,))
            extra["scratch"] = {"stress_held": held, "memory_held": held, "sems": sems, **ends}
        else:
            outs.update(stress_inner=(6, *inner), memory_inner=(6, *inner), strip_inner=plane)
        done = call(
            functools.partial(stress_inner, last),
            "stress_inner",
            {**ins, **band},
            outs,
            micros=3,
            vmem=11,
            **extra,
        )
        velocity = done["velocity"]
        ins = {"velocity": velocity, "part": done["part"], **parts, **halos}
        if last:
            ins.update(stress_done=done["stress"], memory_done=done["memory"])
            held = pltpu.VMEM((6, *edge), jnp.float32)
            packed = call(
                functools.partial(stress_edge, count, last),
                "stress_edge",
                ins,
                {"stress": stress.shape, "memory": memory.shape},
                scratch={
                    "stress_held": held,
                    "memory_held": held,
                    "sems": pltpu.SemaphoreType.DMA((4,)),
                },
                apart=("stress_done", "memory_done", "stress_out", "memory_out"),
                onto={"stress_done": "stress", "memory_done": "memory"},
                vmem=10,
            )
            velocity = done["new_velocity"]
            stress, memory = packed["stress"], packed["memory"]
            slip = done.get("new_slip", slip)
        else:
            ins["strip_inner"] = done["strip_inner"]
            packed = call(
                functools.partial(stress_edge, count, last),
                "stress_edge",
                ins,
                {"stress_edge": (6, *edge), "memory_edge": (6, *edge), **travelling},
                vmem=10,
            )
            parts = {
                "stress_inner": done["stress_inner"],
                "stress_edge": packed["stress_edge"],
                "memory_inner": done["memory_inner"],
                "memory_edge": packed["memory_edge"],
            }
    if banded:
        held = jnp.where(lax.axis_index(GY) == middle, slip, 0.0)
        slip = lax.psum_scatter(held, GY, scatter_dimension=0, tiled=True)
    return (velocity, stress, memory, slip)


def solution(mesh):
    in_specs = (
        P(None, (ENS, GX), GY, GZ),
        P(None, (ENS, GX), GY, GZ),
        P(None, (ENS, GX), GY, GZ),
        P((ENS, GX), GY, GZ),
        P(None, ENS),
        P((ENS, GX, GY), GZ),
        P((ENS, GX, GY), GZ),
        P(ENS),
        P(None, ENS),
        P((ENS, GX, GY), None, GZ),
        P((ENS, GX, GY), GZ),
        P((ENS, GX, GY), GZ),
    )
    out_specs = (
        P(None, (ENS, GX), GY, GZ),
        P(None, (ENS, GX), GY, GZ),
        P(None, (ENS, GX), GY, GZ),
        P((ENS, GX, GY), GZ),
    )
    return jax.shard_map(shards, mesh=mesh, in_specs=in_specs, out_specs=out_specs, check_vma=False)
```
